32 devices in a mesh: dp: 8 (over y, x, core), chan: 4 (over z).
Axes of the slice: x: 2, y: 2, z: 4, core: 2. Of those that a mesh axis runs over, the one named last changes fastest.
Arguments:
- slow_input: bfloat16 [24, 8, 14, 14, 1024], P('dp', None, None, None, 'chan'), may hold values from -6 to 6
- fast_input: bfloat16 [24, 32, 14, 14, 128], P('dp', None, None, None, 'chan'), may hold values from -6 to 6
- clip_counts: int32 [8], replicated, may hold values from 1 to 3, as said below
- frame_counts: int32 [24], replicated, may hold values from 1 to 8, as said below
- fast_reduce: float32 [3, 128, 32], replicated, may hold values from -0.3125 to 0.3125
- fast_spatial: float32 [3, 3, 32, 32], replicated, may hold values from -0.375 to 0.375
- fast_expand: float32 [32, 128], replicated, may hold values from -1 to 1
- lateral_kernel: float32 [5, 128, 256], P(None, None, 'chan'), may hold values from -0.25 to 0.25
- slow_reduce: float32 [3, 1024, 256], P(None, None, 'chan'), may hold values from -0.09375 to 0.09375
- lateral_reduce: float32 [3, 256, 256], P(None, None, 'chan'), may hold values from -0.09375 to 0.09375
- slow_spatial: float32 [3, 3, 256, 256], P(None, None, None, 'chan'), may hold values from -0.125 to 0.125
- slow_expand: float32 [256, 1024], P('chan'), may hold values from -0.375 to 0.375
- shortcut: float32 [1024, 1024], P('chan'), may hold values from -0.15625 to 0.15625
- lateral_shortcut: float32 [256, 1024], P('chan'), may hold values from -0.15625 to 0.15625
- fast_inner_norm: float32 [2, 2, 32], replicated, may hold values from 0.4 to 1.4
- fast_outer_norm: float32 [2, 128], replicated, may hold values from 0.4 to 1.4
- lateral_norm: float32 [2, 256], P(None, 'chan'), may hold values from 0.4 to 1.4
- slow_inner_norm: float32 [2, 2, 256], P(None, None, 'chan'), may hold values from 0.4 to 1.4
- slow_outer_norm: float32 [2, 2, 1024], P(None, None, 'chan'), may hold values from 0.4 to 1.4
- slow_cotangent: bfloat16 [24, 8, 14, 14, 1024], P('dp', None, None, None, 'chan'), may hold values from -6 to 6
- fast_cotangent: bfloat16 [24, 32, 14, 14, 128], P('dp', None, None, None, 'chan'), may hold values from -6 to 6
Outputs:
- slow_output: bfloat16 [24, 8, 14, 14, 1024], P('dp', None, None, None, 'chan')
- fast_output: bfloat16 [24, 32, 14, 14, 128], P('dp', None, None, None, 'chan')
- slow_input_grad: bfloat16 [24, 8, 14, 14, 1024], P('dp', None, None, None, 'chan')
- fast_input_grad: bfloat16 [24, 32, 14, 14, 128], P('dp', None, None, None, 'chan')
- fast_reduce_grad: float32 [3, 128, 32], replicated
- fast_spatial_grad: float32 [3, 3, 32, 32], replicated
- fast_expand_grad: float32 [32, 128], replicated
- lateral_kernel_grad: float32 [5, 128, 256], P(None, None, 'chan')
- slow_reduce_grad: float32 [3, 1024, 256], P(None, None, 'chan')
- lateral_reduce_grad: float32 [3, 256, 256], P(None, None, 'chan')
- slow_spatial_grad: float32 [3, 3, 256, 256], P(None, None, None, 'chan')
- slow_expand_grad: float32 [256, 1024], P('chan')
- shortcut_grad: float32 [1024, 1024], P('chan')
- lateral_shortcut_grad: float32 [256, 1024], P('chan')
- fast_inner_norm_grad: float32 [2, 2, 32], replicated
- fast_outer_norm_grad: float32 [2, 128], replicated
- lateral_norm_grad: float32 [2, 256], P(None, 'chan')
- slow_inner_norm_grad: float32 [2, 2, 256], P(None, None, 'chan')
- slow_outer_norm_grad: float32 [2, 2, 1024], P(None, None, 'chan')
The draws below stay inside these ranges and needn't reach their ends.
Inputs may be any that keep to these rules, and one draw needn't show every extreme that they name: `clip_counts`: some index of dp holds 3 clips; the clips of an index are its first slots. `frame_counts`: the valid frames of a clip are its first ones; the first slot of every index of dp has 8.
All inputs are finite; a program needn't handle non-finite values.
Results may differ from the reference program's by a relative error of at most 0.024.
Values may be sent and summed in bfloat16 or wider, within the bound.
No kernel may reach another device: no remote copies, remote signals or barrier semaphores. Data moves between devices by JAX's collectives and lax.ppermute only.
A program may use at most 448 MiB of HBM per device.

```python
from functools import partial
import jax
import jax.numpy as jnp
from jax import lax

SC = 1024
LAT = 256
SM = 256
FC = 128
FM = 32
SIDE = 14
SLOW_T = 8
CLIPS_DEV = 3
FAST_T = 32
CLIPS = 24


def draw_clip_counts(key, part):
    key = jax.random.fold_in(key, 11)
    groups = CLIPS // CLIPS_DEV
    shifts = jax.random.randint(jax.random.fold_in(key, 1), (groups,), 0, 4)
    counts = jnp.maximum(jnp.right_shift(jnp.full((groups,), CLIPS_DEV, jnp.int32), shifts), 1)
    busiest = jax.random.randint(jax.random.fold_in(key, 2), (), 0, groups)
    return counts.at[busiest].set(CLIPS_DEV).astype(jnp.int32)


def draw_frame_counts(key, part):
    key = jax.random.fold_in(key, 23)
    frames = jax.random.randint(key, (CLIPS,), 1, SLOW_T + 1)
    first_slot = jnp.arange(CLIPS) % CLIPS_DEV == 0
    return jnp.where(first_slot, SLOW_T, frames).astype(jnp.int32)


def level_of(rng, extent, cuts, low, largest):
    loudness, own = 1.0, jax.random.fold_in(rng, 6)
    for dim, blocks in cuts:
        heights = jnp.exp(jax.random.uniform(jax.random.fold_in(own, dim), (blocks,), jnp.float32, low / len(cuts), largest / len(cuts)))
        loudness = loudness * jnp.repeat(heights, extent[dim] // blocks).reshape([-1 if axis == dim else 1 for axis in range(len(extent))])
    return loudness


def normal_values(key, extent, scale, bound, pieces=(), kind=jnp.bfloat16):
    loudness = level_of(key, extent, pieces, -0.22, 0.18) if pieces else 1.0
    array = jax.random.normal(key, extent, jnp.float32) * scale * loudness
    return jnp.minimum(jnp.maximum(array, -bound), bound).astype(kind)


def setup_inputs(seed: int = 0) -> dict:
    streams_of = jax.random.split(jax.random.key(seed), 22)
    slow_input = normal_values(streams_of[0], (CLIPS, SLOW_T, SIDE, SIDE, SC), 1.0, 6.0, ((0, 8), (4, 4)))
    fast_input = normal_values(streams_of[1], (CLIPS, FAST_T, SIDE, SIDE, FC), 1.0, 6.0, ((0, 8), (4, 4)))
    clip_counts = draw_clip_counts(jax.random.fold_in(streams_of[21], 71), 0)
    frame_counts = draw_frame_counts(jax.random.fold_in(streams_of[21], 71), 0)
    fast_reduce = normal_values(streams_of[4], (3, FC, FM), (3 * FC) ** -0.5, 0.3125, (), jnp.float32)
    fast_spatial = normal_values(streams_of[5], (3, 3, FM, FM), (9 * FM) ** -0.5, 0.375, (), jnp.float32)
    fast_expand = normal_values(streams_of[6], (FM, FC), FM ** -0.5, 1.0, (), jnp.float32)
    lateral_kernel = normal_values(streams_of[7], (5, FC, LAT), (5 * FC) ** -0.5, 0.25, ((2, 4),), jnp.float32)
    slow_reduce = normal_values(streams_of[8], (3, SC, SM), (3 * (SC + LAT)) ** -0.5, 0.09375, ((2, 4),), jnp.float32)
    lateral_reduce = normal_values(streams_of[9], (3, LAT, SM), (3 * (SC + LAT)) ** -0.5, 0.09375, ((2, 4),), jnp.float32)
    slow_spatial = normal_values(streams_of[10], (3, 3, SM, SM), (9 * SM) ** -0.5, 0.125, ((3, 4),), jnp.float32)
    slow_expand = normal_values(streams_of[11], (SM, SC), SM ** -0.5, 0.375, ((0, 4),), jnp.float32)
    shortcut = normal_values(streams_of[12], (SC, SC), (SC + LAT) ** -0.5, 0.15625, ((0, 4),), jnp.float32)
    lateral_shortcut = normal_values(streams_of[13], (LAT, SC), (SC + LAT) ** -0.5, 0.15625, ((0, 4),), jnp.float32)
    fast_inner_norm = jnp.clip(jax.random.uniform(streams_of[14], (2, 2, FM), jnp.float32, 0.4, 1.4), 0.4, 1.4)
    fast_outer_norm = jnp.clip(jax.random.uniform(streams_of[15], (2, FC), jnp.float32, 0.4, 1.4), 0.4, 1.4)
    lateral_norm = jnp.clip(0.4 + 1 * jax.random.uniform(streams_of[16], (2, LAT), jnp.float32) ** level_of(streams_of[16], (2, LAT), ((1, 4),), -0.2, 0.2), 0.4, 1.4)
    slow_inner_norm = jnp.clip(0.4 + 1 * jax.random.uniform(streams_of[17], (2, 2, SM), jnp.float32) ** level_of(streams_of[17], (2, 2, SM), ((2, 4),), -0.2, 0.2), 0.4, 1.4)
    slow_outer_norm = jnp.clip(0.4 + 1 * jax.random.uniform(streams_of[18], (2, 2, SC), jnp.float32) ** level_of(streams_of[18], (2, 2, SC), ((2, 4),), -0.2, 0.2), 0.4, 1.4)
    slow_cotangent = normal_values(streams_of[19], (CLIPS, SLOW_T, SIDE, SIDE, SC), 1.0, 6.0, ((0, 8), (4, 4)))
    fast_cotangent = normal_values(streams_of[20], (CLIPS, FAST_T, SIDE, SIDE, FC), 1.0, 6.0, ((0, 8), (4, 4)))
    return dict(slow_input=slow_input, fast_input=fast_input, clip_counts=clip_counts, frame_counts=frame_counts, fast_reduce=fast_reduce, fast_spatial=fast_spatial, fast_expand=fast_expand, lateral_kernel=lateral_kernel, slow_reduce=slow_reduce, lateral_reduce=lateral_reduce, slow_spatial=slow_spatial, slow_expand=slow_expand, shortcut=shortcut, lateral_shortcut=lateral_shortcut, fast_inner_norm=fast_inner_norm, fast_outer_norm=fast_outer_norm, lateral_norm=lateral_norm, slow_inner_norm=slow_inner_norm, slow_outer_norm=slow_outer_norm, slow_cotangent=slow_cotangent, fast_cotangent=fast_cotangent)


EPSILON = 1e-05
HIGHEST = lax.Precision.HIGHEST

@jax.custom_vjp
def low(v):
    return lax.optimization_barrier(v.astype(jnp.bfloat16)).astype(jnp.float32)

@jax.custom_vjp
def low_back(v):
    return v

def low_keep(v):
    return (low(v), None)

def low_pass(kept, grad):
    return (grad,)

def back_keep(v):
    return (v, None)

def back_low(kept, grad):
    return (low(grad),)
low.defvjp(low_keep, low_pass)
low_back.defvjp(back_keep, back_low)

def gelu_tanh(value):
    return jax.nn.gelu(value, approximate=True)

def apply_mix(source, kernel):
    return jnp.einsum('cthwi,io->cthwo', source, kernel, precision=HIGHEST)

def temporal(source, kernel):
    half_width = kernel.shape[0] // 2
    length = source.shape[1]
    padded = jnp.pad(source, ((0, 0), (half_width, half_width), (0, 0), (0, 0), (0, 0)))
    summed = apply_mix(padded[:, 0:length], kernel[0])
    for offset in range(1, kernel.shape[0]):
        summed = summed + apply_mix(padded[:, offset:offset + length], kernel[offset])
    return summed

def spatial(source, kernel):
    height, across = (source.shape[2], source.shape[3])
    padded = jnp.pad(source, ((0, 0), (0, 0), (1, 1), (1, 1), (0, 0)))
    summed = apply_mix(padded[:, :, 0:height, 0:across], kernel[0, 0])
    for row_step in range(3):
        for col_step in range(3):
            if row_step + col_step > 0:
                summed = summed + apply_mix(padded[:, :, row_step:row_step + height, col_step:col_step + across], kernel[row_step, col_step])
    return summed

def lateral(source, kernel, step_ratio):
    frames = source.shape[1] // step_ratio
    padded = jnp.pad(source, ((0, 0), (2, 2), (0, 0), (0, 0), (0, 0)))
    summed = apply_mix(padded[:, 0:step_ratio * frames:step_ratio], kernel[0])
    for offset in range(1, kernel.shape[0]):
        summed = summed + apply_mix(padded[:, offset:offset + step_ratio * frames:step_ratio], kernel[offset])
    return summed

def batch_norm(values, live_mask, voxels, gain, bias):
    first_sum = lax.optimization_barrier(jnp.sum(values * live_mask, axis=(0, 1, 2, 3)))
    square_sum = lax.optimization_barrier(jnp.sum(values * values * live_mask, axis=(0, 1, 2, 3)))
    center = first_sum / voxels
    spread = square_sum / voxels - center * center
    return (values - center) * lax.rsqrt(spread + EPSILON) * gain + bias

def block_forward(masks, params):
    mask_slow, mask_fast, voxels_slow, voxels_fast, step_ratio = masks
    slow_input, fast_input, fast_reduce, fast_spatial, fast_expand, lateral_kernel, slow_reduce, lateral_reduce, slow_spatial, slow_expand, shortcut, lateral_shortcut, fast_inner_norm, fast_outer_norm, lateral_norm, slow_inner_norm, slow_outer_norm = params
    slow_x = slow_input * mask_slow
    fast_x = fast_input * mask_fast
    fast_reduced = low_back(temporal(fast_x, low(fast_reduce)))
    fast_hidden = low(gelu_tanh(batch_norm(fast_reduced, mask_fast, voxels_fast, fast_inner_norm[0, 0], fast_inner_norm[0, 1])) * mask_fast)
    fast_spread = low_back(spatial(fast_hidden, low(fast_spatial)))
    fast_second = low(gelu_tanh(batch_norm(fast_spread, mask_fast, voxels_fast, fast_inner_norm[1, 0], fast_inner_norm[1, 1])) * mask_fast)
    fast_widened = low_back(apply_mix(fast_second, low(fast_expand)))
    fast_total = batch_norm(fast_widened, mask_fast, voxels_fast, fast_outer_norm[0], fast_outer_norm[1]) + fast_x
    fast_output = gelu_tanh(fast_total) * mask_fast
    lateral_raw = low_back(lateral(fast_x, low(lateral_kernel), step_ratio))
    lateral_hidden = low(gelu_tanh(batch_norm(lateral_raw, mask_slow, voxels_slow, lateral_norm[0], lateral_norm[1])) * mask_slow)
    slow_reduced = low_back(temporal(slow_x, low(slow_reduce)) + temporal(lateral_hidden, low(lateral_reduce)))
    slow_hidden = low(gelu_tanh(batch_norm(slow_reduced, mask_slow, voxels_slow, slow_inner_norm[0, 0], slow_inner_norm[0, 1])) * mask_slow)
    slow_spread = low_back(spatial(slow_hidden, low(slow_spatial)))
    slow_second = low(gelu_tanh(batch_norm(slow_spread, mask_slow, voxels_slow, slow_inner_norm[1, 0], slow_inner_norm[1, 1])) * mask_slow)
    slow_widened = low_back(apply_mix(slow_second, low(slow_expand)))
    slow_bypass = low_back(apply_mix(slow_x, low(shortcut)) + apply_mix(lateral_hidden, low(lateral_shortcut)))
    slow_total = batch_norm(slow_widened, mask_slow, voxels_slow, slow_outer_norm[0, 0], slow_outer_norm[0, 1])
    slow_total = slow_total + batch_norm(slow_bypass, mask_slow, voxels_slow, slow_outer_norm[1, 0], slow_outer_norm[1, 1])
    slow_output = gelu_tanh(slow_total) * mask_slow
    return (slow_output, fast_output)

def reference(slow_input, fast_input, clip_counts, frame_counts, fast_reduce, fast_spatial, fast_expand, lateral_kernel, slow_reduce, lateral_reduce, slow_spatial, slow_expand, shortcut, lateral_shortcut, fast_inner_norm, fast_outer_norm, lateral_norm, slow_inner_norm, slow_outer_norm, slow_cotangent, fast_cotangent):
    clips = slow_input.shape[0]
    slow_frames = slow_input.shape[1]
    fast_frames = fast_input.shape[1]
    step_ratio = fast_frames // slow_frames
    cells = slow_input.shape[2] * slow_input.shape[3]
    clip_ids = jnp.arange(clips, dtype=jnp.int32)
    held_all = jnp.repeat(clip_counts, CLIPS_DEV)
    live_all = clip_ids % CLIPS_DEV < held_all
    slow_live = live_all[:, None] & (jnp.arange(slow_frames, dtype=jnp.int32)[None, :] < frame_counts[:, None])
    fast_live = live_all[:, None] & ((jnp.arange(fast_frames, dtype=jnp.int32) // step_ratio)[None, :] < frame_counts[:, None])
    mask_slow = slow_live.astype(jnp.float32)[:, :, None, None, None]
    mask_fast = fast_live.astype(jnp.float32)[:, :, None, None, None]
    voxels_slow = jnp.sum(mask_slow) * cells
    voxels_fast = jnp.sum(mask_fast) * cells
    masks = (mask_slow, mask_fast, voxels_slow, voxels_fast, step_ratio)
    params = (slow_input.astype(jnp.float32), fast_input.astype(jnp.float32), fast_reduce, fast_spatial, fast_expand, lateral_kernel, slow_reduce, lateral_reduce, slow_spatial, slow_expand, shortcut, lateral_shortcut, fast_inner_norm, fast_outer_norm, lateral_norm, slow_inner_norm, slow_outer_norm)
    outputs, pullback = jax.vjp(partial(block_forward, masks), params)
    grads = pullback((slow_cotangent.astype(jnp.float32), fast_cotangent.astype(jnp.float32)))[0]
    return (outputs[0].astype(jnp.bfloat16), outputs[1].astype(jnp.bfloat16), grads[0].astype(jnp.bfloat16), grads[1].astype(jnp.bfloat16), grads[2], grads[3], grads[4], grads[5], grads[6], grads[7], grads[8], grads[9], grads[10], grads[11], grads[12], grads[13], grads[14], grads[15], grads[16])
```

```python
import functools

import jax
import jax.numpy as jnp
from jax import lax
from jax.experimental import pallas as pl
from jax.experimental.pallas import tpu as pltpu
from jax.sharding import PartitionSpec as P

F32 = jnp.float32
BF16 = jnp.bfloat16
EPSILON = 1e-05
ROOT = 0.7978845608028654
CUBIC = 0.044715
BIG = 49
SMALL = 7


def gelu(v):
    return 0.5 * v * (1.0 + jnp.tanh(ROOT * (v * (1.0 + CUBIC * (v * v)))))


def gelu_slope(v):
    square = v * v
    th = jnp.tanh(ROOT * (v * (1.0 + CUBIC * square)))
    half = 0.5 * (1.0 + th)
    return half + (0.5 * ROOT) * v * (1.0 - th * th) * (1.0 + 3.0 * CUBIC * square)


def gelu_pair(v):
    square = v * v
    th = jnp.tanh(ROOT * (v * (1.0 + CUBIC * square)))
    half = 0.5 * (1.0 + th)
    slope = half + (0.5 * ROOT) * v * (1.0 - th * th) * (1.0 + 3.0 * CUBIC * square)
    return v * half, slope


def rows(v):
    return v.reshape(v.shape[0] * v.shape[1], v.shape[2])


def cells(v):
    return v.reshape(v.shape[0] // 8, 8, v.shape[1])


def rows_bf(v):
    return rows(v.astype(F32)).astype(BF16)


def wide(mask, width):
    repeats = width // 128
    return mask if repeats == 1 else jnp.concatenate([mask] * repeats, axis=-1)


def nn(a, b):
    return jnp.dot(a, b, preferred_element_type=F32)


def nt(a, b):
    return lax.dot_general(a, b, (((1,), (1,)), ((), ())), preferred_element_type=F32)


def later(v):
    rolled = pltpu.roll(v, 1, 1)
    return jnp.where(lax.broadcasted_iota(jnp.int32, v.shape, 1) == 0, 0.0, rolled)


def sooner(v):
    rolled = pltpu.roll(v, 7, 1)
    return jnp.where(lax.broadcasted_iota(jnp.int32, v.shape, 1) == 7, 0.0, rolled)


def folded(v):
    out = []
    for block in range(v.shape[-1] // 128):
        part = v[:, 128 * block : 128 * block + 128]
        part = part + pltpu.roll(part, 64, 1)
        out.append(part + pltpu.roll(part, 32, 1))
    return out[0] if len(out) == 1 else jnp.concatenate(out, axis=-1)


def scale_of(sums, gains, inv_n):
    center = sums[0:1] * inv_n
    spread = sums[1:2] * inv_n - center * center
    inv_std = lax.rsqrt(spread + EPSILON)
    factor = gains[0:1] * inv_std
    return factor, gains[1:2] - center * factor, center, inv_std


def slope_of(slopes, factor, center, inv_std, inv_n):
    k1 = factor * slopes[1:2] * inv_n * inv_std
    k0 = factor * slopes[0:1] * inv_n - k1 * center
    return k0, k1


def down(v):
    return jnp.sum(v, axis=0)


def flat(v):
    return jnp.sum(v, axis=0, keepdims=True)


def steps(count, step, body, carry):
    return lax.fori_loop(0, count // step, lambda i, c: body(i * step, c), carry)


def call(kernel, outs, args, scratch=(), smem=0, flops=0, name=None):
    count = len(args)
    specs = [
        pl.BlockSpec(memory_space=pltpu.SMEM if i < smem else pltpu.VMEM) for i in range(count)
    ]
    total = sum(a.size * a.dtype.itemsize for a in args)
    total += sum(o.size * o.dtype.itemsize for o in outs)
    return pl.pallas_call(
        kernel,
        out_shape=tuple(outs),
        in_specs=specs,
        out_specs=tuple(pl.BlockSpec(memory_space=pltpu.VMEM) for _ in outs),
        scratch_shapes=list(scratch),
        compiler_params=pltpu.CompilerParams(vmem_limit_bytes=56 * 1024 * 1024),
        cost_estimate=pl.CostEstimate(flops=flops, bytes_accessed=total, transcendentals=0),
        name=name,
    )(*args)


def shape(dims, dtype=F32):
    return jax.ShapeDtypeStruct(dims, dtype)


def pack_kernel(per_clip, chunk, x_ref, mask_ref, out_ref, tmp_ref):
    def body(i, carry):
        begin = i * chunk
        tmp_ref[...] = x_ref[pl.ds(begin, chunk)].astype(F32).reshape(chunk * 32, 32)
        parts = [tmp_ref[pl.ds(r, chunk * 8, stride=4), :] for r in range(4)]
        joined = cells(jnp.concatenate(parts, axis=1))
        out_ref[pl.ds(begin, chunk)] = (joined * mask_ref[i // per_clip][None]).astype(BF16)
        return carry

    lax.fori_loop(0, x_ref.shape[0] // chunk, body, 0)


def unpack_kernel(chunk, x_ref, out_ref, tmp_ref):
    def body(i, carry):
        begin = i * chunk
        joined = rows(x_ref[pl.ds(begin, chunk)].astype(F32))
        for r in range(4):
            tmp_ref[pl.ds(r, chunk * 8, stride=4), :] = joined[:, 32 * r : 32 * r + 32]
        out_ref[pl.ds(begin, chunk)] = tmp_ref[...].reshape(chunk, 32, 32).astype(BF16)
        return carry

    lax.fori_loop(0, x_ref.shape[0] // chunk, body, 0)


def fast_first_kernel(fx_ref, mask_ref, w_ref, fa_ref, lp_ref, sums_ref):
    def body(p, carry):
        x = jnp.concatenate([rows_bf(fx_ref[z, pl.ds(p, BIG)]) for z in range(4)], axis=1)
        acc = cells(nn(x, w_ref[...]))
        fa = acc[:, :, 0:128] + later(acc[:, :, 128:256]) + sooner(acc[:, :, 256:384])
        lp = acc[:, :, 384:640] + later(acc[:, :, 640:896])
        fa_ref[pl.ds(p, BIG)] = fa
        lp_ref[pl.ds(p, BIG)] = lp
        mask = mask_ref[pl.ds(p, BIG)]
        fm, lm = fa * mask, lp * wide(mask, 256)
        return tuple(c + down(v) for c, v in zip(carry, (fm, fm * fa, lm, lm * lp)))

    zero = (jnp.zeros((8, 128), F32),) * 2 + (jnp.zeros((8, 256), F32),) * 2
    a, b, c, d = steps(fa_ref.shape[0], BIG, body, zero)
    sums_ref[0:1, 0:128], sums_ref[1:2, 0:128] = flat(a), flat(b)
    sums_ref[0:1, 128:384], sums_ref[1:2, 128:384] = flat(c), flat(d)


def fill_padded(y_refs, masks_ref, out_ref, value, halo, size):
    for (lo_ref, begin, count, step) in (
        (y_refs[0], 0, halo, 5),
        (y_refs[1], halo, size, SMALL),
        (y_refs[2], halo + size, halo, 5),
    ):
        def body(p, carry, lo_ref=lo_ref, begin=begin, step=step):
            v = value(lo_ref, p, step)
            for k in range(3):
                mask = wide(masks_ref[k, pl.ds(begin + p, step)], v.shape[-1])
                out_ref[k, pl.ds(begin + p, step)] = v * mask
            return carry

        steps(count, step, body, 0)


def conv_rows(pad_ref, edge_ref, weight, p, halo, row_len, dot):
    total = None
    for i in range(3):
        begin = p + halo + row_len * (i - 1)
        taps = [rows(pad_ref[j, pl.ds(begin + j - 1, BIG)]).astype(BF16) for j in range(3)]
        acc = None
        for j in range(3):
            part = dot(taps[j], weight(i, j))
            acc = part if acc is None else acc + part
        acc = cells(acc)
        if i != 1:
            acc = acc * wide(edge_ref[i // 2, pl.ds(p, BIG)], acc.shape[-1])
        total = acc if total is None else total + acc
    return total


def conv_kernel(halo, row_len, off, fold, n_ref, sums_ref, gains_ref, lo_ref, y_ref, hi_ref, masks_ref,
                edge_ref, w_ref, act_ref, out_ref, osums_ref, pad_ref):
    size, width = y_ref.shape[0], y_ref.shape[2]
    sums = sums_ref[:, off : off + width]
    sums = folded(sums) if fold else sums
    factor, shift, _, _ = scale_of(sums, gains_ref[...], n_ref[0])

    def value(ref, p, step):
        return gelu(ref[pl.ds(p, step)] * factor[None] + shift[None]).astype(BF16).astype(F32)

    fill_padded((lo_ref, y_ref, hi_ref), masks_ref, pad_ref, value, halo, size)

    def copy(p, carry):
        for k in range(3):
            act_ref[k, pl.ds(p, 3)] = pad_ref[k, pl.ds(p, 3)].astype(BF16)
        return carry

    steps(size + 2 * halo, 3, copy, 0)

    def body(p, carry):
        total = conv_rows(pad_ref, edge_ref, lambda i, j: w_ref[3 * i + j], p, halo, row_len, nn if fold else nt)
        out_ref[pl.ds(p, BIG)] = total
        masked = total * wide(masks_ref[1, pl.ds(halo + p, BIG)], width)
        return carry[0] + down(masked), carry[1] + down(masked * total)

    a, b = steps(size, BIG, body, (jnp.zeros((8, width), F32),) * 2)
    osums_ref[0:1], osums_ref[1:2] = flat(a), flat(b)


def slow_first_kernel(n_ref, xs_ref, lp_ref, lsums_ref, gains_ref, mask_ref, w_ref, wl_ref,
                      x_ref, lat_ref, sa_ref, sums_ref):
    size = lp_ref.shape[0]
    factor, shift, _, _ = scale_of(lsums_ref[:, 128:384], gains_ref[...], n_ref[0])

    def fill(p, carry):
        mask = wide(mask_ref[pl.ds(p, SMALL)], 256)
        lat_ref[pl.ds(p, SMALL)] = (gelu(lp_ref[pl.ds(p, SMALL)] * factor[None] + shift[None]) * mask).astype(BF16)
        for z in range(4):
            v = xs_ref[z, pl.ds(p, SMALL)].astype(F32) * mask
            x_ref[pl.ds(p, SMALL), :, 256 * z : 256 * z + 256] = v.astype(BF16)
        return carry

    steps(size, SMALL, fill, 0)

    def body(p, carry):
        acc = nt(rows_bf(x_ref[pl.ds(p, BIG)]), w_ref[...]) + nt(rows_bf(lat_ref[pl.ds(p, BIG)]), wl_ref[...])
        acc = cells(acc)
        sa = later(acc[:, :, 0:256]) + acc[:, :, 256:512] + sooner(acc[:, :, 512:768])
        sa_ref[pl.ds(p, BIG)] = sa
        masked = sa * wide(mask_ref[pl.ds(p, BIG)], 256)
        return carry[0] + down(masked), carry[1] + down(masked * sa)

    a, b = steps(size, BIG, body, (jnp.zeros((8, 256), F32),) * 2)
    sums_ref[0:1], sums_ref[1:2] = flat(a), flat(b)


def bypass_kernel(x_ref, lat_ref, mask_ref, w_ref, wl_ref, sp_ref, sums_ref):
    def body(p, carry):
        sp = cells(nn(rows_bf(x_ref[pl.ds(p, BIG)]), w_ref[...]) + nn(rows_bf(lat_ref[pl.ds(p, BIG)]), wl_ref[...]))
        sp_ref[pl.ds(p, BIG)] = sp
        masked = sp * wide(mask_ref[pl.ds(p, BIG)], sp.shape[-1])
        return carry[0] + down(masked), carry[1] + down(masked * sp)

    a, b = steps(sp_ref.shape[0], BIG, body, (jnp.zeros((8, sp_ref.shape[2]), F32),) * 2)
    sums_ref[0:1], sums_ref[1:2] = flat(a), flat(b)


def expand_kernel(fold, n_ref, y_ref, sums_ref, gains_ref, mask_ref, w_ref, h_ref, out_ref, osums_ref):
    size, width = y_ref.shape[0], y_ref.shape[2]
    sums = folded(sums_ref[...]) if fold else sums_ref[...]
    factor, shift, _, _ = scale_of(sums, gains_ref[...], n_ref[0])

    def fill(p, carry):
        mask = wide(mask_ref[pl.ds(p, SMALL)], width)
        h_ref[pl.ds(p, SMALL)] = (gelu(y_ref[pl.ds(p, SMALL)] * factor[None] + shift[None]) * mask).astype(BF16)
        return carry

    steps(size, SMALL, fill, 0)

    def body(p, carry):
        out = cells(nn(rows_bf(h_ref[pl.ds(p, BIG)]), w_ref[...]))
        out_ref[pl.ds(p, BIG)] = out
        masked = out * wide(mask_ref[pl.ds(p, BIG)], out.shape[-1])
        return carry[0] + down(masked), carry[1] + down(masked * out)

    a, b = steps(size, BIG, body, (jnp.zeros((8, out_ref.shape[2]), F32),) * 2)
    osums_ref[0:1], osums_ref[1:2] = flat(a), flat(b)


def fast_out_kernel(n_ref, fc_ref, sums_ref, gains_ref, mask_ref, fx_ref, cot_ref, out_ref, up_ref, slopes_ref):
    size = fc_ref.shape[0]
    factor, shift, center, inv_std = scale_of(folded(sums_ref[...]), gains_ref[...], n_ref[0])
    for z in range(4):
        lanes = slice(128 * z, 128 * z + 128)
        fz, sz, cz, rz = (v[:, lanes][None] for v in (factor, shift, center, inv_std))

        def body(p, carry, z=z, lanes=lanes, fz=fz, sz=sz, cz=cz, rz=rz):
            y = fc_ref[pl.ds(p, SMALL), :, lanes]
            mask = mask_ref[pl.ds(p, SMALL)]
            total = y * fz + sz + fx_ref[z, pl.ds(p, SMALL)].astype(F32)
            value, slope = gelu_pair(total)
            out_ref[z, pl.ds(p, SMALL)] = (value * mask).astype(BF16)
            up = slope * (cot_ref[z, pl.ds(p, SMALL)].astype(F32) * mask)
            up_ref[pl.ds(p, SMALL), :, lanes] = up
            return carry[0] + down(up), carry[1] + down(up * ((y - cz) * rz))

        a, b = steps(size, SMALL, body, (jnp.zeros((8, 128), F32),) * 2)
        slopes_ref[0:1, lanes], slopes_ref[1:2, lanes] = flat(a), flat(b)


def slow_out_kernel(n_ref, sc_ref, sp_ref, csums_ref, psums_ref, gains_ref, mask_ref, cot_ref, out_ref, up_ref, slopes_ref):
    size = sc_ref.shape[0]
    cf, cs, cc, cr = scale_of(csums_ref[...], gains_ref[0], n_ref[0])
    pf, ps, pc, pr = scale_of(psums_ref[...], gains_ref[1], n_ref[0])
    for z in range(4):
        lanes = slice(256 * z, 256 * z + 256)
        vecs = [v[:, lanes][None] for v in (cf, cs + ps, cc, cr, pf, pc, pr)]

        def body(p, carry, z=z, lanes=lanes, vecs=vecs):
            cf, shift, cc, cr, pf, pc, pr = vecs
            yc, yp = sc_ref[pl.ds(p, SMALL), :, lanes], sp_ref[pl.ds(p, SMALL), :, lanes]
            mask = wide(mask_ref[pl.ds(p, SMALL)], 256)
            value, slope = gelu_pair(yc * cf + yp * pf + shift)
            out_ref[z, pl.ds(p, SMALL)] = (value * mask).astype(BF16)
            up = slope * (cot_ref[z, pl.ds(p, SMALL)].astype(F32) * mask)
            up_ref[pl.ds(p, SMALL), :, lanes] = up
            return (carry[0] + down(up), carry[1] + down(up * ((yc - cc) * cr)), carry[2] + down(up * ((yp - pc) * pr)))

        a, b, c = steps(size, SMALL, body, (jnp.zeros((8, 256), F32),) * 3)
        slopes_ref[0:1, lanes], slopes_ref[1:2, lanes], slopes_ref[2:3, lanes] = flat(a), flat(b), flat(c)


def expand_back_kernel(fold, n_ref, up_ref, y_ref, sums_ref, gains_ref, slopes_ref, z_ref, zsums_ref, zgains_ref, mask_ref,
                       w_ref, dy_ref, dz_ref, oslopes_ref):
    size, width, inner = y_ref.shape[0], y_ref.shape[2], z_ref.shape[2]
    fix = folded if fold else (lambda v: v)
    factor, shift, center, inv_std = scale_of(fix(sums_ref[...]), gains_ref[...], n_ref[0])
    k0, k1 = slope_of(fix(slopes_ref[...]), factor, center, inv_std, n_ref[0])

    def fill(p, carry):
        mask = mask_ref[pl.ds(p, SMALL)]
        for q in range(width // 128):
            lanes = slice(128 * q, 128 * q + 128)
            y = y_ref[pl.ds(p, SMALL), :, lanes]
            dy = up_ref[pl.ds(p, SMALL), :, lanes] * factor[:, lanes][None]
            dy = dy - mask * (k0[:, lanes][None] + k1[:, lanes][None] * y)
            dy_ref[pl.ds(p, SMALL), :, lanes] = dy.astype(BF16)
        return carry

    steps(size, SMALL, fill, 0)
    zf, zs, zc, zr = scale_of(fix(zsums_ref[...]), zgains_ref[...], n_ref[0])

    def body(p, carry):
        dh = cells(nt(rows_bf(dy_ref[pl.ds(p, BIG)]), w_ref[...]))
        z = z_ref[pl.ds(p, BIG)]
        dz = gelu_slope(z * zf[None] + zs[None]) * dh * wide(mask_ref[pl.ds(p, BIG)], inner)
        dz_ref[pl.ds(p, BIG)] = dz
        return carry[0] + down(dz), carry[1] + down(dz * ((z - zc[None]) * zr[None]))

    a, b = steps(size, BIG, body, (jnp.zeros((8, inner), F32),) * 2)
    oslopes_ref[0:1], oslopes_ref[1:2] = flat(a), flat(b)


def bypass_back_kernel(n_ref, up_ref, y_ref, sums_ref, gains_ref, slopes_ref, mask_ref, w_ref, wl_ref, dy_ref, dx_ref, dl_ref):
    size, width = y_ref.shape[0], y_ref.shape[2]
    factor, shift, center, inv_std = scale_of(sums_ref[...], gains_ref[...], n_ref[0])
    k0, k1 = slope_of(slopes_ref[...], factor, center, inv_std, n_ref[0])

    def fill(p, carry):
        mask = mask_ref[pl.ds(p, SMALL)]
        for q in range(width // 128):
            lanes = slice(128 * q, 128 * q + 128)
            y = y_ref[pl.ds(p, SMALL), :, lanes]
            dy = up_ref[pl.ds(p, SMALL), :, lanes] * factor[:, lanes][None]
            dy = dy - mask * (k0[:, lanes][None] + k1[:, lanes][None] * y)
            dy_ref[pl.ds(p, SMALL), :, lanes] = dy.astype(BF16)
        return carry

    steps(size, SMALL, fill, 0)

    def body(p, carry):
        dy = rows_bf(dy_ref[pl.ds(p, BIG)])
        dx_ref[pl.ds(p, BIG)] = cells(nt(dy, w_ref[...]))
        dl_ref[pl.ds(p, BIG)] = cells(nt(dy, wl_ref[...]))
        return carry

    steps(size, BIG, body, 0)


def conv_back_kernel(halo, row_len, off, fold, n_ref, ysums_ref, ygains_ref, slopes_ref, ylo_ref, y_ref, yhi_ref, dlo_ref, d_ref,
                     dhi_ref, masks_ref, edge_ref, w_ref, z_ref, zsums_ref, zgains_ref, dy_ref, dz_ref, oslopes_ref, pad_ref):
    size, width = y_ref.shape[0], y_ref.shape[2]
    fix = folded if fold else (lambda v: v)
    factor, shift, center, inv_std = scale_of(fix(ysums_ref[...]), ygains_ref[...], n_ref[0])
    k0, k1 = slope_of(fix(slopes_ref[...]), factor, center, inv_std, n_ref[0])
    uppers = {id(ylo_ref): dlo_ref, id(y_ref): d_ref, id(yhi_ref): dhi_ref}

    def value(ref, p, step):
        dy = uppers[id(ref)][pl.ds(p, step)] * factor[None] - (k0[None] + k1[None] * ref[pl.ds(p, step)])
        return dy.astype(BF16).astype(F32)

    fill_padded((ylo_ref, y_ref, yhi_ref), masks_ref, pad_ref, value, halo, size)

    def copy(p, carry):
        dy = pad_ref[1, pl.ds(halo + p, SMALL)]
        dy_ref[1, pl.ds(p, SMALL)] = dy.astype(BF16)
        for k in (0, 1):
            dy_ref[2 * k, pl.ds(p, SMALL)] = (dy * wide(edge_ref[k, pl.ds(p, SMALL)], width)).astype(BF16)
        return carry

    steps(size, SMALL, copy, 0)
    zf, zs, zc, zr = scale_of(fix(zsums_ref[:, off : off + width]), zgains_ref[...], n_ref[0])

    def body(p, carry):
        dh = conv_rows(pad_ref, edge_ref, lambda i, j: w_ref[8 - 3 * i - j], p, halo, row_len, nt if fold else nn)
        z = z_ref[pl.ds(p, BIG)]
        dz = gelu_slope(z * zf[None] + zs[None]) * dh * wide(masks_ref[1, pl.ds(halo + p, BIG)], width)
        dz_ref[pl.ds(p, BIG)] = dz
        return carry[0] + down(dz), carry[1] + down(dz * ((z - zc[None]) * zr[None]))

    a, b = steps(size, BIG, body, (jnp.zeros((8, width), F32),) * 2)
    oslopes_ref[0:1], oslopes_ref[1:2] = flat(a), flat(b)


def slow_back_kernel(n_ref, dz_ref, y_ref, sums_ref, gains_ref, slopes_ref, mask_ref, w_ref, wl_ref, dx_ref, dl_ref,
                     lp_ref, lsums_ref, lgains_ref, taps_ref, out_ref, dzl_ref, oslopes_ref):
    size = y_ref.shape[0]
    factor, shift, center, inv_std = scale_of(sums_ref[...], gains_ref[...], n_ref[0])
    k0, k1 = slope_of(slopes_ref[...], factor, center, inv_std, n_ref[0])

    def fill(p, carry):
        mask = wide(mask_ref[pl.ds(p, SMALL)], 256)
        dy = dz_ref[pl.ds(p, SMALL)] * factor[None]
        dy = dy - mask * (k0[None] + k1[None] * y_ref[pl.ds(p, SMALL)])
        taps_ref[pl.ds(p, SMALL), :, 0:256] = sooner(dy).astype(BF16)
        taps_ref[pl.ds(p, SMALL), :, 256:512] = dy.astype(BF16)
        taps_ref[pl.ds(p, SMALL), :, 512:768] = later(dy).astype(BF16)
        return carry

    steps(size, SMALL, fill, 0)
    lf, ls, lc, lr = scale_of(lsums_ref[:, 128:384], lgains_ref[...], n_ref[0])

    def body(p, carry):
        taps = rows_bf(taps_ref[pl.ds(p, BIG)])
        mask = wide(mask_ref[pl.ds(p, BIG)], 256)
        for z in range(4):
            lanes = slice(256 * z, 256 * z + 256)
            dx = cells(nn(taps, w_ref[:, lanes])) + dx_ref[pl.ds(p, BIG), :, lanes]
            out_ref[z, pl.ds(p, BIG)] = (dx * mask).astype(BF16)
        dl = cells(nn(taps, wl_ref[...])) + dl_ref[pl.ds(p, BIG)]
        y = lp_ref[pl.ds(p, BIG)]
        dz = gelu_slope(y * lf[None] + ls[None]) * dl * mask
        dzl_ref[pl.ds(p, BIG)] = dz
        return carry[0] + down(dz), carry[1] + down(dz * ((y - lc[None]) * lr[None]))

    a, b = steps(size, BIG, body, (jnp.zeros((8, 256), F32),) * 2)
    oslopes_ref[0:1], oslopes_ref[1:2] = flat(a), flat(b)


def fast_back_kernel(n_ref, sums_ref, fgains_ref, lgains_ref, fslopes_ref, lslopes_ref, dzf_ref, fa_ref, dzl_ref, lp_ref, up_ref,
                     mask_ref, w_ref, taps_ref, out_ref):
    size = fa_ref.shape[0]
    ff, fs, fc, fr = scale_of(folded(sums_ref[:, 0:128]), fgains_ref[...], n_ref[1])
    f0, f1 = slope_of(folded(fslopes_ref[...]), ff, fc, fr, n_ref[1])
    lf, ls, lc, lr = scale_of(sums_ref[:, 128:384], lgains_ref[...], n_ref[0])
    l0, l1 = slope_of(lslopes_ref[...], lf, lc, lr, n_ref[0])

    def fill(p, carry):
        mask = mask_ref[pl.ds(p, SMALL)]
        dy = dzf_ref[pl.ds(p, SMALL)] * ff[None] - mask * (f0[None] + f1[None] * fa_ref[pl.ds(p, SMALL)])
        taps_ref[pl.ds(p, SMALL), :, 0:128] = dy.astype(BF16)
        taps_ref[pl.ds(p, SMALL), :, 128:256] = sooner(dy).astype(BF16)
        taps_ref[pl.ds(p, SMALL), :, 256:384] = later(dy).astype(BF16)
        mask = wide(mask, 256)
        dy = dzl_ref[pl.ds(p, SMALL)] * lf[None] - mask * (l0[None] + l1[None] * lp_ref[pl.ds(p, SMALL)])
        taps_ref[pl.ds(p, SMALL), :, 384:640] = dy.astype(BF16)
        taps_ref[pl.ds(p, SMALL), :, 640:896] = sooner(dy).astype(BF16)
        return carry

    steps(size, SMALL, fill, 0)

    def body(p, carry):
        dx = cells(nt(rows_bf(taps_ref[pl.ds(p, BIG)]), w_ref[...]))
        mask = mask_ref[pl.ds(p, BIG)]
        for z in range(4):
            lanes = slice(128 * z, 128 * z + 128)
            out_ref[z, pl.ds(p, BIG)] = ((dx[:, :, lanes] + up_ref[pl.ds(p, BIG), :, lanes]) * mask).astype(BF16)
        return carry

    steps(size, BIG, body, 0)


def swap(tree, axis, size, distance):
    pairs = [(i, i ^ distance) for i in range(size)]
    return jax.tree.map(lambda v: lax.ppermute(v, axis, pairs), tree)


def add(a, b):
    return jax.tree.map(jnp.add, a, b)


def stages(size, first_alone):
    bits = [1 << i for i in range(size.bit_length() - 1)]
    out = []
    if first_alone and bits:
        out.append(bits[:1])
        bits = bits[1:]
    while bits:
        out.append(bits[:2])
        bits = bits[2:]
    return out


def everywhere(tree, sizes):
    for axis, size in sizes.items():
        if size & (size - 1):
            tree = jax.tree.map(lambda v: lax.psum(v, axis), tree)
            continue
        for bits in stages(size, axis == "dp"):
            if len(bits) == 1:
                tree = add(tree, swap(tree, axis, size, bits[0]))
            else:
                a, b = bits
                near, far, both = (swap(tree, axis, size, k) for k in (a, b, a + b))
                tree = add(add(tree, near), add(far, both))
    return tree


def halos(v, halo, count):
    low = lax.ppermute(v[-halo:], "chan", [(i, i + 1) for i in range(count - 1)])
    high = lax.ppermute(v[:halo], "chan", [(i + 1, i) for i in range(count - 1)])
    return low, high


def share(parts, sizes):
    ways, blocks = sizes["dp"], sizes["chan"]
    me = lax.axis_index("dp")
    pieces = []
    for part in parts:
        lead, count, width = part.shape
        piece = lax.dynamic_slice_in_dim(part, me * (count // ways), count // ways, 1)
        pieces.append(piece.astype(BF16).reshape(-1))
    packed = jnp.concatenate(pieces)
    length = packed.shape[0]
    packed = jnp.pad(packed, (0, -length % 1024))
    whole = lax.all_gather(packed.reshape(-1, 1024), "chan", axis=0, tiled=False)
    whole = lax.all_gather(whole, "dp", axis=0, tiled=False).reshape(ways, blocks, -1)
    out, offset = [], 0
    for part in parts:
        lead, count, width = part.shape
        amount = lead * (count // ways) * width
        piece = whole[:, :, offset : offset + amount].reshape(ways, blocks, lead, count // ways, width)
        out.append(piece.transpose(2, 1, 0, 3, 4).reshape(lead, blocks * count, width))
        offset += amount
    return out


def collect(parts, sizes):
    ways, blocks = sizes["dp"], sizes["chan"]
    pieces = []
    for part in parts:
        lead, count, width = part.shape
        piece = part.astype(BF16).reshape(lead, blocks, ways, count // (blocks * ways), width)
        pieces.append(piece.transpose(2, 1, 0, 3, 4).reshape(ways, blocks, -1))
    packed = jnp.concatenate(pieces, axis=2)
    length = packed.shape[2]
    packed = jnp.pad(packed, ((0, 0), (0, 0), (0, -length % 1024)))
    mine = lax.psum_scatter(packed.reshape(ways, blocks, -1, 1024), "dp", scatter_dimension=0, tiled=False)
    mine = lax.psum_scatter(mine, "chan", scatter_dimension=0, tiled=False)
    whole = lax.all_gather(mine, "dp", axis=0, tiled=False).reshape(ways, -1)
    out, offset = [], 0
    for part in parts:
        lead, count, width = part.shape
        per = count // (blocks * ways)
        piece = whole[:, offset : offset + lead * per * width].reshape(ways, lead, per, width)
        out.append(piece.transpose(1, 0, 2, 3).reshape(lead, ways * per, width).astype(F32))
        offset += lead * per * width
    return out


def resplit(v):
    return lax.all_to_all(v, "chan", 0, 0, tiled=True)


def weight_sum(a, b):
    return jnp.einsum("pti,pto->io", a, b, preferred_element_type=F32)


def local(
    sizes,
    slow_input,
    fast_input,
    clip_counts,
    frame_counts,
    fast_reduce,
    fast_spatial,
    fast_expand,
    lateral_kernel,
    slow_reduce,
    lateral_reduce,
    slow_spatial,
    slow_expand,
    shortcut,
    lateral_shortcut,
    fast_inner_norm,
    fast_outer_norm,
    lateral_norm,
    slow_inner_norm,
    slow_outer_norm,
    slow_cotangent,
    fast_cotangent,
):
    ways = sizes["chan"]
    clips, slow_t, height, across, slow_part = slow_input.shape
    fast_t, fast_part = fast_input.shape[1], fast_input.shape[4]
    ratio = fast_t // slow_t
    area = height * across
    places = clips * area
    mine = places // ways
    halo = across + 1
    me = lax.axis_index("chan")
    wide_in = ways * slow_part

    all_clips = frame_counts.shape[0]
    live = (jnp.arange(all_clips, dtype=jnp.int32) % clips) < jnp.repeat(clip_counts, clips)
    valid = jnp.where(live, frame_counts, 0)
    count = jnp.sum(valid).astype(F32) * area
    inv_n = jnp.stack([1.0 / count, 1.0 / (count * ratio)])
    inv_slow, inv_fast = inv_n[0:1], inv_n[1:2]
    here = lax.dynamic_slice_in_dim(valid, lax.axis_index("dp") * clips, clips, 0)
    clip_mask = jnp.broadcast_to(
        (jnp.arange(slow_t)[None, :] < here[:, None]).astype(F32)[:, :, None], (clips, slow_t, 128)
    )
    place = me * mine - halo + jnp.arange(mine + 2 * halo)
    there = (place >= 0) & (place < places)
    frames = jnp.where(there, here[jnp.clip(place // area, 0, clips - 1)], 0)
    column = jnp.mod(place, across)
    row = jnp.mod(place // across, height)
    base = jnp.arange(slow_t)[None, :] < frames[:, None]
    masks = jnp.stack([base & (column != across - 1)[:, None], base, base & (column != 0)[:, None]])
    masks = jnp.broadcast_to(masks.astype(F32)[..., None], (3, mine + 2 * halo, slow_t, 128))
    own_row = row[halo : halo + mine]
    edges = jnp.stack([own_row != 0, own_row != height - 1]).astype(F32)
    edges = jnp.broadcast_to(edges[:, :, None, None], (2, mine, slow_t, 128))
    mask = masks[1, halo : halo + mine]

    chunk = 28

    def packed(v):
        v = v.transpose(0, 2, 3, 1, 4).reshape(places, fast_t, fast_part)
        (out,) = call(
            functools.partial(pack_kernel, area // chunk, chunk),
            [shape((places, slow_t, 128), BF16)],
            [v, clip_mask],
            [pltpu.VMEM((chunk * fast_t, fast_part), F32)],
            name="fast_pack",
        )
        return out.reshape(ways, mine, slow_t, 128)

    def unpacked(v):
        (out,) = call(
            functools.partial(unpack_kernel, chunk),
            [shape((places, fast_t, fast_part), BF16)],
            [v.reshape(places, slow_t, 128)],
            [pltpu.VMEM((chunk * fast_t, fast_part), F32)],
            name="fast_unpack",
        )
        return out.reshape(clips, height, across, fast_t, fast_part).transpose(0, 3, 1, 2, 4)

    def split(v):
        return v.transpose(0, 2, 3, 1, 4).reshape(ways, mine, slow_t, slow_part)

    def joined(v):
        return v.reshape(clips, height, across, slow_t, slow_part).transpose(0, 3, 1, 2, 4)

    fx = resplit(packed(fast_input))
    xs = resplit(split(slow_input))

    lat_t, red_t, lred_t = (v.transpose(0, 2, 1) for v in (lateral_kernel, slow_reduce, lateral_reduce))
    spatial_t = slow_spatial.reshape(9, slow_spatial.shape[2], -1).transpose(0, 2, 1)
    lat_w, red_w, lred_w = share([lat_t, red_t, lred_t], sizes)
    spat_w, exp_w, short_w, lshort_w = share([spatial_t, slow_expand[None], shortcut[None], lateral_shortcut[None]], sizes)
    red_w, lred_w = red_w.reshape(-1, red_w.shape[2]), lred_w.reshape(-1, lred_w.shape[2])
    exp_w, short_w, lshort_w = exp_w[0], short_w[0], lshort_w[0]

    norms = jnp.concatenate(
        [lateral_norm.reshape(-1), slow_inner_norm.reshape(-1), slow_outer_norm.reshape(-1)]
    )
    norms = lax.all_gather(norms, "chan", axis=0, tiled=False)
    lw, sw, ow = lateral_norm.shape[1], slow_inner_norm.shape[2], slow_outer_norm.shape[2]
    lat_g = norms[:, : 2 * lw].reshape(ways, 2, lw).transpose(1, 0, 2).reshape(2, -1)
    in_g = norms[:, 2 * lw : 2 * lw + 4 * sw].reshape(ways, 2, 2, sw).transpose(1, 2, 0, 3).reshape(2, 2, -1)
    out_g = norms[:, 2 * lw + 4 * sw :].reshape(ways, 2, 2, ow).transpose(1, 2, 0, 3).reshape(2, 2, -1)
    fin_g = jnp.concatenate([fast_inner_norm] * ratio, axis=2)
    fout_g = jnp.broadcast_to(fast_outer_norm.reshape(2, ways, 1, fast_part), (2, ways, ratio, fast_part)).reshape(2, -1)

    def in_blocks(w, frames_in, frames_out):
        width = next(v for line in w for v in line if v is not None).shape[1]
        blank = jnp.zeros((ways, fast_part, width), BF16)
        lines = []
        for r in range(frames_in):
            line = [blank if w[r][q] is None else w[r][q].reshape(ways, fast_part, width) for q in range(frames_out)]
            lines.append(jnp.concatenate(line, axis=2))
        return jnp.stack(lines, axis=1).reshape(ways * frames_in * fast_part, -1)

    fr = fast_reduce.astype(BF16)
    none = [None] * ratio
    main = [[fr[r - q + 1] if abs(r - q) <= 1 else None for q in range(ratio)] for r in range(ratio)]
    prev = [none] * (ratio - 1) + [[fr[0]] + none[1:]]
    after = [none[1:] + [fr[2]]] + [none] * (ratio - 1)
    taps = lat_w.transpose(0, 2, 1)
    lat_main = [[taps[2]], [taps[3]], [taps[4]], [None]]
    lat_prev = [[None], [None], [taps[0]], [taps[1]]]
    w_first = jnp.concatenate([in_blocks(v, ratio, len(v[0])) for v in (main, prev, after, lat_main, lat_prev)], axis=1)
    same = jnp.eye(ratio, dtype=BF16)
    fsp = fast_spatial.astype(BF16).reshape(9, fast_spatial.shape[2], -1)
    w_fsp = jnp.einsum("rq,kio->kriqo", same, fsp).reshape(9, 128, 128)
    fex = fast_expand.astype(BF16).reshape(-1, ways, fast_part)
    w_fex = jnp.einsum("rq,izc->rizqc", same, fex).reshape(128, -1)

    ext = mine + 2 * halo
    wide_f = ways * 128
    mid = 256
    fa, lp, sums1 = call(
        fast_first_kernel,
        [shape((mine, 8, 128)), shape((mine, 8, mid)), shape((2, 384))],
        [fx, mask, w_first],
        name="fast_first",
    )
    fa_lo, fa_hi = halos(fa, halo, ways)
    sums1 = everywhere(sums1, sizes)
    pad = [pltpu.VMEM((3, ext, 8, 128), F32)]
    h1, fb, fb_sums = call(
        functools.partial(conv_kernel, halo, across, 0, True),
        [shape((3, ext, 8, 128), BF16), shape((mine, 8, 128)), shape((2, 128))],
        [inv_fast, sums1, fin_g[0], fa_lo, fa, fa_hi, masks, edges, w_fsp],
        pad,
        smem=1,
        name="fast_second",
    )
    x, lat, sa, sa_sums = call(
        slow_first_kernel,
        [shape((mine, 8, wide_in), BF16), shape((mine, 8, mid), BF16), shape((mine, 8, mid)), shape((2, mid))],
        [inv_slow, xs, lp, sums1, lat_g, mask, red_w, lred_w],
        smem=1,
        name="slow_first",
    )
    sa_lo, sa_hi = halos(sa, halo, ways)
    sa_sums, fb_sums = everywhere((sa_sums, fb_sums), sizes)
    sp, sp_sums = call(
        bypass_kernel,
        [shape((mine, 8, wide_in)), shape((2, wide_in))],
        [x, lat, mask, short_w, lshort_w],
        name="bypass",
    )
    ha, sb, sb_sums = call(
        functools.partial(conv_kernel, halo, across, 0, False),
        [shape((3, ext, 8, mid), BF16), shape((mine, 8, mid)), shape((2, mid))],
        [inv_slow, sa_sums, in_g[0], sa_lo, sa, sa_hi, masks, edges, spat_w],
        [pltpu.VMEM((3, ext, 8, mid), F32)],
        smem=1,
        name="slow_second",
    )
    h2, fc, fc_sums = call(
        functools.partial(expand_kernel, True),
        [shape((mine, 8, 128), BF16), shape((mine, 8, wide_f)), shape((2, wide_f))],
        [inv_fast, fb, fb_sums, fin_g[1], mask, w_fex],
        smem=1,
        name="fast_third",
    )
    sb_lo, sb_hi = halos(sb, halo, ways)
    fb_lo, fb_hi = halos(fb, halo, ways)
    sb_sums, fc_sums = everywhere((sb_sums, fc_sums), sizes)
    cot = resplit(split(slow_cotangent))
    fcot = resplit(packed(fast_cotangent))
    hb, sc, sc_sums = call(
        functools.partial(expand_kernel, False),
        [shape((mine, 8, mid), BF16), shape((mine, 8, wide_in)), shape((2, wide_in))],
        [inv_slow, sb, sb_sums, in_g[1], mask, exp_w],
        smem=1,
        name="slow_third",
    )
    fast_out, dfs, fc_slopes = call(
        fast_out_kernel,
        [shape((ways, mine, 8, 128), BF16), shape((mine, 8, wide_f)), shape((2, wide_f))],
        [inv_fast, fc, fc_sums, fout_g, mask, fx, fcot],
        smem=1,
        name="fast_out",
    )
    sc_sums, sp_sums, fc_slopes = everywhere((sc_sums, sp_sums, fc_slopes), sizes)
    slow_out, dss, out_slopes = call(
        slow_out_kernel,
        [shape((ways, mine, 8, mid), BF16), shape((mine, 8, wide_in)), shape((3, wide_in))],
        [inv_slow, sc, sp, sc_sums, sp_sums, out_g, mask, cot],
        smem=1,
        name="slow_out",
    )

    dfc, dzfb, fb_slopes = call(
        functools.partial(expand_back_kernel, True),
        [shape((mine, 8, wide_f), BF16), shape((mine, 8, 128)), shape((2, 128))],
        [inv_fast, dfs, fc, fc_sums, fout_g, fc_slopes, fb, fb_sums, fin_g[1], mask, w_fex],
        smem=1,
        name="fast_third_back",
    )
    dzfb_lo, dzfb_hi = halos(dzfb, halo, ways)
    out_slopes, fb_slopes = everywhere((out_slopes, fb_slopes), sizes)
    sc_slopes = out_slopes[0:2]
    sp_slopes = jnp.concatenate([out_slopes[0:1], out_slopes[2:3]])
    dsc, dzsb, sb_slopes = call(
        functools.partial(expand_back_kernel, False),
        [shape((mine, 8, wide_in), BF16), shape((mine, 8, mid)), shape((2, mid))],
        [inv_slow, dss, sc, sc_sums, out_g[0], sc_slopes, sb, sb_sums, in_g[1], mask, exp_w],
        smem=1,
        name="slow_third_back",
    )
    dzsb_lo, dzsb_hi = halos(dzsb, halo, ways)
    dfb, dzfa, fa_slopes = call(
        functools.partial(conv_back_kernel, halo, across, 0, True),
        [shape((3, mine, 8, 128), BF16), shape((mine, 8, 128)), shape((2, 128))],
        [inv_fast, fb_sums, fin_g[1], fb_slopes, fb_lo, fb, fb_hi, dzfb_lo, dzfb, dzfb_hi, masks, edges, w_fsp, fa, sums1, fin_g[0]],
        pad,
        smem=1,
        name="fast_second_back",
    )
    sb_slopes, fa_slopes = everywhere((sb_slopes, fa_slopes), sizes)
    dsp, dx, dl = call(
        bypass_back_kernel,
        [shape((mine, 8, wide_in), BF16), shape((mine, 8, wide_in)), shape((mine, 8, mid))],
        [inv_slow, dss, sp, sp_sums, out_g[1], sp_slopes, mask, short_w, lshort_w],
        smem=1,
        name="bypass_back",
    )
    dsb, dzsa, sa_slopes = call(
        functools.partial(conv_back_kernel, halo, across, 0, False),
        [shape((3, mine, 8, mid), BF16), shape((mine, 8, mid)), shape((2, mid))],
        [inv_slow, sb_sums, in_g[1], sb_slopes, sb_lo, sb, sb_hi, dzsb_lo, dzsb, dzsb_hi, masks, edges, spat_w, sa, sa_sums, in_g[0]],
        [pltpu.VMEM((3, ext, 8, mid), F32)],
        smem=1,
        name="slow_second_back",
    )
    sa_slopes = everywhere(sa_slopes, sizes)
    dsa, dslow, dzlp, lp_slopes = call(
        slow_back_kernel,
        [shape((mine, 8, 3 * mid), BF16), shape((ways, mine, 8, mid), BF16), shape((mine, 8, mid)), shape((2, mid))],
        [inv_slow, dzsa, sa, sa_sums, in_g[0], sa_slopes, mask, red_w, lred_w, dx, dl, lp, sums1, lat_g],
        smem=1,
        name="slow_first_back",
    )
    lp_slopes = everywhere(lp_slopes, sizes)
    dfirst, dfast = call(
        fast_back_kernel,
        [shape((mine, 8, 896), BF16), shape((ways, mine, 8, 128), BF16)],
        [inv_n, sums1, fin_g[0], lat_g, fa_slopes, lp_slopes, dzfa, fa, dzlp, lp, dfs, mask, w_first],
        smem=1,
        name="fast_first_back",
    )

    slow_output = joined(resplit(slow_out))
    fast_output = unpacked(resplit(fast_out))
    slow_input_grad = joined(resplit(dslow))
    fast_input_grad = unpacked(resplit(dfast))

    def conv_weight(act, dy):
        taps = []
        for i in range(3):
            for j in range(3):
                begin = halo + across * (i - 1) + j - 1
                taps.append(weight_sum(dy[i], act[j, begin : begin + mine]))
        return jnp.stack(taps)

    g_exp = weight_sum(hb, dsc)
    g_short = weight_sum(x, dsp)
    g_lshort = weight_sum(lat, dsp)
    g_exp, g_short, g_lshort = collect([g_exp[None], g_short[None], g_lshort[None]], sizes)
    (g_spat,) = collect([conv_weight(ha, dsb)], sizes)
    g_red = weight_sum(dsa, x).reshape(3, mid, wide_in)
    g_lred = weight_sum(dsa, lat).reshape(3, mid, mid)
    g_red, g_lred = collect([g_red, g_lred], sizes)
    fx_whole = jnp.concatenate([fx[z] for z in range(ways)], axis=2)
    g_first = weight_sum(fx_whole, dfirst).reshape(ways, ratio, fast_part, 896)
    g_lat_main = g_first[:, :, :, 384:640].transpose(1, 3, 0, 2).reshape(ratio, mid, -1)
    g_lat_prev = g_first[:, :, :, 640:896].transpose(1, 3, 0, 2).reshape(ratio, mid, -1)
    g_lat = jnp.stack([g_lat_prev[2], g_lat_prev[3], g_lat_main[0], g_lat_main[1], g_lat_main[2]])
    (g_lat,) = collect([g_lat], sizes)
    g_main = g_first[:, :, :, 0:128].reshape(ways, ratio, fast_part, ratio, -1)
    inner = g_main.shape[-1]
    g_prev, g_after = g_first[:, :, :, 128:256], g_first[:, :, :, 256:384]
    g_fred = []
    for j in range(3):
        total = sum(g_main[:, q + j - 1, :, q] for q in range(ratio) if 0 <= q + j - 1 < ratio)
        if j == 0:
            total = total + g_prev[:, ratio - 1, :, 0:inner]
        if j == 2:
            total = total + g_after[:, 0, :, 128 - inner :]
        g_fred.append(total.reshape(-1, inner))
    g_fred = jnp.stack(g_fred)
    g_fsp = conv_weight(h1, dfb).reshape(9, ratio, inner, ratio, inner)
    g_fsp = sum(g_fsp[:, r, :, r] for r in range(ratio)).transpose(0, 2, 1).reshape(3, 3, inner, inner)
    g_fex = weight_sum(h2, dfc).reshape(ratio, inner, ways, ratio, fast_part)
    g_fex = sum(g_fex[r, :, :, r] for r in range(ratio)).reshape(inner, -1)
    g_fred, g_fsp, g_fex = jax.tree.map(
        lambda v: v.astype(F32), everywhere(jax.tree.map(lambda v: v.astype(BF16), (g_fred, g_fsp, g_fex)), sizes)
    )

    def pair(slopes):
        return slopes[::-1]

    def own(v, width):
        return lax.dynamic_slice_in_dim(v, me * width, width, v.ndim - 1)

    def fold_in(slopes):
        return jnp.sum(slopes.reshape(2, ratio, inner), axis=1)

    fast_inner_grad = jnp.stack([pair(fold_in(fa_slopes)), pair(fold_in(fb_slopes))])
    fast_outer_grad = pair(jnp.sum(fc_slopes.reshape(2, ways, ratio, fast_part), axis=2).reshape(2, -1))
    lateral_grad = pair(own(lp_slopes, lw))
    slow_inner_grad = own(jnp.stack([pair(sa_slopes), pair(sb_slopes)]), sw)
    slow_outer_grad = own(jnp.stack([pair(sc_slopes), pair(sp_slopes)]), ow)
    return (
        slow_output,
        fast_output,
        slow_input_grad,
        fast_input_grad,
        g_fred,
        g_fsp,
        g_fex,
        g_lat.transpose(0, 2, 1),
        g_red.transpose(0, 2, 1),
        g_lred.transpose(0, 2, 1),
        g_spat.transpose(0, 2, 1).reshape(slow_spatial.shape),
        g_exp[0],
        g_short[0],
        g_lshort[0],
        fast_inner_grad,
        fast_outer_grad,
        lateral_grad,
        slow_inner_grad,
        slow_outer_grad,
    )


def solution(mesh):
    sizes = {"dp": mesh.shape["dp"], "chan": mesh.shape["chan"]}
    big = P("dp", None, None, None, "chan")
    last2, last3, last4 = P(None, "chan"), P(None, None, "chan"), P(None, None, None, "chan")
    first = P("chan", None)
    return jax.shard_map(
        functools.partial(local, sizes),
        mesh=mesh,
        in_specs=(
            big, big, P(), P(), P(), P(), P(), last3, last3, last3, last4, first, first, first,
            P(), P(), last2, last3, last3, big, big,
        ),
        out_specs=(
            big, big, big, big, P(), P(), P(), last3, last3, last3, last4, first, first, first,
            P(), P(), last2, last3, last3,
        ),
        check_vma=False,
    )
```

```python
import functools

import jax
import jax.numpy as jnp
from jax import lax
from jax.experimental import pallas as pl
from jax.experimental.pallas import tpu as pltpu
from jax.sharding import PartitionSpec as P

F32 = jnp.float32
BF16 = jnp.bfloat16
EPSILON = 1e-05
ROOT = 0.7978845608028654
CUBIC = 0.044715
BIG = 49
SMALL = 7


def gelu(v):
    return 0.5 * v * (1.0 + jnp.tanh(ROOT * (v * (1.0 + CUBIC * (v * v)))))


def gelu_slope(v):
    square = v * v
    th = jnp.tanh(ROOT * (v * (1.0 + CUBIC * square)))
    half = 0.5 * (1.0 + th)
    return half + (0.5 * ROOT) * v * (1.0 - th * th) * (1.0 + 3.0 * CUBIC * square)


def gelu_pair(v):
    square = v * v
    th = jnp.tanh(ROOT * (v * (1.0 + CUBIC * square)))
    half = 0.5 * (1.0 + th)
    slope = half + (0.5 * ROOT) * v * (1.0 - th * th) * (1.0 + 3.0 * CUBIC * square)
    return v * half, slope


def rows(v):
    return v.reshape(v.shape[0] * v.shape[1], v.shape[2])


def cells(v):
    return v.reshape(v.shape[0] // 8, 8, v.shape[1])


def rows_bf(v):
    return rows(v.astype(F32)).astype(BF16)


def wide(mask, width):
    repeats = width // 128
    return mask if repeats == 1 else jnp.concatenate([mask] * repeats, axis=-1)


def nn(a, b):
    return jnp.dot(a, b, preferred_element_type=F32)


def nt(a, b):
    return lax.dot_general(a, b, (((1,), (1,)), ((), ())), preferred_element_type=F32)


def later(v):
    rolled = pltpu.roll(v, 1, 1)
    return jnp.where(lax.broadcasted_iota(jnp.int32, v.shape, 1) == 0, 0.0, rolled)


def sooner(v):
    rolled = pltpu.roll(v, 7, 1)
    return jnp.where(lax.broadcasted_iota(jnp.int32, v.shape, 1) == 7, 0.0, rolled)


def folded(v):
    out = []
    for block in range(v.shape[-1] // 128):
        part = v[:, 128 * block : 128 * block + 128]
        part = part + pltpu.roll(part, 64, 1)
        out.append(part + pltpu.roll(part, 32, 1))
    return out[0] if len(out) == 1 else jnp.concatenate(out, axis=-1)


def scale_of(sums, gains, inv_n):
    center = sums[0:1] * inv_n
    spread = sums[1:2] * inv_n - center * center
    inv_std = lax.rsqrt(spread + EPSILON)
    factor = gains[0:1] * inv_std
    return factor, gains[1:2] - center * factor, center, inv_std


def slope_of(slopes, factor, center, inv_std, inv_n):
    k1 = factor * slopes[1:2] * inv_n * inv_std
    k0 = factor * slopes[0:1] * inv_n - k1 * center
    return k0, k1


def down(v):
    return jnp.sum(v, axis=0)


def flat(v):
    return jnp.sum(v, axis=0, keepdims=True)


def steps(count, step, body, carry):
    return lax.fori_loop(0, count // step, lambda i, c: body(i * step, c), carry)


def call(kernel, outs, args, scratch=(), smem=0, flops=0, name=None):
    specs = [pl.BlockSpec(memory_space=pltpu.SMEM if i < smem else pltpu.VMEM) for i in range(len(args))]
    total = sum(a.size * a.dtype.itemsize for a in args)
    total += sum(o.size * o.dtype.itemsize for o in outs)
    def padded(v):
        dims = list(v.shape)
        if len(dims) < 2:
            return 4096
        dims[-1] = -(-dims[-1] // 128) * 128
        dims[-2] = -(-dims[-2] // 8) * 8
        amount = v.dtype.itemsize
        for d in dims:
            amount *= d
        return amount

    room = sum(padded(v) for v in (*args, *outs, *scratch)) + 6 * 1024 * 1024
    return pl.pallas_call(
        kernel,
        out_shape=tuple(outs),
        in_specs=specs,
        out_specs=tuple(pl.BlockSpec(memory_space=pltpu.VMEM) for _ in outs),
        scratch_shapes=list(scratch),
        compiler_params=pltpu.CompilerParams(vmem_limit_bytes=room),
        cost_estimate=pl.CostEstimate(flops=flops, bytes_accessed=total, transcendentals=0),
        name=name,
    )(*args)


def shape(dims, dtype=F32):
    return jax.ShapeDtypeStruct(dims, dtype)


def tile_mask(frames, width):
    tile = (lax.broadcasted_iota(jnp.int32, (8, 128), 0) < frames).astype(F32)
    return wide(tile, width)[None]


def sweep(table_ref, size, step, body, carry=0):
    def run(i, kept):
        p = i * step
        return body(p, table_ref[1 + p // BIG], kept)

    return lax.fori_loop(0, size // step, run, carry)


def lane_group(v, group):
    return jnp.where(lax.broadcasted_iota(jnp.int32, v.shape, v.ndim - 1) // 32 == group, v, 0.0)


def moved(v, shift):
    shift = shift % 128
    return v if shift == 0 else pltpu.roll(v, shift, v.ndim - 1)


def pack_kernel(per_clip, clips, ids_ref, counts_ref, frames_ref, x_ref, out_ref, tmp_ref):
    clip, dp = pl.program_id(0) // per_clip, ids_ref[0]
    chunk = x_ref.shape[0]
    frames = jnp.where(clip < counts_ref[dp], frames_ref[dp * clips + clip], 0)
    tmp_ref[...] = x_ref[...].astype(F32).reshape(chunk * 32, 32)
    parts = [tmp_ref[pl.ds(r, chunk * 8, stride=4), :] for r in range(4)]
    out_ref[...] = (cells(jnp.concatenate(parts, axis=1)) * tile_mask(frames, 128)).astype(BF16)


def unpack_kernel(ids_ref, *refs):
    pieces, out_ref, tmp_ref = refs[:4], refs[4], refs[5]
    size = pieces[0].shape[0]
    for k in range(4):
        begin = (ids_ref[1] ^ k) * size

        def body(p, carry, k=k, begin=begin):
            joined = rows(pieces[k][pl.ds(p, BIG)].astype(F32))
            for r in range(4):
                tmp_ref[pl.ds(r, BIG * 8, stride=4), :] = joined[:, 32 * r : 32 * r + 32]
            out_ref[pl.ds(begin + p, BIG)] = tmp_ref[...].reshape(BIG, 32, 32).astype(BF16)
            return carry

        steps(size, BIG, body, 0)


def place_kernel(ids_ref, *refs):
    pieces, out_ref = refs[:4], refs[4]
    for k in range(4):

        def body(p, carry, k=k):
            out_ref[ids_ref[1] ^ k, pl.ds(p, SMALL)] = pieces[k][pl.ds(p, SMALL)]
            return carry

        steps(pieces[0].shape[0], SMALL, body, 0)


def first_weights_kernel(ids_ref, *refs):
    shares, lat_shares = refs[0:8], refs[8:16]
    fr_ref, fsp_ref, fex_ref, fin_ref, fout_ref = refs[16:21]
    red_ref, lred_ref, first_ref, wsp_ref, wex_ref, gin_ref, gout_ref, lat_ref = refs[21:]
    for kd in range(8):
        d = ids_ref[2] ^ kd
        for kz in range(4):
            z = ids_ref[1] ^ kz
            for j in range(3):
                red_ref[j, z, d] = shares[kd][kz, j, :, 0:1024]
                lred_ref[j, z, d] = shares[kd][kz, j, :, 1024:1280]
            for j in range(5):
                lat_ref[j, z, d] = lat_shares[kd][kz, j].astype(F32)
    first_ref[...] = jnp.zeros_like(first_ref)
    wsp_ref[...] = jnp.zeros_like(wsp_ref)
    for z in range(4):
        lanes = slice(128 * z, 128 * z + 128)

        def put(v, r, z=z):
            return lane_group(moved(v, 32 * r - 32 * z), r)

        for q in range(4):
            total = sum(put(fr_ref[r - q + 1], r) for r in range(4) if abs(r - q) <= 1)
            first_ref[32 * q : 32 * q + 32, lanes] = total.astype(BF16)
        first_ref[128:160, lanes] = put(fr_ref[0], 3).astype(BF16)
        first_ref[352:384, lanes] = put(fr_ref[2], 0).astype(BF16)
        taps = [lat_ref[j].reshape(256, 128) for j in range(5)]
        first_ref[384:640, lanes] = sum(put(taps[2 + r], r) for r in range(3)).astype(BF16)
        first_ref[640:896, lanes] = (put(taps[0], 2) + put(taps[1], 3)).astype(BF16)
        for r in range(4):
            wex_ref[32 * r : 32 * r + 32, lanes] = put(fex_ref[...], r).astype(BF16)
        gout_ref[:, lanes] = sum(put(fout_ref[...], r) for r in range(4))
    blank = jnp.zeros((32, 96), F32)
    for k in range(9):
        tap = jnp.concatenate([fsp_ref[k], blank], axis=1)
        for r in range(4):
            wsp_ref[k, 32 * r : 32 * r + 32, :] = moved(tap, 32 * r).astype(BF16)
    gin_ref[...] = jnp.concatenate([fin_ref[...]] * 4, axis=1)


def second_weights_kernel(ids_ref, *refs):
    shares, sp_shares = refs[0:8], refs[8:16]
    exp_ref, short_ref, lshort_ref, sp_ref = refs[16:]
    for kd in range(8):
        d = ids_ref[2] ^ kd
        for kz in range(4):
            z = ids_ref[1] ^ kz
            exp_ref[z, d] = shares[kd][kz, 0]
            lshort_ref[z, d] = shares[kd][kz, 5]
            for a in range(4):
                short_ref[z, d, a] = shares[kd][kz, 1 + a]
            for k in range(9):
                sp_ref[k, z, d] = sp_shares[kd][kz, k]


def first_grads_kernel(ids_ref, *refs):
    shares, sp_shares = refs[0:8], refs[8:16]
    exp_ref, short_ref, lshort_ref, sp_ref = refs[16:]
    for kd in range(8):
        d = ids_ref[2] ^ kd
        exp_ref[d] = shares[kd][0].astype(F32)
        lshort_ref[d] = shares[kd][5].astype(F32)
        for a in range(4):
            short_ref[d, a] = shares[kd][1 + a].astype(F32)
        for k in range(9):
            sp_ref[k, d] = sp_shares[kd][k].astype(F32)


def second_grads_kernel(ids_ref, *refs):
    shares, lat_shares = refs[0:8], refs[8:16]
    red_ref, lred_ref, lat_ref = refs[16:]
    for kd in range(8):
        d = ids_ref[2] ^ kd
        for j in range(3):
            red_ref[j, d] = shares[kd][j, :, 0:1024].astype(F32)
            lred_ref[j, d] = shares[kd][j, :, 1024:1280].astype(F32)
        for j in range(5):
            lat_ref[j, d] = lat_shares[kd][j].astype(F32)


def lanes_at(block, width):
    return pl.ds(pl.multiple_of(block * width, width), width)


def fast_first_kernel(table_ref, f0_ref, f1_ref, f2_ref, f3_ref, w_ref, fx_ref, fa_ref, lp_ref, sums_ref, first_ref, last_ref):
    size = fa_ref.shape[0]
    for k, ref in enumerate((f0_ref, f1_ref, f2_ref, f3_ref)):

        def fill(p, carry, ref=ref, lanes=lanes_at(table_ref[5] ^ k, 128)):
            fx_ref[pl.ds(p, SMALL), :, lanes] = ref[pl.ds(p, SMALL)]
            return carry

        steps(size, SMALL, fill, 0)

    def body(p, frames, carry):
        acc = cells(nt(rows_bf(fx_ref[pl.ds(p, BIG)]), w_ref[...]))
        fa = acc[:, :, 0:128] + later(acc[:, :, 128:256]) + sooner(acc[:, :, 256:384])
        lp = acc[:, :, 384:640] + later(acc[:, :, 640:896])
        fa_ref[pl.ds(p, BIG)] = fa
        lp_ref[pl.ds(p, BIG)] = lp
        fm, lm = fa * tile_mask(frames, 128), lp * tile_mask(frames, 256)
        return tuple(c + down(v) for c, v in zip(carry, (fm, fm * fa, lm, lm * lp)))

    zero = (jnp.zeros((8, 128), F32),) * 2 + (jnp.zeros((8, 256), F32),) * 2
    a, b, c, d = sweep(table_ref, size, BIG, body, zero)
    sums_ref[0:1, 0:128], sums_ref[1:2, 0:128] = flat(a), flat(b)
    sums_ref[0:1, 128:384], sums_ref[1:2, 128:384] = flat(c), flat(d)
    halo = first_ref.shape[0]
    first_ref[...], last_ref[...] = fa_ref[0:halo], fa_ref[size - halo : size]


def fill_padded(table_ref, refs, offset, out_ref, value, halo, size):
    low, middle, high = refs
    phase = table_ref[5] * (size // SMALL)

    def put(v, at, part, count, step=SMALL):
        even = ((phase + part + 2 * count) % 2 == 0).astype(F32)
        out_ref[1, pl.ds(at, step)] = v
        if step == 1:
            out_ref[0, pl.ds(at, 1)] = v * even
            out_ref[2, pl.ds(at, 1)] = v * (1.0 - even)
            return
        out_ref[0, pl.ds(at, step)] = v
        out_ref[2, pl.ds(at, step)] = v
        out_ref[0, pl.ds(at + step - 1, 1)] = v[step - 1 : step] * even
        out_ref[2, pl.ds(at, 1)] = v[0:1] * (1.0 - even)

    width = out_ref.shape[-1]
    lo_mask, hi_mask = tile_mask(table_ref[0], width), tile_mask(table_ref[4], width)
    put(value(low, 0, 1) * lo_mask, 0, -3, 4, 1)
    put(value(low, 1, SMALL) * lo_mask, 1, -2, 4)
    put(value(low, 1 + SMALL, SMALL) * lo_mask, 1 + SMALL, -1, 4)
    parts = size // SMALL
    put(value(high, 0, SMALL) * hi_mask, halo + size, parts, 0)
    put(value(high, SMALL, SMALL) * hi_mask, halo + size + SMALL, parts + 1, 0)
    put(value(high, 2 * SMALL, 1) * hi_mask, halo + size + 2 * SMALL, parts + 2, 0, 1)

    def body(p, frames, carry):
        put(value(middle, p, SMALL) * tile_mask(frames, width), halo + p, p // SMALL, 0)
        return carry

    sweep(table_ref, size, SMALL, body)


def edge_scales(table_ref, p, per_clip):
    part = table_ref[5] * table_ref[6] + p // BIG
    return (part % per_clip != 0).astype(F32), ((part + 1) % per_clip != 0).astype(F32)


def conv_rows(table_ref, per_clip, pad_ref, weight, p, halo, row_len, dot):
    top, bottom = edge_scales(table_ref, p, per_clip)
    total = None
    for i in (1, 0, 2):
        begin = p + halo + row_len * (i - 1)
        acc = None
        for j in range(3):
            tap = rows(pad_ref[j, pl.ds(begin + j - 1, BIG)]).astype(BF16)
            part = dot(tap, weight(i, j))
            acc = part if acc is None else acc + part
        acc = cells(acc)
        if i == 0:
            acc = jnp.concatenate([acc[0:row_len] * top, acc[row_len:]], axis=0)
        if i == 2:
            acc = jnp.concatenate([acc[: BIG - row_len], acc[BIG - row_len :] * bottom], axis=0)
        total = acc if total is None else total + acc
    return total


def conv_kernel(halo, row_len, per_clip, fold, offsets, table_ref, n_ref, sums_ref, gains_ref, lo_ref, y_ref, hi_ref, w_ref, *refs):
    if fold:
        act_ref, out_ref, osums_ref, pad_ref = refs
    else:
        more_ref, act_ref, out_ref, osums_ref, pad_ref = refs
    size, width = y_ref.shape[0], y_ref.shape[2]
    sums = sums_ref[:, offsets[0] : offsets[0] + width]
    sums = folded(sums) if fold else sums
    factor, shift, _, _ = scale_of(sums, gains_ref[...], n_ref[1 if fold else 0])
    lanes = slice(offsets[1], offsets[1] + width)

    def value(ref, p, step):
        y = ref[pl.ds(p, step)] if ref is y_ref else ref[pl.ds(p, step), :, lanes]
        return gelu(y * factor[None] + shift[None]).astype(BF16).astype(F32)

    fill_padded(table_ref, (lo_ref, y_ref, hi_ref), 0, pad_ref, value, halo, size)

    def copy(p, carry):
        act_ref[pl.ds(p, 3)] = pad_ref[1, pl.ds(p, 3)].astype(BF16)
        return carry

    steps(size + 2 * halo, 3, copy, 0)

    def body(p, frames, carry):
        total = conv_rows(table_ref, per_clip, pad_ref, lambda i, j: w_ref[3 * i + j], p, halo, row_len, nn if fold else nt)
        out_ref[pl.ds(p, BIG)] = total
        masked = total * tile_mask(frames, width)
        return carry[0] + down(masked), carry[1] + down(masked * total)

    a, b = sweep(table_ref, size, BIG, body, (jnp.zeros((8, width), F32),) * 2)
    osums_ref[0:1, 0:width], osums_ref[1:2, 0:width] = flat(a), flat(b)
    if not fold:
        osums_ref[:, width:] = more_ref[...]


def slow_first_kernel(table_ref, n_ref, x0_ref, x1_ref, x2_ref, x3_ref, lp_ref, lsums_ref, gains_ref, w_ref, wl_ref, fb_ref, more_ref,
                      x_ref, lat_ref, sa_ref, sums_ref, first_ref, last_ref):
    size = lp_ref.shape[0]
    factor, shift, _, _ = scale_of(lsums_ref[:, 128:384], gains_ref[...], n_ref[0])

    def fill(p, frames, carry):
        mask = tile_mask(frames, 256)
        lat_ref[pl.ds(p, SMALL)] = (gelu(lp_ref[pl.ds(p, SMALL)] * factor[None] + shift[None]) * mask).astype(BF16)
        for k, ref in enumerate((x0_ref, x1_ref, x2_ref, x3_ref)):
            v = ref[pl.ds(p, SMALL)].astype(F32) * mask
            x_ref[pl.ds(p, SMALL), :, lanes_at(table_ref[5] ^ k, 256)] = v.astype(BF16)
        return carry

    sweep(table_ref, size, SMALL, fill)

    def body(p, frames, carry):
        acc = nt(rows_bf(x_ref[pl.ds(p, BIG)]), w_ref[...]) + nt(rows_bf(lat_ref[pl.ds(p, BIG)]), wl_ref[...])
        acc = cells(acc)
        sa = later(acc[:, :, 0:256]) + acc[:, :, 256:512] + sooner(acc[:, :, 512:768])
        sa_ref[pl.ds(p, BIG)] = sa
        masked = sa * tile_mask(frames, 256)
        return carry[0] + down(masked), carry[1] + down(masked * sa)

    a, b = sweep(table_ref, size, BIG, body, (jnp.zeros((8, 256), F32),) * 2)
    sums_ref[0:1, 0:256], sums_ref[1:2, 0:256] = flat(a), flat(b)
    sums_ref[:, 256:] = more_ref[...]
    halo = first_ref.shape[0]
    first_ref[:, :, 0:256], last_ref[:, :, 0:256] = sa_ref[0:halo], sa_ref[size - halo : size]
    first_ref[:, :, 256:], last_ref[:, :, 256:] = fb_ref[0:halo], fb_ref[size - halo : size]


def bypass_kernel(table_ref, x_ref, lat_ref, w_ref, wl_ref, sp_ref, sums_ref):
    def body(p, frames, carry):
        sp = cells(nn(rows_bf(x_ref[pl.ds(p, BIG)]), w_ref[...]) + nn(rows_bf(lat_ref[pl.ds(p, BIG)]), wl_ref[...]))
        sp_ref[pl.ds(p, BIG)] = sp.astype(BF16)
        masked = sp * tile_mask(frames, sp.shape[-1])
        return carry[0] + down(masked), carry[1] + down(masked * sp)

    a, b = sweep(table_ref, sp_ref.shape[0], BIG, body, (jnp.zeros((8, sp_ref.shape[2]), F32),) * 2)
    sums_ref[0:1], sums_ref[1:2] = flat(a), flat(b)


def expand_kernel(fold, offset, table_ref, n_ref, y_ref, sums_ref, gains_ref, w_ref, *refs):
    more, (h_ref, out_ref, osums_ref) = refs[:-3], refs[-3:]
    size, width = y_ref.shape[0], y_ref.shape[2]
    sums = sums_ref[:, offset : offset + width]
    sums = folded(sums) if fold else sums
    factor, shift, _, _ = scale_of(sums, gains_ref[...], n_ref[1 if fold else 0])

    def fill(p, frames, carry):
        v = gelu(y_ref[pl.ds(p, SMALL)] * factor[None] + shift[None])
        h_ref[pl.ds(p, SMALL)] = (v * tile_mask(frames, width)).astype(BF16)
        return carry

    sweep(table_ref, size, SMALL, fill)

    def body(p, frames, carry):
        out = cells(nn(rows_bf(h_ref[pl.ds(p, BIG)]), w_ref[...]))
        out_ref[pl.ds(p, BIG)] = out.astype(BF16)
        masked = out * tile_mask(frames, out.shape[-1])
        return carry[0] + down(masked), carry[1] + down(masked * out)

    wide_out = out_ref.shape[2]
    a, b = sweep(table_ref, size, BIG, body, (jnp.zeros((8, wide_out), F32),) * 2)
    osums_ref[0:1, 0:wide_out], osums_ref[1:2, 0:wide_out] = flat(a), flat(b)
    for ref in more:
        osums_ref[:, wide_out : wide_out + ref.shape[1]] = ref[...]
        wide_out += ref.shape[1]


def fast_out_kernel(offset, table_ref, n_ref, fc_ref, sums_ref, gains_ref, fx_ref, cot_ref, out_ref, up_ref, slopes_ref):
    size, width = fc_ref.shape[0], fc_ref.shape[2]
    factor, shift, center, inv_std = scale_of(folded(sums_ref[:, offset : offset + width]), gains_ref[...], n_ref[1])
    for z in range(4):
        lanes = slice(128 * z, 128 * z + 128)
        vecs = [v[:, lanes][None] for v in (factor, shift, center, inv_std)]

        def body(p, frames, carry, z=z, lanes=lanes, vecs=vecs):
            fz, sz, cz, rz = vecs
            y = fc_ref[pl.ds(p, SMALL), :, lanes].astype(F32)
            mask = tile_mask(frames, 128)
            total = y * fz + sz + fx_ref[pl.ds(p, SMALL), :, lanes].astype(F32)
            value, slope = gelu_pair(total)
            out_ref[z ^ table_ref[5], pl.ds(p, SMALL)] = (value * mask).astype(BF16)
            up = slope * (cot_ref[z ^ table_ref[5], pl.ds(p, SMALL)].astype(F32) * mask)
            up_ref[pl.ds(p, SMALL), :, lanes] = up.astype(BF16)
            return carry[0] + down(up), carry[1] + down(up * ((y - cz) * rz))

        a, b = sweep(table_ref, size, SMALL, body, (jnp.zeros((8, 128), F32),) * 2)
        slopes_ref[0:1, lanes], slopes_ref[1:2, lanes] = flat(a), flat(b)


def slow_out_kernel(table_ref, n_ref, sc_ref, sp_ref, sums_ref, gains_ref, cot_ref, more_ref, out_ref, up_ref, slopes_ref):
    size, width = sc_ref.shape[0], sc_ref.shape[2]
    cf, cs, cc, cr = scale_of(sums_ref[:, 0:width], gains_ref[0:2], n_ref[0])
    pf, ps, pc, pr = scale_of(sums_ref[:, width : 2 * width], gains_ref[2:4], n_ref[0])
    for z in range(4):
        lanes = slice(256 * z, 256 * z + 256)
        vecs = [v[:, lanes][None] for v in (cf, cs + ps, cc, cr, pf, pc, pr)]

        def body(p, frames, carry, z=z, lanes=lanes, vecs=vecs):
            cf, shift, cc, cr, pf, pc, pr = vecs
            yc, yp = (ref[pl.ds(p, SMALL), :, lanes].astype(F32) for ref in (sc_ref, sp_ref))
            mask = tile_mask(frames, 256)
            value, slope = gelu_pair(yc * cf + yp * pf + shift)
            out_ref[z ^ table_ref[5], pl.ds(p, SMALL)] = (value * mask).astype(BF16)
            up = slope * (cot_ref[z ^ table_ref[5], pl.ds(p, SMALL)].astype(F32) * mask)
            up_ref[pl.ds(p, SMALL), :, lanes] = up.astype(BF16)
            return (carry[0] + down(up), carry[1] + down(up * ((yc - cc) * cr)), carry[2] + down(up * ((yp - pc) * pr)))

        a, b, c = sweep(table_ref, size, SMALL, body, (jnp.zeros((8, 256), F32),) * 3)
        own, other = lanes, slice(width + 256 * z, width + 256 * z + 256)
        slopes_ref[0:1, own], slopes_ref[1:2, own] = flat(a), flat(b)
        slopes_ref[0:1, other], slopes_ref[1:2, other] = flat(a), flat(c)
    slopes_ref[:, 2 * width :] = more_ref[...]


def norm_back_fill(table_ref, up_ref, y_ref, dy_ref, factor, k0, k1):
    def fill(p, frames, carry):
        mask = tile_mask(frames, 128)
        for q in range(y_ref.shape[2] // 128):
            lanes = slice(128 * q, 128 * q + 128)
            y = y_ref[pl.ds(p, SMALL), :, lanes].astype(F32)
            dy = up_ref[pl.ds(p, SMALL), :, lanes].astype(F32) * factor[:, lanes][None]
            dy = dy - mask * (k0[:, lanes][None] + k1[:, lanes][None] * y)
            dy_ref[pl.ds(p, SMALL), :, lanes] = dy.astype(BF16)
        return carry

    sweep(table_ref, y_ref.shape[0], SMALL, fill)


def expand_back_kernel(fold, offsets, table_ref, n_ref, up_ref, y_ref, sums_ref, gains_ref, slopes_ref, z_ref, zsums_ref, zgains_ref,
                       w_ref, other_ref, dy_ref, dz_ref, oslopes_ref, first_ref, last_ref):
    size, width, inner = y_ref.shape[0], y_ref.shape[2], z_ref.shape[2]
    fix = folded if fold else (lambda v: v)
    inv_n = n_ref[1 if fold else 0]
    at_y, at_s, at_z = offsets
    factor, shift, center, inv_std = scale_of(fix(sums_ref[:, at_y : at_y + width]), gains_ref[...], inv_n)
    k0, k1 = slope_of(fix(slopes_ref[:, at_s : at_s + width]), factor, center, inv_std, inv_n)
    norm_back_fill(table_ref, up_ref, y_ref, dy_ref, factor, k0, k1)
    zf, zs, zc, zr = scale_of(fix(zsums_ref[:, at_z : at_z + inner]), zgains_ref[...], inv_n)

    def body(p, frames, carry):
        dh = cells(nt(rows_bf(dy_ref[pl.ds(p, BIG)]), w_ref[...]))
        z = z_ref[pl.ds(p, BIG)]
        dz = gelu_slope(z * zf[None] + zs[None]) * dh * tile_mask(frames, inner)
        dz_ref[pl.ds(p, BIG)] = dz
        return carry[0] + down(dz), carry[1] + down(dz * ((z - zc[None]) * zr[None]))

    a, b = sweep(table_ref, size, BIG, body, (jnp.zeros((8, inner), F32),) * 2)
    oslopes_ref[0:1, 0:inner], oslopes_ref[1:2, 0:inner] = flat(a), flat(b)
    halo = first_ref.shape[0]
    first_ref[:, :, 0:inner], last_ref[:, :, 0:inner] = dz_ref[0:halo], dz_ref[size - halo : size]
    if fold:
        first_ref[:, :, inner:], last_ref[:, :, inner:] = other_ref[0:halo], other_ref[size - halo : size]
    else:
        oslopes_ref[:, inner:] = other_ref[...]


def bypass_back_kernel(table_ref, n_ref, up_ref, y_ref, sums_ref, gains_ref, slopes_ref, w_ref, wl_ref, dy_ref, dx_ref, dl_ref):
    size, width = y_ref.shape[0], y_ref.shape[2]
    factor, shift, center, inv_std = scale_of(sums_ref[:, width : 2 * width], gains_ref[...], n_ref[0])
    k0, k1 = slope_of(slopes_ref[:, width : 2 * width], factor, center, inv_std, n_ref[0])
    norm_back_fill(table_ref, up_ref, y_ref, dy_ref, factor, k0, k1)

    def body(p, carry):
        dy = rows_bf(dy_ref[pl.ds(p, BIG)])
        dx_ref[pl.ds(p, BIG)] = cells(nt(dy, w_ref[...])).astype(BF16)
        dl_ref[pl.ds(p, BIG)] = cells(nt(dy, wl_ref[...]))
        return carry

    steps(size, BIG, body, 0)


def conv_back_kernel(halo, row_len, per_clip, fold, offsets, table_ref, n_ref, ysums_ref, ygains_ref, slopes_ref, ylo_ref, y_ref, yhi_ref,
                     dlo_ref, d_ref, dhi_ref, w_ref, z_ref, zsums_ref, zgains_ref, dy_ref, dz_ref, oslopes_ref, pad_ref):
    size, width = y_ref.shape[0], y_ref.shape[2]
    fix = folded if fold else (lambda v: v)
    inv_n = n_ref[1 if fold else 0]
    at_y, at_s, at_z, at_yhalo, at_dhalo = offsets
    factor, shift, center, inv_std = scale_of(fix(ysums_ref[:, at_y : at_y + width]), ygains_ref[...], inv_n)
    k0, k1 = slope_of(fix(slopes_ref[:, at_s : at_s + width]), factor, center, inv_std, inv_n)

    def value(refs, p, step):
        y_of, d_of = refs
        if y_of is y_ref:
            y, d = y_of[pl.ds(p, step)], d_of[pl.ds(p, step)]
        else:
            y, d = y_of[pl.ds(p, step), :, at_yhalo : at_yhalo + width], d_of[pl.ds(p, step), :, at_dhalo : at_dhalo + width]
        return (d * factor[None] - (k0[None] + k1[None] * y)).astype(BF16).astype(F32)

    fill_padded(table_ref, ((ylo_ref, dlo_ref), (y_ref, d_ref), (yhi_ref, dhi_ref)), 0, pad_ref, value, halo, size)

    def copy(p, carry):
        dy_ref[pl.ds(p, SMALL)] = pad_ref[1, pl.ds(halo + p, SMALL)].astype(BF16)
        return carry

    steps(size, SMALL, copy, 0)
    zf, zs, zc, zr = scale_of(fix(zsums_ref[:, at_z : at_z + width]), zgains_ref[...], inv_n)

    def body(p, frames, carry):
        dh = conv_rows(table_ref, per_clip, pad_ref, lambda i, j: w_ref[8 - 3 * i - j], p, halo, row_len, nt if fold else nn)
        z = z_ref[pl.ds(p, BIG)]
        dz = gelu_slope(z * zf[None] + zs[None]) * dh * tile_mask(frames, width)
        dz_ref[pl.ds(p, BIG)] = dz
        return carry[0] + down(dz), carry[1] + down(dz * ((z - zc[None]) * zr[None]))

    a, b = sweep(table_ref, size, BIG, body, (jnp.zeros((8, width), F32),) * 2)
    oslopes_ref[0:1], oslopes_ref[1:2] = flat(a), flat(b)


def slow_back_kernel(table_ref, n_ref, dz_ref, y_ref, sums_ref, gains_ref, slopes_ref, w_ref, wl_ref, dx_ref, dl_ref,
                     lp_ref, lsums_ref, lgains_ref, taps_ref, out_ref, dzl_ref, oslopes_ref):
    size = y_ref.shape[0]
    factor, shift, center, inv_std = scale_of(sums_ref[:, 0:256], gains_ref[...], n_ref[0])
    k0, k1 = slope_of(slopes_ref[...], factor, center, inv_std, n_ref[0])

    def fill(p, frames, carry):
        dy = dz_ref[pl.ds(p, SMALL)] * factor[None]
        dy = dy - tile_mask(frames, 256) * (k0[None] + k1[None] * y_ref[pl.ds(p, SMALL)])
        taps_ref[pl.ds(p, SMALL), :, 0:256] = sooner(dy).astype(BF16)
        taps_ref[pl.ds(p, SMALL), :, 256:512] = dy.astype(BF16)
        taps_ref[pl.ds(p, SMALL), :, 512:768] = later(dy).astype(BF16)
        return carry

    sweep(table_ref, size, SMALL, fill)
    lf, ls, lc, lr = scale_of(lsums_ref[:, 128:384], lgains_ref[...], n_ref[0])

    def body(p, frames, carry):
        taps = rows_bf(taps_ref[pl.ds(p, BIG)])
        mask = tile_mask(frames, 256)
        for z in range(4):
            lanes = slice(256 * z, 256 * z + 256)
            dx = cells(nn(taps, w_ref[:, lanes])) + dx_ref[pl.ds(p, BIG), :, lanes].astype(F32)
            out_ref[z ^ table_ref[5], pl.ds(p, BIG)] = (dx * mask).astype(BF16)
        dl = cells(nn(taps, wl_ref[...])) + dl_ref[pl.ds(p, BIG)]
        y = lp_ref[pl.ds(p, BIG)]
        dz = gelu_slope(y * lf[None] + ls[None]) * dl * mask
        dzl_ref[pl.ds(p, BIG)] = dz
        return carry[0] + down(dz), carry[1] + down(dz * ((y - lc[None]) * lr[None]))

    a, b = sweep(table_ref, size, BIG, body, (jnp.zeros((8, 256), F32),) * 2)
    oslopes_ref[0:1], oslopes_ref[1:2] = flat(a), flat(b)


def fast_back_kernel(at_s, table_ref, n_ref, sums_ref, fgains_ref, lgains_ref, fslopes_ref, lslopes_ref, dzf_ref, fa_ref, dzl_ref, lp_ref,
                     up_ref, w_ref, taps_ref, out_ref):
    size = fa_ref.shape[0]
    ff, fs, fc, fr = scale_of(folded(sums_ref[:, 0:128]), fgains_ref[...], n_ref[1])
    f0, f1 = slope_of(folded(fslopes_ref[:, at_s : at_s + 128]), ff, fc, fr, n_ref[1])
    lf, ls, lc, lr = scale_of(sums_ref[:, 128:384], lgains_ref[...], n_ref[0])
    l0, l1 = slope_of(lslopes_ref[...], lf, lc, lr, n_ref[0])

    def fill(p, frames, carry):
        dy = dzf_ref[pl.ds(p, SMALL)] * ff[None]
        dy = dy - tile_mask(frames, 128) * (f0[None] + f1[None] * fa_ref[pl.ds(p, SMALL)])
        taps_ref[pl.ds(p, SMALL), :, 0:128] = dy.astype(BF16)
        taps_ref[pl.ds(p, SMALL), :, 128:256] = sooner(dy).astype(BF16)
        taps_ref[pl.ds(p, SMALL), :, 256:384] = later(dy).astype(BF16)
        dy = dzl_ref[pl.ds(p, SMALL)] * lf[None]
        dy = dy - tile_mask(frames, 256) * (l0[None] + l1[None] * lp_ref[pl.ds(p, SMALL)])
        taps_ref[pl.ds(p, SMALL), :, 384:640] = dy.astype(BF16)
        taps_ref[pl.ds(p, SMALL), :, 640:896] = sooner(dy).astype(BF16)
        return carry

    sweep(table_ref, size, SMALL, fill)

    def body(p, frames, carry):
        dx = cells(nn(rows_bf(taps_ref[pl.ds(p, BIG)]), w_ref[...]))
        mask = tile_mask(frames, 128)
        for z in range(4):
            lanes = slice(128 * z, 128 * z + 128)
            up = up_ref[pl.ds(p, BIG), :, lanes].astype(F32)
            out_ref[z ^ table_ref[5], pl.ds(p, BIG)] = ((dx[:, :, lanes] + up) * mask).astype(BF16)
        return carry

    sweep(table_ref, size, BIG, body)


def tn(a, b):
    return lax.dot_general(a, b, (((0,), (0,)), ((), ())), preferred_element_type=F32)


def conv_weight_kernel(halo, row_len, per_clip, fold, table_ref, act_ref, dy_ref, out_ref, pad_ref, acc_ref):
    size, width = dy_ref.shape[0], dy_ref.shape[2]
    phase = table_ref[5] * (size // SMALL)

    def copy(p, carry):
        v = act_ref[pl.ds(p, 3)].astype(F32)
        for k in range(3):
            pad_ref[k, pl.ds(p, 3)] = v
        return carry

    steps(size + 2 * halo, 3, copy, 0)
    parts = size // SMALL

    def clear(i, carry):
        even = ((phase + i) % 2 == 0).astype(F32)
        at = halo + (i - 2) * SMALL
        pad_ref[0, pl.ds(at + SMALL - 1, 1)] = pad_ref[0, pl.ds(at + SMALL - 1, 1)] * even
        pad_ref[2, pl.ds(at, 1)] = pad_ref[2, pl.ds(at, 1)] * (1.0 - even)
        return carry

    lax.fori_loop(0, parts + 4, clear, 0)
    low_even = ((phase + 1) % 2 == 0).astype(F32)
    pad_ref[0, 0:1] = pad_ref[0, 0:1] * low_even
    high_even = ((phase + parts) % 2 == 0).astype(F32)
    end = size + 2 * halo
    pad_ref[2, end - 1 : end] = pad_ref[2, end - 1 : end] * (1.0 - high_even)

    for c in range(size // BIG):
        p = c * BIG
        top, bottom = edge_scales(table_ref, p, per_clip)
        dy = rows_bf(dy_ref[p : p + BIG])
        for i in range(3):
            begin = p + halo + row_len * (i - 1)
            taps = []
            for j in range(3):
                v = pad_ref[j, begin + j - 1 : begin + j - 1 + BIG]
                if i == 0:
                    v = jnp.concatenate([v[0:row_len] * top, v[row_len:]], axis=0)
                if i == 2:
                    v = jnp.concatenate([v[: BIG - row_len], v[BIG - row_len :] * bottom], axis=0)
                taps.append(rows(v).astype(BF16))
            taps = jnp.concatenate(taps, axis=1)
            part = tn(taps, dy) if fold else tn(dy, taps)
            acc_ref[i] = part if c == 0 else acc_ref[i] + part
    if fold:
        out_ref[...] = acc_ref[...]
        return
    for i in range(3):
        for j in range(3):
            v = acc_ref[i, :, width * j : width * j + width].reshape(4, 8, 8, width)
            out_ref[:, :, 3 * i + j] = v.astype(BF16)


def fast_grads_kernel(first_ref, sp_ref, ex_ref, lat_ref, out_ref):
    def pick(at, count, r, ref=first_ref):
        return sum(lane_group(moved(ref[at : at + count, 128 * z : 128 * z + 128], 32 * z - 32 * r), z) for z in range(4))

    taps = [pick(640, 256, 2), pick(640, 256, 3), pick(384, 256, 0), pick(384, 256, 1), pick(384, 256, 2)]
    for j in range(5):
        lat_ref[:, :, j] = taps[j].reshape(4, 8, 8, 128).astype(BF16)
    for j in range(3):
        total = sum(pick(32 * q, 32, q + j - 1) for q in range(4) if 0 <= q + j - 1 < 4)
        if j == 0:
            total = total + pick(128, 32, 3)
        if j == 2:
            total = total + pick(352, 32, 0)
        out_ref[4 * j : 4 * j + 4] = total.reshape(4, 8, 128).astype(BF16)
    total = sum(pick(32 * r, 32, r, ex_ref) for r in range(4))
    out_ref[12:16] = total.reshape(4, 8, 128).astype(BF16)
    for i in range(3):
        total = None
        for j in range(3):
            tap = sum(
                lane_group(moved(sp_ref[i, 128 * j + 32 * r : 128 * j + 32 * r + 32, :], 32 * j - 32 * r), j) for r in range(4)
            )
            total = tap if total is None else total + tap
        out_ref[16 + 4 * i : 20 + 4 * i] = total.reshape(4, 8, 128).astype(BF16)


def swap(tree, axis, size, distance):
    pairs = [(i, i ^ distance) for i in range(size)]
    return jax.tree.map(lambda v: lax.ppermute(v, axis, pairs), tree)


def add(*trees):
    def total(*vs):
        wide_vs = [v.astype(F32) for v in vs]
        out = wide_vs[0] + wide_vs[1]
        if len(vs) == 4:
            out = out + (wide_vs[2] + wide_vs[3])
        return out.astype(vs[0].dtype)

    return jax.tree.map(total, *trees)


def stages(size, first_alone):
    bits = [1 << i for i in range(size.bit_length() - 1)]
    out = []
    if first_alone and bits:
        out.append(bits[:1])
        bits = bits[1:]
    while bits:
        out.append(bits[:2])
        bits = bits[2:]
    return out


def butterfly(tree, axis, size, bits):
    if len(bits) == 1:
        return add(tree, swap(tree, axis, size, bits[0]))
    near, far, both = (swap(tree, axis, size, k) for k in (bits[0], bits[1], bits[0] + bits[1]))
    return add(tree, near, far, both)


def everywhere(tree, sizes):
    for axis, size in sizes.items():
        for bits in stages(size, axis == "dp"):
            tree = butterfly(tree, axis, size, bits)
    return tree


def halos(first, last, count):
    low = lax.ppermute(last, "chan", [(i, i + 1) for i in range(count - 1)])
    high = lax.ppermute(first, "chan", [(i + 1, i) for i in range(count - 1)])
    return low, high


def gather_group(tree, sizes):
    dp = sizes["dp"]
    by_chip = [tree] + [swap(tree, "dp", dp, 2 * k) for k in (1, 2, 3)]
    out = []
    for piece in by_chip:
        out += [piece, swap(piece, "dp", dp, 1)]
    return out


def pick(v, index, axis):
    return lax.dynamic_index_in_dim(v, index, axis, keepdims=False)


def scatter_sum(tree, sizes, group, chan):
    dp = sizes["dp"]
    core, chip = group % 2, group // 2
    tree = jax.tree.map(lambda v: v.reshape(v.shape[0], 4, 2, *v.shape[2:]), tree)
    sent = jax.tree.map(lambda v: pick(v, 1 - core, 2), tree)
    kept = jax.tree.map(lambda v: pick(v, core, 2), tree)
    tree = add(kept, swap(sent, "dp", dp, 1))
    got = [swap(jax.tree.map(lambda v: pick(v, chip ^ k, 1), tree), "dp", dp, 2 * k) for k in (1, 2, 3)]
    tree = add(jax.tree.map(lambda v: pick(v, chip, 1), tree), *got)
    size = sizes["chan"]
    got = [swap(jax.tree.map(lambda v: pick(v, chan ^ k, 0), tree), "chan", size, k) for k in (1, 2, 3)]
    tree = add(jax.tree.map(lambda v: pick(v, chan, 0), tree), *got)
    bits = [1 << i for i in range(3, dp.bit_length() - 1)]
    while bits:
        tree = butterfly(tree, "dp", dp, bits[:2])
        bits = bits[2:]
    return tree


def send_blocks(blocks, size):
    return [blocks[0]] + [swap(blocks[k], "chan", size, k) for k in range(1, size)]


def weight_sum(a, b, dtype=BF16):
    return jnp.einsum("pti,pto->io", a, b, preferred_element_type=F32).astype(dtype)


def local(
    sizes,
    slow_input,
    fast_input,
    clip_counts,
    frame_counts,
    fast_reduce,
    fast_spatial,
    fast_expand,
    lateral_kernel,
    slow_reduce,
    lateral_reduce,
    slow_spatial,
    slow_expand,
    shortcut,
    lateral_shortcut,
    fast_inner_norm,
    fast_outer_norm,
    lateral_norm,
    slow_inner_norm,
    slow_outer_norm,
    slow_cotangent,
    fast_cotangent,
):
    ways = sizes["chan"]
    clips, slow_t, height, across, slow_part = slow_input.shape
    fast_t, fast_part = fast_input.shape[1], fast_input.shape[4]
    ratio = fast_t // slow_t
    area = height * across
    places = clips * area
    mine = places // ways
    halo = across + 1
    chan, dp = lax.axis_index("chan"), lax.axis_index("dp")
    group = dp % 8
    ids = jnp.stack([dp, chan, group]).astype(jnp.int32)
    wide_in = ways * slow_part
    wide_f = ways * 128
    mid = 256
    ext = mine + 2 * halo
    per_clip = area // BIG
    chunk = 98

    def packed(v):
        v = v.transpose(0, 2, 3, 1, 4).reshape(places, fast_t, fast_part)
        return pl.pallas_call(
            functools.partial(pack_kernel, area // chunk, clips),
            grid=(places // chunk,),
            out_shape=shape((places, slow_t, 128), BF16),
            in_specs=[pl.BlockSpec(memory_space=pltpu.SMEM)] * 3
            + [pl.BlockSpec((chunk, fast_t, fast_part), lambda i: (i, 0, 0))],
            out_specs=pl.BlockSpec((chunk, slow_t, 128), lambda i: (i, 0, 0)),
            scratch_shapes=[pltpu.VMEM((chunk * fast_t, fast_part), F32)],
            compiler_params=pltpu.CompilerParams(vmem_limit_bytes=12 * 1024 * 1024),
            name="fast_pack",
        )(ids, clip_counts, frame_counts, v).reshape(ways, mine, slow_t, 128)

    def unpacked(pieces):
        (out,) = call(
            unpack_kernel,
            [shape((places, fast_t, fast_part), BF16)],
            [ids, *pieces],
            [pltpu.VMEM((BIG * fast_t, fast_part), F32)],
            smem=1,
            name="fast_unpack",
        )
        return out.reshape(clips, height, across, fast_t, fast_part).transpose(0, 3, 1, 2, 4)

    def split(v):
        return v.transpose(0, 2, 3, 1, 4).reshape(ways, mine, slow_t, slow_part)

    def joined(pieces):
        (v,) = call(
            place_kernel, [shape((ways, mine, slow_t, slow_part), BF16)], [ids, *pieces], smem=1, name="slow_place"
        )
        return v.reshape(clips, height, across, slow_t, slow_part).transpose(0, 3, 1, 2, 4)

    def exchanged(v):
        return send_blocks([pick(v, chan ^ k, 0) for k in range(ways)], ways)

    def returned(v):
        return send_blocks([v[k] for k in range(ways)], ways)

    fx_pieces = exchanged(packed(fast_input))
    x_pieces = exchanged(split(slow_input))

    all_clips = frame_counts.shape[0]
    live = (jnp.arange(all_clips, dtype=jnp.int32) % clips) < jnp.repeat(clip_counts, clips)
    valid = jnp.where(live, frame_counts, 0)
    count = jnp.sum(valid).astype(F32) * area
    inv_n = jnp.stack([1.0 / count, 1.0 / (count * ratio)])
    parts = mine // BIG
    clip = (chan * parts + jnp.arange(-1, parts + 1)) // per_clip
    clip = jnp.clip(clip, 0, clips - 1) + dp * clips
    around = jnp.sum(jnp.where(clip[:, None] == jnp.arange(all_clips)[None, :], valid[None, :], 0), axis=1)
    table = jnp.concatenate([around, jnp.stack([chan, jnp.full_like(chan, parts)])]).astype(jnp.int32)

    def share_of(v, axis):
        amount = v.shape[axis] // 8
        return lax.dynamic_slice_in_dim(v, group * amount, amount, axis).astype(BF16)

    def over_chan(tree):
        pieces = [tree] + [swap(tree, "chan", ways, k) for k in (1, 2, 3)]
        return jax.tree.map(lambda *vs: jnp.stack(vs), *pieces)

    lat_t, red_t, lred_t = (v.transpose(0, 2, 1) for v in (lateral_kernel, slow_reduce, lateral_reduce))
    tree = (jnp.concatenate([share_of(red_t, 1), share_of(lred_t, 1)], axis=2), share_of(lat_t, 1))

    def blocks_of(v):
        width = v.shape[-1]
        tiled = jnp.concatenate([v] * ways, axis=1)
        return jnp.where(jnp.arange(ways * width)[None, :] // width == chan, tiled, 0.0)

    mid_g = blocks_of(jnp.concatenate([lateral_norm, slow_inner_norm.reshape(4, -1)]))
    out_g = blocks_of(slow_outer_norm.reshape(4, -1))
    mid_g, out_g = butterfly((mid_g, out_g), "chan", ways, (1, 2))
    lat_g, in_g = mid_g[0:2], (mid_g[2:4], mid_g[4:6])
    pieces = gather_group(over_chan(tree), sizes)
    fr_t = fast_reduce.transpose(0, 2, 1)
    red_w, lred_w, w_first, w_fsp, w_fex, fin_g, fout_g = call(
        first_weights_kernel,
        [
            shape((3, ways, 8, 8, wide_in), BF16),
            shape((3, ways, 8, 8, mid), BF16),
            shape((896, wide_f), BF16),
            shape((9, 128, 128), BF16),
            shape((128, wide_f), BF16),
            shape((4, 128)),
            shape((2, wide_f)),
        ],
        [ids, *(p[0] for p in pieces), *(p[1] for p in pieces), fr_t, fast_spatial.reshape(9, *fast_spatial.shape[2:]), fast_expand,
         fast_inner_norm.reshape(4, -1), fast_outer_norm],
        [pltpu.VMEM((5, ways, 8, 8, 128), F32)],
        smem=1,
        name="first_weights",
    )
    red_w, lred_w = red_w.reshape(-1, wide_in), lred_w.reshape(-1, mid)
    fin_g = (fin_g[0:2], fin_g[2:4])
    spatial_t = slow_spatial.reshape(9, slow_spatial.shape[2], -1).transpose(0, 2, 1)
    tree = (
        jnp.concatenate([share_of(v, 0).reshape(-1, 8, wide_in) for v in (slow_expand, shortcut, lateral_shortcut)]),
        share_of(spatial_t, 1),
    )
    pieces = gather_group(over_chan(tree), sizes)
    exp_w, short_w, lshort_w, spat_w = call(
        second_weights_kernel,
        [
            shape((ways, 8, 8, wide_in), BF16),
            shape((ways, 8, 4, 8, wide_in), BF16),
            shape((ways, 8, 8, wide_in), BF16),
            shape((9, ways, 8, 8, mid), BF16),
        ],
        [ids, *(p[0] for p in pieces), *(p[1] for p in pieces)],
        smem=1,
        name="second_weights",
    )
    exp_w, short_w, lshort_w = (v.reshape(-1, wide_in) for v in (exp_w, short_w, lshort_w))
    spat_w = spat_w.reshape(9, mid, mid)

    edge = [shape((halo, 8, 128))] * 2
    edges = [shape((halo, 8, 384))] * 2
    narrow, middle = shape((mine, 8, 128)), shape((mine, 8, mid))
    fx, fa, lp, sums1, first, last = call(
        fast_first_kernel,
        [shape((mine, 8, wide_f), BF16), narrow, middle, shape((2, 384)), *edge],
        [table, *fx_pieces, w_first],
        smem=1,
        name="fast_first",
    )
    sums1, fast_cotangent, slow_cotangent = lax.optimization_barrier((sums1, fast_cotangent, slow_cotangent))
    fa_lo, fa_hi = halos(first, last, ways)
    sums1 = everywhere(sums1, sizes)
    fast_pad = [pltpu.VMEM((3, ext, 8, 128), F32)]
    slow_pad = [pltpu.VMEM((3, ext, 8, mid), F32)]
    h1, fb, fb_sums = call(
        functools.partial(conv_kernel, halo, across, per_clip, True, (0, 0)),
        [shape((ext, 8, 128), BF16), narrow, shape((2, 128))],
        [table, inv_n, sums1, fin_g[0], fa_lo, fa, fa_hi, w_fsp],
        fast_pad,
        smem=2,
        name="fast_second",
    )
    x, lat, sa, sums2, first, last = call(
        slow_first_kernel,
        [shape((mine, 8, wide_in), BF16), shape((mine, 8, mid), BF16), middle, shape((2, mid + 128)), *edges],
        [table, inv_n, *x_pieces, lp, sums1, lat_g, red_w, lred_w, fb, fb_sums],
        smem=2,
        name="slow_first",
    )
    sa_lo, sa_hi = halos(first, last, ways)
    sums2 = everywhere(sums2, sizes)
    h2, fc, fc_sums = call(
        functools.partial(expand_kernel, True, mid),
        [shape((mine, 8, 128), BF16), shape((mine, 8, wide_f), BF16), shape((2, wide_f))],
        [table, inv_n, fb, sums2, fin_g[1], w_fex],
        smem=2,
        name="fast_third",
    )
    ha, sb, sums3 = call(
        functools.partial(conv_kernel, halo, across, per_clip, False, (0, 0)),
        [shape((ext, 8, mid), BF16), middle, shape((2, mid + wide_f))],
        [table, inv_n, sums2, in_g[0], sa_lo, sa, sa_hi, spat_w, fc_sums],
        slow_pad,
        smem=2,
        name="slow_second",
    )
    sums3 = everywhere(sums3, sizes)
    sp, sp_sums = call(
        bypass_kernel,
        [shape((mine, 8, wide_in), BF16), shape((2, wide_in))],
        [table, x, lat, short_w, lshort_w],
        smem=1,
        name="bypass",
    )
    fcot = jnp.stack(exchanged(packed(fast_cotangent)))
    cot = jnp.stack(exchanged(split(slow_cotangent)))
    fast_out, dfs, fc_slopes = call(
        functools.partial(fast_out_kernel, mid),
        [shape((ways, mine, 8, 128), BF16), shape((mine, 8, wide_f), BF16), shape((2, wide_f))],
        [table, inv_n, fc, sums3, fout_g, fx, fcot],
        smem=2,
        name="fast_out",
    )
    hb, sc, sums4 = call(
        functools.partial(expand_kernel, False, 0),
        [shape((mine, 8, mid), BF16), shape((mine, 8, wide_in), BF16), shape((2, 2 * wide_in + wide_f))],
        [table, inv_n, sb, sums3, in_g[1], exp_w, sp_sums, fc_slopes],
        smem=2,
        name="slow_third",
    )
    sums4 = everywhere(sums4, sizes)
    dfc, dzfb, fb_slopes, first, last = call(
        functools.partial(expand_back_kernel, True, (mid, 2 * wide_in, mid)),
        [shape((mine, 8, wide_f), BF16), narrow, shape((2, 128)), *edges],
        [table, inv_n, dfs, fc, sums3, fout_g, sums4, fb, sums2, fin_g[1], w_fex, sb],
        smem=2,
        name="fast_third_back",
    )
    slow_out, dss, sums5 = call(
        slow_out_kernel,
        [shape((ways, mine, 8, mid), BF16), shape((mine, 8, wide_in), BF16), shape((2, 2 * wide_in + 128))],
        [table, inv_n, sc, sp, sums4, out_g, cot, fb_slopes],
        smem=2,
        name="slow_out",
    )

    low5, high5 = halos(first, last, ways)
    sums5 = everywhere(sums5, sizes)
    dfb, dzfa, fa_slopes = call(
        functools.partial(conv_back_kernel, halo, across, per_clip, True, (mid, 2 * wide_in, 0, mid, 0)),
        [shape((mine, 8, 128), BF16), narrow, shape((2, 128))],
        [table, inv_n, sums2, fin_g[1], sums5, sa_lo, fb, sa_hi, low5, dzfb, high5, w_fsp, fa, sums1, fin_g[0]],
        fast_pad,
        smem=2,
        name="fast_second_back",
    )
    dsc, dzsb, sums6, first, last = call(
        functools.partial(expand_back_kernel, False, (0, 0, 0)),
        [shape((mine, 8, wide_in), BF16), middle, shape((2, mid + 128)), *[shape((halo, 8, mid))] * 2],
        [table, inv_n, dss, sc, sums4, out_g[0:2], sums5, sb, sums3, in_g[1], exp_w, fa_slopes],
        smem=2,
        name="slow_third_back",
    )
    low6, high6 = halos(first, last, ways)
    sums6 = everywhere(sums6, sizes)
    fast_output = unpacked(returned(fast_out))
    dzsb, fast_output = lax.optimization_barrier((dzsb, fast_output))
    dsp, dx, dl = call(
        bypass_back_kernel,
        [shape((mine, 8, wide_in), BF16), shape((mine, 8, wide_in), BF16), middle],
        [table, inv_n, dss, sp, sums4, out_g[2:4], sums5, short_w, lshort_w],
        smem=2,
        name="bypass_back",
    )
    dsb, dzsa, sums7 = call(
        functools.partial(conv_back_kernel, halo, across, per_clip, False, (0, 0, 0, 128, 0)),
        [shape((mine, 8, mid), BF16), middle, shape((2, mid))],
        [table, inv_n, sums3, in_g[1], sums6, low5, sb, high5, low6, dzsb, high6, spat_w, sa, sums2, in_g[0]],
        slow_pad,
        smem=2,
        name="slow_second_back",
    )
    sums7 = everywhere(sums7, sizes)
    slow_output = joined(returned(slow_out))
    dzsa, slow_output = lax.optimization_barrier((dzsa, slow_output))
    dsa, dslow, dzlp, sums8 = call(
        slow_back_kernel,
        [shape((mine, 8, 3 * mid), BF16), shape((ways, mine, 8, mid), BF16), middle, shape((2, mid))],
        [table, inv_n, dzsa, sa, sums2, in_g[0], sums7, red_w, lred_w, dx, dl, lp, sums1, lat_g],
        smem=2,
        name="slow_first_back",
    )
    slow_input_grad = joined(returned(dslow))
    sums8 = everywhere(sums8, sizes)
    dfirst, dfast = call(
        functools.partial(fast_back_kernel, mid),
        [shape((mine, 8, 896), BF16), shape((ways, mine, 8, 128), BF16)],
        [table, inv_n, sums1, fin_g[0], lat_g, sums6, sums8, dzfa, fa, dzlp, lp, dfs, w_first],
        smem=2,
        name="fast_first_back",
    )

    fast_input_grad = unpacked(returned(dfast))

    def shares(v, lead):
        return v.reshape(ways, 8, lead, 8, v.shape[-1])

    g_wide = jnp.concatenate(
        [shares(weight_sum(hb, dsc), 1), shares(weight_sum(x, dsp), 4), shares(weight_sum(lat, dsp), 1)], axis=2
    )
    (g_spat,) = call(
        functools.partial(conv_weight_kernel, halo, across, per_clip, False),
        [shape((ways, 8, 9, 8, mid), BF16)],
        [table, ha, dsb],
        [*slow_pad, pltpu.VMEM((3, mid, 3 * mid), F32)],
        smem=1,
        name="slow_spatial_grad",
    )
    pieces = gather_group(scatter_sum((g_wide, g_spat), sizes, group, chan), sizes)
    g_exp, g_short, g_lshort, g_spat = call(
        first_grads_kernel,
        [shape((8, 8, wide_in)), shape((8, 4, 8, wide_in)), shape((8, 8, wide_in)), shape((9, 8, 8, mid))],
        [ids, *(p[0] for p in pieces), *(p[1] for p in pieces)],
        smem=1,
        name="first_grads",
    )
    (g_fsp,) = call(
        functools.partial(conv_weight_kernel, halo, across, per_clip, True),
        [shape((3, 384, 128))],
        [table, h1, dfb],
        [*fast_pad, pltpu.VMEM((3, 384, 128), F32)],
        smem=1,
        name="fast_spatial_grad",
    )
    g_fex = weight_sum(h2, dfc, F32)
    g_lat, g_fast = call(
        fast_grads_kernel,
        [shape((ways, 8, 5, 8, 128), BF16), shape((28, 8, 128), BF16)],
        [weight_sum(dfirst, fx, F32), g_fsp, g_fex],
        name="fast_grads",
    )
    g_red = weight_sum(dsa, jnp.concatenate([x, lat], axis=2)).reshape(3, ways, 8, 8, wide_in + mid).transpose(1, 2, 0, 3, 4)
    g_fast = everywhere(g_fast, sizes)
    pieces = gather_group(scatter_sum((g_red, g_lat), sizes, group, chan), sizes)
    g_red, g_lred, g_lat = call(
        second_grads_kernel,
        [shape((3, 8, 8, wide_in)), shape((3, 8, 8, mid)), shape((5, 8, 8, 128))],
        [ids, *(p[0] for p in pieces), *(p[1] for p in pieces)],
        smem=1,
        name="second_grads",
    )
    g_fast = g_fast.astype(F32)
    g_fred = g_fast[0:12].reshape(3, 32, 128).transpose(0, 2, 1)
    g_fex = g_fast[12:16].reshape(32, 128)
    g_fsp = g_fast[16:28].reshape(3, 32, 128)[:, :, 0:96].reshape(3, 32, 3, 32).transpose(0, 2, 1, 3)

    def pair(slopes):
        return slopes[::-1]

    def own(v, width):
        return lax.dynamic_slice_in_dim(v, chan * width, width, v.ndim - 1)

    def fold_in(slopes):
        return jnp.sum(slopes.reshape(2, ratio, 128 // ratio), axis=1)

    lw, sw, ow = lateral_norm.shape[1], slow_inner_norm.shape[2], slow_outer_norm.shape[2]
    fast_inner_grad = jnp.stack([pair(fold_in(sums6[:, mid:])), pair(fold_in(sums5[:, 2 * wide_in :]))])
    fc_slopes = sums4[:, 2 * wide_in :].reshape(2, ways, ratio, fast_part)
    fast_outer_grad = pair(jnp.sum(fc_slopes, axis=2).reshape(2, -1))
    lateral_grad = pair(own(sums8, lw))
    slow_inner_grad = own(jnp.stack([pair(sums7), pair(sums6[:, 0:mid])]), sw)
    slow_outer_grad = own(jnp.stack([pair(sums5[:, 0:wide_in]), pair(sums5[:, wide_in : 2 * wide_in])]), ow)
    return (
        slow_output,
        fast_output,
        slow_input_grad,
        fast_input_grad,
        g_fred,
        g_fsp,
        g_fex,
        g_lat.reshape(5, -1, 128).transpose(0, 2, 1),
        g_red.reshape(3, -1, wide_in).transpose(0, 2, 1),
        g_lred.reshape(3, -1, mid).transpose(0, 2, 1),
        g_spat.reshape(9, -1, mid).transpose(0, 2, 1).reshape(slow_spatial.shape),
        g_exp.reshape(-1, wide_in),
        g_short.reshape(-1, wide_in),
        g_lshort.reshape(-1, wide_in),
        fast_inner_grad,
        fast_outer_grad,
        lateral_grad,
        slow_inner_grad,
        slow_outer_grad,
    )


def solution(mesh):
    sizes = {"dp": mesh.shape["dp"], "chan": mesh.shape["chan"]}
    big = P("dp", None, None, None, "chan")
    last2, last3, last4 = P(None, "chan"), P(None, None, "chan"), P(None, None, None, "chan")
    first = P("chan", None)
    return jax.shard_map(
        functools.partial(local, sizes),
        mesh=mesh,
        in_specs=(
            big, big, P(), P(), P(), P(), P(), last3, last3, last3, last4, first, first, first,
            P(), P(), last2, last3, last3, big, big,
        ),
        out_specs=(
            big, big, big, big, P(), P(), P(), last3, last3, last3, last4, first, first, first,
            P(), P(), last2, last3, last3,
        ),
        check_vma=False,
    )
```

```python
import functools

import jax
import jax.numpy as jnp
from jax import lax
from jax.experimental import pallas as pl
from jax.experimental.pallas import tpu as pltpu
from jax.sharding import PartitionSpec as P

F32 = jnp.float32
BF16 = jnp.bfloat16
EPSILON = 1e-05
ROOT = 0.7978845608028654
CUBIC = 0.044715
BIG = 49
SMALL = 7


def gelu(v):
    return 0.5 * v * (1.0 + jnp.tanh(ROOT * (v * (1.0 + CUBIC * (v * v)))))


def gelu_slope(v):
    square = v * v
    th = jnp.tanh(ROOT * (v * (1.0 + CUBIC * square)))
    half = 0.5 * (1.0 + th)
    return half + (0.5 * ROOT) * v * (1.0 - th * th) * (1.0 + 3.0 * CUBIC * square)


def gelu_pair(v):
    square = v * v
    th = jnp.tanh(ROOT * (v * (1.0 + CUBIC * square)))
    half = 0.5 * (1.0 + th)
    slope = half + (0.5 * ROOT) * v * (1.0 - th * th) * (1.0 + 3.0 * CUBIC * square)
    return v * half, slope


def rows(v):
    return v.reshape(v.shape[0] * v.shape[1], v.shape[2])


def cells(v):
    return v.reshape(v.shape[0] // 8, 8, v.shape[1])


def rows_bf(v):
    return rows(v.astype(F32)).astype(BF16)


def wide(mask, width):
    repeats = width // 128
    return mask if repeats == 1 else jnp.concatenate([mask] * repeats, axis=-1)


def nn(a, b):
    return jnp.dot(a, b, preferred_element_type=F32)


def nt(a, b):
    return lax.dot_general(a, b, (((1,), (1,)), ((), ())), preferred_element_type=F32)


def later(v):
    rolled = pltpu.roll(v, 1, 1)
    return jnp.where(lax.broadcasted_iota(jnp.int32, v.shape, 1) == 0, 0.0, rolled)


def sooner(v):
    rolled = pltpu.roll(v, 7, 1)
    return jnp.where(lax.broadcasted_iota(jnp.int32, v.shape, 1) == 7, 0.0, rolled)


def folded(v):
    out = []
    for block in range(v.shape[-1] // 128):
        part = v[:, 128 * block : 128 * block + 128]
        part = part + pltpu.roll(part, 64, 1)
        out.append(part + pltpu.roll(part, 32, 1))
    return out[0] if len(out) == 1 else jnp.concatenate(out, axis=-1)


def scale_of(sums, gains, inv_n):
    center = sums[0:1] * inv_n
    spread = sums[1:2] * inv_n - center * center
    inv_std = lax.rsqrt(spread + EPSILON)
    factor = gains[0:1] * inv_std
    return factor, gains[1:2] - center * factor, center, inv_std


def slope_of(slopes, factor, center, inv_std, inv_n):
    k1 = factor * slopes[1:2] * inv_n * inv_std
    k0 = factor * slopes[0:1] * inv_n - k1 * center
    return k0, k1


def down(v):
    return jnp.sum(v, axis=0)


def flat(v):
    return jnp.sum(v, axis=0, keepdims=True)


def steps(count, step, body, carry):
    return lax.fori_loop(0, count // step, lambda i, c: body(i * step, c), carry)


def call(kernel, outs, args, scratch=(), smem=0, flops=0, name=None):
    specs = [pl.BlockSpec(memory_space=pltpu.SMEM if i < smem else pltpu.VMEM) for i in range(len(args))]
    total = sum(a.size * a.dtype.itemsize for a in args)
    total += sum(o.size * o.dtype.itemsize for o in outs)
    def padded(v):
        dims = list(v.shape)
        if len(dims) < 2:
            return 4096
        dims[-1] = -(-dims[-1] // 128) * 128
        dims[-2] = -(-dims[-2] // 8) * 8
        amount = v.dtype.itemsize
        for d in dims:
            amount *= d
        return amount

    room = sum(padded(v) for v in (*args, *outs, *scratch)) + 6 * 1024 * 1024
    return pl.pallas_call(
        kernel,
        out_shape=tuple(outs),
        in_specs=specs,
        out_specs=tuple(pl.BlockSpec(memory_space=pltpu.VMEM) for _ in outs),
        scratch_shapes=list(scratch),
        compiler_params=pltpu.CompilerParams(vmem_limit_bytes=room),
        cost_estimate=pl.CostEstimate(flops=flops, bytes_accessed=1, transcendentals=0),
        name=name,
    )(*args)


def shape(dims, dtype=F32):
    return jax.ShapeDtypeStruct(dims, dtype)


def tile_mask(frames, width):
    tile = (lax.broadcasted_iota(jnp.int32, (8, 128), 0) < frames).astype(F32)
    return wide(tile, width)[None]


def sweep(table_ref, size, step, body, carry=0):
    def run(i, kept):
        p = i * step
        return body(p, table_ref[1 + p // BIG], kept)

    return lax.fori_loop(0, size // step, run, carry)


def lane_group(v, group):
    return jnp.where(lax.broadcasted_iota(jnp.int32, v.shape, v.ndim - 1) // 32 == group, v, 0.0)


def moved(v, shift):
    shift = shift % 128
    return v if shift == 0 else pltpu.roll(v, shift, v.ndim - 1)


def pack_kernel(per_clip, clips, ids_ref, counts_ref, frames_ref, x_ref, *refs):
    out_ref, tmp_ref = refs[-2:]
    clip, dp = pl.program_id(0) // per_clip, ids_ref[0]
    chunk = x_ref.shape[0]
    frames = jnp.where(clip < counts_ref[dp], frames_ref[dp * clips + clip], 0)
    tmp_ref[...] = x_ref[...].astype(F32).reshape(chunk * 32, 32)
    parts = [tmp_ref[pl.ds(r, chunk * 8, stride=4), :] for r in range(4)]
    out_ref[:, :, 0:128] = (cells(jnp.concatenate(parts, axis=1)) * tile_mask(frames, 128)).astype(BF16)
    if len(refs) == 3:
        out_ref[:, :, 128:384] = refs[0][...]


def unpack_kernel(width, ids_ref, *refs):
    pieces, tmp_ref = refs[:4], refs[-1]
    size = pieces[0].shape[0]
    for k in range(4):
        begin = (ids_ref[1] ^ k) * size

        def body(p, carry, k=k, begin=begin):
            joined = rows(pieces[k][pl.ds(p, BIG), :, 0:128].astype(F32))
            for r in range(4):
                tmp_ref[pl.ds(r, BIG * 8, stride=4), :] = joined[:, 32 * r : 32 * r + 32]
            refs[-2][pl.ds(begin + p, BIG)] = tmp_ref[...].reshape(BIG, 32, 32).astype(BF16)
            if width > 128:
                refs[4][pl.ds(begin + p, BIG)] = pieces[k][pl.ds(p, BIG), :, 128:width]
            return carry

        steps(size, BIG, body, 0)


def place_kernel(ids_ref, *refs):
    pieces, out_ref = refs[:4], refs[4]
    size = pieces[0].shape[0]
    for k in range(4):
        begin = (ids_ref[1] ^ k) * size

        def body(p, carry, k=k, begin=begin):
            out_ref[pl.ds(begin + p, SMALL)] = pieces[k][pl.ds(p, SMALL)]
            return carry

        steps(size, SMALL, body, 0)


def lanes_at(block, width):
    return pl.ds(pl.multiple_of(block * width, width), width)


LREDUCE = [(3, 256 * k) for k in range(3)]
LATERAL = [(4, 128 * k) for k in range(5)]
GAINS = [(3, 768), (3, 896), (4, 640), (4, 768)]
SPATIAL = [(6 + k // 4, 256 * (k % 4)) for k in range(9)]


def weight_slab_kernel(ids_ref, red_ref, lred_ref, lat_ref, exp_ref, short_ref, lshort_ref, sp_ref, ln_ref, sn_ref, on_ref, out_ref, more_ref,
                       red_s, lred_s, lat_s, exp_s, short_s, lshort_s, sp_s, sem):
    group = ids_ref[2]
    eight, more = pl.ds(pl.multiple_of(group * 8, 8), 8), pl.ds(pl.multiple_of(group * 32, 32), 32)
    copies = []
    for i, (src, dst) in enumerate((
        (red_ref.at[:, eight], red_s), (lred_ref.at[:, eight], lred_s), (lat_ref.at[:, eight], lat_s), (exp_ref.at[eight], exp_s),
        (short_ref.at[more], short_s), (lshort_ref.at[eight], lshort_s), (sp_ref.at[:, eight], sp_s),
    )):
        copies.append(pltpu.make_async_copy(src, dst, sem.at[i]))
    for copy in copies:
        copy.start()
    out_ref[4, :, 896:1024] = jnp.zeros((8, 128), BF16)
    more_ref[8, :, 256:1024] = jnp.zeros((8, 768), BF16)
    blank = jnp.zeros((2, 128), F32)
    half = jnp.zeros((2, 64), F32)
    inner = jnp.concatenate([jnp.concatenate([v, half], axis=1) for v in (ln_ref[...], sn_ref[0:2], sn_ref[2:4])] + [blank], axis=0)
    outer = jnp.concatenate([on_ref[:, 0:128], on_ref[:, 128:256]], axis=0)
    for i, v in enumerate((inner, outer)):
        high = v.astype(BF16)
        for k, part in ((i, high), (2 + i, (v - high.astype(F32)).astype(BF16))):
            at, lane = GAINS[k]
            out_ref[at, :, lane : lane + 128] = part
    for copy in copies:
        copy.wait()
    for j in range(3):
        out_ref[j] = red_s[j].astype(BF16)
        at, lane = LREDUCE[j]
        out_ref[at, :, lane : lane + 256] = lred_s[j].astype(BF16)
    more_ref[0], more_ref[5] = exp_s[...].astype(BF16), lshort_s[...].astype(BF16)
    for a in range(4):
        more_ref[1 + a] = short_s[8 * a : 8 * a + 8].astype(BF16)
    for k in range(9):
        at, lane = SPATIAL[k]
        more_ref[at, :, lane : lane + 256] = sp_s[k].astype(BF16)
    for k in range(5):
        at, lane = LATERAL[k]
        out_ref[at, :, lane : lane + 128] = lat_s[k].astype(BF16)


def more_weights_kernel(ids_ref, own_ref, other_ref, exp_ref, short_ref, lshort_ref, sp_ref):
    me, group = ids_ref[1], ids_ref[2]

    def place(i, carry):
        chip, kz = i // 4, i % 4
        z = me ^ kz
        for core, ref in ((0, own_ref), (1, other_ref)):
            d = group ^ (2 * chip + core)
            exp_ref[z, d], lshort_ref[z, d] = ref[chip, kz, 0], ref[chip, kz, 5]
            for a in range(4):
                short_ref[z, d, a] = ref[chip, kz, 1 + a]
            for k in range(9):
                at, lane = SPATIAL[k]
                sp_ref[k, z, d] = ref[chip, kz, at, :, lane : lane + 256]
        return carry

    lax.fori_loop(0, 16, place, 0)


def weights_kernel(ids_ref, own_ref, other_ref, fr_ref, fsp_ref, fex_ref, fin_ref, fout_ref, red_ref, lred_ref, first_ref, wsp_ref, wex_ref,
                   gin_ref, gout_ref, gmid_ref, gwide_ref, lat_ref):
    me, group = ids_ref[1], ids_ref[2]

    def place(i, carry):
        chip, kz = i // 4, i % 4
        z = me ^ kz
        for core, ref in ((0, own_ref), (1, other_ref)):
            d = group ^ (2 * chip + core)
            for j in range(3):
                red_ref[j, z, d] = ref[chip, kz, j]
                at, lane = LREDUCE[j]
                lred_ref[j, z, d] = ref[chip, kz, at, :, lane : lane + 256]
            for k in range(5):
                at, lane = LATERAL[k]
                lat_ref[k, z, d] = ref[chip, kz, at, :, lane : lane + 128].astype(F32)
        return carry

    lax.fori_loop(0, 16, place, 0)

    mids = [jnp.zeros((8, 128), F32) for _ in range(2)]
    for kz in range(4):
        z = me ^ kz
        parts = [own_ref[0, kz, at, :, lane : lane + 128].astype(F32) for at, lane in GAINS]
        inner, outer = parts[0] + parts[2], parts[1] + parts[3]
        for half in range(2):
            for block in range(2):
                here = (z == 2 * block + half).astype(F32)
                mids[block] = mids[block] + moved(inner, 64 * half) * here
        gwide_ref[z, :, 0:128], gwide_ref[z, :, 128:256] = outer[0:4], outer[4:8]
    gmid_ref[:, 0:128], gmid_ref[:, 128:256] = mids[0], mids[1]

    first_ref[...] = jnp.zeros_like(first_ref)
    wsp_ref[...] = jnp.zeros_like(wsp_ref)
    for z in range(4):
        lanes = slice(128 * z, 128 * z + 128)

        def put(v, r, z=z):
            return lane_group(moved(v, 32 * r - 32 * z), r)

        for q in range(4):
            total = sum(put(fr_ref[r - q + 1], r) for r in range(4) if abs(r - q) <= 1)
            first_ref[32 * q : 32 * q + 32, lanes] = total.astype(BF16)
        first_ref[128:160, lanes] = put(fr_ref[0], 3).astype(BF16)
        first_ref[352:384, lanes] = put(fr_ref[2], 0).astype(BF16)
        taps = [lat_ref[j].reshape(256, 128) for j in range(5)]
        first_ref[384:640, lanes] = sum(put(taps[2 + r], r) for r in range(3)).astype(BF16)
        first_ref[640:896, lanes] = (put(taps[0], 2) + put(taps[1], 3)).astype(BF16)
        for r in range(4):
            wex_ref[32 * r : 32 * r + 32, lanes] = put(fex_ref[...], r).astype(BF16)
        gout_ref[:, lanes] = sum(put(fout_ref[...], r) for r in range(4))
    blank = jnp.zeros((32, 96), F32)
    for k in range(9):
        tap = jnp.concatenate([fsp_ref[k], blank], axis=1)
        for r in range(4):
            wsp_ref[k, 32 * r : 32 * r + 32, :] = moved(tap, 32 * r).astype(BF16)
    gin_ref[...] = jnp.concatenate([fin_ref[...]] * 4, axis=1)


def first_grads_kernel(ids_ref, own_ref, other_ref, exp_ref, short_ref, lshort_ref):
    def place(chip, carry):
        for core, ref in ((0, own_ref), (1, other_ref)):
            d = ids_ref[2] ^ (2 * chip + core)
            exp_ref[d], lshort_ref[d] = ref[chip, 0].astype(F32), ref[chip, 5].astype(F32)
            for a in range(4):
                short_ref[d, a] = ref[chip, 1 + a].astype(F32)
        return carry

    lax.fori_loop(0, 4, place, 0)


def second_grads_kernel(ids_ref, own_ref, other_ref, red_ref, lred_ref, sp_ref):
    def place(chip, carry):
        for core, ref in ((0, own_ref), (1, other_ref)):
            d = ids_ref[2] ^ (2 * chip + core)
            for j in range(3):
                red_ref[j, d] = ref[chip, j].astype(F32)
                lred_ref[j, d] = ref[chip, 3, :, 256 * j : 256 * j + 256].astype(F32)
            for k in range(8):
                sp_ref[k, d] = ref[chip, 4 + k // 4, :, 256 * (k % 4) : 256 * (k % 4) + 256].astype(F32)
            sp_ref[8, d] = ref[chip, 3, :, 768:1024].astype(F32)
        return carry

    lax.fori_loop(0, 4, place, 0)


def fast_first_kernel(table_ref, f0_ref, f1_ref, f2_ref, f3_ref, w_ref, fx_ref, fa_ref, lp_ref, sums_ref, first_ref, last_ref):
    size = fa_ref.shape[0]

    def fill(p, carry):
        for k, ref in enumerate((f0_ref, f1_ref, f2_ref, f3_ref)):
            fx_ref[pl.ds(p, SMALL), :, lanes_at(table_ref[5] ^ k, 128)] = ref[pl.ds(p, SMALL)]
        return carry

    steps(size, SMALL, fill, 0)

    def body(p, frames, carry):
        acc = cells(nt(rows_bf(fx_ref[pl.ds(p, BIG)]), w_ref[...]))
        fa = acc[:, :, 0:128] + later(acc[:, :, 128:256]) + sooner(acc[:, :, 256:384])
        lp = acc[:, :, 384:640] + later(acc[:, :, 640:896])
        fa_ref[pl.ds(p, BIG)] = fa
        lp_ref[pl.ds(p, BIG)] = lp
        fm, lm = fa * tile_mask(frames, 128), lp * tile_mask(frames, 256)
        return tuple(c + down(v) for c, v in zip(carry, (fm, fm * fa, lm, lm * lp)))

    zero = (jnp.zeros((8, 128), F32),) * 2 + (jnp.zeros((8, 256), F32),) * 2
    a, b, c, d = sweep(table_ref, size, BIG, body, zero)
    sums_ref[0:1, 0:128], sums_ref[1:2, 0:128] = flat(a), flat(b)
    sums_ref[0:1, 128:384], sums_ref[1:2, 128:384] = flat(c), flat(d)
    halo = first_ref.shape[0]
    first_ref[...], last_ref[...] = fa_ref[0:halo], fa_ref[size - halo : size]


def fill_padded(table_ref, refs, offset, out_ref, value, halo, size):
    low, middle, high = refs
    phase = table_ref[5] * (size // SMALL)

    def put(v, at, part, count, step=SMALL):
        even = ((phase + part + 2 * count) % 2 == 0).astype(F32)
        out_ref[1, pl.ds(at, step)] = v
        if step == 1:
            out_ref[0, pl.ds(at, 1)] = v * even
            out_ref[2, pl.ds(at, 1)] = v * (1.0 - even)
            return
        out_ref[0, pl.ds(at, step)] = v
        out_ref[2, pl.ds(at, step)] = v
        out_ref[0, pl.ds(at + step - 1, 1)] = v[step - 1 : step] * even
        out_ref[2, pl.ds(at, 1)] = v[0:1] * (1.0 - even)

    width = out_ref.shape[-1]
    lo_mask, hi_mask = tile_mask(table_ref[0], width), tile_mask(table_ref[4], width)
    put(value(low, 0, 1) * lo_mask, 0, -3, 4, 1)
    put(value(low, 1, SMALL) * lo_mask, 1, -2, 4)
    put(value(low, 1 + SMALL, SMALL) * lo_mask, 1 + SMALL, -1, 4)
    parts = size // SMALL
    put(value(high, 0, SMALL) * hi_mask, halo + size, parts, 0)
    put(value(high, SMALL, SMALL) * hi_mask, halo + size + SMALL, parts + 1, 0)
    put(value(high, 2 * SMALL, 1) * hi_mask, halo + size + 2 * SMALL, parts + 2, 0, 1)

    def body(p, frames, carry):
        put(value(middle, p, SMALL) * tile_mask(frames, width), halo + p, p // SMALL, 0)
        return carry

    sweep(table_ref, size, SMALL, body)


def edge_scales(table_ref, p, per_clip):
    part = table_ref[5] * table_ref[6] + p // BIG
    return (part % per_clip != 0).astype(F32), ((part + 1) % per_clip != 0).astype(F32)


def conv_rows(table_ref, per_clip, pad_ref, weight, p, halo, row_len, dot):
    top, bottom = edge_scales(table_ref, p, per_clip)
    total = None
    for i in (1, 0, 2):
        begin = p + halo + row_len * (i - 1)
        acc = None
        for j in range(3):
            tap = rows(pad_ref[j, pl.ds(begin + j - 1, BIG)]).astype(BF16)
            part = dot(tap, weight(i, j))
            acc = part if acc is None else acc + part
        acc = cells(acc)
        if i == 0:
            acc = jnp.concatenate([acc[0:row_len] * top, acc[row_len:]], axis=0)
        if i == 2:
            acc = jnp.concatenate([acc[: BIG - row_len], acc[BIG - row_len :] * bottom], axis=0)
        total = acc if total is None else total + acc
    return total


def conv_kernel(halo, row_len, per_clip, fold, offsets, table_ref, n_ref, sums_ref, gains_ref, lo_ref, y_ref, hi_ref, w_ref, *refs):
    if fold:
        act_ref, out_ref, osums_ref, pad_ref = refs
    else:
        more_ref, act_ref, out_ref, osums_ref, pad_ref = refs
    size, width = y_ref.shape[0], y_ref.shape[2]
    sums = sums_ref[:, offsets[0] : offsets[0] + width]
    sums = folded(sums) if fold else sums
    factor, shift, _, _ = scale_of(sums, gains_ref[...], n_ref[1 if fold else 0])
    lanes = slice(offsets[1], offsets[1] + width)

    def value(ref, p, step):
        y = ref[pl.ds(p, step)] if ref is y_ref else ref[pl.ds(p, step), :, lanes]
        return gelu(y * factor[None] + shift[None]).astype(BF16).astype(F32)

    fill_padded(table_ref, (lo_ref, y_ref, hi_ref), 0, pad_ref, value, halo, size)

    def copy(p, carry):
        act_ref[pl.ds(p, 3)] = pad_ref[1, pl.ds(p, 3)].astype(BF16)
        return carry

    steps(size + 2 * halo, 3, copy, 0)

    def body(p, frames, carry):
        total = conv_rows(table_ref, per_clip, pad_ref, lambda i, j: w_ref[3 * i + j], p, halo, row_len, nn if fold else nt)
        out_ref[pl.ds(p, BIG)] = total
        masked = total * tile_mask(frames, width)
        return carry[0] + down(masked), carry[1] + down(masked * total)

    a, b = sweep(table_ref, size, BIG, body, (jnp.zeros((8, width), F32),) * 2)
    osums_ref[0:1, 0:width], osums_ref[1:2, 0:width] = flat(a), flat(b)
    if not fold:
        osums_ref[:, width:] = more_ref[...]


def slow_first_kernel(table_ref, n_ref, x0_ref, x1_ref, x2_ref, x3_ref, lp_ref, lsums_ref, gains_ref, w_ref, wl_ref, fb_ref, more_ref,
                      x_ref, lat_ref, sa_ref, sums_ref, first_ref, last_ref):
    size = lp_ref.shape[0]
    factor, shift, _, _ = scale_of(lsums_ref[:, 128:384], gains_ref[...], n_ref[0])

    def fill(p, frames, carry):
        mask = tile_mask(frames, 256)
        lat_ref[pl.ds(p, SMALL)] = (gelu(lp_ref[pl.ds(p, SMALL)] * factor[None] + shift[None]) * mask).astype(BF16)
        for k, ref in enumerate((x0_ref, x1_ref, x2_ref, x3_ref)):
            v = ref[pl.ds(p, SMALL)].astype(F32) * mask
            x_ref[pl.ds(p, SMALL), :, lanes_at(table_ref[5] ^ k, 256)] = v.astype(BF16)
        return carry

    sweep(table_ref, size, SMALL, fill)

    def body(p, frames, carry):
        acc = nt(rows_bf(x_ref[pl.ds(p, BIG)]), w_ref[...]) + nt(rows_bf(lat_ref[pl.ds(p, BIG)]), wl_ref[...])
        acc = cells(acc)
        sa = later(acc[:, :, 0:256]) + acc[:, :, 256:512] + sooner(acc[:, :, 512:768])
        sa_ref[pl.ds(p, BIG)] = sa
        masked = sa * tile_mask(frames, 256)
        return carry[0] + down(masked), carry[1] + down(masked * sa)

    a, b = sweep(table_ref, size, BIG, body, (jnp.zeros((8, 256), F32),) * 2)
    sums_ref[0:1, 0:256], sums_ref[1:2, 0:256] = flat(a), flat(b)
    sums_ref[:, 256:] = more_ref[...]
    halo = first_ref.shape[0]
    first_ref[:, :, 0:256], last_ref[:, :, 0:256] = sa_ref[0:halo], sa_ref[size - halo : size]
    first_ref[:, :, 256:], last_ref[:, :, 256:] = fb_ref[0:halo], fb_ref[size - halo : size]


def bypass_kernel(table_ref, x_ref, lat_ref, w_ref, wl_ref, sp_ref, sums_ref):
    def body(p, frames, carry):
        sp = cells(nn(rows_bf(x_ref[pl.ds(p, BIG)]), w_ref[...]) + nn(rows_bf(lat_ref[pl.ds(p, BIG)]), wl_ref[...]))
        sp_ref[pl.ds(p, BIG)] = sp.astype(BF16)
        masked = sp * tile_mask(frames, sp.shape[-1])
        return carry[0] + down(masked), carry[1] + down(masked * sp)

    a, b = sweep(table_ref, sp_ref.shape[0], BIG, body, (jnp.zeros((8, sp_ref.shape[2]), F32),) * 2)
    sums_ref[0:1], sums_ref[1:2] = flat(a), flat(b)


def expand_kernel(fold, offset, table_ref, n_ref, y_ref, sums_ref, gains_ref, w_ref, *refs):
    more, (h_ref, out_ref, osums_ref) = refs[:-3], refs[-3:]
    size, width = y_ref.shape[0], y_ref.shape[2]
    sums = sums_ref[:, offset : offset + width]
    sums = folded(sums) if fold else sums
    factor, shift, _, _ = scale_of(sums, gains_ref[...], n_ref[1 if fold else 0])

    def fill(p, frames, carry):
        v = gelu(y_ref[pl.ds(p, SMALL)] * factor[None] + shift[None])
        h_ref[pl.ds(p, SMALL)] = (v * tile_mask(frames, width)).astype(BF16)
        return carry

    sweep(table_ref, size, SMALL, fill)

    def body(p, frames, carry):
        out = cells(nn(rows_bf(h_ref[pl.ds(p, BIG)]), w_ref[...]))
        out_ref[pl.ds(p, BIG)] = out.astype(BF16)
        masked = out * tile_mask(frames, out.shape[-1])
        return carry[0] + down(masked), carry[1] + down(masked * out)

    wide_out = out_ref.shape[2]
    a, b = sweep(table_ref, size, BIG, body, (jnp.zeros((8, wide_out), F32),) * 2)
    osums_ref[0:1, 0:wide_out], osums_ref[1:2, 0:wide_out] = flat(a), flat(b)
    for ref in more:
        osums_ref[:, wide_out : wide_out + ref.shape[1]] = ref[...]
        wide_out += ref.shape[1]


def fast_out_kernel(offset, table_ref, n_ref, fc_ref, sums_ref, gains_ref, fx_ref, c0_ref, c1_ref, c2_ref, c3_ref, out_ref, up_ref,
                    slopes_ref, vec_ref):
    size, width = fc_ref.shape[0], fc_ref.shape[2]
    vecs = scale_of(folded(sums_ref[:, offset : offset + width]), gains_ref[...], n_ref[1])
    for i, v in enumerate(vecs):
        vec_ref[i : i + 1] = v
    for k, cot_ref in enumerate((c0_ref, c1_ref, c2_ref, c3_ref)):
        lanes = lanes_at(table_ref[5] ^ k, 128)
        fz, sz, cz, rz = (vec_ref[i : i + 1, lanes][None] for i in range(4))

        def body(p, frames, carry, k=k, lanes=lanes, fz=fz, sz=sz, cz=cz, rz=rz, cot_ref=cot_ref):
            y = fc_ref[pl.ds(p, SMALL), :, lanes].astype(F32)
            mask = tile_mask(frames, 128)
            total = y * fz + sz + fx_ref[pl.ds(p, SMALL), :, lanes].astype(F32)
            value, slope = gelu_pair(total)
            out_ref[k, pl.ds(p, SMALL)] = (value * mask).astype(BF16)
            up = slope * (cot_ref[pl.ds(p, SMALL), :, 0:128].astype(F32) * mask)
            up_ref[pl.ds(p, SMALL), :, lanes] = up.astype(BF16)
            return carry[0] + down(up), carry[1] + down(up * ((y - cz) * rz))

        a, b = sweep(table_ref, size, SMALL, body, (jnp.zeros((8, 128), F32),) * 2)
        slopes_ref[0:1, lanes], slopes_ref[1:2, lanes] = flat(a), flat(b)


def slow_out_kernel(table_ref, n_ref, sc_ref, sp_ref, sums_ref, gains_ref, c0_ref, c1_ref, c2_ref, c3_ref, fast_ref, more_ref,
                    o0_ref, o1_ref, o2_ref, o3_ref, up_ref, slopes_ref, vec_ref):
    size, width = sc_ref.shape[0], sc_ref.shape[2]
    cf, cs, cc, cr = scale_of(sums_ref[:, 0:width], gains_ref[0:2], n_ref[0])
    pf, ps, pc, pr = scale_of(sums_ref[:, width : 2 * width], gains_ref[2:4], n_ref[0])
    for i, v in enumerate((cf, cs + ps, cc, cr, pf, pc, pr)):
        vec_ref[i : i + 1] = v
    for k, (cot_ref, out_ref) in enumerate(((c0_ref, o0_ref), (c1_ref, o1_ref), (c2_ref, o2_ref), (c3_ref, o3_ref))):
        block = table_ref[5] ^ k
        lanes = lanes_at(block, 256)
        vecs = [vec_ref[i : i + 1, lanes][None] for i in range(7)]

        def body(p, frames, carry, k=k, lanes=lanes, vecs=vecs, cot_ref=cot_ref, out_ref=out_ref):
            cf, shift, cc, cr, pf, pc, pr = vecs
            yc, yp = (ref[pl.ds(p, SMALL), :, lanes].astype(F32) for ref in (sc_ref, sp_ref))
            mask = tile_mask(frames, 256)
            value, slope = gelu_pair(yc * cf + yp * pf + shift)
            out_ref[pl.ds(p, SMALL), :, 128:384] = (value * mask).astype(BF16)
            out_ref[pl.ds(p, SMALL), :, 0:128] = fast_ref[k, pl.ds(p, SMALL)]
            up = slope * (cot_ref[pl.ds(p, SMALL), :, 128:384].astype(F32) * mask)
            up_ref[pl.ds(p, SMALL), :, lanes] = up.astype(BF16)
            return (carry[0] + down(up), carry[1] + down(up * ((yc - cc) * cr)), carry[2] + down(up * ((yp - pc) * pr)))

        a, b, c = sweep(table_ref, size, SMALL, body, (jnp.zeros((8, 256), F32),) * 3)
        own, other = lanes, lanes_at(4 + block, 256)
        slopes_ref[0:1, own], slopes_ref[1:2, own] = flat(a), flat(b)
        slopes_ref[0:1, other], slopes_ref[1:2, other] = flat(a), flat(c)
    slopes_ref[:, 2 * width :] = more_ref[...]


def norm_back_fill(table_ref, up_ref, y_ref, dy_ref, factor, k0, k1):
    def fill(p, frames, carry):
        mask = tile_mask(frames, 128)
        for q in range(y_ref.shape[2] // 128):
            lanes = slice(128 * q, 128 * q + 128)
            y = y_ref[pl.ds(p, SMALL), :, lanes].astype(F32)
            dy = up_ref[pl.ds(p, SMALL), :, lanes].astype(F32) * factor[:, lanes][None]
            dy = dy - mask * (k0[:, lanes][None] + k1[:, lanes][None] * y)
            dy_ref[pl.ds(p, SMALL), :, lanes] = dy.astype(BF16)
        return carry

    sweep(table_ref, y_ref.shape[0], SMALL, fill)


def expand_back_kernel(fold, offsets, table_ref, n_ref, up_ref, y_ref, sums_ref, gains_ref, slopes_ref, z_ref, zsums_ref, zgains_ref,
                       w_ref, other_ref, dy_ref, dz_ref, oslopes_ref, first_ref, last_ref):
    size, width, inner = y_ref.shape[0], y_ref.shape[2], z_ref.shape[2]
    fix = folded if fold else (lambda v: v)
    inv_n = n_ref[1 if fold else 0]
    at_y, at_s, at_z = offsets
    factor, shift, center, inv_std = scale_of(fix(sums_ref[:, at_y : at_y + width]), gains_ref[...], inv_n)
    k0, k1 = slope_of(fix(slopes_ref[:, at_s : at_s + width]), factor, center, inv_std, inv_n)
    norm_back_fill(table_ref, up_ref, y_ref, dy_ref, factor, k0, k1)
    zf, zs, zc, zr = scale_of(fix(zsums_ref[:, at_z : at_z + inner]), zgains_ref[...], inv_n)

    def body(p, frames, carry):
        dh = cells(nt(rows_bf(dy_ref[pl.ds(p, BIG)]), w_ref[...]))
        z = z_ref[pl.ds(p, BIG)]
        dz = gelu_slope(z * zf[None] + zs[None]) * dh * tile_mask(frames, inner)
        dz_ref[pl.ds(p, BIG)] = dz
        return carry[0] + down(dz), carry[1] + down(dz * ((z - zc[None]) * zr[None]))

    a, b = sweep(table_ref, size, BIG, body, (jnp.zeros((8, inner), F32),) * 2)
    oslopes_ref[0:1, 0:inner], oslopes_ref[1:2, 0:inner] = flat(a), flat(b)
    halo = first_ref.shape[0]
    first_ref[:, :, 0:inner], last_ref[:, :, 0:inner] = dz_ref[0:halo], dz_ref[size - halo : size]
    if fold:
        first_ref[:, :, inner:], last_ref[:, :, inner:] = other_ref[0:halo], other_ref[size - halo : size]
    else:
        oslopes_ref[:, inner:] = other_ref[...]


def bypass_back_kernel(table_ref, n_ref, up_ref, y_ref, sums_ref, gains_ref, slopes_ref, w_ref, wl_ref, dy_ref, dx_ref, dl_ref):
    size, width = y_ref.shape[0], y_ref.shape[2]
    factor, shift, center, inv_std = scale_of(sums_ref[:, width : 2 * width], gains_ref[...], n_ref[0])
    k0, k1 = slope_of(slopes_ref[:, width : 2 * width], factor, center, inv_std, n_ref[0])
    norm_back_fill(table_ref, up_ref, y_ref, dy_ref, factor, k0, k1)

    def body(p, carry):
        dy = rows_bf(dy_ref[pl.ds(p, BIG)])
        dx_ref[pl.ds(p, BIG)] = cells(nt(dy, w_ref[...])).astype(BF16)
        dl_ref[pl.ds(p, BIG)] = cells(nt(dy, wl_ref[...]))
        return carry

    steps(size, BIG, body, 0)


def conv_back_kernel(halo, row_len, per_clip, fold, offsets, table_ref, n_ref, ysums_ref, ygains_ref, slopes_ref, ylo_ref, y_ref, yhi_ref,
                     dlo_ref, d_ref, dhi_ref, w_ref, z_ref, zsums_ref, zgains_ref, *refs):
    dy_ref, dz_ref, oslopes_ref, pad_ref = refs[-4:]
    size, width = y_ref.shape[0], y_ref.shape[2]
    fix = folded if fold else (lambda v: v)
    inv_n = n_ref[1 if fold else 0]
    at_y, at_s, at_z, at_yhalo, at_dhalo = offsets
    factor, shift, center, inv_std = scale_of(fix(ysums_ref[:, at_y : at_y + width]), ygains_ref[...], inv_n)
    k0, k1 = slope_of(fix(slopes_ref[:, at_s : at_s + width]), factor, center, inv_std, inv_n)

    def value(refs, p, step):
        y_of, d_of = refs
        if y_of is y_ref:
            y, d = y_of[pl.ds(p, step)], d_of[pl.ds(p, step)]
        else:
            y, d = y_of[pl.ds(p, step), :, at_yhalo : at_yhalo + width], d_of[pl.ds(p, step), :, at_dhalo : at_dhalo + width]
        return (d * factor[None] - (k0[None] + k1[None] * y)).astype(BF16).astype(F32)

    fill_padded(table_ref, ((ylo_ref, dlo_ref), (y_ref, d_ref), (yhi_ref, dhi_ref)), 0, pad_ref, value, halo, size)

    def copy(p, carry):
        dy_ref[pl.ds(p, SMALL)] = pad_ref[1, pl.ds(halo + p, SMALL)].astype(BF16)
        return carry

    steps(size, SMALL, copy, 0)
    zf, zs, zc, zr = scale_of(fix(zsums_ref[:, at_z : at_z + width]), zgains_ref[...], inv_n)

    def body(p, frames, carry):
        dh = conv_rows(table_ref, per_clip, pad_ref, lambda i, j: w_ref[8 - 3 * i - j], p, halo, row_len, nt if fold else nn)
        z = z_ref[pl.ds(p, BIG)]
        dz = gelu_slope(z * zf[None] + zs[None]) * dh * tile_mask(frames, width)
        dz_ref[pl.ds(p, BIG)] = dz
        return carry[0] + down(dz), carry[1] + down(dz * ((z - zc[None]) * zr[None]))

    a, b = sweep(table_ref, size, BIG, body, (jnp.zeros((8, width), F32),) * 2)
    oslopes_ref[0:1, 0:width], oslopes_ref[1:2, 0:width] = flat(a), flat(b)
    if not fold:
        oslopes_ref[:, width:] = refs[0][...]


def slow_back_kernel(table_ref, n_ref, dz_ref, y_ref, sums_ref, gains_ref, slopes_ref, w_ref, wl_ref, dx_ref, dl_ref,
                     lp_ref, lsums_ref, lgains_ref, taps_ref, o0_ref, o1_ref, o2_ref, o3_ref, dzl_ref, oslopes_ref):
    size = y_ref.shape[0]
    factor, shift, center, inv_std = scale_of(sums_ref[:, 0:256], gains_ref[...], n_ref[0])
    k0, k1 = slope_of(slopes_ref[:, 0:256], factor, center, inv_std, n_ref[0])

    def fill(p, frames, carry):
        dy = dz_ref[pl.ds(p, SMALL)] * factor[None]
        dy = dy - tile_mask(frames, 256) * (k0[None] + k1[None] * y_ref[pl.ds(p, SMALL)])
        taps_ref[pl.ds(p, SMALL), :, 0:256] = sooner(dy).astype(BF16)
        taps_ref[pl.ds(p, SMALL), :, 256:512] = dy.astype(BF16)
        taps_ref[pl.ds(p, SMALL), :, 512:768] = later(dy).astype(BF16)
        return carry

    sweep(table_ref, size, SMALL, fill)
    lf, ls, lc, lr = scale_of(lsums_ref[:, 128:384], lgains_ref[...], n_ref[0])

    def body(p, frames, carry):
        taps = rows_bf(taps_ref[pl.ds(p, BIG)])
        mask = tile_mask(frames, 256)
        for k, out_ref in enumerate((o0_ref, o1_ref, o2_ref, o3_ref)):
            lanes = lanes_at(table_ref[5] ^ k, 256)
            dx = cells(nn(taps, w_ref[:, lanes])) + dx_ref[pl.ds(p, BIG), :, lanes].astype(F32)
            out_ref[pl.ds(p, BIG)] = (dx * mask).astype(BF16)
        dl = cells(nn(taps, wl_ref[...])) + dl_ref[pl.ds(p, BIG)]
        y = lp_ref[pl.ds(p, BIG)]
        dz = gelu_slope(y * lf[None] + ls[None]) * dl * mask
        dzl_ref[pl.ds(p, BIG)] = dz
        return carry[0] + down(dz), carry[1] + down(dz * ((y - lc[None]) * lr[None]))

    a, b = sweep(table_ref, size, BIG, body, (jnp.zeros((8, 256), F32),) * 2)
    oslopes_ref[0:1], oslopes_ref[1:2] = flat(a), flat(b)


def fast_back_kernel(at_s, table_ref, n_ref, sums_ref, fgains_ref, lgains_ref, fslopes_ref, lslopes_ref, dzf_ref, fa_ref, dzl_ref, lp_ref,
                     up_ref, w_ref, taps_ref, o0_ref, o1_ref, o2_ref, o3_ref):
    size = fa_ref.shape[0]
    ff, fs, fc, fr = scale_of(folded(sums_ref[:, 0:128]), fgains_ref[...], n_ref[1])
    f0, f1 = slope_of(folded(fslopes_ref[:, at_s : at_s + 128]), ff, fc, fr, n_ref[1])
    lf, ls, lc, lr = scale_of(sums_ref[:, 128:384], lgains_ref[...], n_ref[0])
    l0, l1 = slope_of(lslopes_ref[...], lf, lc, lr, n_ref[0])

    def fill(p, frames, carry):
        dy = dzf_ref[pl.ds(p, SMALL)] * ff[None]
        dy = dy - tile_mask(frames, 128) * (f0[None] + f1[None] * fa_ref[pl.ds(p, SMALL)])
        taps_ref[pl.ds(p, SMALL), :, 0:128] = dy.astype(BF16)
        taps_ref[pl.ds(p, SMALL), :, 128:256] = sooner(dy).astype(BF16)
        taps_ref[pl.ds(p, SMALL), :, 256:384] = later(dy).astype(BF16)
        dy = dzl_ref[pl.ds(p, SMALL)] * lf[None]
        dy = dy - tile_mask(frames, 256) * (l0[None] + l1[None] * lp_ref[pl.ds(p, SMALL)])
        taps_ref[pl.ds(p, SMALL), :, 384:640] = dy.astype(BF16)
        taps_ref[pl.ds(p, SMALL), :, 640:896] = sooner(dy).astype(BF16)
        return carry

    sweep(table_ref, size, SMALL, fill)

    def body(p, frames, carry):
        taps = rows_bf(taps_ref[pl.ds(p, BIG)])
        mask = tile_mask(frames, 128)
        for k, out_ref in enumerate((o0_ref, o1_ref, o2_ref, o3_ref)):
            lanes = lanes_at(table_ref[5] ^ k, 128)
            dx = cells(nn(taps, w_ref[:, lanes])) + up_ref[pl.ds(p, BIG), :, lanes].astype(F32)
            out_ref[pl.ds(p, BIG)] = (dx * mask).astype(BF16)
        return carry

    sweep(table_ref, size, BIG, body)


def tn(a, b):
    return lax.dot_general(a, b, (((0,), (0,)), ((), ())), preferred_element_type=F32)


def chunks(size):
    return range(0, size, BIG)


def added(acc_ref, at, part, first):
    acc_ref[at] = part if first else acc_ref[at] + part


def conv_weight(halo, row_len, per_clip, fold, table_ref, act_ref, dy_ref, pad_ref, acc_ref):
    size = dy_ref.shape[0]
    phase = table_ref[5] * (size // SMALL)

    def copy(p, carry):
        v = act_ref[pl.ds(p, 3)].astype(F32)
        for k in range(3):
            pad_ref[k, pl.ds(p, 3)] = v
        return carry

    steps(size + 2 * halo, 3, copy, 0)
    parts = size // SMALL

    def clear(i, carry):
        even = ((phase + i) % 2 == 0).astype(F32)
        at = halo + (i - 2) * SMALL
        pad_ref[0, pl.ds(at + SMALL - 1, 1)] = pad_ref[0, pl.ds(at + SMALL - 1, 1)] * even
        pad_ref[2, pl.ds(at, 1)] = pad_ref[2, pl.ds(at, 1)] * (1.0 - even)
        return carry

    lax.fori_loop(0, parts + 4, clear, 0)
    low_even = ((phase + 1) % 2 == 0).astype(F32)
    pad_ref[0, 0:1] = pad_ref[0, 0:1] * low_even
    high_even = ((phase + parts) % 2 == 0).astype(F32)
    end = size + 2 * halo
    pad_ref[2, end - 1 : end] = pad_ref[2, end - 1 : end] * (1.0 - high_even)

    for p in chunks(size):
        top, bottom = edge_scales(table_ref, p, per_clip)
        dy = rows_bf(dy_ref[p : p + BIG])
        for i in range(3):
            begin = p + halo + row_len * (i - 1)
            taps = []
            for j in range(3):
                v = pad_ref[j, begin + j - 1 : begin + j - 1 + BIG]
                if i == 0:
                    v = jnp.concatenate([v[0:row_len] * top, v[row_len:]], axis=0)
                if i == 2:
                    v = jnp.concatenate([v[: BIG - row_len], v[BIG - row_len :] * bottom], axis=0)
                taps.append(rows(v).astype(BF16))
            taps = jnp.concatenate(taps, axis=1)
            added(acc_ref, i, tn(taps, dy) if fold else tn(dy, taps), p == 0)


def first_slab_kernel(hb_ref, dsc_ref, x_ref, lat_ref, dsp_ref, out_ref, acc_ref):
    for p in chunks(hb_ref.shape[0]):
        at = slice(p, p + BIG)
        dsc, dsp = rows_bf(dsc_ref[at]), rows_bf(dsp_ref[at])
        added(acc_ref, 4, tn(rows_bf(hb_ref[at]), dsc), p == 0)
        added(acc_ref, 5, tn(rows_bf(lat_ref[at]), dsp), p == 0)
        for z in range(4):
            added(acc_ref, z, tn(rows_bf(x_ref[at, :, 256 * z : 256 * z + 256]), dsp), p == 0)
    out_ref[:, :, 0] = acc_ref[4].reshape(4, 8, 8, 1024).astype(BF16)
    out_ref[:, :, 5] = acc_ref[5].reshape(4, 8, 8, 1024).astype(BF16)
    for z in range(4):
        out_ref[z, :, 1:5] = acc_ref[z].reshape(8, 4, 8, 1024).astype(BF16)


def second_slab_kernel(halo, row_len, per_clip, table_ref, act_ref, dy_ref, taps_ref, x_ref, lat_ref, out_ref, pad_ref, acc_ref, red_ref,
                       lred_ref):
    conv_weight(halo, row_len, per_clip, False, table_ref, act_ref, dy_ref, pad_ref, acc_ref)
    for k in range(9):
        v = acc_ref[k // 3, :, 256 * (k % 3) : 256 * (k % 3) + 256].reshape(4, 8, 8, 256).astype(BF16)
        at, lane = (3, 768) if k == 8 else (4 + k // 4, 256 * (k % 4))
        out_ref[:, :, at, :, lane : lane + 256] = v
    for p in chunks(dy_ref.shape[0]):
        at = slice(p, p + BIG)
        x, lat = rows_bf(x_ref[at]), rows_bf(lat_ref[at])
        for j in range(3):
            taps = rows_bf(taps_ref[at, :, 256 * j : 256 * j + 256])
            added(red_ref, j, tn(taps, x), p == 0)
            added(lred_ref, j, tn(taps, lat), p == 0)
    for j in range(3):
        out_ref[:, :, j] = red_ref[j].reshape(4, 8, 8, 1024).astype(BF16)
        out_ref[:, :, 3, :, 256 * j : 256 * j + 256] = lred_ref[j].reshape(4, 8, 8, 256).astype(BF16)


def fast_grads_kernel(halo, row_len, per_clip, table_ref, act_ref, dy_ref, taps_ref, fx_ref, h_ref, dfc_ref, lat_ref, out_ref,
                      pad_ref, sp_ref, first_ref, ex_ref):
    conv_weight(halo, row_len, per_clip, True, table_ref, act_ref, dy_ref, pad_ref, sp_ref)
    for p in chunks(dy_ref.shape[0]):
        at = slice(p, p + BIG)
        added(first_ref, slice(0, 896), tn(rows_bf(taps_ref[at]), rows_bf(fx_ref[at])), p == 0)
        added(ex_ref, slice(0, 128), tn(rows_bf(h_ref[at]), rows_bf(dfc_ref[at])), p == 0)

    def gather(at, count, r, ref=first_ref):
        return sum(lane_group(moved(ref[at : at + count, 128 * z : 128 * z + 128], 32 * z - 32 * r), z) for z in range(4))

    taps = [gather(640, 256, 2), gather(640, 256, 3), gather(384, 256, 0), gather(384, 256, 1), gather(384, 256, 2)]
    for j in range(5):
        lat_ref[:, 8 * j : 8 * j + 8] = taps[j].reshape(4, 8, 8, 128).astype(BF16)

    def tiles(first, v):
        for i in range(v.shape[0] // 8):
            out_ref[first + i] = v[8 * i : 8 * i + 8].astype(BF16)

    for j in range(3):
        total = sum(gather(32 * q, 32, q + j - 1) for q in range(4) if 0 <= q + j - 1 < 4)
        if j == 0:
            total = total + gather(128, 32, 3)
        if j == 2:
            total = total + gather(352, 32, 0)
        tiles(4 * j, total)
    tiles(12, sum(gather(32 * r, 32, r, ex_ref) for r in range(4)))
    for i in range(3):
        total = None
        for j in range(3):
            tap = sum(
                lane_group(moved(sp_ref[i, 128 * j + 32 * r : 128 * j + 32 * r + 32, :], 32 * j - 32 * r), j) for r in range(4)
            )
            total = tap if total is None else total + tap
        tiles(16 + 4 * i, total)


def swap(tree, axis, size, distance):
    pairs = [(i, i ^ distance) for i in range(size)]
    return jax.tree.map(lambda v: lax.ppermute(v, axis, pairs), tree)


def add(*trees):
    def total(*vs):
        wide_vs = [v.astype(F32) for v in vs]
        out = wide_vs[0] + wide_vs[1]
        if len(vs) == 4:
            out = out + (wide_vs[2] + wide_vs[3])
        return out.astype(vs[0].dtype)

    return jax.tree.map(total, *trees)


def stages(size, first_alone):
    bits = [1 << i for i in range(size.bit_length() - 1)]
    out = []
    if first_alone and bits:
        out.append(bits[:1])
        bits = bits[1:]
    while bits:
        out.append(bits[:2])
        bits = bits[2:]
    return out


def butterfly(tree, axis, size, bits):
    if len(bits) == 1:
        return add(tree, swap(tree, axis, size, bits[0]))
    near, far, both = (swap(tree, axis, size, k) for k in (bits[0], bits[1], bits[0] + bits[1]))
    return add(tree, near, far, both)


def everywhere(tree, sizes, bulk=None):
    for axis, size in sizes.items():
        if axis == "chan" and bulk is not None:
            tree = after(tree, bulk)
        for bits in stages(size, axis == "dp"):
            tree = butterfly(tree, axis, size, bits)
    return tree


def halos(first, last, count):
    low = lax.ppermute(last, "chan", [(i, i + 1) for i in range(count - 1)])
    high = lax.ppermute(first, "chan", [(i + 1, i) for i in range(count - 1)])
    return low, high


def gather_group(v, sizes):
    dp = sizes["dp"]
    own = jnp.stack([v] + [swap(v, "dp", dp, 2 * k) for k in (1, 2, 3)])
    return own, swap(own, "dp", dp, 1)


def pick(v, index, axis):
    return lax.dynamic_index_in_dim(v, index, axis, keepdims=False)


def scatter_sum(tree, sizes, group, chan):
    dp = sizes["dp"]
    core, chip = group % 2, group // 2
    tree = jax.tree.map(lambda v: v.reshape(v.shape[0], 4, 2, *v.shape[2:]), tree)
    sent = jax.tree.map(lambda v: pick(v, 1 - core, 2), tree)
    kept = jax.tree.map(lambda v: pick(v, core, 2), tree)
    tree = add(kept, swap(sent, "dp", dp, 1))
    got = [swap(jax.tree.map(lambda v: pick(v, chip ^ k, 1), tree), "dp", dp, 2 * k) for k in (1, 2, 3)]
    tree = add(jax.tree.map(lambda v: pick(v, chip, 1), tree), *got)
    size = sizes["chan"]
    got = [swap(jax.tree.map(lambda v: pick(v, chan ^ k, 0), tree), "chan", size, k) for k in (1, 2, 3)]
    tree = add(jax.tree.map(lambda v: pick(v, chan, 0), tree), *got)
    bits = [1 << i for i in range(3, dp.bit_length() - 1)]
    while bits:
        tree = butterfly(tree, "dp", dp, bits[:2])
        bits = bits[2:]
    return tree


def after(tree, gate):
    return lax.optimization_barrier((tree, gate))[0]


def local(
    sizes,
    slow_input,
    fast_input,
    clip_counts,
    frame_counts,
    fast_reduce,
    fast_spatial,
    fast_expand,
    lateral_kernel,
    slow_reduce,
    lateral_reduce,
    slow_spatial,
    slow_expand,
    shortcut,
    lateral_shortcut,
    fast_inner_norm,
    fast_outer_norm,
    lateral_norm,
    slow_inner_norm,
    slow_outer_norm,
    slow_cotangent,
    fast_cotangent,
):
    ways = sizes["chan"]
    clips, slow_t, height, across, slow_part = slow_input.shape
    fast_t, fast_part = fast_input.shape[1], fast_input.shape[4]
    ratio = fast_t // slow_t
    area = height * across
    places = clips * area
    mine = places // ways
    halo = across + 1
    chan, dp = lax.axis_index("chan"), lax.axis_index("dp")
    group = dp % 8
    ids = jnp.stack([dp, chan, group]).astype(jnp.int32)
    wide_in = ways * slow_part
    wide_f = ways * 128
    mid = 256
    ext = mine + 2 * halo
    per_clip = area // BIG
    chunk = 98

    def packed(v, slow=None):
        v = v.transpose(0, 2, 3, 1, 4).reshape(places, fast_t, fast_part)
        more = [] if slow is None else [slow.reshape(places, slow_t, slow_part)]
        width = 128 if slow is None else 128 + slow_part
        return pl.pallas_call(
            functools.partial(pack_kernel, area // chunk, clips),
            grid=(places // chunk,),
            out_shape=shape((places, slow_t, width), BF16),
            in_specs=[pl.BlockSpec(memory_space=pltpu.SMEM)] * 3
            + [pl.BlockSpec((chunk, *u.shape[1:]), lambda i: (i, 0, 0)) for u in (v, *more)],
            out_specs=pl.BlockSpec((chunk, slow_t, width), lambda i: (i, 0, 0)),
            scratch_shapes=[pltpu.VMEM((chunk * fast_t, fast_part), F32)],
            compiler_params=pltpu.CompilerParams(vmem_limit_bytes=16 * 1024 * 1024),
            name="fast_pack",
        )(ids, clip_counts, frame_counts, v, *more).reshape(ways, mine, slow_t, width)

    def unpacked(pieces):
        width = pieces[0].shape[2]
        outs = [shape((places, fast_t, fast_part), BF16)]
        if width > 128:
            outs = [shape((places, slow_t, slow_part), BF16)] + outs
        out = call(
            functools.partial(unpack_kernel, width),
            outs,
            [ids, *pieces],
            [pltpu.VMEM((BIG * fast_t, fast_part), F32)],
            smem=1,
            name="fast_unpack",
        )
        fast = out[-1].reshape(clips, height, across, fast_t, fast_part).transpose(0, 3, 1, 2, 4)
        return (joined(out[0]), fast) if len(out) == 2 else fast

    def split(v):
        return v.transpose(0, 2, 3, 1, 4).reshape(ways, mine, slow_t, slow_part)

    def joined(v):
        return v.reshape(clips, height, across, slow_t, slow_part).transpose(0, 3, 1, 2, 4)

    def at_once(v):
        return [v[0]] + [swap(v[k], "chan", ways, k) for k in range(1, ways)]

    def blocks_of(v):
        return [pick(v, chan ^ k, 0) for k in range(ways)]

    def send(v, k):
        return swap(v, "chan", ways, k)

    x_blocks = blocks_of(split(slow_input))
    fx_pieces = at_once(blocks_of(packed(fast_input)))

    all_clips = frame_counts.shape[0]
    live = (jnp.arange(all_clips, dtype=jnp.int32) % clips) < jnp.repeat(clip_counts, clips)
    valid = jnp.where(live, frame_counts, 0)
    count = jnp.sum(valid).astype(F32) * area
    inv_n = jnp.stack([1.0 / count, 1.0 / (count * ratio)])
    parts = mine // BIG
    clip = (chan * parts + jnp.arange(-1, parts + 1)) // per_clip
    clip = jnp.clip(clip, 0, clips - 1) + dp * clips
    around = jnp.sum(jnp.where(clip[:, None] == jnp.arange(all_clips)[None, :], valid[None, :], 0), axis=1)
    table = jnp.concatenate([around, jnp.stack([chan, jnp.full_like(chan, parts)])]).astype(jnp.int32)

    lat_t, red_t, lred_t = (v.transpose(0, 2, 1) for v in (lateral_kernel, slow_reduce, lateral_reduce))
    spatial_t = slow_spatial.reshape(9, slow_spatial.shape[2], -1).transpose(0, 2, 1)
    params = [red_t, lred_t, lat_t, slow_expand, shortcut, lateral_shortcut, spatial_t]
    scratch = [(3, 8, wide_in), (3, 8, mid), (5, 8, 128), (8, wide_in), (32, wide_in), (8, wide_in), (9, 8, mid)]
    small = [lateral_norm, slow_inner_norm.reshape(4, -1), slow_outer_norm.reshape(4, -1)]
    any_spec, vmem_spec = pl.BlockSpec(memory_space=pl.ANY), pl.BlockSpec(memory_space=pltpu.VMEM)
    slab_a, slab_b = pl.pallas_call(
        weight_slab_kernel,
        out_shape=(shape((5, 8, wide_in), BF16), shape((9, 8, wide_in), BF16)),
        in_specs=[pl.BlockSpec(memory_space=pltpu.SMEM)] + [any_spec] * 7 + [vmem_spec] * 3,
        out_specs=(vmem_spec, vmem_spec),
        scratch_shapes=[pltpu.VMEM(dims, F32) for dims in scratch] + [pltpu.SemaphoreType.DMA((7,))],
        compiler_params=pltpu.CompilerParams(vmem_limit_bytes=8 * 1024 * 1024),
        name="weight_slab",
    )(ids, *params, *small)
    slab_a = at_once([slab_a] * ways)
    x_blocks = after(x_blocks, slab_a)
    x_second = send(x_blocks[2], 2)
    near = after((x_blocks[1], x_blocks[3]), (x_second, fx_pieces))
    x_pieces = [x_blocks[0], send(near[0], 1), x_second, send(near[1], 3)]
    slab_a = after(jnp.stack(slab_a), fx_pieces)
    by_chip = jnp.stack([slab_a] + [swap(slab_a, "dp", sizes["dp"], 2 * k) for k in (1, 2, 3)])
    own_slabs, other_slabs = by_chip, swap(by_chip, "dp", sizes["dp"], 1)
    fr_t = fast_reduce.transpose(0, 2, 1)
    red_w, lred_w, w_first, w_fsp, w_fex, fin_g, fout_g, mid_g, out_g = call(
        weights_kernel,
        [
            shape((3, ways, 8, 8, wide_in), BF16),
            shape((3, ways, 8, 8, mid), BF16),
            shape((896, wide_f), BF16),
            shape((9, 128, 128), BF16),
            shape((128, wide_f), BF16),
            shape((4, 128)),
            shape((2, wide_f)),
            shape((8, mid)),
            shape((ways, 4, mid)),
        ],
        [ids, own_slabs, other_slabs, fr_t, fast_spatial.reshape(9, *fast_spatial.shape[2:]), fast_expand,
         fast_inner_norm.reshape(4, -1), fast_outer_norm],
        [pltpu.VMEM((5, ways, 8, 8, 128), F32)],
        smem=1,
        name="weights",
    )
    red_w, lred_w = red_w.reshape(-1, wide_in), lred_w.reshape(-1, mid)
    fin_g = (fin_g[0:2], fin_g[2:4])
    lat_g, in_g = mid_g[0:2], (mid_g[2:4], mid_g[4:6])
    out_g = out_g.transpose(1, 0, 2).reshape(4, wide_in)

    edge = [shape((halo, 8, 128))] * 2
    edges = [shape((halo, 8, 384))] * 2
    narrow, middle = shape((mine, 8, 128)), shape((mine, 8, mid))
    fx, fa, lp, sums1, first, last = call(
        fast_first_kernel,
        [shape((mine, 8, wide_f), BF16), narrow, middle, shape((2, 384)), *edge],
        [table, *fx_pieces, w_first],
        smem=1,
        name="fast_first",
    )
    fa_lo, fa_hi = halos(first, last, ways)
    sums1 = everywhere(sums1, sizes, (x_pieces, fa_lo, fa_hi))
    slab_b = jnp.stack(at_once([after(slab_b, sums1)] * ways))
    cots = blocks_of(packed(fast_cotangent, split(slow_cotangent)))
    cots[1] = send(after(cots[1], sums1), 1)
    own_slabs, other_slabs = gather_group(slab_b, sizes)
    exp_w, short_w, lshort_w, spat_w = call(
        more_weights_kernel,
        [
            shape((ways, 8, 8, wide_in), BF16),
            shape((ways, 8, 4, 8, wide_in), BF16),
            shape((ways, 8, 8, wide_in), BF16),
            shape((9, ways, 8, 8, mid), BF16),
        ],
        [ids, own_slabs, other_slabs],
        smem=1,
        name="more_weights",
    )
    exp_w, short_w, lshort_w = (v.reshape(-1, wide_in) for v in (exp_w, short_w, lshort_w))
    spat_w = spat_w.reshape(9, mid, mid)
    fast_pad = [pltpu.VMEM((3, ext, 8, 128), F32)]
    slow_pad = [pltpu.VMEM((3, ext, 8, mid), F32)]
    h1, fb, fb_sums = call(
        functools.partial(conv_kernel, halo, across, per_clip, True, (0, 0)),
        [shape((ext, 8, 128), BF16), narrow, shape((2, 128))],
        [table, inv_n, sums1, fin_g[0], fa_lo, fa, fa_hi, w_fsp],
        fast_pad,
        smem=2,
        name="fast_second",
    )
    x, lat, sa, sums2, first, last = call(
        slow_first_kernel,
        [shape((mine, 8, wide_in), BF16), shape((mine, 8, mid), BF16), middle, shape((2, mid + 128)), *edges],
        [table, inv_n, *x_pieces, lp, sums1, lat_g, red_w, lred_w, fb, fb_sums],
        smem=2,
        name="slow_first",
    )
    sa_lo, sa_hi = halos(first, last, ways)
    sums2 = everywhere(sums2, sizes, (slab_b, cots[1], sa_lo, sa_hi))
    cots[2] = send(after(cots[2], sums2), 2)
    h2, fc, fc_sums = call(
        functools.partial(expand_kernel, True, mid),
        [shape((mine, 8, 128), BF16), shape((mine, 8, wide_f), BF16), shape((2, wide_f))],
        [table, inv_n, fb, sums2, fin_g[1], w_fex],
        smem=2,
        name="fast_third",
    )
    ha, sb, sums3 = call(
        functools.partial(conv_kernel, halo, across, per_clip, False, (0, 0)),
        [shape((ext, 8, mid), BF16), middle, shape((2, mid + wide_f))],
        [table, inv_n, sums2, in_g[0], sa_lo, sa, sa_hi, spat_w, fc_sums],
        slow_pad,
        smem=2,
        name="slow_second",
    )
    sums3 = everywhere(sums3, sizes, cots[2])
    cots[3] = send(after(cots[3], sums3), 3)
    sp, sp_sums = call(
        bypass_kernel,
        [shape((mine, 8, wide_in), BF16), shape((2, wide_in))],
        [table, x, lat, short_w, lshort_w],
        smem=1,
        name="bypass",
    )
    hb, sc, sums4 = call(
        functools.partial(expand_kernel, False, 0),
        [shape((mine, 8, mid), BF16), shape((mine, 8, wide_in), BF16), shape((2, 2 * wide_in))],
        [table, inv_n, sb, sums3, in_g[1], exp_w, sp_sums],
        smem=2,
        name="slow_third",
    )
    sums4 = everywhere(sums4, sizes, cots[3])
    fast_out, dfs, fc_slopes = call(
        functools.partial(fast_out_kernel, mid),
        [shape((ways, mine, 8, 128), BF16), shape((mine, 8, wide_f), BF16), shape((2, wide_f))],
        [table, inv_n, fc, sums3, fout_g, fx, *cots],
        [pltpu.VMEM((8, wide_f), F32)],
        smem=2,
        name="fast_out",
    )
    *outs, dss, sums5 = call(
        slow_out_kernel,
        [*[shape((mine, 8, 384), BF16)] * 4, shape((mine, 8, wide_in), BF16), shape((2, 2 * wide_in + wide_f))],
        [table, inv_n, sc, sp, sums4, out_g, *cots, fast_out, fc_slopes],
        [pltpu.VMEM((8, wide_in), F32)],
        smem=2,
        name="slow_out",
    )

    outs[1] = send(outs[1], 1)
    sums5 = everywhere(sums5, sizes, outs[1])
    outs[2] = send(after(outs[2], sums5), 2)
    dfc, dzfb, fb_slopes, first, last = call(
        functools.partial(expand_back_kernel, True, (mid, 2 * wide_in, mid)),
        [shape((mine, 8, wide_f), BF16), narrow, shape((2, 128)), *edges],
        [table, inv_n, dfs, fc, sums3, fout_g, sums5, fb, sums2, fin_g[1], w_fex, sb],
        smem=2,
        name="fast_third_back",
    )
    low6, high6 = halos(first, last, ways)
    dsc, dzsb, sums6, first, last = call(
        functools.partial(expand_back_kernel, False, (0, 0, 0)),
        [shape((mine, 8, wide_in), BF16), middle, shape((2, mid + 128)), *[shape((halo, 8, mid))] * 2],
        [table, inv_n, dss, sc, sums4, out_g[0:2], sums5, sb, sums3, in_g[1], exp_w, fb_slopes],
        smem=2,
        name="slow_third_back",
    )
    low_sb, high_sb = halos(first, last, ways)
    dss_late, = after((dss,), sums6)
    sums6 = everywhere(sums6, sizes, (outs[2], low6, high6, low_sb, high_sb))
    outs[3] = send(after(outs[3], sums6), 3)
    dsp, dx, dl = call(
        bypass_back_kernel,
        [shape((mine, 8, wide_in), BF16), shape((mine, 8, wide_in), BF16), middle],
        [table, inv_n, dss_late, sp, sums4, out_g[2:4], sums5, short_w, lshort_w],
        smem=2,
        name="bypass_back",
    )

    (slab1,) = call(
        first_slab_kernel,
        [shape((ways, 8, 6, 8, wide_in), BF16)],
        [hb, dsc, x, lat, dsp],
        [pltpu.VMEM((6, mid, wide_in), F32)],
        name="first_slab",
    )
    dfb, dzfa, fa_slopes = call(
        functools.partial(conv_back_kernel, halo, across, per_clip, True, (mid, mid, 0, mid, 0)),
        [shape((mine, 8, 128), BF16), narrow, shape((2, 128))],
        [table, inv_n, sums2, fin_g[1], sums6, sa_lo, fb, sa_hi, low6, dzfb, high6, w_fsp, fa, sums1, fin_g[0]],
        fast_pad,
        smem=2,
        name="fast_second_back",
    )
    dsb, dzsa, sums7 = call(
        functools.partial(conv_back_kernel, halo, across, per_clip, False, (0, 0, 0, 128, 0)),
        [shape((mine, 8, mid), BF16), middle, shape((2, mid + 128))],
        [table, inv_n, sums3, in_g[1], sums6, low6, sb, high6, low_sb, dzsb, high_sb, spat_w, sa, sums2, in_g[0], fa_slopes],
        slow_pad,
        smem=2,
        name="slow_second_back",
    )
    slab1, sums7 = lax.optimization_barrier((slab1, sums7))
    sums7 = everywhere(sums7, sizes, outs[3])
    slab1 = scatter_sum(slab1, sizes, group, chan)
    dsa, *dslow, dzlp, sums8 = call(
        slow_back_kernel,
        [shape((mine, 8, 3 * mid), BF16), *[shape((mine, 8, mid), BF16)] * 4, middle, shape((2, mid))],
        [table, inv_n, dzsa, sa, sums2, in_g[0], sums7, red_w, lred_w, dx, dl, lp, sums1, lat_g],
        smem=2,
        name="slow_first_back",
    )
    dslow[1] = send(dslow[1], 1)
    dsa, dsb_late = after((dsa, dsb), sums8)
    sums8 = everywhere(sums8, sizes, dslow[1])
    dslow[2] = send(after(dslow[2], sums8), 2)
    dslow[3] = send(after(dslow[3], dslow[2]), 3)
    slow_output, fast_output = unpacked(after(outs, sums8))
    (slab2,) = call(
        functools.partial(second_slab_kernel, halo, across, per_clip),
        [shape((ways, 8, 6, 8, wide_in), BF16)],
        [table, ha, dsb_late, dsa, x, lat],
        [*slow_pad, pltpu.VMEM((3, mid, 3 * mid), F32), pltpu.VMEM((3, mid, wide_in), F32), pltpu.VMEM((3, mid, mid), F32)],
        smem=1,
        name="second_slab",
    )
    slab2 = scatter_sum(slab2, sizes, group, chan)
    dfirst, *dfast = call(
        functools.partial(fast_back_kernel, mid),
        [shape((mine, 8, 896), BF16), *[shape((mine, 8, 128), BF16)] * 4],
        [table, inv_n, sums1, fin_g[0], lat_g, sums7, sums8, dzfa, fa, dzlp, lp, dfs, w_first],
        smem=2,
        name="fast_first_back",
    )

    g_lat, g_fast = call(
        functools.partial(fast_grads_kernel, halo, across, per_clip),
        [shape((ways, 40, 8, 128), BF16), shape((28, 8, 128), BF16)],
        [table, h1, dfb, dfirst, fx, h2, dfc],
        [*fast_pad, pltpu.VMEM((3, 384, 128), F32), pltpu.VMEM((896, wide_f), F32), pltpu.VMEM((128, wide_f), F32)],
        smem=1,
        name="fast_grads",
    )
    small = [jnp.concatenate([pick(g_lat, chan ^ k, 0), g_fast]) for k in range(ways)]
    small = add(*at_once(after(small, dslow[2])))
    for bits in stages(sizes["dp"], True):
        small = butterfly(small, "dp", sizes["dp"], bits)
    g_lat, g_fast = small[0:40].astype(F32), small[40:68].astype(F32)
    own1, other1 = gather_group(slab1, sizes)
    g_exp, g_short, g_lshort = call(
        first_grads_kernel,
        [shape((8, 8, wide_in)), shape((8, 4, 8, wide_in)), shape((8, 8, wide_in))],
        [ids, own1, other1],
        smem=1,
        name="first_grads",
    )
    own2, other2 = gather_group(slab2, sizes)
    g_red, g_lred, g_spat = call(
        second_grads_kernel,
        [shape((3, 8, 8, wide_in)), shape((3, 8, 8, mid)), shape((9, 8, 8, mid))],
        [ids, own2, other2],
        smem=1,
        name="second_grads",
    )
    (slow_input_grad,) = call(place_kernel, [shape((places, slow_t, slow_part), BF16)], [ids, *dslow], smem=1, name="slow_place")
    slow_input_grad = joined(slow_input_grad)
    fast_input_grad = unpacked(at_once(after(dfast, dslow[3])))
    g_fred = g_fast[0:12].reshape(3, 32, 128).transpose(0, 2, 1)
    g_fex = g_fast[12:16].reshape(32, 128)
    g_fsp = g_fast[16:28].reshape(3, 32, 128)[:, :, 0:96].reshape(3, 32, 3, 32).transpose(0, 2, 1, 3)

    def pair(slopes):
        return slopes[::-1]

    def own(v, width):
        return lax.dynamic_slice_in_dim(v, chan * width, width, v.ndim - 1)

    def fold_in(slopes):
        return jnp.sum(slopes.reshape(2, ratio, 128 // ratio), axis=1)

    lw, sw, ow = lateral_norm.shape[1], slow_inner_norm.shape[2], slow_outer_norm.shape[2]
    fast_inner_grad = jnp.stack([pair(fold_in(sums7[:, mid:])), pair(fold_in(sums6[:, mid:]))])
    fc_slopes = sums5[:, 2 * wide_in :].reshape(2, ways, ratio, fast_part)
    fast_outer_grad = pair(jnp.sum(fc_slopes, axis=2).reshape(2, -1))
    lateral_grad = pair(own(sums8, lw))
    slow_inner_grad = own(jnp.stack([pair(sums7[:, 0:mid]), pair(sums6[:, 0:mid])]), sw)
    slow_outer_grad = own(jnp.stack([pair(sums5[:, 0:wide_in]), pair(sums5[:, wide_in : 2 * wide_in])]), ow)
    return (
        slow_output,
        fast_output,
        slow_input_grad,
        fast_input_grad,
        g_fred,
        g_fsp,
        g_fex,
        g_lat.reshape(5, -1, 128).transpose(0, 2, 1),
        g_red.reshape(3, -1, wide_in).transpose(0, 2, 1),
        g_lred.reshape(3, -1, mid).transpose(0, 2, 1),
        g_spat.reshape(9, -1, mid).transpose(0, 2, 1).reshape(slow_spatial.shape),
        g_exp.reshape(-1, wide_in),
        g_short.reshape(-1, wide_in),
        g_lshort.reshape(-1, wide_in),
        fast_inner_grad,
        fast_outer_grad,
        lateral_grad,
        slow_inner_grad,
        slow_outer_grad,
    )


def solution(mesh):
    sizes = {"dp": mesh.shape["dp"], "chan": mesh.shape["chan"]}
    big = P("dp", None, None, None, "chan")
    last2, last3, last4 = P(None, "chan"), P(None, None, "chan"), P(None, None, None, "chan")
    first = P("chan", None)
    return jax.shard_map(
        functools.partial(local, sizes),
        mesh=mesh,
        in_specs=(
            big, big, P(), P(), P(), P(), P(), last3, last3, last3, last4, first, first, first,
            P(), P(), last2, last3, last3, big, big,
        ),
        out_specs=(
            big, big, big, big, P(), P(), P(), last3, last3, last3, last4, first, first, first,
            P(), P(), last2, last3, last3,
        ),
        check_vma=False,
    )
```

```python
import functools

import jax
import jax.numpy as jnp
from jax import lax
from jax.experimental import pallas as pl
from jax.experimental.pallas import tpu as pltpu
from jax.sharding import PartitionSpec as P

F32 = jnp.float32
BF16 = jnp.bfloat16
EPSILON = 1e-05
ROOT = 0.7978845608028654
CUBIC = 0.044715
BIG = 49
PARTS = ((0, 0), (1, 0), (2, 0), (2, 98), (3, 0), (3, 49))
SMALL = 7


def gelu(v):
    return 0.5 * v * (1.0 + jnp.tanh(ROOT * (v * (1.0 + CUBIC * (v * v)))))


def gelu_slope(v):
    square = v * v
    th = jnp.tanh(ROOT * (v * (1.0 + CUBIC * square)))
    half = 0.5 * (1.0 + th)
    return half + (0.5 * ROOT) * v * (1.0 - th * th) * (1.0 + 3.0 * CUBIC * square)


def gelu_pair(v):
    square = v * v
    th = jnp.tanh(ROOT * (v * (1.0 + CUBIC * square)))
    half = 0.5 * (1.0 + th)
    slope = half + (0.5 * ROOT) * v * (1.0 - th * th) * (1.0 + 3.0 * CUBIC * square)
    return v * half, slope


def rows(v):
    return v.reshape(v.shape[0] * v.shape[1], v.shape[2])


def cells(v):
    return v.reshape(v.shape[0] // 8, 8, v.shape[1])


def rows_bf(v):
    return rows(v.astype(F32)).astype(BF16)


def wide(mask, width):
    repeats = width // 128
    return mask if repeats == 1 else jnp.concatenate([mask] * repeats, axis=-1)


def nn(a, b):
    return jnp.dot(a, b, preferred_element_type=F32)


def nt(a, b):
    return lax.dot_general(a, b, (((1,), (1,)), ((), ())), preferred_element_type=F32)


def later(v):
    rolled = pltpu.roll(v, 1, 1)
    return jnp.where(lax.broadcasted_iota(jnp.int32, v.shape, 1) == 0, 0.0, rolled)


def sooner(v):
    rolled = pltpu.roll(v, 7, 1)
    return jnp.where(lax.broadcasted_iota(jnp.int32, v.shape, 1) == 7, 0.0, rolled)


def folded(v):
    out = []
    for block in range(v.shape[-1] // 128):
        part = v[:, 128 * block : 128 * block + 128]
        part = part + pltpu.roll(part, 64, 1)
        out.append(part + pltpu.roll(part, 32, 1))
    return out[0] if len(out) == 1 else jnp.concatenate(out, axis=-1)


def scale_of(sums, gains, inv_n):
    center = sums[0:1] * inv_n
    spread = sums[1:2] * inv_n - center * center
    inv_std = lax.rsqrt(spread + EPSILON)
    factor = gains[0:1] * inv_std
    return factor, gains[1:2] - center * factor, center, inv_std


def slope_of(slopes, factor, center, inv_std, inv_n):
    k1 = factor * slopes[1:2] * inv_n * inv_std
    k0 = factor * slopes[0:1] * inv_n - k1 * center
    return k0, k1


def down(v):
    return jnp.sum(v, axis=0)


def flat(v):
    return jnp.sum(v, axis=0, keepdims=True)


def steps(count, step, body, carry):
    return lax.fori_loop(0, count // step, lambda i, c: body(i * step, c), carry)


def call(kernel, outs, args, scratch=(), smem=0, flops=0, name=None):
    specs = [pl.BlockSpec(memory_space=pltpu.SMEM if i < smem else pltpu.VMEM) for i in range(len(args))]
    total = sum(a.size * a.dtype.itemsize for a in args)
    total += sum(o.size * o.dtype.itemsize for o in outs)
    def padded(v):
        dims = list(v.shape)
        if len(dims) < 2:
            return 4096
        dims[-1] = -(-dims[-1] // 128) * 128
        dims[-2] = -(-dims[-2] // 8) * 8
        amount = v.dtype.itemsize
        for d in dims:
            amount *= d
        return amount

    room = sum(padded(v) for v in (*args, *outs, *scratch)) + 6 * 1024 * 1024
    return pl.pallas_call(
        kernel,
        out_shape=tuple(outs),
        in_specs=specs,
        out_specs=tuple(pl.BlockSpec(memory_space=pltpu.VMEM) for _ in outs),
        scratch_shapes=list(scratch),
        compiler_params=pltpu.CompilerParams(vmem_limit_bytes=room),
        cost_estimate=pl.CostEstimate(flops=flops, bytes_accessed=1, transcendentals=0),
        name=name,
    )(*args)


def shape(dims, dtype=F32):
    return jax.ShapeDtypeStruct(dims, dtype)


def tile_mask(frames, width):
    tile = (lax.broadcasted_iota(jnp.int32, (8, 128), 0) < frames).astype(F32)
    return wide(tile, width)[None]


def sweep(table_ref, size, step, body, carry=0, begin=0):
    def run(i, kept):
        p = i * step
        return body(p, table_ref[1 + (begin + p) // BIG], kept)

    return lax.fori_loop(0, size // step, run, carry)


def lane_group(v, group):
    return jnp.where(lax.broadcasted_iota(jnp.int32, v.shape, v.ndim - 1) // 32 == group, v, 0.0)


def moved(v, shift):
    shift = shift % 128
    return v if shift == 0 else pltpu.roll(v, shift, v.ndim - 1)


def pack_kernel(per_clip, clips, ids_ref, counts_ref, frames_ref, x_ref, *refs):
    out_ref, tmp_ref = refs[-2:]
    clip, dp = pl.program_id(0) // per_clip, ids_ref[0]
    chunk = x_ref.shape[0]
    frames = jnp.where(clip < counts_ref[dp], frames_ref[dp * clips + clip], 0)
    tmp_ref[...] = x_ref[...].astype(F32).reshape(chunk * 32, 32)
    parts = [tmp_ref[pl.ds(r, chunk * 8, stride=4), :] for r in range(4)]
    out_ref[:, :, 0:128] = (cells(jnp.concatenate(parts, axis=1)) * tile_mask(frames, 128)).astype(BF16)
    if len(refs) == 3:
        out_ref[:, :, 128:384] = refs[0][...]


def unpack_kernel(ids_ref, *refs):
    slow_ref, fast_ref, tmp_ref = refs[-3:]
    size = refs[0].shape[0]
    for (k, first), ref in zip(PARTS, refs):
        begin = (ids_ref[1] ^ k) * size + first

        def body(p, carry, ref=ref, begin=begin):
            joined = rows(ref[pl.ds(p, BIG), :, 0:128].astype(F32))
            for r in range(4):
                tmp_ref[pl.ds(r, BIG * 8, stride=4), :] = joined[:, 32 * r : 32 * r + 32]
            fast_ref[pl.ds(begin + p, BIG)] = tmp_ref[...].reshape(BIG, 32, 32).astype(BF16)
            slow_ref[pl.ds(begin + p, BIG)] = ref[pl.ds(p, BIG), :, 128:384]
            return carry

        steps(ref.shape[0], BIG, body, 0)


def unpack_fast_kernel(x_ref, out_ref, tmp_ref):
    chunk = x_ref.shape[0]
    joined = rows(x_ref[...].astype(F32))
    for r in range(4):
        tmp_ref[pl.ds(r, chunk * 8, stride=4), :] = joined[:, 32 * r : 32 * r + 32]
    out_ref[...] = tmp_ref[...].reshape(chunk, 32, 32).astype(BF16)


def lanes_at(block, width):
    return pl.ds(pl.multiple_of(block * width, width), width)


LREDUCE = [(3, 256 * k) for k in range(3)]
LATERAL = [(4, 128 * k) for k in range(5)]
GAINS = [(3, 768), (3, 896), (4, 640), (4, 768)]
SPATIAL = [(11 + k // 4, 256 * (k % 4)) for k in range(9)]


def weight_slab_kernel(ids_ref, red_ref, lred_ref, lat_ref, exp_ref, short_ref, lshort_ref, sp_ref, ln_ref, sn_ref, on_ref, out_ref,
                       red_s, lred_s, lat_s, exp_s, short_s, lshort_s, sp_s, sem):
    group = ids_ref[2]
    eight, more = pl.ds(pl.multiple_of(group * 8, 8), 8), pl.ds(pl.multiple_of(group * 32, 32), 32)
    copies = []
    for i, (src, dst) in enumerate((
        (red_ref.at[:, eight], red_s), (lred_ref.at[:, eight], lred_s), (lat_ref.at[:, eight], lat_s), (exp_ref.at[eight], exp_s),
        (short_ref.at[more], short_s), (lshort_ref.at[eight], lshort_s), (sp_ref.at[:, eight], sp_s),
    )):
        copies.append(pltpu.make_async_copy(src, dst, sem.at[i]))
    for copy in copies:
        copy.start()
    out_ref[4, :, 896:1024] = jnp.zeros((8, 128), BF16)
    out_ref[13, :, 256:1024] = jnp.zeros((8, 768), BF16)
    blank = jnp.zeros((2, 128), F32)
    half = jnp.zeros((2, 64), F32)
    inner = jnp.concatenate([jnp.concatenate([v, half], axis=1) for v in (ln_ref[...], sn_ref[0:2], sn_ref[2:4])] + [blank], axis=0)
    outer = jnp.concatenate([on_ref[:, 0:128], on_ref[:, 128:256]], axis=0)
    for i, v in enumerate((inner, outer)):
        high = v.astype(BF16)
        for k, part in ((i, high), (2 + i, (v - high.astype(F32)).astype(BF16))):
            at, lane = GAINS[k]
            out_ref[at, :, lane : lane + 128] = part
    for copy in copies:
        copy.wait()
    for j in range(3):
        out_ref[j] = red_s[j].astype(BF16)
        at, lane = LREDUCE[j]
        out_ref[at, :, lane : lane + 256] = lred_s[j].astype(BF16)
    out_ref[5], out_ref[10] = exp_s[...].astype(BF16), lshort_s[...].astype(BF16)
    for a in range(4):
        out_ref[6 + a] = short_s[8 * a : 8 * a + 8].astype(BF16)
    for k in range(9):
        at, lane = SPATIAL[k]
        out_ref[at, :, lane : lane + 256] = sp_s[k].astype(BF16)
    for k in range(5):
        at, lane = LATERAL[k]
        out_ref[at, :, lane : lane + 128] = lat_s[k].astype(BF16)


def more_weights_kernel(ids_ref, own_ref, other_ref, exp_ref, short_ref, lshort_ref, sp_ref):
    me, group = ids_ref[1], ids_ref[2]

    def place(i, carry):
        chip, kz = i // 4, i % 4
        z = me ^ kz
        for core, ref in ((0, own_ref), (1, other_ref)):
            d = group ^ (2 * chip + core)
            exp_ref[z, d], lshort_ref[z, d] = ref[chip, kz, 0], ref[chip, kz, 5]
            for a in range(4):
                short_ref[z, d, a] = ref[chip, kz, 1 + a]
            for k in range(9):
                at, lane = SPATIAL[k]
                sp_ref[k, z, d] = ref[chip, kz, at - 5, :, lane : lane + 256]
        return carry

    lax.fori_loop(0, 16, place, 0)


def weights_kernel(ids_ref, own_ref, other_ref, fr_ref, fsp_ref, fex_ref, fin_ref, fout_ref, red_ref, lred_ref, first_ref, wsp_ref, wex_ref,
                   gin_ref, gout_ref, gmid_ref, gwide_ref, lat_ref):
    me, group = ids_ref[1], ids_ref[2]

    def place(i, carry):
        chip, kz = i // 4, i % 4
        z = me ^ kz
        for core, ref in ((0, own_ref), (1, other_ref)):
            d = group ^ (2 * chip + core)
            for j in range(3):
                red_ref[j, z, d] = ref[chip, kz, j]
                at, lane = LREDUCE[j]
                lred_ref[j, z, d] = ref[chip, kz, at, :, lane : lane + 256]
            for k in range(5):
                at, lane = LATERAL[k]
                lat_ref[k, z, d] = ref[chip, kz, at, :, lane : lane + 128].astype(F32)
        return carry

    lax.fori_loop(0, 16, place, 0)

    mids = [jnp.zeros((8, 128), F32) for _ in range(2)]
    for kz in range(4):
        z = me ^ kz
        parts = [own_ref[0, kz, at, :, lane : lane + 128].astype(F32) for at, lane in GAINS]
        inner, outer = parts[0] + parts[2], parts[1] + parts[3]
        for half in range(2):
            for block in range(2):
                here = (z == 2 * block + half).astype(F32)
                mids[block] = mids[block] + moved(inner, 64 * half) * here
        gwide_ref[z, :, 0:128], gwide_ref[z, :, 128:256] = outer[0:4], outer[4:8]
    gmid_ref[:, 0:128], gmid_ref[:, 128:256] = mids[0], mids[1]

    first_ref[...] = jnp.zeros_like(first_ref)
    wsp_ref[...] = jnp.zeros_like(wsp_ref)
    for z in range(4):
        lanes = slice(128 * z, 128 * z + 128)

        def put(v, r, z=z):
            return lane_group(moved(v, 32 * r - 32 * z), r)

        for q in range(4):
            total = sum(put(fr_ref[r - q + 1], r) for r in range(4) if abs(r - q) <= 1)
            first_ref[32 * q : 32 * q + 32, lanes] = total.astype(BF16)
        first_ref[128:160, lanes] = put(fr_ref[0], 3).astype(BF16)
        first_ref[352:384, lanes] = put(fr_ref[2], 0).astype(BF16)
        taps = [lat_ref[j].reshape(256, 128) for j in range(5)]
        first_ref[384:640, lanes] = sum(put(taps[2 + r], r) for r in range(3)).astype(BF16)
        first_ref[640:896, lanes] = (put(taps[0], 2) + put(taps[1], 3)).astype(BF16)
        for r in range(4):
            wex_ref[32 * r : 32 * r + 32, lanes] = put(fex_ref[...], r).astype(BF16)
        gout_ref[:, lanes] = sum(put(fout_ref[...], r) for r in range(4))
    blank = jnp.zeros((32, 96), F32)
    for k in range(9):
        tap = jnp.concatenate([fsp_ref[k], blank], axis=1)
        for r in range(4):
            wsp_ref[k, 32 * r : 32 * r + 32, :] = moved(tap, 32 * r).astype(BF16)
    gin_ref[...] = jnp.concatenate([fin_ref[...]] * 4, axis=1)


def grads_kernel(ids_ref, own_ref, other_ref, exp_ref, short_ref, lshort_ref, red_ref, lred_ref, sp_ref):
    def place(chip, carry):
        for core, ref in ((0, own_ref), (1, other_ref)):
            d = ids_ref[2] ^ (2 * chip + core)
            exp_ref[d], lshort_ref[d] = ref[chip, 0].astype(F32), ref[chip, 5].astype(F32)
            for a in range(4):
                short_ref[d, a] = ref[chip, 1 + a].astype(F32)
            for j in range(3):
                red_ref[j, d] = ref[chip, 6 + j].astype(F32)
                lred_ref[j, d] = ref[chip, 9, :, 256 * j : 256 * j + 256].astype(F32)
            for k in range(8):
                sp_ref[k, d] = ref[chip, 10 + k // 4, :, 256 * (k % 4) : 256 * (k % 4) + 256].astype(F32)
            sp_ref[8, d] = ref[chip, 9, :, 768:1024].astype(F32)
        return carry

    lax.fori_loop(0, 4, place, 0)


def fast_first_kernel(table_ref, f0_ref, f1_ref, f2_ref, f3_ref, w_ref, fx_ref, fa_ref, lp_ref, sums_ref, first_ref, last_ref):
    size = fa_ref.shape[0]

    def fill(p, carry):
        for k, ref in enumerate((f0_ref, f1_ref, f2_ref, f3_ref)):
            fx_ref[pl.ds(p, SMALL), :, lanes_at(table_ref[5] ^ k, 128)] = ref[pl.ds(p, SMALL)]
        return carry

    steps(size, SMALL, fill, 0)

    def body(p, frames, carry):
        acc = cells(nt(rows_bf(fx_ref[pl.ds(p, BIG)]), w_ref[...]))
        fa = acc[:, :, 0:128] + later(acc[:, :, 128:256]) + sooner(acc[:, :, 256:384])
        lp = acc[:, :, 384:640] + later(acc[:, :, 640:896])
        fa_ref[pl.ds(p, BIG)] = fa
        lp_ref[pl.ds(p, BIG)] = lp
        fm, lm = fa * tile_mask(frames, 128), lp * tile_mask(frames, 256)
        return tuple(c + down(v) for c, v in zip(carry, (fm, fm * fa, lm, lm * lp)))

    zero = (jnp.zeros((8, 128), F32),) * 2 + (jnp.zeros((8, 256), F32),) * 2
    a, b, c, d = sweep(table_ref, size, BIG, body, zero)
    sums_ref[0:1, 0:128], sums_ref[1:2, 0:128] = flat(a), flat(b)
    sums_ref[0:1, 128:384], sums_ref[1:2, 128:384] = flat(c), flat(d)
    halo = first_ref.shape[0]
    first_ref[...], last_ref[...] = fa_ref[0:halo], fa_ref[size - halo : size]


def fill_padded(table_ref, refs, offset, out_ref, value, halo, size):
    low, middle, high = refs
    phase = table_ref[5] * (size // SMALL)

    def put(v, at, part, count, step=SMALL):
        even = ((phase + part + 2 * count) % 2 == 0).astype(F32)
        out_ref[1, pl.ds(at, step)] = v
        if step == 1:
            out_ref[0, pl.ds(at, 1)] = v * even
            out_ref[2, pl.ds(at, 1)] = v * (1.0 - even)
            return
        out_ref[0, pl.ds(at, step)] = v
        out_ref[2, pl.ds(at, step)] = v
        out_ref[0, pl.ds(at + step - 1, 1)] = v[step - 1 : step] * even
        out_ref[2, pl.ds(at, 1)] = v[0:1] * (1.0 - even)

    width = out_ref.shape[-1]
    lo_mask, hi_mask = tile_mask(table_ref[0], width), tile_mask(table_ref[4], width)
    put(value(low, 0, 1) * lo_mask, 0, -3, 4, 1)
    put(value(low, 1, SMALL) * lo_mask, 1, -2, 4)
    put(value(low, 1 + SMALL, SMALL) * lo_mask, 1 + SMALL, -1, 4)
    parts = size // SMALL
    put(value(high, 0, SMALL) * hi_mask, halo + size, parts, 0)
    put(value(high, SMALL, SMALL) * hi_mask, halo + size + SMALL, parts + 1, 0)
    put(value(high, 2 * SMALL, 1) * hi_mask, halo + size + 2 * SMALL, parts + 2, 0, 1)

    def body(p, frames, carry):
        put(value(middle, p, SMALL) * tile_mask(frames, width), halo + p, p // SMALL, 0)
        return carry

    sweep(table_ref, size, SMALL, body)


def edge_scales(table_ref, p, per_clip):
    part = table_ref[5] * table_ref[6] + p // BIG
    return (part % per_clip != 0).astype(F32), ((part + 1) % per_clip != 0).astype(F32)


def conv_rows(table_ref, per_clip, pad_ref, weight, p, halo, row_len, dot):
    top, bottom = edge_scales(table_ref, p, per_clip)
    total = None
    for i in (1, 0, 2):
        begin = p + halo + row_len * (i - 1)
        acc = None
        for j in range(3):
            tap = rows(pad_ref[j, pl.ds(begin + j - 1, BIG)]).astype(BF16)
            part = dot(tap, weight(i, j))
            acc = part if acc is None else acc + part
        acc = cells(acc)
        if i == 0:
            acc = jnp.concatenate([acc[0:row_len] * top, acc[row_len:]], axis=0)
        if i == 2:
            acc = jnp.concatenate([acc[: BIG - row_len], acc[BIG - row_len :] * bottom], axis=0)
        total = acc if total is None else total + acc
    return total


def conv_kernel(halo, row_len, per_clip, fold, offsets, table_ref, n_ref, sums_ref, gains_ref, lo_ref, y_ref, hi_ref, w_ref, *refs):
    if fold:
        act_ref, out_ref, osums_ref, pad_ref = refs
    else:
        more_ref, act_ref, out_ref, osums_ref, pad_ref = refs
    size, width = y_ref.shape[0], y_ref.shape[2]
    sums = sums_ref[:, offsets[0] : offsets[0] + width]
    sums = folded(sums) if fold else sums
    factor, shift, _, _ = scale_of(sums, gains_ref[...], n_ref[1 if fold else 0])
    lanes = slice(offsets[1], offsets[1] + width)

    def value(ref, p, step):
        y = ref[pl.ds(p, step)] if ref is y_ref else ref[pl.ds(p, step), :, lanes]
        return gelu(y * factor[None] + shift[None]).astype(BF16).astype(F32)

    fill_padded(table_ref, (lo_ref, y_ref, hi_ref), 0, pad_ref, value, halo, size)

    def copy(p, carry):
        act_ref[pl.ds(p, 3)] = pad_ref[1, pl.ds(p, 3)].astype(BF16)
        return carry

    steps(size + 2 * halo, 3, copy, 0)

    def body(p, frames, carry):
        total = conv_rows(table_ref, per_clip, pad_ref, lambda i, j: w_ref[3 * i + j], p, halo, row_len, nn if fold else nt)
        out_ref[pl.ds(p, BIG)] = total
        masked = total * tile_mask(frames, width)
        return carry[0] + down(masked), carry[1] + down(masked * total)

    a, b = sweep(table_ref, size, BIG, body, (jnp.zeros((8, width), F32),) * 2)
    osums_ref[0:1, 0:width], osums_ref[1:2, 0:width] = flat(a), flat(b)
    if not fold:
        osums_ref[:, width:] = more_ref[...]


def slow_first_kernel(table_ref, n_ref, xs_ref, lp_ref, lsums_ref, gains_ref, w_ref, wl_ref,
                      x_ref, lat_ref, sa_ref, sums_ref, first_ref, last_ref):
    size = lp_ref.shape[0]
    factor, shift, _, _ = scale_of(lsums_ref[:, 128:384], gains_ref[...], n_ref[0])

    def fill(p, frames, carry):
        mask = tile_mask(frames, 256)
        lat_ref[pl.ds(p, SMALL)] = (gelu(lp_ref[pl.ds(p, SMALL)] * factor[None] + shift[None]) * mask).astype(BF16)
        for z in range(4):
            v = xs_ref[z, pl.ds(p, SMALL)].astype(F32) * mask
            x_ref[pl.ds(p, SMALL), :, 256 * z : 256 * z + 256] = v.astype(BF16)
        return carry

    sweep(table_ref, size, SMALL, fill)

    def body(p, frames, carry):
        acc = nt(rows_bf(x_ref[pl.ds(p, BIG)]), w_ref[...]) + nt(rows_bf(lat_ref[pl.ds(p, BIG)]), wl_ref[...])
        acc = cells(acc)
        sa = later(acc[:, :, 0:256]) + acc[:, :, 256:512] + sooner(acc[:, :, 512:768])
        sa_ref[pl.ds(p, BIG)] = sa
        masked = sa * tile_mask(frames, 256)
        return carry[0] + down(masked), carry[1] + down(masked * sa)

    a, b = sweep(table_ref, size, BIG, body, (jnp.zeros((8, 256), F32),) * 2)
    sums_ref[0:1], sums_ref[1:2] = flat(a), flat(b)
    halo = first_ref.shape[0]
    first_ref[...], last_ref[...] = sa_ref[0:halo], sa_ref[size - halo : size]


def bypass_kernel(table_ref, x_ref, lat_ref, w_ref, wl_ref, sp_ref, sums_ref):
    def body(p, frames, carry):
        sp = cells(nn(rows_bf(x_ref[pl.ds(p, BIG)]), w_ref[...]) + nn(rows_bf(lat_ref[pl.ds(p, BIG)]), wl_ref[...]))
        sp_ref[pl.ds(p, BIG)] = sp.astype(BF16)
        masked = sp * tile_mask(frames, sp.shape[-1])
        return carry[0] + down(masked), carry[1] + down(masked * sp)

    a, b = sweep(table_ref, sp_ref.shape[0], BIG, body, (jnp.zeros((8, sp_ref.shape[2]), F32),) * 2)
    sums_ref[0:1], sums_ref[1:2] = flat(a), flat(b)


def expand_kernel(fold, offset, table_ref, n_ref, y_ref, sums_ref, gains_ref, w_ref, *refs):
    more, (h_ref, out_ref, osums_ref) = refs[:-3], refs[-3:]
    size, width = y_ref.shape[0], y_ref.shape[2]
    sums = sums_ref[:, offset : offset + width]
    sums = folded(sums) if fold else sums
    factor, shift, _, _ = scale_of(sums, gains_ref[...], n_ref[1 if fold else 0])

    def fill(p, frames, carry):
        v = gelu(y_ref[pl.ds(p, SMALL)] * factor[None] + shift[None])
        h_ref[pl.ds(p, SMALL)] = (v * tile_mask(frames, width)).astype(BF16)
        return carry

    sweep(table_ref, size, SMALL, fill)

    def body(p, frames, carry):
        out = cells(nn(rows_bf(h_ref[pl.ds(p, BIG)]), w_ref[...]))
        out_ref[pl.ds(p, BIG)] = out.astype(BF16)
        masked = out * tile_mask(frames, out.shape[-1])
        return carry[0] + down(masked), carry[1] + down(masked * out)

    wide_out = out_ref.shape[2]
    a, b = sweep(table_ref, size, BIG, body, (jnp.zeros((8, wide_out), F32),) * 2)
    osums_ref[0:1, 0:wide_out], osums_ref[1:2, 0:wide_out] = flat(a), flat(b)
    for ref in more:
        osums_ref[:, wide_out : wide_out + ref.shape[1]] = ref[...]
        wide_out += ref.shape[1]


def fast_out_kernel(offset, table_ref, n_ref, fc_ref, sums_ref, gains_ref, fx_ref, *refs):
    cots, (out_ref, up_ref, slopes_ref, vec_ref) = refs[: len(PARTS)], refs[len(PARTS) :]
    width = fc_ref.shape[2]
    vecs = scale_of(folded(sums_ref[:, offset : offset + width]), gains_ref[...], n_ref[1])
    for i, v in enumerate(vecs):
        vec_ref[i : i + 1] = v
    kept = (jnp.zeros((8, 128), F32),) * 2
    for part, ((k, begin), cot_ref) in enumerate(zip(PARTS, cots)):
        lanes = lanes_at(table_ref[5] ^ k, 128)
        fz, sz, cz, rz = (vec_ref[i : i + 1, lanes][None] for i in range(4))

        def body(p, frames, carry, k=k, lanes=lanes, fz=fz, sz=sz, cz=cz, rz=rz, cot_ref=cot_ref, begin=begin):
            here = pl.ds(begin + p, SMALL)
            y = fc_ref[here, :, lanes].astype(F32)
            mask = tile_mask(frames, 128)
            total = y * fz + sz + fx_ref[here, :, lanes].astype(F32)
            value, slope = gelu_pair(total)
            out_ref[k, here] = (value * mask).astype(BF16)
            up = slope * (cot_ref[pl.ds(p, SMALL), :, 0:128].astype(F32) * mask)
            up_ref[here, :, lanes] = up.astype(BF16)
            return carry[0] + down(up), carry[1] + down(up * ((y - cz) * rz))

        zero = (jnp.zeros((8, 128), F32),) * 2
        kept = sweep(table_ref, cot_ref.shape[0], SMALL, body, kept if begin else zero, begin)
        slopes_ref[0:1, lanes], slopes_ref[1:2, lanes] = flat(kept[0]), flat(kept[1])


def slow_out_kernel(table_ref, n_ref, sc_ref, sp_ref, sums_ref, gains_ref, *refs):
    count = len(PARTS)
    cots, (fast_ref, more_ref), outs = refs[:count], refs[count : count + 2], refs[count + 2 : 2 * count + 2]
    up_ref, slopes_ref, vec_ref = refs[2 * count + 2 :]
    width = sc_ref.shape[2]
    cf, cs, cc, cr = scale_of(sums_ref[:, 0:width], gains_ref[0:2], n_ref[0])
    pf, ps, pc, pr = scale_of(sums_ref[:, width : 2 * width], gains_ref[2:4], n_ref[0])
    for i, v in enumerate((cf, cs + ps, cc, cr, pf, pc, pr)):
        vec_ref[i : i + 1] = v
    kept = ()
    for (k, begin), cot_ref, out_ref in zip(PARTS, cots, outs):
        block = table_ref[5] ^ k
        lanes = lanes_at(block, 256)
        vecs = [vec_ref[i : i + 1, lanes][None] for i in range(7)]

        def body(p, frames, carry, k=k, lanes=lanes, vecs=vecs, cot_ref=cot_ref, out_ref=out_ref, begin=begin):
            cf, shift, cc, cr, pf, pc, pr = vecs
            here = pl.ds(begin + p, SMALL)
            yc, yp = (ref[here, :, lanes].astype(F32) for ref in (sc_ref, sp_ref))
            mask = tile_mask(frames, 256)
            value, slope = gelu_pair(yc * cf + yp * pf + shift)
            out_ref[pl.ds(p, SMALL), :, 128:384] = (value * mask).astype(BF16)
            out_ref[pl.ds(p, SMALL), :, 0:128] = fast_ref[k, here]
            up = slope * (cot_ref[pl.ds(p, SMALL), :, 128:384].astype(F32) * mask)
            up_ref[here, :, lanes] = up.astype(BF16)
            return (carry[0] + down(up), carry[1] + down(up * ((yc - cc) * cr)), carry[2] + down(up * ((yp - pc) * pr)))

        zero = (jnp.zeros((8, 256), F32),) * 3
        kept = sweep(table_ref, cot_ref.shape[0], SMALL, body, kept if begin else zero, begin)
        a, b, c = kept
        own, other = lanes, lanes_at(4 + block, 256)
        slopes_ref[0:1, own], slopes_ref[1:2, own] = flat(a), flat(b)
        slopes_ref[0:1, other], slopes_ref[1:2, other] = flat(a), flat(c)
    slopes_ref[:, 2 * width :] = more_ref[...]


def norm_back_fill(table_ref, up_ref, y_ref, dy_ref, factor, k0, k1):
    def fill(p, frames, carry):
        mask = tile_mask(frames, 128)
        for q in range(y_ref.shape[2] // 128):
            lanes = slice(128 * q, 128 * q + 128)
            y = y_ref[pl.ds(p, SMALL), :, lanes].astype(F32)
            dy = up_ref[pl.ds(p, SMALL), :, lanes].astype(F32) * factor[:, lanes][None]
            dy = dy - mask * (k0[:, lanes][None] + k1[:, lanes][None] * y)
            dy_ref[pl.ds(p, SMALL), :, lanes] = dy.astype(BF16)
        return carry

    sweep(table_ref, y_ref.shape[0], SMALL, fill)


def expand_back_kernel(fold, offsets, table_ref, n_ref, up_ref, y_ref, sums_ref, gains_ref, slopes_ref, z_ref, zsums_ref, zgains_ref,
                       w_ref, other_ref, dy_ref, dz_ref, oslopes_ref, first_ref, last_ref):
    size, width, inner = y_ref.shape[0], y_ref.shape[2], z_ref.shape[2]
    fix = folded if fold else (lambda v: v)
    inv_n = n_ref[1 if fold else 0]
    at_y, at_s, at_z = offsets
    factor, shift, center, inv_std = scale_of(fix(sums_ref[:, at_y : at_y + width]), gains_ref[...], inv_n)
    k0, k1 = slope_of(fix(slopes_ref[:, at_s : at_s + width]), factor, center, inv_std, inv_n)
    norm_back_fill(table_ref, up_ref, y_ref, dy_ref, factor, k0, k1)
    zf, zs, zc, zr = scale_of(fix(zsums_ref[:, at_z : at_z + inner]), zgains_ref[...], inv_n)

    def body(p, frames, carry):
        dh = cells(nt(rows_bf(dy_ref[pl.ds(p, BIG)]), w_ref[...]))
        z = z_ref[pl.ds(p, BIG)]
        dz = gelu_slope(z * zf[None] + zs[None]) * dh * tile_mask(frames, inner)
        dz_ref[pl.ds(p, BIG)] = dz
        return carry[0] + down(dz), carry[1] + down(dz * ((z - zc[None]) * zr[None]))

    a, b = sweep(table_ref, size, BIG, body, (jnp.zeros((8, inner), F32),) * 2)
    oslopes_ref[0:1, 0:inner], oslopes_ref[1:2, 0:inner] = flat(a), flat(b)
    halo = first_ref.shape[0]
    first_ref[:, :, 0:inner], last_ref[:, :, 0:inner] = dz_ref[0:halo], dz_ref[size - halo : size]
    if fold:
        wide_edge = inner + other_ref.shape[2]
        first_ref[:, :, inner:wide_edge], last_ref[:, :, inner:wide_edge] = other_ref[0:halo], other_ref[size - halo : size]
        first_ref[:, :, wide_edge:], last_ref[:, :, wide_edge:] = z_ref[0:halo], z_ref[size - halo : size]
    else:
        oslopes_ref[:, inner:] = other_ref[...]


def bypass_back_kernel(table_ref, n_ref, up_ref, y_ref, sums_ref, gains_ref, slopes_ref, w_ref, wl_ref, dy_ref, dx_ref, dl_ref):
    size, width = y_ref.shape[0], y_ref.shape[2]
    factor, shift, center, inv_std = scale_of(sums_ref[:, width : 2 * width], gains_ref[...], n_ref[0])
    k0, k1 = slope_of(slopes_ref[:, width : 2 * width], factor, center, inv_std, n_ref[0])
    norm_back_fill(table_ref, up_ref, y_ref, dy_ref, factor, k0, k1)

    def body(p, carry):
        dy = rows_bf(dy_ref[pl.ds(p, BIG)])
        dx_ref[pl.ds(p, BIG)] = cells(nt(dy, w_ref[...])).astype(BF16)
        dl_ref[pl.ds(p, BIG)] = cells(nt(dy, wl_ref[...]))
        return carry

    steps(size, BIG, body, 0)


def conv_back_kernel(halo, row_len, per_clip, fold, offsets, table_ref, n_ref, ysums_ref, ygains_ref, slopes_ref, ylo_ref, y_ref, yhi_ref,
                     dlo_ref, d_ref, dhi_ref, w_ref, z_ref, zsums_ref, zgains_ref, *refs):
    dy_ref, dz_ref, oslopes_ref, pad_ref = refs[-4:]
    size, width = y_ref.shape[0], y_ref.shape[2]
    fix = folded if fold else (lambda v: v)
    inv_n = n_ref[1 if fold else 0]
    at_y, at_s, at_z, at_yhalo, at_dhalo = offsets
    factor, shift, center, inv_std = scale_of(fix(ysums_ref[:, at_y : at_y + width]), ygains_ref[...], inv_n)
    k0, k1 = slope_of(fix(slopes_ref[:, at_s : at_s + width]), factor, center, inv_std, inv_n)

    def value(refs, p, step):
        y_of, d_of = refs
        if y_of is y_ref:
            y, d = y_of[pl.ds(p, step)], d_of[pl.ds(p, step)]
        else:
            y, d = y_of[pl.ds(p, step), :, at_yhalo : at_yhalo + width], d_of[pl.ds(p, step), :, at_dhalo : at_dhalo + width]
        return (d * factor[None] - (k0[None] + k1[None] * y)).astype(BF16).astype(F32)

    fill_padded(table_ref, ((ylo_ref, dlo_ref), (y_ref, d_ref), (yhi_ref, dhi_ref)), 0, pad_ref, value, halo, size)

    def copy(p, carry):
        dy_ref[pl.ds(p, SMALL)] = pad_ref[1, pl.ds(halo + p, SMALL)].astype(BF16)
        return carry

    steps(size, SMALL, copy, 0)
    zf, zs, zc, zr = scale_of(fix(zsums_ref[:, at_z : at_z + width]), zgains_ref[...], inv_n)

    def body(p, frames, carry):
        dh = conv_rows(table_ref, per_clip, pad_ref, lambda i, j: w_ref[8 - 3 * i - j], p, halo, row_len, nt if fold else nn)
        z = z_ref[pl.ds(p, BIG)]
        dz = gelu_slope(z * zf[None] + zs[None]) * dh * tile_mask(frames, width)
        dz_ref[pl.ds(p, BIG)] = dz
        return carry[0] + down(dz), carry[1] + down(dz * ((z - zc[None]) * zr[None]))

    a, b = sweep(table_ref, size, BIG, body, (jnp.zeros((8, width), F32),) * 2)
    oslopes_ref[0:1, 0:width], oslopes_ref[1:2, 0:width] = flat(a), flat(b)
    if not fold:
        oslopes_ref[:, width:] = refs[0][...]


def slow_back_kernel(table_ref, n_ref, dz_ref, y_ref, sums_ref, gains_ref, slopes_ref, w_ref, wl_ref, dx_ref, dl_ref,
                     lp_ref, lsums_ref, lgains_ref, taps_ref, out_ref, dzl_ref, oslopes_ref):
    size = y_ref.shape[0]
    factor, shift, center, inv_std = scale_of(sums_ref[:, 0:256], gains_ref[...], n_ref[0])
    k0, k1 = slope_of(slopes_ref[:, 0:256], factor, center, inv_std, n_ref[0])

    def fill(p, frames, carry):
        dy = dz_ref[pl.ds(p, SMALL)] * factor[None]
        dy = dy - tile_mask(frames, 256) * (k0[None] + k1[None] * y_ref[pl.ds(p, SMALL)])
        taps_ref[pl.ds(p, SMALL), :, 0:256] = sooner(dy).astype(BF16)
        taps_ref[pl.ds(p, SMALL), :, 256:512] = dy.astype(BF16)
        taps_ref[pl.ds(p, SMALL), :, 512:768] = later(dy).astype(BF16)
        return carry

    sweep(table_ref, size, SMALL, fill)
    lf, ls, lc, lr = scale_of(lsums_ref[:, 128:384], lgains_ref[...], n_ref[0])

    def body(p, frames, carry):
        taps = rows_bf(taps_ref[pl.ds(p, BIG)])
        mask = tile_mask(frames, 256)
        for z in range(4):
            lanes = slice(256 * z, 256 * z + 256)
            dx = cells(nn(taps, w_ref[:, lanes])) + dx_ref[pl.ds(p, BIG), :, lanes].astype(F32)
            out_ref[z, pl.ds(p, BIG)] = (dx * mask).astype(BF16)
        dl = cells(nn(taps, wl_ref[...])) + dl_ref[pl.ds(p, BIG)]
        y = lp_ref[pl.ds(p, BIG)]
        dz = gelu_slope(y * lf[None] + ls[None]) * dl * mask
        dzl_ref[pl.ds(p, BIG)] = dz
        return carry[0] + down(dz), carry[1] + down(dz * ((y - lc[None]) * lr[None]))

    a, b = sweep(table_ref, size, BIG, body, (jnp.zeros((8, 256), F32),) * 2)
    oslopes_ref[0:1], oslopes_ref[1:2] = flat(a), flat(b)


def fast_back_kernel(at_s, table_ref, n_ref, sums_ref, fgains_ref, lgains_ref, fslopes_ref, lslopes_ref, dzf_ref, fa_ref, dzl_ref, lp_ref,
                     up_ref, w_ref, taps_ref, out_ref):
    size = fa_ref.shape[0]
    ff, fs, fc, fr = scale_of(folded(sums_ref[:, 0:128]), fgains_ref[...], n_ref[1])
    f0, f1 = slope_of(folded(fslopes_ref[:, at_s : at_s + 128]), ff, fc, fr, n_ref[1])
    lf, ls, lc, lr = scale_of(sums_ref[:, 128:384], lgains_ref[...], n_ref[0])
    l0, l1 = slope_of(lslopes_ref[...], lf, lc, lr, n_ref[0])

    def fill(p, frames, carry):
        dy = dzf_ref[pl.ds(p, SMALL)] * ff[None]
        dy = dy - tile_mask(frames, 128) * (f0[None] + f1[None] * fa_ref[pl.ds(p, SMALL)])
        taps_ref[pl.ds(p, SMALL), :, 0:128] = dy.astype(BF16)
        taps_ref[pl.ds(p, SMALL), :, 128:256] = sooner(dy).astype(BF16)
        taps_ref[pl.ds(p, SMALL), :, 256:384] = later(dy).astype(BF16)
        dy = dzl_ref[pl.ds(p, SMALL)] * lf[None]
        dy = dy - tile_mask(frames, 256) * (l0[None] + l1[None] * lp_ref[pl.ds(p, SMALL)])
        taps_ref[pl.ds(p, SMALL), :, 384:640] = dy.astype(BF16)
        taps_ref[pl.ds(p, SMALL), :, 640:896] = sooner(dy).astype(BF16)
        return carry

    sweep(table_ref, size, SMALL, fill)

    def body(p, frames, carry):
        dx = cells(nn(rows_bf(taps_ref[pl.ds(p, BIG)]), w_ref[...]))
        mask = tile_mask(frames, 128)
        for z in range(4):
            lanes = slice(128 * z, 128 * z + 128)
            out_ref[z, pl.ds(p, BIG)] = ((dx[:, :, lanes] + up_ref[pl.ds(p, BIG), :, lanes].astype(F32)) * mask).astype(BF16)
        return carry

    sweep(table_ref, size, BIG, body)


def tn(a, b):
    return lax.dot_general(a, b, (((0,), (0,)), ((), ())), preferred_element_type=F32)


def chunks(size):
    return range(0, size, BIG)


def added(acc_ref, at, part, first):
    acc_ref[at] = part if first else acc_ref[at] + part


def conv_weight(halo, row_len, per_clip, fold, table_ref, act_ref, dy_ref, pad_ref, acc_ref):
    size = dy_ref.shape[0]
    phase = table_ref[5] * (size // SMALL)

    def copy(p, carry):
        v = act_ref[pl.ds(p, 3)].astype(F32)
        for k in range(3):
            pad_ref[k, pl.ds(p, 3)] = v
        return carry

    steps(size + 2 * halo, 3, copy, 0)
    parts = size // SMALL

    def clear(i, carry):
        even = ((phase + i) % 2 == 0).astype(F32)
        at = halo + (i - 2) * SMALL
        pad_ref[0, pl.ds(at + SMALL - 1, 1)] = pad_ref[0, pl.ds(at + SMALL - 1, 1)] * even
        pad_ref[2, pl.ds(at, 1)] = pad_ref[2, pl.ds(at, 1)] * (1.0 - even)
        return carry

    lax.fori_loop(0, parts + 4, clear, 0)
    low_even = ((phase + 1) % 2 == 0).astype(F32)
    pad_ref[0, 0:1] = pad_ref[0, 0:1] * low_even
    high_even = ((phase + parts) % 2 == 0).astype(F32)
    end = size + 2 * halo
    pad_ref[2, end - 1 : end] = pad_ref[2, end - 1 : end] * (1.0 - high_even)

    for p in chunks(size):
        top, bottom = edge_scales(table_ref, p, per_clip)
        dy = rows_bf(dy_ref[p : p + BIG])
        for i in range(3):
            begin = p + halo + row_len * (i - 1)
            taps = []
            for j in range(3):
                v = pad_ref[j, begin + j - 1 : begin + j - 1 + BIG]
                if i == 0:
                    v = jnp.concatenate([v[0:row_len] * top, v[row_len:]], axis=0)
                if i == 2:
                    v = jnp.concatenate([v[: BIG - row_len], v[BIG - row_len :] * bottom], axis=0)
                taps.append(rows(v).astype(BF16))
            taps = jnp.concatenate(taps, axis=1)
            added(acc_ref, i, tn(taps, dy) if fold else tn(dy, taps), p == 0)


def by_share(v):
    return v.reshape(4, 4, 2, 8, v.shape[1]).transpose(2, 1, 0, 3, 4).astype(BF16)


def first_slab_kernel(hb_ref, dsc_ref, x_ref, lat_ref, dsp_ref, out_ref, acc_ref):
    for p in chunks(hb_ref.shape[0]):
        at = slice(p, p + BIG)
        dsc, dsp = rows_bf(dsc_ref[at]), rows_bf(dsp_ref[at])
        added(acc_ref, 4, tn(rows_bf(hb_ref[at]), dsc), p == 0)
        added(acc_ref, 5, tn(rows_bf(lat_ref[at]), dsp), p == 0)
        for z in range(4):
            added(acc_ref, z, tn(rows_bf(x_ref[at, :, 256 * z : 256 * z + 256]), dsp), p == 0)
    out_ref[:, :, :, 0], out_ref[:, :, :, 5] = by_share(acc_ref[4]), by_share(acc_ref[5])
    for z in range(4):
        part = acc_ref[z].reshape(4, 2, 4, 8, 1024).astype(BF16)
        for core in range(2):
            out_ref[core, :, z, 1:5] = part[:, core]


def second_slab_kernel(halo, row_len, per_clip, table_ref, act_ref, dy_ref, taps_ref, x_ref, lat_ref, out_ref, pad_ref, acc_ref, red_ref,
                       lred_ref):
    conv_weight(halo, row_len, per_clip, False, table_ref, act_ref, dy_ref, pad_ref, acc_ref)
    for k in range(9):
        at, lane = (3, 768) if k == 8 else (4 + k // 4, 256 * (k % 4))
        out_ref[:, :, :, at, :, lane : lane + 256] = by_share(acc_ref[k // 3, :, 256 * (k % 3) : 256 * (k % 3) + 256])
    for p in chunks(dy_ref.shape[0]):
        at = slice(p, p + BIG)
        x, lat = rows_bf(x_ref[at]), rows_bf(lat_ref[at])
        for j in range(3):
            taps = rows_bf(taps_ref[at, :, 256 * j : 256 * j + 256])
            added(red_ref, j, tn(taps, x), p == 0)
            added(lred_ref, j, tn(taps, lat), p == 0)
    for j in range(3):
        out_ref[:, :, :, j] = by_share(red_ref[j])
        out_ref[:, :, :, 3, :, 256 * j : 256 * j + 256] = by_share(lred_ref[j])


def fast_grads_kernel(halo, row_len, per_clip, table_ref, act_ref, dy_ref, taps_ref, fx_ref, h_ref, dfc_ref, lat_ref, out_ref,
                      pad_ref, sp_ref, first_ref, ex_ref):
    conv_weight(halo, row_len, per_clip, True, table_ref, act_ref, dy_ref, pad_ref, sp_ref)
    for p in chunks(dy_ref.shape[0]):
        at = slice(p, p + BIG)
        added(first_ref, slice(0, 896), tn(rows_bf(taps_ref[at]), rows_bf(fx_ref[at])), p == 0)
        added(ex_ref, slice(0, 128), tn(rows_bf(h_ref[at]), rows_bf(dfc_ref[at])), p == 0)

    def gather(at, count, r, ref=first_ref):
        return sum(lane_group(moved(ref[at : at + count, 128 * z : 128 * z + 128], 32 * z - 32 * r), z) for z in range(4))

    taps = [gather(640, 256, 2), gather(640, 256, 3), gather(384, 256, 0), gather(384, 256, 1), gather(384, 256, 2)]
    for j in range(5):
        lat_ref[:, 8 * j : 8 * j + 8] = taps[j].reshape(4, 8, 8, 128).astype(BF16)

    def tiles(first, v):
        for i in range(v.shape[0] // 8):
            out_ref[first + i] = v[8 * i : 8 * i + 8].astype(BF16)

    for j in range(3):
        total = sum(gather(32 * q, 32, q + j - 1) for q in range(4) if 0 <= q + j - 1 < 4)
        if j == 0:
            total = total + gather(128, 32, 3)
        if j == 2:
            total = total + gather(352, 32, 0)
        tiles(4 * j, total)
    tiles(12, sum(gather(32 * r, 32, r, ex_ref) for r in range(4)))
    for i in range(3):
        total = None
        for j in range(3):
            tap = sum(
                lane_group(moved(sp_ref[i, 128 * j + 32 * r : 128 * j + 32 * r + 32, :], 32 * j - 32 * r), j) for r in range(4)
            )
            total = tap if total is None else total + tap
        tiles(16 + 4 * i, total)


def swap(tree, axis, size, distance):
    pairs = [(i, i ^ distance) for i in range(size)]
    return jax.tree.map(lambda v: lax.ppermute(v, axis, pairs), tree)


def add(*trees):
    def total(*vs):
        wide_vs = [v.astype(F32) for v in vs]
        out = wide_vs[0] + wide_vs[1]
        if len(vs) == 4:
            out = out + (wide_vs[2] + wide_vs[3])
        return out.astype(vs[0].dtype)

    return jax.tree.map(total, *trees)


def stages(size, first_alone):
    bits = [1 << i for i in range(size.bit_length() - 1)]
    out = []
    if first_alone and bits:
        out.append(bits[:1])
        bits = bits[1:]
    while bits:
        out.append(bits[:2])
        bits = bits[2:]
    return out


def butterfly(tree, axis, size, bits):
    if len(bits) == 1:
        return add(tree, swap(tree, axis, size, bits[0]))
    near, far, both = (swap(tree, axis, size, k) for k in (bits[0], bits[1], bits[0] + bits[1]))
    return add(tree, near, far, both)


def over_dp(tree, sizes, early=None):
    for i, bits in enumerate(stages(sizes["dp"], True)):
        if i == 1 and early is not None:
            tree = after(tree, early)
        tree = butterfly(tree, "dp", sizes["dp"], bits)
    return tree


def over_chan(tree, sizes, bulk=None):
    if bulk is not None:
        tree = after(tree, bulk)
    for bits in stages(sizes["chan"], False):
        tree = butterfly(tree, "chan", sizes["chan"], bits)
    return tree


def everywhere(tree, sizes, bulk=None, early=None):
    return over_chan(over_dp(tree, sizes, early), sizes, bulk)


def halos(first, last, count):
    low = lax.ppermute(last, "chan", [(i, i + 1) for i in range(count - 1)])
    high = lax.ppermute(first, "chan", [(i + 1, i) for i in range(count - 1)])
    return low, high


def gather_group(v, sizes):
    dp = sizes["dp"]
    own = [v] + [swap(v, "dp", dp, 2 * k) for k in (1, 2, 3)]
    return jnp.stack(own), jnp.stack([swap(u, "dp", dp, 1) for u in own])


def pick(v, index, axis):
    return lax.dynamic_index_in_dim(v, index, axis, keepdims=False)


def scatter_group(tree, sizes, group):
    dp = sizes["dp"]
    core, chip = group % 2, group // 2
    sent = jax.tree.map(lambda v: pick(v, 1 - core, 0), tree)
    kept = jax.tree.map(lambda v: pick(v, core, 0), tree)
    tree = add(kept, swap(sent, "dp", dp, 1))
    got = [swap(jax.tree.map(lambda v: pick(v, chip ^ k, 0), tree), "dp", dp, 2 * k) for k in (1, 2, 3)]
    return add(jax.tree.map(lambda v: pick(v, chip, 0), tree), *got)


def scatter_chan(tree, sizes, chan):
    size, dp = sizes["chan"], sizes["dp"]
    got = [swap(jax.tree.map(lambda v: pick(v, chan ^ k, 0), tree), "chan", size, k) for k in (1, 2, 3)]
    tree = add(jax.tree.map(lambda v: pick(v, chan, 0), tree), *got)
    bits = [1 << i for i in range(3, dp.bit_length() - 1)]
    while bits:
        tree = butterfly(tree, "dp", dp, bits[:2])
        bits = bits[2:]
    return tree


def after(tree, gate):
    return lax.optimization_barrier((tree, gate))[0]


def local(
    sizes,
    slow_input,
    fast_input,
    clip_counts,
    frame_counts,
    fast_reduce,
    fast_spatial,
    fast_expand,
    lateral_kernel,
    slow_reduce,
    lateral_reduce,
    slow_spatial,
    slow_expand,
    shortcut,
    lateral_shortcut,
    fast_inner_norm,
    fast_outer_norm,
    lateral_norm,
    slow_inner_norm,
    slow_outer_norm,
    slow_cotangent,
    fast_cotangent,
):
    ways = sizes["chan"]
    clips, slow_t, height, across, slow_part = slow_input.shape
    fast_t, fast_part = fast_input.shape[1], fast_input.shape[4]
    ratio = fast_t // slow_t
    area = height * across
    places = clips * area
    mine = places // ways
    halo = across + 1
    chan, dp = lax.axis_index("chan"), lax.axis_index("dp")
    group = dp % 8
    ids = jnp.stack([dp, chan, group]).astype(jnp.int32)
    wide_in = ways * slow_part
    wide_f = ways * 128
    mid = 256
    ext = mine + 2 * halo
    per_clip = area // BIG
    chunk = 98

    def packed(v, slow=None):
        v = v.transpose(0, 2, 3, 1, 4).reshape(places, fast_t, fast_part)
        more = [] if slow is None else [slow.reshape(places, slow_t, slow_part)]
        width = 128 if slow is None else 128 + slow_part
        return pl.pallas_call(
            functools.partial(pack_kernel, area // chunk, clips),
            grid=(places // chunk,),
            out_shape=shape((places, slow_t, width), BF16),
            in_specs=[pl.BlockSpec(memory_space=pltpu.SMEM)] * 3
            + [pl.BlockSpec((chunk, *u.shape[1:]), lambda i: (i, 0, 0)) for u in (v, *more)],
            out_specs=pl.BlockSpec((chunk, slow_t, width), lambda i: (i, 0, 0)),
            scratch_shapes=[pltpu.VMEM((chunk * fast_t, fast_part), F32)],
            compiler_params=pltpu.CompilerParams(vmem_limit_bytes=16 * 1024 * 1024),
            name="fast_pack",
        )(ids, clip_counts, frame_counts, v, *more).reshape(ways, mine, slow_t, width)

    def unpacked(parts):
        slow, fast = call(
            unpack_kernel,
            [shape((places, slow_t, slow_part), BF16), shape((places, fast_t, fast_part), BF16)],
            [ids, *parts],
            [pltpu.VMEM((BIG * fast_t, fast_part), F32)],
            smem=1,
            name="outputs",
        )
        return joined(slow), fast.reshape(clips, height, across, fast_t, fast_part).transpose(0, 3, 1, 2, 4)

    def split(v):
        return v.transpose(0, 2, 3, 1, 4).reshape(ways, mine, slow_t, slow_part)

    def joined(v):
        return v.reshape(clips, height, across, slow_t, slow_part).transpose(0, 3, 1, 2, 4)

    def at_once(v):
        return [v[0]] + [swap(v[k], "chan", ways, k) for k in range(1, ways)]

    def blocks_of(v):
        return [pick(v, chan ^ k, 0) for k in range(ways)]

    def all_to_all(v):
        return lax.all_to_all(v, "chan", 0, 0, tiled=True)

    def parted(blocks):
        bounds = PARTS + ((len(blocks), 0),)
        ends = [b[1] if a[0] == b[0] else mine for a, b in zip(bounds, bounds[1:])]
        return [blocks[k][begin:end] for (k, begin), end in zip(PARTS, ends)]

    def send_parts(parts, which, gate):
        for i in which:
            parts[i] = swap(after(parts[i], gate), "chan", ways, PARTS[i][0])


    all_clips = frame_counts.shape[0]
    live = (jnp.arange(all_clips, dtype=jnp.int32) % clips) < jnp.repeat(clip_counts, clips)
    valid = jnp.where(live, frame_counts, 0)
    count = jnp.sum(valid).astype(F32) * area
    inv_n = jnp.stack([1.0 / count, 1.0 / (count * ratio)])
    parts = mine // BIG
    clip = (chan * parts + jnp.arange(-1, parts + 1)) // per_clip
    clip = jnp.clip(clip, 0, clips - 1) + dp * clips
    around = jnp.sum(jnp.where(clip[:, None] == jnp.arange(all_clips)[None, :], valid[None, :], 0), axis=1)
    table = jnp.concatenate([around, jnp.stack([chan, jnp.full_like(chan, parts)])]).astype(jnp.int32)

    lat_t, red_t, lred_t = (v.transpose(0, 2, 1) for v in (lateral_kernel, slow_reduce, lateral_reduce))
    spatial_t = slow_spatial.reshape(9, slow_spatial.shape[2], -1).transpose(0, 2, 1)
    params = [red_t, lred_t, lat_t, slow_expand, shortcut, lateral_shortcut, spatial_t]
    scratch = [(3, 8, wide_in), (3, 8, mid), (5, 8, 128), (8, wide_in), (32, wide_in), (8, wide_in), (9, 8, mid)]
    small = [lateral_norm, slow_inner_norm.reshape(4, -1), slow_outer_norm.reshape(4, -1)]
    any_spec, vmem_spec = pl.BlockSpec(memory_space=pl.ANY), pl.BlockSpec(memory_space=pltpu.VMEM)
    slab = pl.pallas_call(
        weight_slab_kernel,
        out_shape=shape((14, 8, wide_in), BF16),
        in_specs=[pl.BlockSpec(memory_space=pltpu.SMEM)] + [any_spec] * 7 + [vmem_spec] * 3,
        out_specs=vmem_spec,
        scratch_shapes=[pltpu.VMEM(dims, F32) for dims in scratch] + [pltpu.SemaphoreType.DMA((7,))],
        compiler_params=pltpu.CompilerParams(vmem_limit_bytes=58 * 1024 * 1024),
        name="weight_slab",
    )(ids, *params, *small)
    slabs = at_once([slab] * ways)
    fx_pieces = at_once(blocks_of(packed(after(fast_input, slab))))
    xs = all_to_all(after(split(slow_input), (slabs, fx_pieces)))
    early, late = jnp.stack([v[0:5] for v in slabs]), jnp.stack([v[5:14] for v in slabs])
    own_slabs, other_slabs = gather_group(early, sizes)
    fr_t = fast_reduce.transpose(0, 2, 1)
    red_w, lred_w, w_first, w_fsp, w_fex, fin_g, fout_g, mid_g, out_g = call(
        weights_kernel,
        [
            shape((3, ways, 8, 8, wide_in), BF16),
            shape((3, ways, 8, 8, mid), BF16),
            shape((896, wide_f), BF16),
            shape((9, 128, 128), BF16),
            shape((128, wide_f), BF16),
            shape((4, 128)),
            shape((2, wide_f)),
            shape((8, mid)),
            shape((ways, 4, mid)),
        ],
        [ids, own_slabs, other_slabs, fr_t, fast_spatial.reshape(9, *fast_spatial.shape[2:]), fast_expand,
         fast_inner_norm.reshape(4, -1), fast_outer_norm],
        [pltpu.VMEM((5, ways, 8, 8, 128), F32)],
        smem=1,
        name="weights",
    )
    red_w, lred_w = red_w.reshape(-1, wide_in), lred_w.reshape(-1, mid)
    fin_g = (fin_g[0:2], fin_g[2:4])
    lat_g, in_g = mid_g[0:2], (mid_g[2:4], mid_g[4:6])
    out_g = out_g.transpose(1, 0, 2).reshape(4, wide_in)

    edge = [shape((halo, 8, 128))] * 2
    edges = [shape((halo, 8, 512))] * 2
    narrow, middle = shape((mine, 8, 128)), shape((mine, 8, mid))
    fx, fa, lp, sums1, first, last = call(
        fast_first_kernel,
        [shape((mine, 8, wide_f), BF16), narrow, middle, shape((2, 384)), *edge],
        [table, *fx_pieces, w_first],
        smem=1,
        name="fast_first",
    )
    fa_lo, fa_hi = halos(first, last, ways)
    cots = parted(blocks_of(packed(fast_cotangent, split(slow_cotangent))))
    sums1 = over_dp(sums1, sizes)
    own_late, other_late = gather_group(after(late, sums1), sizes)
    exp_w, short_w, lshort_w, spat_w = call(
        more_weights_kernel,
        [
            shape((ways, 8, 8, wide_in), BF16),
            shape((ways, 8, 4, 8, wide_in), BF16),
            shape((ways, 8, 8, wide_in), BF16),
            shape((9, ways, 8, 8, mid), BF16),
        ],
        [ids, own_late, other_late],
        smem=1,
        name="more_weights",
    )
    exp_w, short_w, lshort_w = (v.reshape(-1, wide_in) for v in (exp_w, short_w, lshort_w))
    spat_w = spat_w.reshape(9, mid, mid)
    sums1 = over_chan(sums1, sizes, (xs, fa_lo, fa_hi, cots))
    send_parts(cots, (2,), sums1)
    fast_pad = [pltpu.VMEM((3, ext, 8, 128), F32)]
    slow_pad = [pltpu.VMEM((3, ext, 8, mid), F32)]
    x, lat, sa, sums2, first, last = call(
        slow_first_kernel,
        [shape((mine, 8, wide_in), BF16), shape((mine, 8, mid), BF16), middle, shape((2, mid)), *[shape((halo, 8, mid))] * 2],
        [table, inv_n, xs, lp, sums1, lat_g, red_w, lred_w],
        smem=2,
        name="slow_first",
    )
    sa_lo, sa_hi = halos(first, last, ways)
    fa_late = after(fa, sums2)
    h1, fb, fb_sums = call(
        functools.partial(conv_kernel, halo, across, per_clip, True, (0, 0)),
        [shape((ext, 8, 128), BF16), narrow, shape((2, 128))],
        [table, inv_n, sums1, fin_g[0], fa_lo, fa_late, fa_hi, w_fsp],
        fast_pad,
        smem=2,
        name="fast_second",
    )
    sums2 = everywhere(sums2, sizes, (cots[2], sa_lo, sa_hi))
    send_parts(cots, (3, 4, 1), sums2)
    ha, sb, sums3 = call(
        functools.partial(conv_kernel, halo, across, per_clip, False, (0, 0)),
        [shape((ext, 8, mid), BF16), middle, shape((2, mid + 128))],
        [table, inv_n, sums2, in_g[0], sa_lo, sa, sa_hi, spat_w, fb_sums],
        slow_pad,
        smem=2,
        name="slow_second",
    )
    sums3 = everywhere(sums3, sizes, (cots[3], cots[4], cots[1]))
    send_parts(cots, (5,), sums3)
    sp, sp_sums = call(
        bypass_kernel,
        [shape((mine, 8, wide_in), BF16), shape((2, wide_in))],
        [table, x, lat, short_w, lshort_w],
        smem=1,
        name="bypass",
    )
    h2, fc, fc_sums = call(
        functools.partial(expand_kernel, True, mid),
        [shape((mine, 8, 128), BF16), shape((mine, 8, wide_f), BF16), shape((2, wide_f))],
        [table, inv_n, fb, sums3, fin_g[1], w_fex],
        smem=2,
        name="fast_third",
    )
    hb, sc, sums4 = call(
        functools.partial(expand_kernel, False, 0),
        [shape((mine, 8, mid), BF16), shape((mine, 8, wide_in), BF16), shape((2, 2 * wide_in + wide_f))],
        [table, inv_n, sb, sums3, in_g[1], exp_w, sp_sums, fc_sums],
        smem=2,
        name="slow_third",
    )
    sums4 = everywhere(sums4, sizes, cots[5])
    fast_out, dfs, fc_slopes = call(
        functools.partial(fast_out_kernel, 2 * wide_in),
        [shape((ways, mine, 8, 128), BF16), shape((mine, 8, wide_f), BF16), shape((2, wide_f))],
        [table, inv_n, fc, sums4, fout_g, fx, *cots],
        [pltpu.VMEM((8, wide_f), F32)],
        smem=2,
        name="fast_out",
    )
    *outs, dss, sums5 = call(
        slow_out_kernel,
        [*[shape(c.shape, BF16) for c in cots], shape((mine, 8, wide_in), BF16), shape((2, 2 * wide_in + wide_f))],
        [table, inv_n, sc, sp, sums4, out_g, *cots, fast_out, fc_slopes],
        [pltpu.VMEM((8, wide_in), F32)],
        smem=2,
        name="slow_out",
    )

    send_parts(outs, (2,), dss)
    sums5 = everywhere(sums5, sizes, outs[2])
    send_parts(outs, (3, 4, 1), sums5)
    dfc, dzfb, fb_slopes, first, last = call(
        functools.partial(expand_back_kernel, True, (2 * wide_in, 2 * wide_in, mid)),
        [shape((mine, 8, wide_f), BF16), narrow, shape((2, 128)), *edges],
        [table, inv_n, dfs, fc, sums4, fout_g, sums5, fb, sums3, fin_g[1], w_fex, sb],
        smem=2,
        name="fast_third_back",
    )
    low6, high6 = halos(first, last, ways)
    dsc, dzsb, sums6, first, last = call(
        functools.partial(expand_back_kernel, False, (0, 0, 0)),
        [shape((mine, 8, wide_in), BF16), middle, shape((2, mid + 128)), *[shape((halo, 8, mid))] * 2],
        [table, inv_n, dss, sc, sums4, out_g[0:2], sums5, sb, sums3, in_g[1], exp_w, fb_slopes],
        smem=2,
        name="slow_third_back",
    )
    low_sb, high_sb = halos(first, last, ways)
    dss_late, = after((dss,), sums6)
    dsp, dx, dl = call(
        bypass_back_kernel,
        [shape((mine, 8, wide_in), BF16), shape((mine, 8, wide_in), BF16), middle],
        [table, inv_n, dss_late, sp, sums4, out_g[2:4], sums5, short_w, lshort_w],
        smem=2,
        name="bypass_back",
    )

    sums6 = everywhere(sums6, sizes, (low6, high6, low_sb, high_sb), (outs[3], outs[4], outs[1]))
    send_parts(outs, (5,), sums6)
    dfb, dzfa, fa_slopes = call(
        functools.partial(conv_back_kernel, halo, across, per_clip, True, (mid, mid, 0, 384, 0)),
        [shape((mine, 8, 128), BF16), narrow, shape((2, 128))],
        [table, inv_n, sums3, fin_g[1], sums6, low6, fb, high6, low6, dzfb, high6, w_fsp, fa, sums1, fin_g[0]],
        fast_pad,
        smem=2,
        name="fast_second_back",
    )
    dsb, dzsa, sums7 = call(
        functools.partial(conv_back_kernel, halo, across, per_clip, False, (0, 0, 0, 128, 0)),
        [shape((mine, 8, mid), BF16), middle, shape((2, mid + 128))],
        [table, inv_n, sums3, in_g[1], sums6, low6, sb, high6, low_sb, dzsb, high_sb, spat_w, sa, sums2, in_g[0], fa_slopes],
        slow_pad,
        smem=2,
        name="slow_second_back",
    )
    dsc_late, dsp = after((dsc, dsp), sums7)
    (slab1,) = call(
        first_slab_kernel,
        [shape((2, 4, ways, 6, 8, wide_in), BF16)],
        [hb, dsc_late, x, lat, dsp],
        [pltpu.VMEM((6, mid, wide_in), F32)],
        name="first_slab",
    )
    sums7 = everywhere(sums7, sizes, (outs[5], dx, dl))
    dsa, dslow, dzlp, sums8 = call(
        slow_back_kernel,
        [shape((mine, 8, 3 * mid), BF16), shape((ways, mine, 8, mid), BF16), middle, shape((2, mid))],
        [table, inv_n, dzsa, sa, sums2, in_g[0], sums7, red_w, lred_w, dx, dl, lp, sums1, lat_g],
        smem=2,
        name="slow_first_back",
    )
    sums8 = over_dp(sums8, sizes)
    dslow = all_to_all(dslow)
    dsa, dsb_late = after((dsa, dsb), sums8)
    (slab2,) = call(
        functools.partial(second_slab_kernel, halo, across, per_clip),
        [shape((2, 4, ways, 6, 8, wide_in), BF16)],
        [table, ha, dsb_late, dsa, x, lat],
        [*slow_pad, pltpu.VMEM((3, mid, 3 * mid), F32), pltpu.VMEM((3, mid, wide_in), F32), pltpu.VMEM((3, mid, mid), F32)],
        smem=1,
        name="second_slab",
    )
    slabs = jnp.concatenate(scatter_group((slab1, slab2), sizes, group), axis=1)
    sums8 = over_chan(sums8, sizes, (dslow, slabs))
    dfirst, dfast = call(
        functools.partial(fast_back_kernel, mid),
        [shape((mine, 8, 896), BF16), shape((ways, mine, 8, 128), BF16)],
        [table, inv_n, sums1, fin_g[0], lat_g, sums7, sums8, dzfa, fa, dzlp, lp, dfs, w_first],
        smem=2,
        name="fast_first_back",
    )

    g_lat, g_fast = call(
        functools.partial(fast_grads_kernel, halo, across, per_clip),
        [shape((ways, 40, 8, 128), BF16), shape((28, 8, 128), BF16)],
        [table, h1, dfb, dfirst, fx, h2, dfc],
        [*fast_pad, pltpu.VMEM((3, 384, 128), F32), pltpu.VMEM((896, wide_f), F32), pltpu.VMEM((128, wide_f), F32)],
        smem=1,
        name="fast_grads",
    )
    slow_output, fast_output = unpacked(after(outs, dfirst))
    slabs = scatter_chan(slabs, sizes, chan)
    small = [jnp.concatenate([pick(g_lat, chan ^ k, 0), g_fast]) for k in range(ways)]
    small = add(*at_once(small))
    dfast = all_to_all(dfast)
    for bits in stages(sizes["dp"], True):
        small = butterfly(small, "dp", sizes["dp"], bits)
    g_lat, g_fast = small[0:40].astype(F32), small[40:68].astype(F32)
    own_slabs, other_slabs = gather_group(slabs, sizes)
    g_exp, g_short, g_lshort, g_red, g_lred, g_spat = call(
        grads_kernel,
        [shape((8, 8, wide_in)), shape((8, 4, 8, wide_in)), shape((8, 8, wide_in)), shape((3, 8, 8, wide_in)), shape((3, 8, 8, mid)),
         shape((9, 8, 8, mid))],
        [ids, own_slabs, other_slabs],
        smem=1,
        name="grads",
    )
    slow_input_grad = joined(dslow)
    fast_input_grad = pl.pallas_call(
        unpack_fast_kernel,
        grid=(places // chunk,),
        out_shape=shape((places, fast_t, fast_part), BF16),
        in_specs=[pl.BlockSpec((chunk, slow_t, 128), lambda i: (i, 0, 0))],
        out_specs=pl.BlockSpec((chunk, fast_t, fast_part), lambda i: (i, 0, 0)),
        scratch_shapes=[pltpu.VMEM((chunk * fast_t, fast_part), F32)],
        compiler_params=pltpu.CompilerParams(vmem_limit_bytes=16 * 1024 * 1024),
        name="fast_unpack",
    )(dfast.reshape(places, slow_t, 128))
    fast_input_grad = fast_input_grad.reshape(clips, height, across, fast_t, fast_part).transpose(0, 3, 1, 2, 4)
    g_fred = g_fast[0:12].reshape(3, 32, 128).transpose(0, 2, 1)
    g_fex = g_fast[12:16].reshape(32, 128)
    g_fsp = g_fast[16:28].reshape(3, 32, 128)[:, :, 0:96].reshape(3, 32, 3, 32).transpose(0, 2, 1, 3)

    def pair(slopes):
        return slopes[::-1]

    def own(v, width):
        return lax.dynamic_slice_in_dim(v, chan * width, width, v.ndim - 1)

    def fold_in(slopes):
        return jnp.sum(slopes.reshape(2, ratio, 128 // ratio), axis=1)

    lw, sw, ow = lateral_norm.shape[1], slow_inner_norm.shape[2], slow_outer_norm.shape[2]
    fast_inner_grad = jnp.stack([pair(fold_in(sums7[:, mid:])), pair(fold_in(sums6[:, mid:]))])
    fc_slopes = sums5[:, 2 * wide_in :].reshape(2, ways, ratio, fast_part)
    fast_outer_grad = pair(jnp.sum(fc_slopes, axis=2).reshape(2, -1))
    lateral_grad = pair(own(sums8, lw))
    slow_inner_grad = own(jnp.stack([pair(sums7[:, 0:mid]), pair(sums6[:, 0:mid])]), sw)
    slow_outer_grad = own(jnp.stack([pair(sums5[:, 0:wide_in]), pair(sums5[:, wide_in : 2 * wide_in])]), ow)
    return (
        slow_output,
        fast_output,
        slow_input_grad,
        fast_input_grad,
        g_fred,
        g_fsp,
        g_fex,
        g_lat.reshape(5, -1, 128).transpose(0, 2, 1),
        g_red.reshape(3, -1, wide_in).transpose(0, 2, 1),
        g_lred.reshape(3, -1, mid).transpose(0, 2, 1),
        g_spat.reshape(9, -1, mid).transpose(0, 2, 1).reshape(slow_spatial.shape),
        g_exp.reshape(-1, wide_in),
        g_short.reshape(-1, wide_in),
        g_lshort.reshape(-1, wide_in),
        fast_inner_grad,
        fast_outer_grad,
        lateral_grad,
        slow_inner_grad,
        slow_outer_grad,
    )


def solution(mesh):
    sizes = {"dp": mesh.shape["dp"], "chan": mesh.shape["chan"]}
    big = P("dp", None, None, None, "chan")
    last2, last3, last4 = P(None, "chan"), P(None, None, "chan"), P(None, None, None, "chan")
    first = P("chan", None)
    return jax.shard_map(
        functools.partial(local, sizes),
        mesh=mesh,
        in_specs=(
            big, big, P(), P(), P(), P(), P(), last3, last3, last3, last4, first, first, first,
            P(), P(), last2, last3, last3, big, big,
        ),
        out_specs=(
            big, big, big, big, P(), P(), P(), last3, last3, last3, last4, first, first, first,
            P(), P(), last2, last3, last3,
        ),
        check_vma=False,
    )
```

```python
import functools

import jax
import jax.numpy as jnp
from jax import lax
from jax.experimental import pallas as pl
from jax.experimental.pallas import tpu as pltpu
from jax.sharding import PartitionSpec as P

F32 = jnp.float32
BF16 = jnp.bfloat16
EPSILON = 1e-05
ROOT = 0.7978845608028654
CUBIC = 0.044715
BIG = 49
PARTS = ((0, 0), (1, 0), (2, 0), (2, 98), (3, 0), (3, 49))
SMALL = 7


def gelu(v):
    return 0.5 * v * (1.0 + jnp.tanh(ROOT * (v * (1.0 + CUBIC * (v * v)))))


def gelu_slope(v):
    square = v * v
    th = jnp.tanh(ROOT * (v * (1.0 + CUBIC * square)))
    half = 0.5 * (1.0 + th)
    return half + (0.5 * ROOT) * v * (1.0 - th * th) * (1.0 + 3.0 * CUBIC * square)


def gelu_pair(v):
    square = v * v
    th = jnp.tanh(ROOT * (v * (1.0 + CUBIC * square)))
    half = 0.5 * (1.0 + th)
    slope = half + (0.5 * ROOT) * v * (1.0 - th * th) * (1.0 + 3.0 * CUBIC * square)
    return v * half, slope


def rows(v):
    return v.reshape(v.shape[0] * v.shape[1], v.shape[2])


def cells(v):
    return v.reshape(v.shape[0] // 8, 8, v.shape[1])


def rows_bf(v):
    return rows(v.astype(F32)).astype(BF16)


def wide(mask, width):
    repeats = width // 128
    return mask if repeats == 1 else jnp.concatenate([mask] * repeats, axis=-1)


def nn(a, b):
    return jnp.dot(a, b, preferred_element_type=F32)


def nt(a, b):
    return lax.dot_general(a, b, (((1,), (1,)), ((), ())), preferred_element_type=F32)


def later(v):
    rolled = pltpu.roll(v, 1, 1)
    return jnp.where(lax.broadcasted_iota(jnp.int32, v.shape, 1) == 0, 0.0, rolled)


def sooner(v):
    rolled = pltpu.roll(v, 7, 1)
    return jnp.where(lax.broadcasted_iota(jnp.int32, v.shape, 1) == 7, 0.0, rolled)


def folded(v):
    out = []
    for block in range(v.shape[-1] // 128):
        part = v[:, 128 * block : 128 * block + 128]
        part = part + pltpu.roll(part, 64, 1)
        out.append(part + pltpu.roll(part, 32, 1))
    return out[0] if len(out) == 1 else jnp.concatenate(out, axis=-1)


def scale_of(sums, gains, inv_n):
    center = sums[0:1] * inv_n
    spread = sums[1:2] * inv_n - center * center
    inv_std = lax.rsqrt(spread + EPSILON)
    factor = gains[0:1] * inv_std
    return factor, gains[1:2] - center * factor, center, inv_std


def slope_of(slopes, factor, center, inv_std, inv_n):
    k1 = factor * slopes[1:2] * inv_n * inv_std
    k0 = factor * slopes[0:1] * inv_n - k1 * center
    return k0, k1


def down(v):
    return jnp.sum(v, axis=0)


def flat(v):
    return jnp.sum(v, axis=0, keepdims=True)


def steps(count, step, body, carry):
    return lax.fori_loop(0, count // step, lambda i, c: body(i * step, c), carry)


def call(kernel, outs, args, scratch=(), smem=0, flops=0, name=None):
    specs = [pl.BlockSpec(memory_space=pltpu.SMEM if i < smem else pltpu.VMEM) for i in range(len(args))]
    total = sum(a.size * a.dtype.itemsize for a in args)
    total += sum(o.size * o.dtype.itemsize for o in outs)
    def padded(v):
        dims = list(v.shape)
        if len(dims) < 2:
            return 4096
        dims[-1] = -(-dims[-1] // 128) * 128
        dims[-2] = -(-dims[-2] // 8) * 8
        amount = v.dtype.itemsize
        for d in dims:
            amount *= d
        return amount

    room = sum(padded(v) for v in (*args, *outs, *scratch)) + 6 * 1024 * 1024
    return pl.pallas_call(
        kernel,
        out_shape=tuple(outs),
        in_specs=specs,
        out_specs=tuple(pl.BlockSpec(memory_space=pltpu.VMEM) for _ in outs),
        scratch_shapes=list(scratch),
        compiler_params=pltpu.CompilerParams(vmem_limit_bytes=room),
        cost_estimate=pl.CostEstimate(flops=flops, bytes_accessed=1, transcendentals=0),
        name=name,
    )(*args)


def shape(dims, dtype=F32):
    return jax.ShapeDtypeStruct(dims, dtype)


def tile_mask(frames, width):
    tile = (lax.broadcasted_iota(jnp.int32, (8, 128), 0) < frames).astype(F32)
    return wide(tile, width)[None]


def sweep(table_ref, size, step, body, carry=0, begin=0):
    def run(i, kept):
        p = i * step
        return body(p, table_ref[1 + (begin + p) // BIG], kept)

    return lax.fori_loop(0, size // step, run, carry)


def lane_group(v, group):
    return jnp.where(lax.broadcasted_iota(jnp.int32, v.shape, v.ndim - 1) // 32 == group, v, 0.0)


def moved(v, shift):
    shift = shift % 128
    return v if shift == 0 else pltpu.roll(v, shift, v.ndim - 1)


def pack_kernel(per_clip, clips, ids_ref, counts_ref, frames_ref, x_ref, *refs):
    out_ref, tmp_ref = refs[-2:]
    clip, dp = pl.program_id(0) // per_clip, ids_ref[0]
    chunk = x_ref.shape[0]
    frames = jnp.where(clip < counts_ref[dp], frames_ref[dp * clips + clip], 0)
    tmp_ref[...] = x_ref[...].astype(F32).reshape(chunk * 32, 32)
    parts = [tmp_ref[pl.ds(r, chunk * 8, stride=4), :] for r in range(4)]
    out_ref[:, :, 0:128] = (cells(jnp.concatenate(parts, axis=1)) * tile_mask(frames, 128)).astype(BF16)
    if len(refs) == 3:
        out_ref[:, :, 128:384] = refs[0][...]


def unpack_kernel(ids_ref, *refs):
    slow_ref, fast_ref, tmp_ref = refs[-3:]
    size = refs[0].shape[0]
    for (k, first), ref in zip(PARTS, refs):
        begin = (ids_ref[1] ^ k) * size + first

        def body(p, carry, ref=ref, begin=begin):
            joined = rows(ref[pl.ds(p, BIG), :, 0:128].astype(F32))
            for r in range(4):
                tmp_ref[pl.ds(r, BIG * 8, stride=4), :] = joined[:, 32 * r : 32 * r + 32]
            fast_ref[pl.ds(begin + p, BIG)] = tmp_ref[...].reshape(BIG, 32, 32).astype(BF16)
            slow_ref[pl.ds(begin + p, BIG)] = ref[pl.ds(p, BIG), :, 128:384]
            return carry

        steps(ref.shape[0], BIG, body, 0)


def unpack_fast_kernel(x_ref, out_ref, tmp_ref):
    chunk = x_ref.shape[0]
    joined = rows(x_ref[...].astype(F32))
    for r in range(4):
        tmp_ref[pl.ds(r, chunk * 8, stride=4), :] = joined[:, 32 * r : 32 * r + 32]
    out_ref[...] = tmp_ref[...].reshape(chunk, 32, 32).astype(BF16)


def copy_kernel(x_ref, out_ref):
    def body(p, carry):
        out_ref[pl.ds(p, SMALL)] = x_ref[pl.ds(p, SMALL)]
        return carry

    steps(x_ref.shape[0], SMALL, body, 0)


def lanes_at(block, width):
    return pl.ds(pl.multiple_of(block * width, width), width)


LREDUCE = [(3, 256 * k) for k in range(3)]
LATERAL = [(4, 128 * k) for k in range(5)]
GAINS = [(3, 768), (3, 896), (4, 640), (4, 768)]
SPATIAL = [(11 + k // 4, 256 * (k % 4)) for k in range(9)]


def weight_slab_kernel(ids_ref, red_ref, lred_ref, lat_ref, exp_ref, short_ref, lshort_ref, sp_ref, ln_ref, sn_ref, on_ref, out_ref,
                       red_s, lred_s, lat_s, exp_s, short_s, lshort_s, sp_s, sem):
    group = ids_ref[2]
    eight, more = pl.ds(pl.multiple_of(group * 8, 8), 8), pl.ds(pl.multiple_of(group * 32, 32), 32)
    copies = []
    for i, (src, dst) in enumerate((
        (red_ref.at[:, eight], red_s), (lred_ref.at[:, eight], lred_s), (lat_ref.at[:, eight], lat_s), (exp_ref.at[eight], exp_s),
        (short_ref.at[more], short_s), (lshort_ref.at[eight], lshort_s), (sp_ref.at[:, eight], sp_s),
    )):
        copies.append(pltpu.make_async_copy(src, dst, sem.at[i]))
    for copy in copies:
        copy.start()
    out_ref[4, :, 896:1024] = jnp.zeros((8, 128), BF16)
    out_ref[13, :, 256:1024] = jnp.zeros((8, 768), BF16)
    blank = jnp.zeros((2, 128), F32)
    half = jnp.zeros((2, 64), F32)
    inner = jnp.concatenate([jnp.concatenate([v, half], axis=1) for v in (ln_ref[...], sn_ref[0:2], sn_ref[2:4])] + [blank], axis=0)
    outer = jnp.concatenate([on_ref[:, 0:128], on_ref[:, 128:256]], axis=0)
    for i, v in enumerate((inner, outer)):
        high = v.astype(BF16)
        for k, part in ((i, high), (2 + i, (v - high.astype(F32)).astype(BF16))):
            at, lane = GAINS[k]
            out_ref[at, :, lane : lane + 128] = part
    for copy in copies:
        copy.wait()
    for j in range(3):
        out_ref[j] = red_s[j].astype(BF16)
        at, lane = LREDUCE[j]
        out_ref[at, :, lane : lane + 256] = lred_s[j].astype(BF16)
    out_ref[5], out_ref[10] = exp_s[...].astype(BF16), lshort_s[...].astype(BF16)
    for a in range(4):
        out_ref[6 + a] = short_s[8 * a : 8 * a + 8].astype(BF16)
    for k in range(9):
        at, lane = SPATIAL[k]
        out_ref[at, :, lane : lane + 256] = sp_s[k].astype(BF16)
    for k in range(5):
        at, lane = LATERAL[k]
        out_ref[at, :, lane : lane + 128] = lat_s[k].astype(BF16)


def more_weights_kernel(ids_ref, own_ref, other_ref, exp_ref, short_ref, lshort_ref, sp_ref):
    me, group = ids_ref[1], ids_ref[2]

    def place(i, carry):
        chip, kz = i // 4, i % 4
        z = me ^ kz
        for core, ref in ((0, own_ref), (1, other_ref)):
            d = group ^ (2 * chip + core)
            exp_ref[z, d], lshort_ref[z, d] = ref[chip, kz, 0], ref[chip, kz, 5]
            for a in range(4):
                short_ref[z, d, a] = ref[chip, kz, 1 + a]
            for k in range(9):
                at, lane = SPATIAL[k]
                sp_ref[k, z, d] = ref[chip, kz, at - 5, :, lane : lane + 256]
        return carry

    lax.fori_loop(0, 16, place, 0)


def weights_kernel(ids_ref, own_ref, other_ref, fr_ref, fsp_ref, fex_ref, fin_ref, fout_ref, red_ref, lred_ref, first_ref, wsp_ref, wex_ref,
                   gin_ref, gout_ref, gmid_ref, gwide_ref, lat_ref):
    me, group = ids_ref[1], ids_ref[2]

    def place(i, carry):
        chip, kz = i // 4, i % 4
        z = me ^ kz
        for core, ref in ((0, own_ref), (1, other_ref)):
            d = group ^ (2 * chip + core)
            for j in range(3):
                red_ref[j, z, d] = ref[chip, kz, j]
                at, lane = LREDUCE[j]
                lred_ref[j, z, d] = ref[chip, kz, at, :, lane : lane + 256]
            for k in range(5):
                at, lane = LATERAL[k]
                lat_ref[k, z, d] = ref[chip, kz, at, :, lane : lane + 128].astype(F32)
        return carry

    lax.fori_loop(0, 16, place, 0)

    mids = [jnp.zeros((8, 128), F32) for _ in range(2)]
    for kz in range(4):
        z = me ^ kz
        parts = [own_ref[0, kz, at, :, lane : lane + 128].astype(F32) for at, lane in GAINS]
        inner, outer = parts[0] + parts[2], parts[1] + parts[3]
        for half in range(2):
            for block in range(2):
                here = (z == 2 * block + half).astype(F32)
                mids[block] = mids[block] + moved(inner, 64 * half) * here
        gwide_ref[z, :, 0:128], gwide_ref[z, :, 128:256] = outer[0:4], outer[4:8]
    gmid_ref[:, 0:128], gmid_ref[:, 128:256] = mids[0], mids[1]

    first_ref[...] = jnp.zeros_like(first_ref)
    wsp_ref[...] = jnp.zeros_like(wsp_ref)
    for z in range(4):
        lanes = slice(128 * z, 128 * z + 128)

        def put(v, r, z=z):
            return lane_group(moved(v, 32 * r - 32 * z), r)

        for q in range(4):
            total = sum(put(fr_ref[r - q + 1], r) for r in range(4) if abs(r - q) <= 1)
            first_ref[32 * q : 32 * q + 32, lanes] = total.astype(BF16)
        first_ref[128:160, lanes] = put(fr_ref[0], 3).astype(BF16)
        first_ref[352:384, lanes] = put(fr_ref[2], 0).astype(BF16)
        taps = [lat_ref[j].reshape(256, 128) for j in range(5)]
        first_ref[384:640, lanes] = sum(put(taps[2 + r], r) for r in range(3)).astype(BF16)
        first_ref[640:896, lanes] = (put(taps[0], 2) + put(taps[1], 3)).astype(BF16)
        for r in range(4):
            wex_ref[32 * r : 32 * r + 32, lanes] = put(fex_ref[...], r).astype(BF16)
        gout_ref[:, lanes] = sum(put(fout_ref[...], r) for r in range(4))
    blank = jnp.zeros((32, 96), F32)
    for k in range(9):
        tap = jnp.concatenate([fsp_ref[k], blank], axis=1)
        for r in range(4):
            wsp_ref[k, 32 * r : 32 * r + 32, :] = moved(tap, 32 * r).astype(BF16)
    gin_ref[...] = jnp.concatenate([fin_ref[...]] * 4, axis=1)


def grads_kernel(ids_ref, own_ref, other_ref, exp_ref, short_ref, lshort_ref, red_ref, lred_ref, sp_ref):
    def place(chip, carry):
        for core, ref in ((0, own_ref), (1, other_ref)):
            d = ids_ref[2] ^ (2 * chip + core)
            exp_ref[d], lshort_ref[d] = ref[chip, 0].astype(F32), ref[chip, 5].astype(F32)
            for a in range(4):
                short_ref[d, a] = ref[chip, 1 + a].astype(F32)
            for j in range(3):
                red_ref[j, d] = ref[chip, 6 + j].astype(F32)
                lred_ref[j, d] = ref[chip, 9, :, 256 * j : 256 * j + 256].astype(F32)
            for k in range(8):
                sp_ref[k, d] = ref[chip, 10 + k // 4, :, 256 * (k % 4) : 256 * (k % 4) + 256].astype(F32)
            sp_ref[8, d] = ref[chip, 9, :, 768:1024].astype(F32)
        return carry

    lax.fori_loop(0, 4, place, 0)


def fast_first_kernel(table_ref, f0_ref, f1_ref, f2_ref, f3_ref, w_ref, fx_ref, fa_ref, lp_ref, sums_ref, first_ref, last_ref):
    size = fa_ref.shape[0]

    def fill(p, carry):
        for k, ref in enumerate((f0_ref, f1_ref, f2_ref, f3_ref)):
            fx_ref[pl.ds(p, SMALL), :, lanes_at(table_ref[5] ^ k, 128)] = ref[pl.ds(p, SMALL)]
        return carry

    steps(size, SMALL, fill, 0)

    def body(p, frames, carry):
        acc = cells(nt(rows_bf(fx_ref[pl.ds(p, BIG)]), w_ref[...]))
        fa = acc[:, :, 0:128] + later(acc[:, :, 128:256]) + sooner(acc[:, :, 256:384])
        lp = acc[:, :, 384:640] + later(acc[:, :, 640:896])
        fa_ref[pl.ds(p, BIG)] = fa
        lp_ref[pl.ds(p, BIG)] = lp
        fm, lm = fa * tile_mask(frames, 128), lp * tile_mask(frames, 256)
        return tuple(c + down(v) for c, v in zip(carry, (fm, fm * fa, lm, lm * lp)))

    zero = (jnp.zeros((8, 128), F32),) * 2 + (jnp.zeros((8, 256), F32),) * 2
    a, b, c, d = sweep(table_ref, size, BIG, body, zero)
    sums_ref[0:1, 0:128], sums_ref[1:2, 0:128] = flat(a), flat(b)
    sums_ref[0:1, 128:384], sums_ref[1:2, 128:384] = flat(c), flat(d)
    halo = first_ref.shape[0]
    first_ref[...], last_ref[...] = fa_ref[0:halo], fa_ref[size - halo : size]


def fill_padded(table_ref, refs, offset, out_ref, value, halo, size):
    low, middle, high = refs
    phase = table_ref[5] * (size // SMALL)

    def put(v, at, part, count, step=SMALL):
        even = ((phase + part + 2 * count) % 2 == 0).astype(F32)
        out_ref[1, pl.ds(at, step)] = v
        if step == 1:
            out_ref[0, pl.ds(at, 1)] = v * even
            out_ref[2, pl.ds(at, 1)] = v * (1.0 - even)
            return
        out_ref[0, pl.ds(at, step)] = v
        out_ref[2, pl.ds(at, step)] = v
        out_ref[0, pl.ds(at + step - 1, 1)] = v[step - 1 : step] * even
        out_ref[2, pl.ds(at, 1)] = v[0:1] * (1.0 - even)

    width = out_ref.shape[-1]
    lo_mask, hi_mask = tile_mask(table_ref[0], width), tile_mask(table_ref[4], width)
    put(value(low, 0, 1) * lo_mask, 0, -3, 4, 1)
    put(value(low, 1, SMALL) * lo_mask, 1, -2, 4)
    put(value(low, 1 + SMALL, SMALL) * lo_mask, 1 + SMALL, -1, 4)
    parts = size // SMALL
    put(value(high, 0, SMALL) * hi_mask, halo + size, parts, 0)
    put(value(high, SMALL, SMALL) * hi_mask, halo + size + SMALL, parts + 1, 0)
    put(value(high, 2 * SMALL, 1) * hi_mask, halo + size + 2 * SMALL, parts + 2, 0, 1)

    def body(p, frames, carry):
        put(value(middle, p, SMALL) * tile_mask(frames, width), halo + p, p // SMALL, 0)
        return carry

    sweep(table_ref, size, SMALL, body)


def edge_scales(table_ref, p, per_clip):
    part = table_ref[5] * table_ref[6] + p // BIG
    return (part % per_clip != 0).astype(F32), ((part + 1) % per_clip != 0).astype(F32)


def conv_rows(table_ref, per_clip, pad_ref, weight, p, halo, row_len, dot):
    top, bottom = edge_scales(table_ref, p, per_clip)
    total = None
    for i in (1, 0, 2):
        begin = p + halo + row_len * (i - 1)
        acc = None
        for j in range(3):
            tap = rows(pad_ref[j, pl.ds(begin + j - 1, BIG)]).astype(BF16)
            part = dot(tap, weight(i, j))
            acc = part if acc is None else acc + part
        acc = cells(acc)
        if i == 0:
            acc = jnp.concatenate([acc[0:row_len] * top, acc[row_len:]], axis=0)
        if i == 2:
            acc = jnp.concatenate([acc[: BIG - row_len], acc[BIG - row_len :] * bottom], axis=0)
        total = acc if total is None else total + acc
    return total


def conv_kernel(halo, row_len, per_clip, fold, offsets, table_ref, n_ref, sums_ref, gains_ref, lo_ref, y_ref, hi_ref, w_ref, *refs):
    if fold:
        act_ref, out_ref, osums_ref, pad_ref = refs
    else:
        more_ref, act_ref, out_ref, osums_ref, pad_ref = refs
    size, width = y_ref.shape[0], y_ref.shape[2]
    sums = sums_ref[:, offsets[0] : offsets[0] + width]
    sums = folded(sums) if fold else sums
    factor, shift, _, _ = scale_of(sums, gains_ref[...], n_ref[1 if fold else 0])
    lanes = slice(offsets[1], offsets[1] + width)

    def value(ref, p, step):
        y = ref[pl.ds(p, step)] if ref is y_ref else ref[pl.ds(p, step), :, lanes]
        return gelu(y * factor[None] + shift[None]).astype(BF16).astype(F32)

    fill_padded(table_ref, (lo_ref, y_ref, hi_ref), 0, pad_ref, value, halo, size)

    def copy(p, carry):
        act_ref[pl.ds(p, 3)] = pad_ref[1, pl.ds(p, 3)].astype(BF16)
        return carry

    steps(size + 2 * halo, 3, copy, 0)

    def body(p, frames, carry):
        total = conv_rows(table_ref, per_clip, pad_ref, lambda i, j: w_ref[3 * i + j], p, halo, row_len, nn if fold else nt)
        out_ref[pl.ds(p, BIG)] = total
        masked = total * tile_mask(frames, width)
        return carry[0] + down(masked), carry[1] + down(masked * total)

    a, b = sweep(table_ref, size, BIG, body, (jnp.zeros((8, width), F32),) * 2)
    osums_ref[0:1, 0:width], osums_ref[1:2, 0:width] = flat(a), flat(b)
    if not fold:
        osums_ref[:, width:] = more_ref[...]


def slow_first_kernel(table_ref, n_ref, xs_ref, lp_ref, lsums_ref, gains_ref, w_ref, wl_ref,
                      x_ref, lat_ref, sa_ref, sums_ref, first_ref, last_ref):
    size = lp_ref.shape[0]
    factor, shift, _, _ = scale_of(lsums_ref[:, 128:384], gains_ref[...], n_ref[0])

    def fill(p, frames, carry):
        mask = tile_mask(frames, 256)
        lat_ref[pl.ds(p, SMALL)] = (gelu(lp_ref[pl.ds(p, SMALL)] * factor[None] + shift[None]) * mask).astype(BF16)
        for z in range(4):
            v = xs_ref[z, pl.ds(p, SMALL)].astype(F32) * mask
            x_ref[pl.ds(p, SMALL), :, 256 * z : 256 * z + 256] = v.astype(BF16)
        return carry

    sweep(table_ref, size, SMALL, fill)

    def body(p, frames, carry):
        acc = nt(rows_bf(x_ref[pl.ds(p, BIG)]), w_ref[...]) + nt(rows_bf(lat_ref[pl.ds(p, BIG)]), wl_ref[...])
        acc = cells(acc)
        sa = later(acc[:, :, 0:256]) + acc[:, :, 256:512] + sooner(acc[:, :, 512:768])
        sa_ref[pl.ds(p, BIG)] = sa
        masked = sa * tile_mask(frames, 256)
        return carry[0] + down(masked), carry[1] + down(masked * sa)

    a, b = sweep(table_ref, size, BIG, body, (jnp.zeros((8, 256), F32),) * 2)
    sums_ref[0:1], sums_ref[1:2] = flat(a), flat(b)
    halo = first_ref.shape[0]
    first_ref[...], last_ref[...] = sa_ref[0:halo], sa_ref[size - halo : size]


def bypass_kernel(table_ref, x_ref, lat_ref, w_ref, wl_ref, sp_ref, sums_ref):
    def body(p, frames, carry):
        sp = cells(nn(rows_bf(x_ref[pl.ds(p, BIG)]), w_ref[...]) + nn(rows_bf(lat_ref[pl.ds(p, BIG)]), wl_ref[...]))
        sp_ref[pl.ds(p, BIG)] = sp.astype(BF16)
        masked = sp * tile_mask(frames, sp.shape[-1])
        return carry[0] + down(masked), carry[1] + down(masked * sp)

    a, b = sweep(table_ref, sp_ref.shape[0], BIG, body, (jnp.zeros((8, sp_ref.shape[2]), F32),) * 2)
    sums_ref[0:1], sums_ref[1:2] = flat(a), flat(b)


def expand_kernel(fold, offset, table_ref, n_ref, y_ref, sums_ref, gains_ref, w_ref, *refs):
    more, (h_ref, out_ref, osums_ref) = refs[:-3], refs[-3:]
    size, width = y_ref.shape[0], y_ref.shape[2]
    sums = sums_ref[:, offset : offset + width]
    sums = folded(sums) if fold else sums
    factor, shift, _, _ = scale_of(sums, gains_ref[...], n_ref[1 if fold else 0])

    def fill(p, frames, carry):
        v = gelu(y_ref[pl.ds(p, SMALL)] * factor[None] + shift[None])
        h_ref[pl.ds(p, SMALL)] = (v * tile_mask(frames, width)).astype(BF16)
        return carry

    sweep(table_ref, size, SMALL, fill)

    def body(p, frames, carry):
        out = cells(nn(rows_bf(h_ref[pl.ds(p, BIG)]), w_ref[...]))
        out_ref[pl.ds(p, BIG)] = out.astype(BF16)
        masked = out * tile_mask(frames, out.shape[-1])
        return carry[0] + down(masked), carry[1] + down(masked * out)

    wide_out = out_ref.shape[2]
    a, b = sweep(table_ref, size, BIG, body, (jnp.zeros((8, wide_out), F32),) * 2)
    osums_ref[0:1, 0:wide_out], osums_ref[1:2, 0:wide_out] = flat(a), flat(b)
    for ref in more:
        osums_ref[:, wide_out : wide_out + ref.shape[1]] = ref[...]
        wide_out += ref.shape[1]


def fast_out_kernel(offset, table_ref, n_ref, fc_ref, sums_ref, gains_ref, fx_ref, *refs):
    cots, (out_ref, up_ref, slopes_ref, vec_ref) = refs[: len(PARTS)], refs[len(PARTS) :]
    width = fc_ref.shape[2]
    vecs = scale_of(folded(sums_ref[:, offset : offset + width]), gains_ref[...], n_ref[1])
    for i, v in enumerate(vecs):
        vec_ref[i : i + 1] = v
    kept = (jnp.zeros((8, 128), F32),) * 2
    for part, ((k, begin), cot_ref) in enumerate(zip(PARTS, cots)):
        lanes = lanes_at(table_ref[5] ^ k, 128)
        fz, sz, cz, rz = (vec_ref[i : i + 1, lanes][None] for i in range(4))

        def body(p, frames, carry, k=k, lanes=lanes, fz=fz, sz=sz, cz=cz, rz=rz, cot_ref=cot_ref, begin=begin):
            here = pl.ds(begin + p, SMALL)
            y = fc_ref[here, :, lanes].astype(F32)
            mask = tile_mask(frames, 128)
            total = y * fz + sz + fx_ref[here, :, lanes].astype(F32)
            value, slope = gelu_pair(total)
            out_ref[k, here] = (value * mask).astype(BF16)
            up = slope * (cot_ref[pl.ds(p, SMALL), :, 0:128].astype(F32) * mask)
            up_ref[here, :, lanes] = up.astype(BF16)
            return carry[0] + down(up), carry[1] + down(up * ((y - cz) * rz))

        zero = (jnp.zeros((8, 128), F32),) * 2
        kept = sweep(table_ref, cot_ref.shape[0], SMALL, body, kept if begin else zero, begin)
        slopes_ref[0:1, lanes], slopes_ref[1:2, lanes] = flat(kept[0]), flat(kept[1])


def slow_out_kernel(table_ref, n_ref, sc_ref, sp_ref, sums_ref, gains_ref, *refs):
    count = len(PARTS)
    cots, (fast_ref, more_ref), outs = refs[:count], refs[count : count + 2], refs[count + 2 : 2 * count + 2]
    up_ref, slopes_ref, vec_ref = refs[2 * count + 2 :]
    width = sc_ref.shape[2]
    cf, cs, cc, cr = scale_of(sums_ref[:, 0:width], gains_ref[0:2], n_ref[0])
    pf, ps, pc, pr = scale_of(sums_ref[:, width : 2 * width], gains_ref[2:4], n_ref[0])
    for i, v in enumerate((cf, cs + ps, cc, cr, pf, pc, pr)):
        vec_ref[i : i + 1] = v
    kept = ()
    for (k, begin), cot_ref, out_ref in zip(PARTS, cots, outs):
        block = table_ref[5] ^ k
        lanes = lanes_at(block, 256)
        vecs = [vec_ref[i : i + 1, lanes][None] for i in range(7)]

        def body(p, frames, carry, k=k, lanes=lanes, vecs=vecs, cot_ref=cot_ref, out_ref=out_ref, begin=begin):
            cf, shift, cc, cr, pf, pc, pr = vecs
            here = pl.ds(begin + p, SMALL)
            yc, yp = (ref[here, :, lanes].astype(F32) for ref in (sc_ref, sp_ref))
            mask = tile_mask(frames, 256)
            value, slope = gelu_pair(yc * cf + yp * pf + shift)
            out_ref[pl.ds(p, SMALL), :, 128:384] = (value * mask).astype(BF16)
            out_ref[pl.ds(p, SMALL), :, 0:128] = fast_ref[k, here]
            up = slope * (cot_ref[pl.ds(p, SMALL), :, 128:384].astype(F32) * mask)
            up_ref[here, :, lanes] = up.astype(BF16)
            return (carry[0] + down(up), carry[1] + down(up * ((yc - cc) * cr)), carry[2] + down(up * ((yp - pc) * pr)))

        zero = (jnp.zeros((8, 256), F32),) * 3
        kept = sweep(table_ref, cot_ref.shape[0], SMALL, body, kept if begin else zero, begin)
        a, b, c = kept
        own, other = lanes, lanes_at(4 + block, 256)
        slopes_ref[0:1, own], slopes_ref[1:2, own] = flat(a), flat(b)
        slopes_ref[0:1, other], slopes_ref[1:2, other] = flat(a), flat(c)
    slopes_ref[:, 2 * width :] = more_ref[...]


def norm_back_fill(table_ref, up_ref, y_ref, dy_ref, factor, k0, k1):
    def fill(p, frames, carry):
        mask = tile_mask(frames, 128)
        for q in range(y_ref.shape[2] // 128):
            lanes = slice(128 * q, 128 * q + 128)
            y = y_ref[pl.ds(p, SMALL), :, lanes].astype(F32)
            dy = up_ref[pl.ds(p, SMALL), :, lanes].astype(F32) * factor[:, lanes][None]
            dy = dy - mask * (k0[:, lanes][None] + k1[:, lanes][None] * y)
            dy_ref[pl.ds(p, SMALL), :, lanes] = dy.astype(BF16)
        return carry

    sweep(table_ref, y_ref.shape[0], SMALL, fill)


def expand_back_kernel(fold, offsets, table_ref, n_ref, up_ref, y_ref, sums_ref, gains_ref, slopes_ref, z_ref, zsums_ref, zgains_ref,
                       w_ref, other_ref, dy_ref, dz_ref, oslopes_ref, first_ref, last_ref):
    size, width, inner = y_ref.shape[0], y_ref.shape[2], z_ref.shape[2]
    fix = folded if fold else (lambda v: v)
    inv_n = n_ref[1 if fold else 0]
    at_y, at_s, at_z = offsets
    factor, shift, center, inv_std = scale_of(fix(sums_ref[:, at_y : at_y + width]), gains_ref[...], inv_n)
    k0, k1 = slope_of(fix(slopes_ref[:, at_s : at_s + width]), factor, center, inv_std, inv_n)
    norm_back_fill(table_ref, up_ref, y_ref, dy_ref, factor, k0, k1)
    zf, zs, zc, zr = scale_of(fix(zsums_ref[:, at_z : at_z + inner]), zgains_ref[...], inv_n)

    def body(p, frames, carry):
        dh = cells(nt(rows_bf(dy_ref[pl.ds(p, BIG)]), w_ref[...]))
        z = z_ref[pl.ds(p, BIG)]
        dz = gelu_slope(z * zf[None] + zs[None]) * dh * tile_mask(frames, inner)
        dz_ref[pl.ds(p, BIG)] = dz
        return carry[0] + down(dz), carry[1] + down(dz * ((z - zc[None]) * zr[None]))

    a, b = sweep(table_ref, size, BIG, body, (jnp.zeros((8, inner), F32),) * 2)
    oslopes_ref[0:1, 0:inner], oslopes_ref[1:2, 0:inner] = flat(a), flat(b)
    halo = first_ref.shape[0]
    first_ref[:, :, 0:inner], last_ref[:, :, 0:inner] = dz_ref[0:halo], dz_ref[size - halo : size]
    if fold:
        wide_edge = inner + other_ref.shape[2]
        first_ref[:, :, inner:wide_edge], last_ref[:, :, inner:wide_edge] = other_ref[0:halo], other_ref[size - halo : size]
        first_ref[:, :, wide_edge:], last_ref[:, :, wide_edge:] = z_ref[0:halo], z_ref[size - halo : size]
    else:
        oslopes_ref[:, inner:] = other_ref[...]


def bypass_back_kernel(table_ref, n_ref, up_ref, y_ref, sums_ref, gains_ref, slopes_ref, w_ref, wl_ref, dy_ref, dx_ref, dl_ref):
    size, width = y_ref.shape[0], y_ref.shape[2]
    factor, shift, center, inv_std = scale_of(sums_ref[:, width : 2 * width], gains_ref[...], n_ref[0])
    k0, k1 = slope_of(slopes_ref[:, width : 2 * width], factor, center, inv_std, n_ref[0])
    norm_back_fill(table_ref, up_ref, y_ref, dy_ref, factor, k0, k1)

    def body(p, carry):
        dy = rows_bf(dy_ref[pl.ds(p, BIG)])
        dx_ref[pl.ds(p, BIG)] = cells(nt(dy, w_ref[...])).astype(BF16)
        dl_ref[pl.ds(p, BIG)] = cells(nt(dy, wl_ref[...]))
        return carry

    steps(size, BIG, body, 0)


def conv_back_kernel(halo, row_len, per_clip, fold, offsets, table_ref, n_ref, ysums_ref, ygains_ref, slopes_ref, ylo_ref, y_ref, yhi_ref,
                     dlo_ref, d_ref, dhi_ref, w_ref, z_ref, zsums_ref, zgains_ref, *refs):
    dy_ref, dz_ref, oslopes_ref, pad_ref = refs[-4:]
    size, width = y_ref.shape[0], y_ref.shape[2]
    fix = folded if fold else (lambda v: v)
    inv_n = n_ref[1 if fold else 0]
    at_y, at_s, at_z, at_yhalo, at_dhalo = offsets
    factor, shift, center, inv_std = scale_of(fix(ysums_ref[:, at_y : at_y + width]), ygains_ref[...], inv_n)
    k0, k1 = slope_of(fix(slopes_ref[:, at_s : at_s + width]), factor, center, inv_std, inv_n)

    def value(refs, p, step):
        y_of, d_of = refs
        if y_of is y_ref:
            y, d = y_of[pl.ds(p, step)], d_of[pl.ds(p, step)]
        else:
            y, d = y_of[pl.ds(p, step), :, at_yhalo : at_yhalo + width], d_of[pl.ds(p, step), :, at_dhalo : at_dhalo + width]
        return (d * factor[None] - (k0[None] + k1[None] * y)).astype(BF16).astype(F32)

    fill_padded(table_ref, ((ylo_ref, dlo_ref), (y_ref, d_ref), (yhi_ref, dhi_ref)), 0, pad_ref, value, halo, size)

    def copy(p, carry):
        dy_ref[pl.ds(p, SMALL)] = pad_ref[1, pl.ds(halo + p, SMALL)].astype(BF16)
        return carry

    steps(size, SMALL, copy, 0)
    zf, zs, zc, zr = scale_of(fix(zsums_ref[:, at_z : at_z + width]), zgains_ref[...], inv_n)

    def body(p, frames, carry):
        dh = conv_rows(table_ref, per_clip, pad_ref, lambda i, j: w_ref[8 - 3 * i - j], p, halo, row_len, nt if fold else nn)
        z = z_ref[pl.ds(p, BIG)]
        dz = gelu_slope(z * zf[None] + zs[None]) * dh * tile_mask(frames, width)
        dz_ref[pl.ds(p, BIG)] = dz
        return carry[0] + down(dz), carry[1] + down(dz * ((z - zc[None]) * zr[None]))

    a, b = sweep(table_ref, size, BIG, body, (jnp.zeros((8, width), F32),) * 2)
    oslopes_ref[0:1, 0:width], oslopes_ref[1:2, 0:width] = flat(a), flat(b)
    if not fold:
        oslopes_ref[:, width:] = refs[0][...]


def slow_back_kernel(table_ref, n_ref, dz_ref, y_ref, sums_ref, gains_ref, slopes_ref, w_ref, wl_ref, dx_ref, dl_ref,
                     lp_ref, lsums_ref, lgains_ref, taps_ref, out_ref, dzl_ref, oslopes_ref):
    size = y_ref.shape[0]
    factor, shift, center, inv_std = scale_of(sums_ref[:, 0:256], gains_ref[...], n_ref[0])
    k0, k1 = slope_of(slopes_ref[:, 0:256], factor, center, inv_std, n_ref[0])

    def fill(p, frames, carry):
        dy = dz_ref[pl.ds(p, SMALL)] * factor[None]
        dy = dy - tile_mask(frames, 256) * (k0[None] + k1[None] * y_ref[pl.ds(p, SMALL)])
        taps_ref[pl.ds(p, SMALL), :, 0:256] = sooner(dy).astype(BF16)
        taps_ref[pl.ds(p, SMALL), :, 256:512] = dy.astype(BF16)
        taps_ref[pl.ds(p, SMALL), :, 512:768] = later(dy).astype(BF16)
        return carry

    sweep(table_ref, size, SMALL, fill)
    lf, ls, lc, lr = scale_of(lsums_ref[:, 128:384], lgains_ref[...], n_ref[0])

    def body(p, frames, carry):
        taps = rows_bf(taps_ref[pl.ds(p, BIG)])
        mask = tile_mask(frames, 256)
        for z in range(4):
            lanes = slice(256 * z, 256 * z + 256)
            dx = cells(nn(taps, w_ref[:, lanes])) + dx_ref[pl.ds(p, BIG), :, lanes].astype(F32)
            out_ref[z, pl.ds(p, BIG)] = (dx * mask).astype(BF16)
        dl = cells(nn(taps, wl_ref[...])) + dl_ref[pl.ds(p, BIG)]
        y = lp_ref[pl.ds(p, BIG)]
        dz = gelu_slope(y * lf[None] + ls[None]) * dl * mask
        dzl_ref[pl.ds(p, BIG)] = dz
        return carry[0] + down(dz), carry[1] + down(dz * ((y - lc[None]) * lr[None]))

    a, b = sweep(table_ref, size, BIG, body, (jnp.zeros((8, 256), F32),) * 2)
    oslopes_ref[0:1], oslopes_ref[1:2] = flat(a), flat(b)


def fast_back_kernel(at_s, table_ref, n_ref, sums_ref, fgains_ref, lgains_ref, fslopes_ref, lslopes_ref, dzf_ref, fa_ref, dzl_ref, lp_ref,
                     up_ref, w_ref, taps_ref, out_ref):
    size = fa_ref.shape[0]
    ff, fs, fc, fr = scale_of(folded(sums_ref[:, 0:128]), fgains_ref[...], n_ref[1])
    f0, f1 = slope_of(folded(fslopes_ref[:, at_s : at_s + 128]), ff, fc, fr, n_ref[1])
    lf, ls, lc, lr = scale_of(sums_ref[:, 128:384], lgains_ref[...], n_ref[0])
    l0, l1 = slope_of(lslopes_ref[...], lf, lc, lr, n_ref[0])

    def fill(p, frames, carry):
        dy = dzf_ref[pl.ds(p, SMALL)] * ff[None]
        dy = dy - tile_mask(frames, 128) * (f0[None] + f1[None] * fa_ref[pl.ds(p, SMALL)])
        taps_ref[pl.ds(p, SMALL), :, 0:128] = dy.astype(BF16)
        taps_ref[pl.ds(p, SMALL), :, 128:256] = sooner(dy).astype(BF16)
        taps_ref[pl.ds(p, SMALL), :, 256:384] = later(dy).astype(BF16)
        dy = dzl_ref[pl.ds(p, SMALL)] * lf[None]
        dy = dy - tile_mask(frames, 256) * (l0[None] + l1[None] * lp_ref[pl.ds(p, SMALL)])
        taps_ref[pl.ds(p, SMALL), :, 384:640] = dy.astype(BF16)
        taps_ref[pl.ds(p, SMALL), :, 640:896] = sooner(dy).astype(BF16)
        return carry

    sweep(table_ref, size, SMALL, fill)

    def body(p, frames, carry):
        dx = cells(nn(rows_bf(taps_ref[pl.ds(p, BIG)]), w_ref[...]))
        mask = tile_mask(frames, 128)
        for z in range(4):
            lanes = slice(128 * z, 128 * z + 128)
            out_ref[z, pl.ds(p, BIG)] = ((dx[:, :, lanes] + up_ref[pl.ds(p, BIG), :, lanes].astype(F32)) * mask).astype(BF16)
        return carry

    sweep(table_ref, size, BIG, body)


def tn(a, b):
    return lax.dot_general(a, b, (((0,), (0,)), ((), ())), preferred_element_type=F32)


def chunks(size):
    return range(0, size, BIG)


def added(acc_ref, at, part, first):
    acc_ref[at] = part if first else acc_ref[at] + part


def conv_weight(halo, row_len, per_clip, fold, table_ref, act_ref, dy_ref, pad_ref, acc_ref):
    size = dy_ref.shape[0]
    phase = table_ref[5] * (size // SMALL)

    def copy(p, carry):
        v = act_ref[pl.ds(p, 3)].astype(F32)
        for k in range(3):
            pad_ref[k, pl.ds(p, 3)] = v
        return carry

    steps(size + 2 * halo, 3, copy, 0)
    parts = size // SMALL

    def clear(i, carry):
        even = ((phase + i) % 2 == 0).astype(F32)
        at = halo + (i - 2) * SMALL
        pad_ref[0, pl.ds(at + SMALL - 1, 1)] = pad_ref[0, pl.ds(at + SMALL - 1, 1)] * even
        pad_ref[2, pl.ds(at, 1)] = pad_ref[2, pl.ds(at, 1)] * (1.0 - even)
        return carry

    lax.fori_loop(0, parts + 4, clear, 0)
    low_even = ((phase + 1) % 2 == 0).astype(F32)
    pad_ref[0, 0:1] = pad_ref[0, 0:1] * low_even
    high_even = ((phase + parts) % 2 == 0).astype(F32)
    end = size + 2 * halo
    pad_ref[2, end - 1 : end] = pad_ref[2, end - 1 : end] * (1.0 - high_even)

    for p in chunks(size):
        top, bottom = edge_scales(table_ref, p, per_clip)
        dy = rows_bf(dy_ref[p : p + BIG])
        for i in range(3):
            begin = p + halo + row_len * (i - 1)
            taps = []
            for j in range(3):
                v = pad_ref[j, begin + j - 1 : begin + j - 1 + BIG]
                if i == 0:
                    v = jnp.concatenate([v[0:row_len] * top, v[row_len:]], axis=0)
                if i == 2:
                    v = jnp.concatenate([v[: BIG - row_len], v[BIG - row_len :] * bottom], axis=0)
                taps.append(rows(v).astype(BF16))
            taps = jnp.concatenate(taps, axis=1)
            added(acc_ref, i, tn(taps, dy) if fold else tn(dy, taps), p == 0)


def by_share(v):
    return v.reshape(4, 4, 2, 8, v.shape[1]).transpose(2, 1, 0, 3, 4).astype(BF16)


def first_slab_kernel(hb_ref, dsc_ref, x_ref, lat_ref, dsp_ref, out_ref, acc_ref):
    for p in chunks(hb_ref.shape[0]):
        at = slice(p, p + BIG)
        dsc, dsp = rows_bf(dsc_ref[at]), rows_bf(dsp_ref[at])
        added(acc_ref, 4, tn(rows_bf(hb_ref[at]), dsc), p == 0)
        added(acc_ref, 5, tn(rows_bf(lat_ref[at]), dsp), p == 0)
        for z in range(4):
            added(acc_ref, z, tn(rows_bf(x_ref[at, :, 256 * z : 256 * z + 256]), dsp), p == 0)
    out_ref[:, :, :, 0], out_ref[:, :, :, 5] = by_share(acc_ref[4]), by_share(acc_ref[5])
    for z in range(4):
        part = acc_ref[z].reshape(4, 2, 4, 8, 1024).astype(BF16)
        for core in range(2):
            out_ref[core, :, z, 1:5] = part[:, core]


def second_slab_kernel(halo, row_len, per_clip, table_ref, act_ref, dy_ref, taps_ref, x_ref, lat_ref, out_ref, pad_ref, acc_ref, red_ref,
                       lred_ref):
    conv_weight(halo, row_len, per_clip, False, table_ref, act_ref, dy_ref, pad_ref, acc_ref)
    for k in range(9):
        at, lane = (3, 768) if k == 8 else (4 + k // 4, 256 * (k % 4))
        out_ref[:, :, :, at, :, lane : lane + 256] = by_share(acc_ref[k // 3, :, 256 * (k % 3) : 256 * (k % 3) + 256])
    for p in chunks(dy_ref.shape[0]):
        at = slice(p, p + BIG)
        x, lat = rows_bf(x_ref[at]), rows_bf(lat_ref[at])
        for j in range(3):
            taps = rows_bf(taps_ref[at, :, 256 * j : 256 * j + 256])
            added(red_ref, j, tn(taps, x), p == 0)
            added(lred_ref, j, tn(taps, lat), p == 0)
    for j in range(3):
        out_ref[:, :, :, j] = by_share(red_ref[j])
        out_ref[:, :, :, 3, :, 256 * j : 256 * j + 256] = by_share(lred_ref[j])


def fast_grads_kernel(halo, row_len, per_clip, table_ref, act_ref, dy_ref, taps_ref, fx_ref, h_ref, dfc_ref, lat_ref, out_ref,
                      pad_ref, sp_ref, first_ref, ex_ref):
    conv_weight(halo, row_len, per_clip, True, table_ref, act_ref, dy_ref, pad_ref, sp_ref)
    for p in chunks(dy_ref.shape[0]):
        at = slice(p, p + BIG)
        added(first_ref, slice(0, 896), tn(rows_bf(taps_ref[at]), rows_bf(fx_ref[at])), p == 0)
        added(ex_ref, slice(0, 128), tn(rows_bf(h_ref[at]), rows_bf(dfc_ref[at])), p == 0)

    def gather(at, count, r, ref=first_ref):
        return sum(lane_group(moved(ref[at : at + count, 128 * z : 128 * z + 128], 32 * z - 32 * r), z) for z in range(4))

    taps = [gather(640, 256, 2), gather(640, 256, 3), gather(384, 256, 0), gather(384, 256, 1), gather(384, 256, 2)]
    for j in range(5):
        lat_ref[:, 8 * j : 8 * j + 8] = taps[j].reshape(4, 8, 8, 128).astype(BF16)

    def tiles(first, v):
        for i in range(v.shape[0] // 8):
            out_ref[first + i] = v[8 * i : 8 * i + 8].astype(BF16)

    for j in range(3):
        total = sum(gather(32 * q, 32, q + j - 1) for q in range(4) if 0 <= q + j - 1 < 4)
        if j == 0:
            total = total + gather(128, 32, 3)
        if j == 2:
            total = total + gather(352, 32, 0)
        tiles(4 * j, total)
    tiles(12, sum(gather(32 * r, 32, r, ex_ref) for r in range(4)))
    for i in range(3):
        total = None
        for j in range(3):
            tap = sum(
                lane_group(moved(sp_ref[i, 128 * j + 32 * r : 128 * j + 32 * r + 32, :], 32 * j - 32 * r), j) for r in range(4)
            )
            total = tap if total is None else total + tap
        tiles(16 + 4 * i, total)


def swap(tree, axis, size, distance):
    pairs = [(i, i ^ distance) for i in range(size)]
    return jax.tree.map(lambda v: lax.ppermute(v, axis, pairs), tree)


def add(*trees):
    def total(*vs):
        wide_vs = [v.astype(F32) for v in vs]
        out = wide_vs[0] + wide_vs[1]
        if len(vs) == 4:
            out = out + (wide_vs[2] + wide_vs[3])
        return out.astype(vs[0].dtype)

    return jax.tree.map(total, *trees)


def stages(size, first_alone):
    bits = [1 << i for i in range(size.bit_length() - 1)]
    out = []
    if first_alone and bits:
        out.append(bits[:1])
        bits = bits[1:]
    while bits:
        out.append(bits[:2])
        bits = bits[2:]
    return out


def butterfly(tree, axis, size, bits):
    if len(bits) == 1:
        return add(tree, swap(tree, axis, size, bits[0]))
    near, far, both = (swap(tree, axis, size, k) for k in (bits[0], bits[1], bits[0] + bits[1]))
    return add(tree, near, far, both)


def everywhere(tree, sizes, bulk=None):
    dp, chan = sizes["dp"], sizes["chan"]
    first, *others = stages(dp, True)
    tree = butterfly(tree, "dp", dp, first)
    if bulk is not None:
        tree = after(tree, bulk)
    for bits in stages(chan, False):
        tree = butterfly(tree, "chan", chan, bits)
    passed = tree
    for bits in others:
        tree = butterfly(tree, "dp", dp, bits)
    return tree, passed


def halos(first, last, count):
    low = lax.ppermute(last, "chan", [(i, i + 1) for i in range(count - 1)])
    high = lax.ppermute(first, "chan", [(i + 1, i) for i in range(count - 1)])
    return low, high


def gather_chips(v, sizes):
    return [v] + [swap(v, "dp", sizes["dp"], 2 * k) for k in (1, 2, 3)]


def gather_cores(own, sizes):
    return jnp.stack(own), jnp.stack([swap(v, "dp", sizes["dp"], 1) for v in own])


def pick(v, index, axis):
    return lax.dynamic_index_in_dim(v, index, axis, keepdims=False)


def scatter_cores(v, sizes, group):
    sent, kept = pick(v, 1 - group % 2, 0), pick(v, group % 2, 0)
    got = jnp.concatenate([swap(sent[:2], "dp", sizes["dp"], 1), swap(sent[2:], "dp", sizes["dp"], 1)])
    return add(kept, got)


def scatter_chips(v, sizes, group):
    chip = group // 2
    got = [swap(pick(v, chip ^ k, 0), "dp", sizes["dp"], 2 * k) for k in (1, 2, 3)]
    return add(pick(v, chip, 0), *got)


def scatter_chan(tree, sizes, chan, gate):
    size, dp = sizes["chan"], sizes["dp"]
    got = [swap(jax.tree.map(lambda v: pick(v, chan ^ k, 0), tree), "chan", size, k) for k in (1, 2, 3)]
    tree = add(jax.tree.map(lambda v: pick(v, chan, 0), tree), *after(got, gate))
    bits = [1 << i for i in range(3, dp.bit_length() - 1)]
    while bits:
        tree = butterfly(tree, "dp", dp, bits[:2])
        bits = bits[2:]
    return tree


def after(tree, gate):
    return lax.optimization_barrier((tree, gate))[0]


def local(
    sizes,
    slow_input,
    fast_input,
    clip_counts,
    frame_counts,
    fast_reduce,
    fast_spatial,
    fast_expand,
    lateral_kernel,
    slow_reduce,
    lateral_reduce,
    slow_spatial,
    slow_expand,
    shortcut,
    lateral_shortcut,
    fast_inner_norm,
    fast_outer_norm,
    lateral_norm,
    slow_inner_norm,
    slow_outer_norm,
    slow_cotangent,
    fast_cotangent,
):
    ways = sizes["chan"]
    clips, slow_t, height, across, slow_part = slow_input.shape
    fast_t, fast_part = fast_input.shape[1], fast_input.shape[4]
    ratio = fast_t // slow_t
    area = height * across
    places = clips * area
    mine = places // ways
    halo = across + 1
    chan, dp = lax.axis_index("chan"), lax.axis_index("dp")
    group = dp % 8
    ids = jnp.stack([dp, chan, group]).astype(jnp.int32)
    wide_in = ways * slow_part
    wide_f = ways * 128
    mid = 256
    ext = mine + 2 * halo
    per_clip = area // BIG
    chunk = 98

    def packed(v, slow=None):
        v = v.transpose(0, 2, 3, 1, 4).reshape(places, fast_t, fast_part)
        more = [] if slow is None else [slow.reshape(places, slow_t, slow_part)]
        width = 128 if slow is None else 128 + slow_part
        return pl.pallas_call(
            functools.partial(pack_kernel, area // chunk, clips),
            grid=(places // chunk,),
            out_shape=shape((places, slow_t, width), BF16),
            in_specs=[pl.BlockSpec(memory_space=pltpu.SMEM)] * 3
            + [pl.BlockSpec((chunk, *u.shape[1:]), lambda i: (i, 0, 0)) for u in (v, *more)],
            out_specs=pl.BlockSpec((chunk, slow_t, width), lambda i: (i, 0, 0)),
            scratch_shapes=[pltpu.VMEM((chunk * fast_t, fast_part), F32)],
            compiler_params=pltpu.CompilerParams(vmem_limit_bytes=16 * 1024 * 1024),
            name="fast_pack",
        )(ids, clip_counts, frame_counts, v, *more).reshape(ways, mine, slow_t, width)

    def unpacked(parts):
        slow, fast = call(
            unpack_kernel,
            [shape((places, slow_t, slow_part), BF16), shape((places, fast_t, fast_part), BF16)],
            [ids, *parts],
            [pltpu.VMEM((BIG * fast_t, fast_part), F32)],
            smem=1,
            name="outputs",
        )
        return joined(slow), fast.reshape(clips, height, across, fast_t, fast_part).transpose(0, 3, 1, 2, 4)

    def split(v):
        return v.transpose(0, 2, 3, 1, 4).reshape(ways, mine, slow_t, slow_part)

    def joined(v):
        return v.reshape(clips, height, across, slow_t, slow_part).transpose(0, 3, 1, 2, 4)

    def at_once(v):
        return [v[0]] + [swap(v[k], "chan", ways, k) for k in range(1, ways)]

    def blocks_of(v):
        return [pick(v, chan ^ k, 0) for k in range(ways)]

    def all_to_all(v):
        return lax.all_to_all(v, "chan", 0, 0, tiled=True)

    def parted(blocks):
        bounds = PARTS + ((len(blocks), 0),)
        ends = [b[1] if a[0] == b[0] else mine for a, b in zip(bounds, bounds[1:])]
        return [blocks[k][begin:end] for (k, begin), end in zip(PARTS, ends)]

    def send_parts(parts, which, gate):
        for i in which:
            parts[i] = swap(after(parts[i], gate), "chan", ways, PARTS[i][0])


    all_clips = frame_counts.shape[0]
    live = (jnp.arange(all_clips, dtype=jnp.int32) % clips) < jnp.repeat(clip_counts, clips)
    valid = jnp.where(live, frame_counts, 0)
    count = jnp.sum(valid).astype(F32) * area
    inv_n = jnp.stack([1.0 / count, 1.0 / (count * ratio)])
    parts = mine // BIG
    clip = (chan * parts + jnp.arange(-1, parts + 1)) // per_clip
    clip = jnp.clip(clip, 0, clips - 1) + dp * clips
    around = jnp.sum(jnp.where(clip[:, None] == jnp.arange(all_clips)[None, :], valid[None, :], 0), axis=1)
    table = jnp.concatenate([around, jnp.stack([chan, jnp.full_like(chan, parts)])]).astype(jnp.int32)

    lat_t, red_t, lred_t = (v.transpose(0, 2, 1) for v in (lateral_kernel, slow_reduce, lateral_reduce))
    spatial_t = slow_spatial.reshape(9, slow_spatial.shape[2], -1).transpose(0, 2, 1)
    params = [red_t, lred_t, lat_t, slow_expand, shortcut, lateral_shortcut, spatial_t]
    scratch = [(3, 8, wide_in), (3, 8, mid), (5, 8, 128), (8, wide_in), (32, wide_in), (8, wide_in), (9, 8, mid)]
    small = [lateral_norm, slow_inner_norm.reshape(4, -1), slow_outer_norm.reshape(4, -1)]
    any_spec, vmem_spec = pl.BlockSpec(memory_space=pl.ANY), pl.BlockSpec(memory_space=pltpu.VMEM)
    slab = pl.pallas_call(
        weight_slab_kernel,
        out_shape=shape((14, 8, wide_in), BF16),
        in_specs=[pl.BlockSpec(memory_space=pltpu.SMEM)] + [any_spec] * 7 + [vmem_spec] * 3,
        out_specs=vmem_spec,
        scratch_shapes=[pltpu.VMEM(dims, F32) for dims in scratch] + [pltpu.SemaphoreType.DMA((7,))],
        compiler_params=pltpu.CompilerParams(vmem_limit_bytes=58 * 1024 * 1024),
        name="weight_slab",
    )(ids, *params, *small)
    slabs = at_once([slab] * ways)
    fx_pieces = at_once(after(blocks_of(packed(after(fast_input, slab))), slabs))
    xs = all_to_all(after(split(slow_input), (slabs, fx_pieces)))
    early, late = jnp.stack([v[0:5] for v in slabs]), jnp.stack([v[5:14] for v in slabs])
    own_slabs, other_slabs = gather_cores(gather_chips(early, sizes), sizes)
    fr_t = fast_reduce.transpose(0, 2, 1)
    red_w, lred_w, w_first, w_fsp, w_fex, fin_g, fout_g, mid_g, out_g = call(
        weights_kernel,
        [
            shape((3, ways, 8, 8, wide_in), BF16),
            shape((3, ways, 8, 8, mid), BF16),
            shape((896, wide_f), BF16),
            shape((9, 128, 128), BF16),
            shape((128, wide_f), BF16),
            shape((4, 128)),
            shape((2, wide_f)),
            shape((8, mid)),
            shape((ways, 4, mid)),
        ],
        [ids, own_slabs, other_slabs, fr_t, fast_spatial.reshape(9, *fast_spatial.shape[2:]), fast_expand,
         fast_inner_norm.reshape(4, -1), fast_outer_norm],
        [pltpu.VMEM((5, ways, 8, 8, 128), F32)],
        smem=1,
        name="weights",
    )
    red_w, lred_w = red_w.reshape(-1, wide_in), lred_w.reshape(-1, mid)
    fin_g = (fin_g[0:2], fin_g[2:4])
    lat_g, in_g = mid_g[0:2], (mid_g[2:4], mid_g[4:6])
    out_g = out_g.transpose(1, 0, 2).reshape(4, wide_in)

    edge = [shape((halo, 8, 128))] * 2
    edges = [shape((halo, 8, 512))] * 2
    narrow, middle = shape((mine, 8, 128)), shape((mine, 8, mid))
    fx, fa, lp, sums1, first, last = call(
        fast_first_kernel,
        [shape((mine, 8, wide_f), BF16), narrow, middle, shape((2, 384)), *edge],
        [table, *fx_pieces, w_first],
        smem=1,
        name="fast_first",
    )
    fa_lo, fa_hi = halos(first, last, ways)
    cots = parted(blocks_of(packed(fast_cotangent, split(slow_cotangent))))
    late = gather_chips(after(late, other_slabs), sizes)
    own_late, other_late = gather_cores(late, sizes)
    exp_w, short_w, lshort_w, spat_w = call(
        more_weights_kernel,
        [
            shape((ways, 8, 8, wide_in), BF16),
            shape((ways, 8, 4, 8, wide_in), BF16),
            shape((ways, 8, 8, wide_in), BF16),
            shape((9, ways, 8, 8, mid), BF16),
        ],
        [ids, own_late, other_late],
        smem=1,
        name="more_weights",
    )
    exp_w, short_w, lshort_w = (v.reshape(-1, wide_in) for v in (exp_w, short_w, lshort_w))
    spat_w = spat_w.reshape(9, mid, mid)
    sums1, passed = everywhere(sums1, sizes, (xs, fa_lo, fa_hi, cots, late))
    send_parts(cots, (2,), passed)
    fast_pad = [pltpu.VMEM((3, ext, 8, 128), F32)]
    slow_pad = [pltpu.VMEM((3, ext, 8, mid), F32)]
    x, lat, sa, sums2, first, last = call(
        slow_first_kernel,
        [shape((mine, 8, wide_in), BF16), shape((mine, 8, mid), BF16), middle, shape((2, mid)), *[shape((halo, 8, mid))] * 2],
        [table, inv_n, xs, lp, sums1, lat_g, red_w, lred_w],
        smem=2,
        name="slow_first",
    )
    sa_lo, sa_hi = halos(first, last, ways)
    fa_late = after(fa, sums2)
    h1, fb, fb_sums = call(
        functools.partial(conv_kernel, halo, across, per_clip, True, (0, 0)),
        [shape((ext, 8, 128), BF16), narrow, shape((2, 128))],
        [table, inv_n, sums1, fin_g[0], fa_lo, fa_late, fa_hi, w_fsp],
        fast_pad,
        smem=2,
        name="fast_second",
    )
    sums2, passed = everywhere(sums2, sizes, (cots[2], sa_lo, sa_hi))
    send_parts(cots, (3, 4, 1), passed)
    ha, sb, sums3 = call(
        functools.partial(conv_kernel, halo, across, per_clip, False, (0, 0)),
        [shape((ext, 8, mid), BF16), middle, shape((2, mid + 128))],
        [table, inv_n, sums2, in_g[0], sa_lo, sa, sa_hi, spat_w, fb_sums],
        slow_pad,
        smem=2,
        name="slow_second",
    )
    sums3, passed = everywhere(sums3, sizes, (cots[3], cots[4], cots[1]))
    send_parts(cots, (5,), passed)
    sp, sp_sums = call(
        bypass_kernel,
        [shape((mine, 8, wide_in), BF16), shape((2, wide_in))],
        [table, x, lat, short_w, lshort_w],
        smem=1,
        name="bypass",
    )
    h2, fc, fc_sums = call(
        functools.partial(expand_kernel, True, mid),
        [shape((mine, 8, 128), BF16), shape((mine, 8, wide_f), BF16), shape((2, wide_f))],
        [table, inv_n, fb, sums3, fin_g[1], w_fex],
        smem=2,
        name="fast_third",
    )
    hb, sc, sums4 = call(
        functools.partial(expand_kernel, False, 0),
        [shape((mine, 8, mid), BF16), shape((mine, 8, wide_in), BF16), shape((2, 2 * wide_in + wide_f))],
        [table, inv_n, sb, sums3, in_g[1], exp_w, sp_sums, fc_sums],
        smem=2,
        name="slow_third",
    )
    sums4, _ = everywhere(sums4, sizes, cots[5])
    fast_out, dfs, fc_slopes = call(
        functools.partial(fast_out_kernel, 2 * wide_in),
        [shape((ways, mine, 8, 128), BF16), shape((mine, 8, wide_f), BF16), shape((2, wide_f))],
        [table, inv_n, fc, sums4, fout_g, fx, *cots],
        [pltpu.VMEM((8, wide_f), F32)],
        smem=2,
        name="fast_out",
    )
    *outs, dss, sums5 = call(
        slow_out_kernel,
        [*[shape(c.shape, BF16) for c in cots], shape((mine, 8, wide_in), BF16), shape((2, 2 * wide_in + wide_f))],
        [table, inv_n, sc, sp, sums4, out_g, *cots, fast_out, fc_slopes],
        [pltpu.VMEM((8, wide_in), F32)],
        smem=2,
        name="slow_out",
    )

    sums5, passed = everywhere(sums5, sizes)
    send_parts(outs, (2,), passed)
    dfc, dzfb, fb_slopes, first, last = call(
        functools.partial(expand_back_kernel, True, (2 * wide_in, 2 * wide_in, mid)),
        [shape((mine, 8, wide_f), BF16), narrow, shape((2, 128)), *edges],
        [table, inv_n, dfs, fc, sums4, fout_g, sums5, fb, sums3, fin_g[1], w_fex, sb],
        smem=2,
        name="fast_third_back",
    )
    low6, high6 = halos(first, last, ways)
    dsc, dzsb, sums6, first, last = call(
        functools.partial(expand_back_kernel, False, (0, 0, 0)),
        [shape((mine, 8, wide_in), BF16), middle, shape((2, mid + 128)), *[shape((halo, 8, mid))] * 2],
        [table, inv_n, dss, sc, sums4, out_g[0:2], sums5, sb, sums3, in_g[1], exp_w, fb_slopes],
        smem=2,
        name="slow_third_back",
    )
    low_sb, high_sb = halos(first, last, ways)
    sums6, passed = everywhere(sums6, sizes, (outs[2], low6, high6, low_sb, high_sb))
    send_parts(outs, (3, 4, 1), passed)
    dfb, dzfa, fa_slopes = call(
        functools.partial(conv_back_kernel, halo, across, per_clip, True, (mid, mid, 0, 384, 0)),
        [shape((mine, 8, 128), BF16), narrow, shape((2, 128))],
        [table, inv_n, sums3, fin_g[1], sums6, low6, fb, high6, low6, dzfb, high6, w_fsp, fa, sums1, fin_g[0]],
        fast_pad,
        smem=2,
        name="fast_second_back",
    )
    dsb, dzsa, sums7 = call(
        functools.partial(conv_back_kernel, halo, across, per_clip, False, (0, 0, 0, 128, 0)),
        [shape((mine, 8, mid), BF16), middle, shape((2, mid + 128))],
        [table, inv_n, sums3, in_g[1], sums6, low6, sb, high6, low_sb, dzsb, high_sb, spat_w, sa, sums2, in_g[0], fa_slopes],
        slow_pad,
        smem=2,
        name="slow_second_back",
    )
    dss_late, = after((dss,), sums7)
    dsp, dx, dl = call(
        bypass_back_kernel,
        [shape((mine, 8, wide_in), BF16), shape((mine, 8, wide_in), BF16), middle],
        [table, inv_n, dss_late, sp, sums4, out_g[2:4], sums5, short_w, lshort_w],
        smem=2,
        name="bypass_back",
    )

    sums7, passed = everywhere(sums7, sizes, (outs[3], outs[4], outs[1], dx, dl))
    send_parts(outs, (5,), passed)
    dsa, dslow, dzlp, sums8 = call(
        slow_back_kernel,
        [shape((mine, 8, 3 * mid), BF16), shape((ways, mine, 8, mid), BF16), middle, shape((2, mid))],
        [table, inv_n, dzsa, sa, sums2, in_g[0], sums7, red_w, lred_w, dx, dl, lp, sums1, lat_g],
        smem=2,
        name="slow_first_back",
    )
    dsc_late, dsp = after((dsc, dsp), sums8)
    (slab1,) = call(
        first_slab_kernel,
        [shape((2, 4, ways, 6, 8, wide_in), BF16)],
        [hb, dsc_late, x, lat, dsp],
        [pltpu.VMEM((6, mid, wide_in), F32)],
        name="first_slab",
    )
    sums8, passed = everywhere(sums8, sizes, (outs[5], slab1))
    dslow = all_to_all(after(dslow, passed))
    slab1 = scatter_cores(slab1, sizes, group)
    dsa, dsb_late = after((dsa, dsb), (sums8, slab1))
    (slab2,) = call(
        functools.partial(second_slab_kernel, halo, across, per_clip),
        [shape((2, 4, ways, 6, 8, wide_in), BF16)],
        [table, ha, dsb_late, dsa, x, lat],
        [*slow_pad, pltpu.VMEM((3, mid, 3 * mid), F32), pltpu.VMEM((3, mid, wide_in), F32), pltpu.VMEM((3, mid, mid), F32)],
        smem=1,
        name="second_slab",
    )
    slab1 = scatter_chips(slab1, sizes, group)
    slab2 = scatter_cores(slab2, sizes, group)
    dzlp = after(dzlp, slab2)
    slab2 = scatter_chips(slab2, sizes, group)
    dfirst, dfast = call(
        functools.partial(fast_back_kernel, mid),
        [shape((mine, 8, 896), BF16), shape((ways, mine, 8, 128), BF16)],
        [table, inv_n, sums1, fin_g[0], lat_g, sums7, sums8, dzfa, fa, dzlp, lp, dfs, w_first],
        smem=2,
        name="fast_first_back",
    )

    g_lat, g_fast = call(
        functools.partial(fast_grads_kernel, halo, across, per_clip),
        [shape((ways, 40, 8, 128), BF16), shape((28, 8, 128), BF16)],
        [table, h1, dfb, dfirst, fx, h2, dfc],
        [*fast_pad, pltpu.VMEM((3, 384, 128), F32), pltpu.VMEM((896, wide_f), F32), pltpu.VMEM((128, wide_f), F32)],
        smem=1,
        name="fast_grads",
    )
    (slow_input_grad,) = call(
        copy_kernel, [shape((places, slow_t, slow_part), BF16)], [dslow.reshape(places, slow_t, slow_part)], name="slow_grad"
    )
    slow_output, fast_output = unpacked(after(outs, slow_input_grad))
    slabs = scatter_chan(jnp.concatenate([slab1, slab2], axis=1), sizes, chan, (slow_output, fast_output))
    small = [jnp.concatenate([pick(g_lat, chan ^ k, 0), g_fast]) for k in range(ways)]
    small = add(*at_once(small))
    dfast = all_to_all(after(dfast, (dslow, slabs, small)))
    for bits in stages(sizes["dp"], True):
        small = butterfly(small, "dp", sizes["dp"], bits)
    g_lat, g_fast = small[0:40].astype(F32), small[40:68].astype(F32)
    own_slabs, other_slabs = gather_cores(gather_chips(slabs, sizes), sizes)
    g_exp, g_short, g_lshort, g_red, g_lred, g_spat = call(
        grads_kernel,
        [shape((8, 8, wide_in)), shape((8, 4, 8, wide_in)), shape((8, 8, wide_in)), shape((3, 8, 8, wide_in)), shape((3, 8, 8, mid)),
         shape((9, 8, 8, mid))],
        [ids, own_slabs, other_slabs],
        smem=1,
        name="grads",
    )
    slow_input_grad = joined(slow_input_grad)
    fast_input_grad = pl.pallas_call(
        unpack_fast_kernel,
        grid=(places // chunk,),
        out_shape=shape((places, fast_t, fast_part), BF16),
        in_specs=[pl.BlockSpec((chunk, slow_t, 128), lambda i: (i, 0, 0))],
        out_specs=pl.BlockSpec((chunk, fast_t, fast_part), lambda i: (i, 0, 0)),
        scratch_shapes=[pltpu.VMEM((chunk * fast_t, fast_part), F32)],
        compiler_params=pltpu.CompilerParams(vmem_limit_bytes=16 * 1024 * 1024),
        name="fast_unpack",
    )(dfast.reshape(places, slow_t, 128))
    fast_input_grad = fast_input_grad.reshape(clips, height, across, fast_t, fast_part).transpose(0, 3, 1, 2, 4)
    g_fred = g_fast[0:12].reshape(3, 32, 128).transpose(0, 2, 1)
    g_fex = g_fast[12:16].reshape(32, 128)
    g_fsp = g_fast[16:28].reshape(3, 32, 128)[:, :, 0:96].reshape(3, 32, 3, 32).transpose(0, 2, 1, 3)

    def pair(slopes):
        return slopes[::-1]

    def own(v, width):
        return lax.dynamic_slice_in_dim(v, chan * width, width, v.ndim - 1)

    def fold_in(slopes):
        return jnp.sum(slopes.reshape(2, ratio, 128 // ratio), axis=1)

    lw, sw, ow = lateral_norm.shape[1], slow_inner_norm.shape[2], slow_outer_norm.shape[2]
    fast_inner_grad = jnp.stack([pair(fold_in(sums7[:, mid:])), pair(fold_in(sums6[:, mid:]))])
    fc_slopes = sums5[:, 2 * wide_in :].reshape(2, ways, ratio, fast_part)
    fast_outer_grad = pair(jnp.sum(fc_slopes, axis=2).reshape(2, -1))
    lateral_grad = pair(own(sums8, lw))
    slow_inner_grad = own(jnp.stack([pair(sums7[:, 0:mid]), pair(sums6[:, 0:mid])]), sw)
    slow_outer_grad = own(jnp.stack([pair(sums5[:, 0:wide_in]), pair(sums5[:, wide_in : 2 * wide_in])]), ow)
    return (
        slow_output,
        fast_output,
        slow_input_grad,
        fast_input_grad,
        g_fred,
        g_fsp,
        g_fex,
        g_lat.reshape(5, -1, 128).transpose(0, 2, 1),
        g_red.reshape(3, -1, wide_in).transpose(0, 2, 1),
        g_lred.reshape(3, -1, mid).transpose(0, 2, 1),
        g_spat.reshape(9, -1, mid).transpose(0, 2, 1).reshape(slow_spatial.shape),
        g_exp.reshape(-1, wide_in),
        g_short.reshape(-1, wide_in),
        g_lshort.reshape(-1, wide_in),
        fast_inner_grad,
        fast_outer_grad,
        lateral_grad,
        slow_inner_grad,
        slow_outer_grad,
    )


def solution(mesh):
    sizes = {"dp": mesh.shape["dp"], "chan": mesh.shape["chan"]}
    big = P("dp", None, None, None, "chan")
    last2, last3, last4 = P(None, "chan"), P(None, None, "chan"), P(None, None, None, "chan")
    first = P("chan", None)
    return jax.shard_map(
        functools.partial(local, sizes),
        mesh=mesh,
        in_specs=(
            big, big, P(), P(), P(), P(), P(), last3, last3, last3, last4, first, first, first,
            P(), P(), last2, last3, last3, big, big,
        ),
        out_specs=(
            big, big, big, big, P(), P(), P(), last3, last3, last3, last4, first, first, first,
            P(), P(), last2, last3, last3,
        ),
        check_vma=False,
    )
```

```python
import functools

import jax
import jax.numpy as jnp
from jax import lax
from jax.experimental import pallas as pl
from jax.experimental.pallas import tpu as pltpu
from jax.sharding import PartitionSpec as P

F32 = jnp.float32
BF16 = jnp.bfloat16
EPSILON = 1e-05
ROOT = 0.7978845608028654
CUBIC = 0.044715
BIG = 49
PARTS = ((0, 0), (1, 0), (2, 0), (2, 98), (3, 0), (3, 49))
SMALL = 7


def gelu(v):
    return 0.5 * v * (1.0 + jnp.tanh(ROOT * (v * (1.0 + CUBIC * (v * v)))))


def gelu_slope(v):
    square = v * v
    th = jnp.tanh(ROOT * (v * (1.0 + CUBIC * square)))
    half = 0.5 * (1.0 + th)
    return half + (0.5 * ROOT) * v * (1.0 - th * th) * (1.0 + 3.0 * CUBIC * square)


def gelu_pair(v):
    square = v * v
    th = jnp.tanh(ROOT * (v * (1.0 + CUBIC * square)))
    half = 0.5 * (1.0 + th)
    slope = half + (0.5 * ROOT) * v * (1.0 - th * th) * (1.0 + 3.0 * CUBIC * square)
    return v * half, slope


def rows(v):
    return v.reshape(v.shape[0] * v.shape[1], v.shape[2])


def cells(v):
    return v.reshape(v.shape[0] // 8, 8, v.shape[1])


def rows_bf(v):
    return rows(v.astype(F32)).astype(BF16)


def wide(mask, width):
    repeats = width // 128
    return mask if repeats == 1 else jnp.concatenate([mask] * repeats, axis=-1)


def nn(a, b):
    return jnp.dot(a, b, preferred_element_type=F32)


def nt(a, b):
    return lax.dot_general(a, b, (((1,), (1,)), ((), ())), preferred_element_type=F32)


def later(v):
    rolled = pltpu.roll(v, 1, 1)
    return jnp.where(lax.broadcasted_iota(jnp.int32, v.shape, 1) == 0, 0.0, rolled)


def sooner(v):
    rolled = pltpu.roll(v, 7, 1)
    return jnp.where(lax.broadcasted_iota(jnp.int32, v.shape, 1) == 7, 0.0, rolled)


def folded(v):
    out = []
    for block in range(v.shape[-1] // 128):
        part = v[:, 128 * block : 128 * block + 128]
        part = part + pltpu.roll(part, 64, 1)
        out.append(part + pltpu.roll(part, 32, 1))
    return out[0] if len(out) == 1 else jnp.concatenate(out, axis=-1)


def scale_of(sums, gains, inv_n):
    center = sums[0:1] * inv_n
    spread = sums[1:2] * inv_n - center * center
    inv_std = lax.rsqrt(spread + EPSILON)
    factor = gains[0:1] * inv_std
    return factor, gains[1:2] - center * factor, center, inv_std


def slope_of(slopes, factor, center, inv_std, inv_n):
    k1 = factor * slopes[1:2] * inv_n * inv_std
    k0 = factor * slopes[0:1] * inv_n - k1 * center
    return k0, k1


def down(v):
    return jnp.sum(v, axis=0)


def flat(v):
    return jnp.sum(v, axis=0, keepdims=True)


def steps(count, step, body, carry):
    return lax.fori_loop(0, count // step, lambda i, c: body(i * step, c), carry)


def call(kernel, outs, args, scratch=(), smem=0, flops=0, name=None):
    specs = [pl.BlockSpec(memory_space=pltpu.SMEM if i < smem else pltpu.VMEM) for i in range(len(args))]
    total = sum(a.size * a.dtype.itemsize for a in args)
    total += sum(o.size * o.dtype.itemsize for o in outs)
    def padded(v):
        dims = list(v.shape)
        if len(dims) < 2:
            return 4096
        dims[-1] = -(-dims[-1] // 128) * 128
        dims[-2] = -(-dims[-2] // 8) * 8
        amount = v.dtype.itemsize
        for d in dims:
            amount *= d
        return amount

    room = sum(padded(v) for v in (*args, *outs, *scratch)) + 6 * 1024 * 1024
    return pl.pallas_call(
        kernel,
        out_shape=tuple(outs),
        in_specs=specs,
        out_specs=tuple(pl.BlockSpec(memory_space=pltpu.VMEM) for _ in outs),
        scratch_shapes=list(scratch),
        compiler_params=pltpu.CompilerParams(vmem_limit_bytes=room),
        cost_estimate=pl.CostEstimate(flops=flops, bytes_accessed=1, transcendentals=0),
        name=name,
    )(*args)


def shape(dims, dtype=F32):
    return jax.ShapeDtypeStruct(dims, dtype)


def tile_mask(frames, width):
    tile = (lax.broadcasted_iota(jnp.int32, (8, 128), 0) < frames).astype(F32)
    return wide(tile, width)[None]


def sweep(table_ref, size, step, body, carry=0, begin=0):
    def run(i, kept):
        p = i * step
        return body(p, table_ref[1 + (begin + p) // BIG], kept)

    return lax.fori_loop(0, size // step, run, carry)


def lane_group(v, group):
    return jnp.where(lax.broadcasted_iota(jnp.int32, v.shape, v.ndim - 1) // 32 == group, v, 0.0)


def moved(v, shift):
    shift = shift % 128
    return v if shift == 0 else pltpu.roll(v, shift, v.ndim - 1)


def pack_kernel(per_clip, clips, ids_ref, counts_ref, frames_ref, x_ref, *refs):
    out_ref, tmp_ref = refs[-2:]
    clip, dp = pl.program_id(0) // per_clip, ids_ref[0]
    chunk = x_ref.shape[0]
    frames = jnp.where(clip < counts_ref[dp], frames_ref[dp * clips + clip], 0)
    tmp_ref[...] = x_ref[...].astype(F32).reshape(chunk * 32, 32)
    parts = [tmp_ref[pl.ds(r, chunk * 8, stride=4), :] for r in range(4)]
    out_ref[:, :, 0:128] = (cells(jnp.concatenate(parts, axis=1)) * tile_mask(frames, 128)).astype(BF16)
    if len(refs) == 3:
        out_ref[:, :, 128:384] = refs[0][...]


def unpack_kernel(ids_ref, *refs):
    slow_ref, fast_ref, tmp_ref = refs[-3:]
    size = refs[0].shape[0]
    for (k, first), ref in zip(PARTS, refs):
        begin = (ids_ref[1] ^ k) * size + first

        def body(p, carry, ref=ref, begin=begin):
            joined = rows(ref[pl.ds(p, BIG), :, 0:128].astype(F32))
            for r in range(4):
                tmp_ref[pl.ds(r, BIG * 8, stride=4), :] = joined[:, 32 * r : 32 * r + 32]
            fast_ref[pl.ds(begin + p, BIG)] = tmp_ref[...].reshape(BIG, 32, 32).astype(BF16)
            slow_ref[pl.ds(begin + p, BIG)] = ref[pl.ds(p, BIG), :, 128:384]
            return carry

        steps(ref.shape[0], BIG, body, 0)


def unpack_fast_kernel(x_ref, out_ref, tmp_ref):
    chunk = x_ref.shape[0]
    joined = rows(x_ref[...].astype(F32))
    for r in range(4):
        tmp_ref[pl.ds(r, chunk * 8, stride=4), :] = joined[:, 32 * r : 32 * r + 32]
    out_ref[...] = tmp_ref[...].reshape(chunk, 32, 32).astype(BF16)


def copy_kernel(x_ref, out_ref):
    def body(p, carry):
        out_ref[pl.ds(p, SMALL)] = x_ref[pl.ds(p, SMALL)]
        return carry

    steps(x_ref.shape[0], SMALL, body, 0)


def lanes_at(block, width):
    return pl.ds(pl.multiple_of(block * width, width), width)


LREDUCE = [(3, 256 * k) for k in range(3)]
LATERAL = [(4, 128 * k) for k in range(5)]
GAINS = [(3, 768), (3, 896), (4, 640), (4, 768)]
SPATIAL = [(11 + k // 4, 256 * (k % 4)) for k in range(9)]


def weight_slab_kernel(ids_ref, red_ref, lred_ref, lat_ref, exp_ref, short_ref, lshort_ref, sp_ref, ln_ref, sn_ref, on_ref, out_ref,
                       red_s, lred_s, lat_s, exp_s, short_s, lshort_s, sp_s, sem):
    group = ids_ref[2]
    eight, more = pl.ds(pl.multiple_of(group * 8, 8), 8), pl.ds(pl.multiple_of(group * 32, 32), 32)
    copies = []
    for i, (src, dst) in enumerate((
        (red_ref.at[:, eight], red_s), (lred_ref.at[:, eight], lred_s), (lat_ref.at[:, eight], lat_s), (exp_ref.at[eight], exp_s),
        (short_ref.at[more], short_s), (lshort_ref.at[eight], lshort_s), (sp_ref.at[:, eight], sp_s),
    )):
        copies.append(pltpu.make_async_copy(src, dst, sem.at[i]))
    for copy in copies:
        copy.start()
    out_ref[4, :, 896:1024] = jnp.zeros((8, 128), BF16)
    out_ref[13, :, 256:1024] = jnp.zeros((8, 768), BF16)
    blank = jnp.zeros((2, 128), F32)
    half = jnp.zeros((2, 64), F32)
    inner = jnp.concatenate([jnp.concatenate([v, half], axis=1) for v in (ln_ref[...], sn_ref[0], sn_ref[1])] + [blank], axis=0)
    outer = jnp.concatenate([on_ref[k, :, 128 * h : 128 * h + 128] for h in range(2) for k in range(2)], axis=0)
    for i, v in enumerate((inner, outer)):
        high = v.astype(BF16)
        for k, part in ((i, high), (2 + i, (v - high.astype(F32)).astype(BF16))):
            at, lane = GAINS[k]
            out_ref[at, :, lane : lane + 128] = part
    for copy in copies:
        copy.wait()
    for j in range(3):
        out_ref[j] = red_s[j].astype(BF16)
        at, lane = LREDUCE[j]
        out_ref[at, :, lane : lane + 256] = lred_s[j].astype(BF16)
    out_ref[5], out_ref[10] = exp_s[...].astype(BF16), lshort_s[...].astype(BF16)
    for a in range(4):
        out_ref[6 + a] = short_s[8 * a : 8 * a + 8].astype(BF16)
    for k in range(9):
        at, lane = SPATIAL[k]
        out_ref[at, :, lane : lane + 256] = sp_s[k].astype(BF16)
    for k in range(5):
        at, lane = LATERAL[k]
        out_ref[at, :, lane : lane + 128] = lat_s[k].astype(BF16)


def more_weights_kernel(ids_ref, own_ref, other_ref, exp_ref, short_ref, lshort_ref, sp_ref):
    me, group = ids_ref[1], ids_ref[2]

    def place(i, carry):
        chip, kz = i // 4, i % 4
        z = me ^ kz
        for core, ref in ((0, own_ref), (1, other_ref)):
            d = group ^ (2 * chip + core)
            exp_ref[z, d], lshort_ref[z, d] = ref[chip, kz, 0], ref[chip, kz, 5]
            for a in range(4):
                short_ref[z, d, a] = ref[chip, kz, 1 + a]
            for k in range(9):
                at, lane = SPATIAL[k]
                sp_ref[k, z, d] = ref[chip, kz, at - 5, :, lane : lane + 256]
        return carry

    lax.fori_loop(0, 16, place, 0)


def weights_kernel(ids_ref, own_ref, other_ref, fr_ref, fsp_ref, fex_ref, fin_ref, fout_ref, red_ref, lred_ref, first_ref, wsp_ref, wex_ref,
                   gin_ref, gout_ref, gmid_ref, gwide_ref, lat_ref):
    me, group = ids_ref[1], ids_ref[2]

    def place(i, carry):
        chip, kz = i // 4, i % 4
        z = me ^ kz
        for core, ref in ((0, own_ref), (1, other_ref)):
            d = group ^ (2 * chip + core)
            for j in range(3):
                red_ref[j, z, d] = ref[chip, kz, j]
                at, lane = LREDUCE[j]
                lred_ref[j, z, d] = ref[chip, kz, at, :, lane : lane + 256]
            for k in range(5):
                at, lane = LATERAL[k]
                lat_ref[k, z, d] = ref[chip, kz, at, :, lane : lane + 128].astype(F32)
        return carry

    lax.fori_loop(0, 16, place, 0)

    mids = [jnp.zeros((8, 128), F32) for _ in range(2)]
    for kz in range(4):
        z = me ^ kz
        parts = [own_ref[0, kz, at, :, lane : lane + 128].astype(F32) for at, lane in GAINS]
        inner, outer = parts[0] + parts[2], parts[1] + parts[3]
        for half in range(2):
            for block in range(2):
                here = (z == 2 * block + half).astype(F32)
                mids[block] = mids[block] + moved(inner, 64 * half) * here
        gwide_ref[z, :, 0:128], gwide_ref[z, :, 128:256] = outer[0:4], outer[4:8]
    gmid_ref[:, 0:128], gmid_ref[:, 128:256] = mids[0], mids[1]

    first_ref[...] = jnp.zeros_like(first_ref)
    wsp_ref[...] = jnp.zeros_like(wsp_ref)
    for z in range(4):
        lanes = slice(128 * z, 128 * z + 128)

        def put(v, r, z=z):
            return lane_group(moved(v, 32 * r - 32 * z), r)

        for q in range(4):
            total = sum(put(fr_ref[r - q + 1], r) for r in range(4) if abs(r - q) <= 1)
            first_ref[32 * q : 32 * q + 32, lanes] = total.astype(BF16)
        first_ref[128:160, lanes] = put(fr_ref[0], 3).astype(BF16)
        first_ref[352:384, lanes] = put(fr_ref[2], 0).astype(BF16)
        taps = [lat_ref[j].reshape(256, 128) for j in range(5)]
        first_ref[384:640, lanes] = sum(put(taps[2 + r], r) for r in range(3)).astype(BF16)
        first_ref[640:896, lanes] = (put(taps[0], 2) + put(taps[1], 3)).astype(BF16)
        for r in range(4):
            wex_ref[32 * r : 32 * r + 32, lanes] = put(fex_ref[...], r).astype(BF16)
        gout_ref[:, lanes] = sum(put(fout_ref[...], r) for r in range(4))
    blank = jnp.zeros((32, 96), F32)
    for k in range(9):
        tap = jnp.concatenate([fsp_ref[k], blank], axis=1)
        for r in range(4):
            wsp_ref[k, 32 * r : 32 * r + 32, :] = moved(tap, 32 * r).astype(BF16)
    gin_ref[...] = jnp.concatenate([fin_ref[...]] * 4, axis=1)


def grads_kernel(ids_ref, own_ref, other_ref, exp_ref, short_ref, lshort_ref, red_ref, lred_ref, sp_ref):
    def place(chip, carry):
        for core, ref in ((0, own_ref), (1, other_ref)):
            d = ids_ref[2] ^ (2 * chip + core)
            exp_ref[d], lshort_ref[d] = ref[chip, 0].astype(F32), ref[chip, 5].astype(F32)
            for a in range(4):
                short_ref[d, a] = ref[chip, 1 + a].astype(F32)
            for j in range(3):
                red_ref[j, d] = ref[chip, 6 + j].astype(F32)
                lred_ref[j, d] = ref[chip, 9, :, 256 * j : 256 * j + 256].astype(F32)
            for k in range(8):
                sp_ref[k, d] = ref[chip, 10 + k // 4, :, 256 * (k % 4) : 256 * (k % 4) + 256].astype(F32)
            sp_ref[8, d] = ref[chip, 9, :, 768:1024].astype(F32)
        return carry

    lax.fori_loop(0, 4, place, 0)


def fast_first_kernel(table_ref, f0_ref, f1_ref, f2_ref, f3_ref, w_ref, fx_ref, fa_ref, lp_ref, sums_ref, first_ref, last_ref):
    size = fa_ref.shape[0]

    def fill(p, carry):
        for k, ref in enumerate((f0_ref, f1_ref, f2_ref, f3_ref)):
            fx_ref[pl.ds(p, SMALL), :, lanes_at(table_ref[5] ^ k, 128)] = ref[pl.ds(p, SMALL)]
        return carry

    steps(size, SMALL, fill, 0)

    def body(p, frames, carry):
        acc = cells(nt(rows_bf(fx_ref[pl.ds(p, BIG)]), w_ref[...]))
        fa = acc[:, :, 0:128] + later(acc[:, :, 128:256]) + sooner(acc[:, :, 256:384])
        lp = acc[:, :, 384:640] + later(acc[:, :, 640:896])
        fa_ref[pl.ds(p, BIG)] = fa
        lp_ref[pl.ds(p, BIG)] = lp
        fm, lm = fa * tile_mask(frames, 128), lp * tile_mask(frames, 256)
        return tuple(c + down(v) for c, v in zip(carry, (fm, fm * fa, lm, lm * lp)))

    zero = (jnp.zeros((8, 128), F32),) * 2 + (jnp.zeros((8, 256), F32),) * 2
    a, b, c, d = sweep(table_ref, size, BIG, body, zero)
    sums_ref[0:1, 0:128], sums_ref[1:2, 0:128] = flat(a), flat(b)
    sums_ref[0:1, 128:384], sums_ref[1:2, 128:384] = flat(c), flat(d)
    halo = first_ref.shape[0]
    first_ref[...], last_ref[...] = fa_ref[0:halo], fa_ref[size - halo : size]


def fill_padded(table_ref, refs, offset, out_ref, value, halo, size):
    low, middle, high = refs
    phase = table_ref[5] * (size // SMALL)

    def put(v, at, part, count, step=SMALL):
        even = ((phase + part + 2 * count) % 2 == 0).astype(F32)
        out_ref[1, pl.ds(at, step)] = v
        if step == 1:
            out_ref[0, pl.ds(at, 1)] = v * even
            out_ref[2, pl.ds(at, 1)] = v * (1.0 - even)
            return
        out_ref[0, pl.ds(at, step)] = v
        out_ref[2, pl.ds(at, step)] = v
        out_ref[0, pl.ds(at + step - 1, 1)] = v[step - 1 : step] * even
        out_ref[2, pl.ds(at, 1)] = v[0:1] * (1.0 - even)

    width = out_ref.shape[-1]
    lo_mask, hi_mask = tile_mask(table_ref[0], width), tile_mask(table_ref[4], width)
    put(value(low, 0, 1) * lo_mask, 0, -3, 4, 1)
    put(value(low, 1, SMALL) * lo_mask, 1, -2, 4)
    put(value(low, 1 + SMALL, SMALL) * lo_mask, 1 + SMALL, -1, 4)
    parts = size // SMALL
    put(value(high, 0, SMALL) * hi_mask, halo + size, parts, 0)
    put(value(high, SMALL, SMALL) * hi_mask, halo + size + SMALL, parts + 1, 0)
    put(value(high, 2 * SMALL, 1) * hi_mask, halo + size + 2 * SMALL, parts + 2, 0, 1)

    def body(p, frames, carry):
        put(value(middle, p, SMALL) * tile_mask(frames, width), halo + p, p // SMALL, 0)
        return carry

    sweep(table_ref, size, SMALL, body)


def edge_scales(table_ref, p, per_clip):
    part = table_ref[5] * table_ref[6] + p // BIG
    return (part % per_clip != 0).astype(F32), ((part + 1) % per_clip != 0).astype(F32)


def conv_rows(table_ref, per_clip, pad_ref, weight, p, halo, row_len, dot):
    top, bottom = edge_scales(table_ref, p, per_clip)
    total = None
    for i in (1, 0, 2):
        begin = p + halo + row_len * (i - 1)
        acc = None
        for j in range(3):
            tap = rows(pad_ref[j, pl.ds(begin + j - 1, BIG)]).astype(BF16)
            part = dot(tap, weight(i, j))
            acc = part if acc is None else acc + part
        acc = cells(acc)
        if i == 0:
            acc = jnp.concatenate([acc[0:row_len] * top, acc[row_len:]], axis=0)
        if i == 2:
            acc = jnp.concatenate([acc[: BIG - row_len], acc[BIG - row_len :] * bottom], axis=0)
        total = acc if total is None else total + acc
    return total


def conv_kernel(halo, row_len, per_clip, fold, offsets, table_ref, n_ref, sums_ref, gains_ref, lo_ref, y_ref, hi_ref, w_ref, *refs):
    if fold:
        act_ref, out_ref, osums_ref, pad_ref = refs
    else:
        more_ref, act_ref, out_ref, osums_ref, pad_ref = refs
    size, width = y_ref.shape[0], y_ref.shape[2]
    sums = sums_ref[:, offsets[0] : offsets[0] + width]
    sums = folded(sums) if fold else sums
    factor, shift, _, _ = scale_of(sums, gains_ref[...], n_ref[1 if fold else 0])
    lanes = slice(offsets[1], offsets[1] + width)

    def value(ref, p, step):
        y = ref[pl.ds(p, step)] if ref is y_ref else ref[pl.ds(p, step), :, lanes]
        return gelu(y * factor[None] + shift[None]).astype(BF16).astype(F32)

    fill_padded(table_ref, (lo_ref, y_ref, hi_ref), 0, pad_ref, value, halo, size)

    def copy(p, carry):
        act_ref[pl.ds(p, 3)] = pad_ref[1, pl.ds(p, 3)].astype(BF16)
        return carry

    steps(size + 2 * halo, 3, copy, 0)

    def body(p, frames, carry):
        total = conv_rows(table_ref, per_clip, pad_ref, lambda i, j: w_ref[3 * i + j], p, halo, row_len, nn if fold else nt)
        out_ref[pl.ds(p, BIG)] = total
        masked = total * tile_mask(frames, width)
        return carry[0] + down(masked), carry[1] + down(masked * total)

    a, b = sweep(table_ref, size, BIG, body, (jnp.zeros((8, width), F32),) * 2)
    osums_ref[0:1, 0:width], osums_ref[1:2, 0:width] = flat(a), flat(b)
    if not fold:
        osums_ref[:, width:] = more_ref[...]


def slow_first_kernel(table_ref, n_ref, xs_ref, lp_ref, lsums_ref, gains_ref, w_ref, wl_ref,
                      x_ref, lat_ref, sa_ref, sums_ref, first_ref, last_ref):
    size = lp_ref.shape[0]
    factor, shift, _, _ = scale_of(lsums_ref[:, 128:384], gains_ref[...], n_ref[0])

    def fill(p, frames, carry):
        mask = tile_mask(frames, 256)
        lat_ref[pl.ds(p, SMALL)] = (gelu(lp_ref[pl.ds(p, SMALL)] * factor[None] + shift[None]) * mask).astype(BF16)
        for z in range(4):
            v = xs_ref[z, pl.ds(p, SMALL)].astype(F32) * mask
            x_ref[pl.ds(p, SMALL), :, 256 * z : 256 * z + 256] = v.astype(BF16)
        return carry

    sweep(table_ref, size, SMALL, fill)

    def body(p, frames, carry):
        acc = nt(rows_bf(x_ref[pl.ds(p, BIG)]), w_ref[...]) + nt(rows_bf(lat_ref[pl.ds(p, BIG)]), wl_ref[...])
        acc = cells(acc)
        sa = later(acc[:, :, 0:256]) + acc[:, :, 256:512] + sooner(acc[:, :, 512:768])
        sa_ref[pl.ds(p, BIG)] = sa
        masked = sa * tile_mask(frames, 256)
        return carry[0] + down(masked), carry[1] + down(masked * sa)

    a, b = sweep(table_ref, size, BIG, body, (jnp.zeros((8, 256), F32),) * 2)
    sums_ref[0:1], sums_ref[1:2] = flat(a), flat(b)
    halo = first_ref.shape[0]
    first_ref[...], last_ref[...] = sa_ref[0:halo], sa_ref[size - halo : size]


def bypass_kernel(table_ref, x_ref, lat_ref, w_ref, wl_ref, sp_ref, sums_ref):
    def body(p, frames, carry):
        sp = cells(nn(rows_bf(x_ref[pl.ds(p, BIG)]), w_ref[...]) + nn(rows_bf(lat_ref[pl.ds(p, BIG)]), wl_ref[...]))
        sp_ref[pl.ds(p, BIG)] = sp.astype(BF16)
        masked = sp * tile_mask(frames, sp.shape[-1])
        return carry[0] + down(masked), carry[1] + down(masked * sp)

    a, b = sweep(table_ref, sp_ref.shape[0], BIG, body, (jnp.zeros((8, sp_ref.shape[2]), F32),) * 2)
    sums_ref[0:1], sums_ref[1:2] = flat(a), flat(b)


def expand_kernel(fold, offset, table_ref, n_ref, y_ref, sums_ref, gains_ref, w_ref, *refs):
    more, (h_ref, out_ref, osums_ref) = refs[:-3], refs[-3:]
    size, width = y_ref.shape[0], y_ref.shape[2]
    sums = sums_ref[:, offset : offset + width]
    sums = folded(sums) if fold else sums
    factor, shift, _, _ = scale_of(sums, gains_ref[...], n_ref[1 if fold else 0])

    def fill(p, frames, carry):
        v = gelu(y_ref[pl.ds(p, SMALL)] * factor[None] + shift[None])
        h_ref[pl.ds(p, SMALL)] = (v * tile_mask(frames, width)).astype(BF16)
        return carry

    sweep(table_ref, size, SMALL, fill)

    def body(p, frames, carry):
        out = cells(nn(rows_bf(h_ref[pl.ds(p, BIG)]), w_ref[...]))
        out_ref[pl.ds(p, BIG)] = out.astype(BF16)
        masked = out * tile_mask(frames, out.shape[-1])
        return carry[0] + down(masked), carry[1] + down(masked * out)

    wide_out = out_ref.shape[2]
    a, b = sweep(table_ref, size, BIG, body, (jnp.zeros((8, wide_out), F32),) * 2)
    osums_ref[0:1, 0:wide_out], osums_ref[1:2, 0:wide_out] = flat(a), flat(b)
    for ref in more:
        osums_ref[:, wide_out : wide_out + ref.shape[1]] = ref[...]
        wide_out += ref.shape[1]


def fast_out_kernel(offset, table_ref, n_ref, fc_ref, sums_ref, gains_ref, fx_ref, *refs):
    cots, (out_ref, up_ref, slopes_ref, vec_ref) = refs[: len(PARTS)], refs[len(PARTS) :]
    width = fc_ref.shape[2]
    vecs = scale_of(folded(sums_ref[:, offset : offset + width]), gains_ref[...], n_ref[1])
    for i, v in enumerate(vecs):
        vec_ref[i : i + 1] = v
    kept = (jnp.zeros((8, 128), F32),) * 2
    for part, ((k, begin), cot_ref) in enumerate(zip(PARTS, cots)):
        lanes = lanes_at(table_ref[5] ^ k, 128)
        fz, sz, cz, rz = (vec_ref[i : i + 1, lanes][None] for i in range(4))

        def body(p, frames, carry, k=k, lanes=lanes, fz=fz, sz=sz, cz=cz, rz=rz, cot_ref=cot_ref, begin=begin):
            here = pl.ds(begin + p, SMALL)
            y = fc_ref[here, :, lanes].astype(F32)
            mask = tile_mask(frames, 128)
            total = y * fz + sz + fx_ref[here, :, lanes].astype(F32)
            value, slope = gelu_pair(total)
            out_ref[k, here] = (value * mask).astype(BF16)
            up = slope * (cot_ref[pl.ds(p, SMALL), :, 0:128].astype(F32) * mask)
            up_ref[here, :, lanes] = up.astype(BF16)
            return carry[0] + down(up), carry[1] + down(up * ((y - cz) * rz))

        zero = (jnp.zeros((8, 128), F32),) * 2
        kept = sweep(table_ref, cot_ref.shape[0], SMALL, body, kept if begin else zero, begin)
        slopes_ref[0:1, lanes], slopes_ref[1:2, lanes] = flat(kept[0]), flat(kept[1])


def slow_out_kernel(table_ref, n_ref, sc_ref, sp_ref, sums_ref, gains_ref, *refs):
    count = len(PARTS)
    cots, (fast_ref, more_ref), outs = refs[:count], refs[count : count + 2], refs[count + 2 : 2 * count + 2]
    up_ref, slopes_ref, vec_ref = refs[2 * count + 2 :]
    width = sc_ref.shape[2]
    cf, cs, cc, cr = scale_of(sums_ref[:, 0:width], gains_ref[0:2], n_ref[0])
    pf, ps, pc, pr = scale_of(sums_ref[:, width : 2 * width], gains_ref[2:4], n_ref[0])
    for i, v in enumerate((cf, cs + ps, cc, cr, pf, pc, pr)):
        vec_ref[i : i + 1] = v
    kept = ()
    for (k, begin), cot_ref, out_ref in zip(PARTS, cots, outs):
        block = table_ref[5] ^ k
        lanes = lanes_at(block, 256)
        vecs = [vec_ref[i : i + 1, lanes][None] for i in range(7)]

        def body(p, frames, carry, k=k, lanes=lanes, vecs=vecs, cot_ref=cot_ref, out_ref=out_ref, begin=begin):
            cf, shift, cc, cr, pf, pc, pr = vecs
            here = pl.ds(begin + p, SMALL)
            yc, yp = (ref[here, :, lanes].astype(F32) for ref in (sc_ref, sp_ref))
            mask = tile_mask(frames, 256)
            value, slope = gelu_pair(yc * cf + yp * pf + shift)
            out_ref[pl.ds(p, SMALL), :, 128:384] = (value * mask).astype(BF16)
            out_ref[pl.ds(p, SMALL), :, 0:128] = fast_ref[k, here]
            up = slope * (cot_ref[pl.ds(p, SMALL), :, 128:384].astype(F32) * mask)
            up_ref[here, :, lanes] = up.astype(BF16)
            return (carry[0] + down(up), carry[1] + down(up * ((yc - cc) * cr)), carry[2] + down(up * ((yp - pc) * pr)))

        zero = (jnp.zeros((8, 256), F32),) * 3
        kept = sweep(table_ref, cot_ref.shape[0], SMALL, body, kept if begin else zero, begin)
        a, b, c = kept
        own, other = lanes, lanes_at(4 + block, 256)
        slopes_ref[0:1, own], slopes_ref[1:2, own] = flat(a), flat(b)
        slopes_ref[0:1, other], slopes_ref[1:2, other] = flat(a), flat(c)
    slopes_ref[:, 2 * width :] = more_ref[...]


def norm_back_fill(table_ref, up_ref, y_ref, dy_ref, factor, k0, k1):
    def fill(p, frames, carry):
        mask = tile_mask(frames, 128)
        for q in range(y_ref.shape[2] // 128):
            lanes = slice(128 * q, 128 * q + 128)
            y = y_ref[pl.ds(p, SMALL), :, lanes].astype(F32)
            dy = up_ref[pl.ds(p, SMALL), :, lanes].astype(F32) * factor[:, lanes][None]
            dy = dy - mask * (k0[:, lanes][None] + k1[:, lanes][None] * y)
            dy_ref[pl.ds(p, SMALL), :, lanes] = dy.astype(BF16)
        return carry

    sweep(table_ref, y_ref.shape[0], SMALL, fill)


def expand_back_kernel(fold, offsets, table_ref, n_ref, up_ref, y_ref, sums_ref, gains_ref, slopes_ref, z_ref, zsums_ref, zgains_ref,
                       w_ref, other_ref, dy_ref, dz_ref, oslopes_ref, first_ref, last_ref):
    size, width, inner = y_ref.shape[0], y_ref.shape[2], z_ref.shape[2]
    fix = folded if fold else (lambda v: v)
    inv_n = n_ref[1 if fold else 0]
    at_y, at_s, at_z = offsets
    factor, shift, center, inv_std = scale_of(fix(sums_ref[:, at_y : at_y + width]), gains_ref[...], inv_n)
    k0, k1 = slope_of(fix(slopes_ref[:, at_s : at_s + width]), factor, center, inv_std, inv_n)
    norm_back_fill(table_ref, up_ref, y_ref, dy_ref, factor, k0, k1)
    zf, zs, zc, zr = scale_of(fix(zsums_ref[:, at_z : at_z + inner]), zgains_ref[...], inv_n)

    def body(p, frames, carry):
        dh = cells(nt(rows_bf(dy_ref[pl.ds(p, BIG)]), w_ref[...]))
        z = z_ref[pl.ds(p, BIG)]
        dz = gelu_slope(z * zf[None] + zs[None]) * dh * tile_mask(frames, inner)
        dz_ref[pl.ds(p, BIG)] = dz
        return carry[0] + down(dz), carry[1] + down(dz * ((z - zc[None]) * zr[None]))

    a, b = sweep(table_ref, size, BIG, body, (jnp.zeros((8, inner), F32),) * 2)
    oslopes_ref[0:1, 0:inner], oslopes_ref[1:2, 0:inner] = flat(a), flat(b)
    halo = first_ref.shape[0]
    first_ref[:, :, 0:inner], last_ref[:, :, 0:inner] = dz_ref[0:halo], dz_ref[size - halo : size]
    if fold:
        wide_edge = inner + other_ref.shape[2]
        first_ref[:, :, inner:wide_edge], last_ref[:, :, inner:wide_edge] = other_ref[0:halo], other_ref[size - halo : size]
        first_ref[:, :, wide_edge:], last_ref[:, :, wide_edge:] = z_ref[0:halo], z_ref[size - halo : size]
    else:
        oslopes_ref[:, inner:] = other_ref[...]


def bypass_back_kernel(table_ref, n_ref, up_ref, y_ref, sums_ref, gains_ref, slopes_ref, w_ref, wl_ref, dy_ref, dx_ref, dl_ref):
    size, width = y_ref.shape[0], y_ref.shape[2]
    factor, shift, center, inv_std = scale_of(sums_ref[:, width : 2 * width], gains_ref[...], n_ref[0])
    k0, k1 = slope_of(slopes_ref[:, width : 2 * width], factor, center, inv_std, n_ref[0])
    norm_back_fill(table_ref, up_ref, y_ref, dy_ref, factor, k0, k1)

    def body(p, carry):
        dy = rows_bf(dy_ref[pl.ds(p, BIG)])
        dx_ref[pl.ds(p, BIG)] = cells(nt(dy, w_ref[...])).astype(BF16)
        dl_ref[pl.ds(p, BIG)] = cells(nt(dy, wl_ref[...]))
        return carry

    steps(size, BIG, body, 0)


def conv_back_kernel(halo, row_len, per_clip, fold, offsets, table_ref, n_ref, ysums_ref, ygains_ref, slopes_ref, ylo_ref, y_ref, yhi_ref,
                     dlo_ref, d_ref, dhi_ref, w_ref, z_ref, zsums_ref, zgains_ref, *refs):
    dy_ref, dz_ref, oslopes_ref, pad_ref = refs[-4:]
    size, width = y_ref.shape[0], y_ref.shape[2]
    fix = folded if fold else (lambda v: v)
    inv_n = n_ref[1 if fold else 0]
    at_y, at_s, at_z, at_yhalo, at_dhalo = offsets
    factor, shift, center, inv_std = scale_of(fix(ysums_ref[:, at_y : at_y + width]), ygains_ref[...], inv_n)
    k0, k1 = slope_of(fix(slopes_ref[:, at_s : at_s + width]), factor, center, inv_std, inv_n)

    def value(refs, p, step):
        y_of, d_of = refs
        if y_of is y_ref:
            y, d = y_of[pl.ds(p, step)], d_of[pl.ds(p, step)]
        else:
            y, d = y_of[pl.ds(p, step), :, at_yhalo : at_yhalo + width], d_of[pl.ds(p, step), :, at_dhalo : at_dhalo + width]
        return (d * factor[None] - (k0[None] + k1[None] * y)).astype(BF16).astype(F32)

    fill_padded(table_ref, ((ylo_ref, dlo_ref), (y_ref, d_ref), (yhi_ref, dhi_ref)), 0, pad_ref, value, halo, size)

    def copy(p, carry):
        dy_ref[pl.ds(p, SMALL)] = pad_ref[1, pl.ds(halo + p, SMALL)].astype(BF16)
        return carry

    steps(size, SMALL, copy, 0)
    zf, zs, zc, zr = scale_of(fix(zsums_ref[:, at_z : at_z + width]), zgains_ref[...], inv_n)

    def body(p, frames, carry):
        dh = conv_rows(table_ref, per_clip, pad_ref, lambda i, j: w_ref[8 - 3 * i - j], p, halo, row_len, nt if fold else nn)
        z = z_ref[pl.ds(p, BIG)]
        dz = gelu_slope(z * zf[None] + zs[None]) * dh * tile_mask(frames, width)
        dz_ref[pl.ds(p, BIG)] = dz
        return carry[0] + down(dz), carry[1] + down(dz * ((z - zc[None]) * zr[None]))

    a, b = sweep(table_ref, size, BIG, body, (jnp.zeros((8, width), F32),) * 2)
    oslopes_ref[0:1, 0:width], oslopes_ref[1:2, 0:width] = flat(a), flat(b)
    if not fold:
        oslopes_ref[:, width:] = refs[0][...]


def slow_back_kernel(table_ref, n_ref, dz_ref, y_ref, sums_ref, gains_ref, slopes_ref, w_ref, wl_ref, dx_ref, dl_ref,
                     lp_ref, lsums_ref, lgains_ref, taps_ref, out_ref, dzl_ref, oslopes_ref):
    size = y_ref.shape[0]
    factor, shift, center, inv_std = scale_of(sums_ref[:, 0:256], gains_ref[...], n_ref[0])
    k0, k1 = slope_of(slopes_ref[:, 0:256], factor, center, inv_std, n_ref[0])

    def fill(p, frames, carry):
        dy = dz_ref[pl.ds(p, SMALL)] * factor[None]
        dy = dy - tile_mask(frames, 256) * (k0[None] + k1[None] * y_ref[pl.ds(p, SMALL)])
        taps_ref[pl.ds(p, SMALL), :, 0:256] = sooner(dy).astype(BF16)
        taps_ref[pl.ds(p, SMALL), :, 256:512] = dy.astype(BF16)
        taps_ref[pl.ds(p, SMALL), :, 512:768] = later(dy).astype(BF16)
        return carry

    sweep(table_ref, size, SMALL, fill)
    lf, ls, lc, lr = scale_of(lsums_ref[:, 128:384], lgains_ref[...], n_ref[0])

    def body(p, frames, carry):
        taps = rows_bf(taps_ref[pl.ds(p, BIG)])
        mask = tile_mask(frames, 256)
        for z in range(4):
            lanes = slice(256 * z, 256 * z + 256)
            dx = cells(nn(taps, w_ref[:, lanes])) + dx_ref[pl.ds(p, BIG), :, lanes].astype(F32)
            out_ref[z, pl.ds(p, BIG)] = (dx * mask).astype(BF16)
        dl = cells(nn(taps, wl_ref[...])) + dl_ref[pl.ds(p, BIG)]
        y = lp_ref[pl.ds(p, BIG)]
        dz = gelu_slope(y * lf[None] + ls[None]) * dl * mask
        dzl_ref[pl.ds(p, BIG)] = dz
        return carry[0] + down(dz), carry[1] + down(dz * ((y - lc[None]) * lr[None]))

    a, b = sweep(table_ref, size, BIG, body, (jnp.zeros((8, 256), F32),) * 2)
    oslopes_ref[0:1], oslopes_ref[1:2] = flat(a), flat(b)


def fast_back_kernel(at_s, table_ref, n_ref, sums_ref, fgains_ref, lgains_ref, fslopes_ref, lslopes_ref, dzf_ref, fa_ref, dzl_ref, lp_ref,
                     up_ref, w_ref, taps_ref, out_ref):
    size = fa_ref.shape[0]
    ff, fs, fc, fr = scale_of(folded(sums_ref[:, 0:128]), fgains_ref[...], n_ref[1])
    f0, f1 = slope_of(folded(fslopes_ref[:, at_s : at_s + 128]), ff, fc, fr, n_ref[1])
    lf, ls, lc, lr = scale_of(sums_ref[:, 128:384], lgains_ref[...], n_ref[0])
    l0, l1 = slope_of(lslopes_ref[...], lf, lc, lr, n_ref[0])

    def fill(p, frames, carry):
        dy = dzf_ref[pl.ds(p, SMALL)] * ff[None]
        dy = dy - tile_mask(frames, 128) * (f0[None] + f1[None] * fa_ref[pl.ds(p, SMALL)])
        taps_ref[pl.ds(p, SMALL), :, 0:128] = dy.astype(BF16)
        taps_ref[pl.ds(p, SMALL), :, 128:256] = sooner(dy).astype(BF16)
        taps_ref[pl.ds(p, SMALL), :, 256:384] = later(dy).astype(BF16)
        dy = dzl_ref[pl.ds(p, SMALL)] * lf[None]
        dy = dy - tile_mask(frames, 256) * (l0[None] + l1[None] * lp_ref[pl.ds(p, SMALL)])
        taps_ref[pl.ds(p, SMALL), :, 384:640] = dy.astype(BF16)
        taps_ref[pl.ds(p, SMALL), :, 640:896] = sooner(dy).astype(BF16)
        return carry

    sweep(table_ref, size, SMALL, fill)

    def body(p, frames, carry):
        dx = cells(nn(rows_bf(taps_ref[pl.ds(p, BIG)]), w_ref[...]))
        mask = tile_mask(frames, 128)
        for z in range(4):
            lanes = slice(128 * z, 128 * z + 128)
            out_ref[z, pl.ds(p, BIG)] = ((dx[:, :, lanes] + up_ref[pl.ds(p, BIG), :, lanes].astype(F32)) * mask).astype(BF16)
        return carry

    sweep(table_ref, size, BIG, body)


def tn(a, b):
    return lax.dot_general(a, b, (((0,), (0,)), ((), ())), preferred_element_type=F32)


def chunks(size):
    return range(0, size, BIG)


def added(acc_ref, at, part, first):
    acc_ref[at] = part if first else acc_ref[at] + part


def conv_weight(halo, row_len, per_clip, fold, table_ref, act_ref, dy_ref, pad_ref, acc_ref):
    size = dy_ref.shape[0]
    phase = table_ref[5] * (size // SMALL)

    def copy(p, carry):
        v = act_ref[pl.ds(p, 3)].astype(F32)
        for k in range(3):
            pad_ref[k, pl.ds(p, 3)] = v
        return carry

    steps(size + 2 * halo, 3, copy, 0)
    parts = size // SMALL

    def clear(i, carry):
        even = ((phase + i) % 2 == 0).astype(F32)
        at = halo + (i - 2) * SMALL
        pad_ref[0, pl.ds(at + SMALL - 1, 1)] = pad_ref[0, pl.ds(at + SMALL - 1, 1)] * even
        pad_ref[2, pl.ds(at, 1)] = pad_ref[2, pl.ds(at, 1)] * (1.0 - even)
        return carry

    lax.fori_loop(0, parts + 4, clear, 0)
    low_even = ((phase + 1) % 2 == 0).astype(F32)
    pad_ref[0, 0:1] = pad_ref[0, 0:1] * low_even
    high_even = ((phase + parts) % 2 == 0).astype(F32)
    end = size + 2 * halo
    pad_ref[2, end - 1 : end] = pad_ref[2, end - 1 : end] * (1.0 - high_even)

    for p in chunks(size):
        top, bottom = edge_scales(table_ref, p, per_clip)
        dy = rows_bf(dy_ref[p : p + BIG])
        for i in range(3):
            begin = p + halo + row_len * (i - 1)
            taps = []
            for j in range(3):
                v = pad_ref[j, begin + j - 1 : begin + j - 1 + BIG]
                if i == 0:
                    v = jnp.concatenate([v[0:row_len] * top, v[row_len:]], axis=0)
                if i == 2:
                    v = jnp.concatenate([v[: BIG - row_len], v[BIG - row_len :] * bottom], axis=0)
                taps.append(rows(v).astype(BF16))
            taps = jnp.concatenate(taps, axis=1)
            added(acc_ref, i, tn(taps, dy) if fold else tn(dy, taps), p == 0)


def by_share(v):
    return v.reshape(4, 4, 2, 8, v.shape[1]).transpose(2, 1, 0, 3, 4).astype(BF16)


def first_slab_kernel(hb_ref, dsc_ref, x_ref, lat_ref, dsp_ref, out_ref, acc_ref):
    for p in chunks(hb_ref.shape[0]):
        at = slice(p, p + BIG)
        dsc, dsp = rows_bf(dsc_ref[at]), rows_bf(dsp_ref[at])
        added(acc_ref, 4, tn(rows_bf(hb_ref[at]), dsc), p == 0)
        added(acc_ref, 5, tn(rows_bf(lat_ref[at]), dsp), p == 0)
        for z in range(4):
            added(acc_ref, z, tn(rows_bf(x_ref[at, :, 256 * z : 256 * z + 256]), dsp), p == 0)
    out_ref[:, :, :, 0], out_ref[:, :, :, 5] = by_share(acc_ref[4]), by_share(acc_ref[5])
    for z in range(4):
        part = acc_ref[z].reshape(4, 2, 4, 8, 1024).astype(BF16)
        for core in range(2):
            out_ref[core, :, z, 1:5] = part[:, core]


def second_slab_kernel(halo, row_len, per_clip, table_ref, act_ref, dy_ref, taps_ref, x_ref, lat_ref, out_ref, pad_ref, acc_ref, red_ref,
                       lred_ref):
    conv_weight(halo, row_len, per_clip, False, table_ref, act_ref, dy_ref, pad_ref, acc_ref)
    for k in range(9):
        at, lane = (3, 768) if k == 8 else (4 + k // 4, 256 * (k % 4))
        out_ref[:, :, :, at, :, lane : lane + 256] = by_share(acc_ref[k // 3, :, 256 * (k % 3) : 256 * (k % 3) + 256])
    for p in chunks(dy_ref.shape[0]):
        at = slice(p, p + BIG)
        x, lat = rows_bf(x_ref[at]), rows_bf(lat_ref[at])
        for j in range(3):
            taps = rows_bf(taps_ref[at, :, 256 * j : 256 * j + 256])
            added(red_ref, j, tn(taps, x), p == 0)
            added(lred_ref, j, tn(taps, lat), p == 0)
    for j in range(3):
        out_ref[:, :, :, j] = by_share(red_ref[j])
        out_ref[:, :, :, 3, :, 256 * j : 256 * j + 256] = by_share(lred_ref[j])


def fast_grads_kernel(halo, row_len, per_clip, table_ref, act_ref, dy_ref, taps_ref, fx_ref, h_ref, dfc_ref, lat_ref, out_ref,
                      pad_ref, sp_ref, first_ref, ex_ref):
    conv_weight(halo, row_len, per_clip, True, table_ref, act_ref, dy_ref, pad_ref, sp_ref)
    for p in chunks(dy_ref.shape[0]):
        at = slice(p, p + BIG)
        added(first_ref, slice(0, 896), tn(rows_bf(taps_ref[at]), rows_bf(fx_ref[at])), p == 0)
        added(ex_ref, slice(0, 128), tn(rows_bf(h_ref[at]), rows_bf(dfc_ref[at])), p == 0)

    def gather(at, count, r, ref=first_ref):
        return sum(lane_group(moved(ref[at : at + count, 128 * z : 128 * z + 128], 32 * z - 32 * r), z) for z in range(4))

    taps = [gather(640, 256, 2), gather(640, 256, 3), gather(384, 256, 0), gather(384, 256, 1), gather(384, 256, 2)]
    for j in range(5):
        lat_ref[:, 8 * j : 8 * j + 8] = taps[j].reshape(4, 8, 8, 128).astype(BF16)

    def tiles(first, v):
        for i in range(v.shape[0] // 8):
            out_ref[first + i] = v[8 * i : 8 * i + 8].astype(BF16)

    for j in range(3):
        total = sum(gather(32 * q, 32, q + j - 1) for q in range(4) if 0 <= q + j - 1 < 4)
        if j == 0:
            total = total + gather(128, 32, 3)
        if j == 2:
            total = total + gather(352, 32, 0)
        tiles(4 * j, total)
    tiles(12, sum(gather(32 * r, 32, r, ex_ref) for r in range(4)))
    for i in range(3):
        total = None
        for j in range(3):
            tap = sum(
                lane_group(moved(sp_ref[i, 128 * j + 32 * r : 128 * j + 32 * r + 32, :], 32 * j - 32 * r), j) for r in range(4)
            )
            total = tap if total is None else total + tap
        tiles(16 + 4 * i, total)


def swap(tree, axis, size, distance):
    pairs = [(i, i ^ distance) for i in range(size)]
    return jax.tree.map(lambda v: lax.ppermute(v, axis, pairs), tree)


def add(*trees):
    def total(*vs):
        wide_vs = [v.astype(F32) for v in vs]
        out = wide_vs[0] + wide_vs[1]
        if len(vs) == 4:
            out = out + (wide_vs[2] + wide_vs[3])
        return out.astype(vs[0].dtype)

    return jax.tree.map(total, *trees)


def stages(size, first_alone):
    bits = [1 << i for i in range(size.bit_length() - 1)]
    out = []
    if first_alone and bits:
        out.append(bits[:1])
        bits = bits[1:]
    while bits:
        out.append(bits[:2])
        bits = bits[2:]
    return out


def butterfly(tree, axis, size, bits):
    if len(bits) == 1:
        return add(tree, swap(tree, axis, size, bits[0]))
    near, far, both = (swap(tree, axis, size, k) for k in (bits[0], bits[1], bits[0] + bits[1]))
    return add(tree, near, far, both)


def everywhere(tree, sizes, bulk=None, chan_last=False):
    dp, chan = sizes["dp"], sizes["chan"]
    first, *others = stages(dp, True)
    before, behind = (others, []) if chan_last else ([], others)
    for bits in [first, *before]:
        tree = butterfly(tree, "dp", dp, bits)
    if bulk is not None:
        tree = after(tree, bulk)
    for bits in stages(chan, False):
        tree = butterfly(tree, "chan", chan, bits)
    passed = tree
    for bits in behind:
        tree = butterfly(tree, "dp", dp, bits)
    return tree, passed


def halos(first, last, count):
    low = lax.ppermute(last, "chan", [(i, i + 1) for i in range(count - 1)])
    high = lax.ppermute(first, "chan", [(i + 1, i) for i in range(count - 1)])
    return low, high


def gather_chips(v, sizes):
    return [v] + [swap(v, "dp", sizes["dp"], 2 * k) for k in (1, 2, 3)]


def gather_cores(own, sizes):
    return jnp.stack(own), jnp.stack([swap(v, "dp", sizes["dp"], 1) for v in own])


def pick(v, index, axis):
    return lax.dynamic_index_in_dim(v, index, axis, keepdims=False)


def scatter_cores(v, sizes, group):
    sent, kept = pick(v, 1 - group % 2, 0), pick(v, group % 2, 0)
    got = jnp.concatenate([swap(sent[:2], "dp", sizes["dp"], 1), swap(sent[2:], "dp", sizes["dp"], 1)])
    return add(kept, got)


def scatter_chips(v, sizes, group):
    chip = group // 2
    got = [swap(pick(v, chip ^ k, 0), "dp", sizes["dp"], 2 * k) for k in (1, 2, 3)]
    return add(pick(v, chip, 0), *got)


def scatter_chan(tree, sizes, chan, gate):
    size, dp = sizes["chan"], sizes["dp"]
    got = [swap(jax.tree.map(lambda v: pick(v, chan ^ k, 0), tree), "chan", size, k) for k in (1, 2, 3)]
    tree = add(jax.tree.map(lambda v: pick(v, chan, 0), tree), *after(got, gate))
    bits = [1 << i for i in range(3, dp.bit_length() - 1)]
    while bits:
        tree = butterfly(tree, "dp", dp, bits[:2])
        bits = bits[2:]
    return tree


def after(tree, gate):
    return lax.optimization_barrier((tree, gate))[0]


def local(
    sizes,
    slow_input,
    fast_input,
    clip_counts,
    frame_counts,
    fast_reduce,
    fast_spatial,
    fast_expand,
    lateral_kernel,
    slow_reduce,
    lateral_reduce,
    slow_spatial,
    slow_expand,
    shortcut,
    lateral_shortcut,
    fast_inner_norm,
    fast_outer_norm,
    lateral_norm,
    slow_inner_norm,
    slow_outer_norm,
    slow_cotangent,
    fast_cotangent,
):
    ways = sizes["chan"]
    clips, slow_t, height, across, slow_part = slow_input.shape
    fast_t, fast_part = fast_input.shape[1], fast_input.shape[4]
    ratio = fast_t // slow_t
    area = height * across
    places = clips * area
    mine = places // ways
    halo = across + 1
    chan, dp = lax.axis_index("chan"), lax.axis_index("dp")
    group = dp % 8
    ids = jnp.stack([dp, chan, group]).astype(jnp.int32)
    wide_in = ways * slow_part
    wide_f = ways * 128
    mid = 256
    ext = mine + 2 * halo
    per_clip = area // BIG
    chunk = 98

    def packed(v, slow=None):
        v = v.transpose(0, 2, 3, 1, 4).reshape(places, fast_t, fast_part)
        more = [] if slow is None else [slow.reshape(places, slow_t, slow_part)]
        width = 128 if slow is None else 128 + slow_part
        return pl.pallas_call(
            functools.partial(pack_kernel, area // chunk, clips),
            grid=(places // chunk,),
            out_shape=shape((places, slow_t, width), BF16),
            in_specs=[pl.BlockSpec(memory_space=pltpu.SMEM)] * 3
            + [pl.BlockSpec((chunk, *u.shape[1:]), lambda i: (i, 0, 0)) for u in (v, *more)],
            out_specs=pl.BlockSpec((chunk, slow_t, width), lambda i: (i, 0, 0)),
            scratch_shapes=[pltpu.VMEM((chunk * fast_t, fast_part), F32)],
            compiler_params=pltpu.CompilerParams(vmem_limit_bytes=16 * 1024 * 1024),
            name="fast_pack",
        )(ids, clip_counts, frame_counts, v, *more).reshape(ways, mine, slow_t, width)

    def unpacked(parts):
        slow, fast = call(
            unpack_kernel,
            [shape((places, slow_t, slow_part), BF16), shape((places, fast_t, fast_part), BF16)],
            [ids, *parts],
            [pltpu.VMEM((BIG * fast_t, fast_part), F32)],
            smem=1,
            name="outputs",
        )
        return joined(slow), fast.reshape(clips, height, across, fast_t, fast_part).transpose(0, 3, 1, 2, 4)

    def split(v):
        return v.transpose(0, 2, 3, 1, 4).reshape(ways, mine, slow_t, slow_part)

    def joined(v):
        return v.reshape(clips, height, across, slow_t, slow_part).transpose(0, 3, 1, 2, 4)

    def at_once(v):
        return [v[0]] + [swap(v[k], "chan", ways, k) for k in range(1, ways)]

    def blocks_of(v):
        return [pick(v, chan ^ k, 0) for k in range(ways)]

    def all_to_all(v):
        return lax.all_to_all(v, "chan", 0, 0, tiled=True)

    def parted(blocks):
        bounds = PARTS + ((len(blocks), 0),)
        ends = [b[1] if a[0] == b[0] else mine for a, b in zip(bounds, bounds[1:])]
        return [blocks[k][begin:end] for (k, begin), end in zip(PARTS, ends)]

    def send_parts(parts, which, gate):
        for i in which:
            parts[i] = swap(after(parts[i], gate), "chan", ways, PARTS[i][0])


    all_clips = frame_counts.shape[0]
    live = (jnp.arange(all_clips, dtype=jnp.int32) % clips) < jnp.repeat(clip_counts, clips)
    valid = jnp.where(live, frame_counts, 0)
    count = jnp.sum(valid).astype(F32) * area
    inv_n = jnp.stack([1.0 / count, 1.0 / (count * ratio)])
    parts = mine // BIG
    clip = (chan * parts + jnp.arange(-1, parts + 1)) // per_clip
    clip = jnp.clip(clip, 0, clips - 1) + dp * clips
    around = jnp.sum(jnp.where(clip[:, None] == jnp.arange(all_clips)[None, :], valid[None, :], 0), axis=1)
    table = jnp.concatenate([around, jnp.stack([chan, jnp.full_like(chan, parts)])]).astype(jnp.int32)

    lat_t, red_t, lred_t = (v.transpose(0, 2, 1) for v in (lateral_kernel, slow_reduce, lateral_reduce))
    spatial_t = slow_spatial.reshape(9, slow_spatial.shape[2], -1).transpose(0, 2, 1)
    params = [red_t, lred_t, lat_t, slow_expand, shortcut, lateral_shortcut, spatial_t]
    scratch = [(3, 8, wide_in), (3, 8, mid), (5, 8, 128), (8, wide_in), (32, wide_in), (8, wide_in), (9, 8, mid)]
    small = [lateral_norm, slow_inner_norm, slow_outer_norm]
    any_spec, vmem_spec = pl.BlockSpec(memory_space=pl.ANY), pl.BlockSpec(memory_space=pltpu.VMEM)
    slab = pl.pallas_call(
        weight_slab_kernel,
        out_shape=shape((14, 8, wide_in), BF16),
        in_specs=[pl.BlockSpec(memory_space=pltpu.SMEM)] + [any_spec] * 7 + [vmem_spec] * 3,
        out_specs=vmem_spec,
        scratch_shapes=[pltpu.VMEM(dims, F32) for dims in scratch] + [pltpu.SemaphoreType.DMA((7,))],
        compiler_params=pltpu.CompilerParams(vmem_limit_bytes=58 * 1024 * 1024),
        name="weight_slab",
    )(ids, *params, *small)
    slabs = at_once([slab] * ways)
    fx_pieces = at_once(after(blocks_of(packed(after(fast_input, slab))), slabs))
    early, late = jnp.stack([v[0:5] for v in slabs]), jnp.stack([v[5:14] for v in slabs])
    early = gather_chips(early, sizes)
    xs = all_to_all(after(split(slow_input), (fx_pieces, early)))
    own_slabs, other_slabs = gather_cores(early, sizes)
    fr_t = fast_reduce.transpose(0, 2, 1)
    red_w, lred_w, w_first, w_fsp, w_fex, fin_g, fout_g, mid_g, out_g = call(
        weights_kernel,
        [
            shape((3, ways, 8, 8, wide_in), BF16),
            shape((3, ways, 8, 8, mid), BF16),
            shape((896, wide_f), BF16),
            shape((9, 128, 128), BF16),
            shape((128, wide_f), BF16),
            shape((4, 128)),
            shape((2, wide_f)),
            shape((8, mid)),
            shape((ways, 4, mid)),
        ],
        [ids, own_slabs, other_slabs, fr_t, fast_spatial.reshape(9, *fast_spatial.shape[2:]), fast_expand,
         fast_inner_norm.reshape(4, -1), fast_outer_norm],
        [pltpu.VMEM((5, ways, 8, 8, 128), F32)],
        smem=1,
        name="weights",
    )
    red_w, lred_w = red_w.reshape(-1, wide_in), lred_w.reshape(-1, mid)
    fin_g = (fin_g[0:2], fin_g[2:4])
    lat_g, in_g = mid_g[0:2], (mid_g[2:4], mid_g[4:6])
    out_g = out_g.transpose(1, 0, 2).reshape(4, wide_in)

    edge = [shape((halo, 8, 128))] * 2
    edges = [shape((halo, 8, 512))] * 2
    narrow, middle = shape((mine, 8, 128)), shape((mine, 8, mid))
    fx, fa, lp, sums1, first, last = call(
        fast_first_kernel,
        [shape((mine, 8, wide_f), BF16), narrow, middle, shape((2, 384)), *edge],
        [table, *fx_pieces, w_first],
        smem=1,
        name="fast_first",
    )
    fa_lo, fa_hi = halos(first, last, ways)
    cots = parted(blocks_of(packed(fast_cotangent, split(slow_cotangent))))
    late = gather_chips(after(late, other_slabs), sizes)
    own_late, other_late = gather_cores(late, sizes)
    exp_w, short_w, lshort_w, spat_w = call(
        more_weights_kernel,
        [
            shape((ways, 8, 8, wide_in), BF16),
            shape((ways, 8, 4, 8, wide_in), BF16),
            shape((ways, 8, 8, wide_in), BF16),
            shape((9, ways, 8, 8, mid), BF16),
        ],
        [ids, own_late, other_late],
        smem=1,
        name="more_weights",
    )
    exp_w, short_w, lshort_w = (v.reshape(-1, wide_in) for v in (exp_w, short_w, lshort_w))
    spat_w = spat_w.reshape(9, mid, mid)
    sums1, passed = everywhere(sums1, sizes, (xs, fa_lo, fa_hi, cots, late), True)
    send_parts(cots, (2,), passed)
    fast_pad = [pltpu.VMEM((3, ext, 8, 128), F32)]
    slow_pad = [pltpu.VMEM((3, ext, 8, mid), F32)]
    x, lat, sa, sums2, first, last = call(
        slow_first_kernel,
        [shape((mine, 8, wide_in), BF16), shape((mine, 8, mid), BF16), middle, shape((2, mid)), *[shape((halo, 8, mid))] * 2],
        [table, inv_n, xs, lp, sums1, lat_g, red_w, lred_w],
        smem=2,
        name="slow_first",
    )
    sa_lo, sa_hi = halos(first, last, ways)
    fa_late = after(fa, sums2)
    h1, fb, fb_sums = call(
        functools.partial(conv_kernel, halo, across, per_clip, True, (0, 0)),
        [shape((ext, 8, 128), BF16), narrow, shape((2, 128))],
        [table, inv_n, sums1, fin_g[0], fa_lo, fa_late, fa_hi, w_fsp],
        fast_pad,
        smem=2,
        name="fast_second",
    )
    sums2, passed = everywhere(sums2, sizes, (cots[2], sa_lo, sa_hi))
    send_parts(cots, (3, 4, 1), passed)
    ha, sb, sums3 = call(
        functools.partial(conv_kernel, halo, across, per_clip, False, (0, 0)),
        [shape((ext, 8, mid), BF16), middle, shape((2, mid + 128))],
        [table, inv_n, sums2, in_g[0], sa_lo, sa, sa_hi, spat_w, fb_sums],
        slow_pad,
        smem=2,
        name="slow_second",
    )
    sums3, passed = everywhere(sums3, sizes, (cots[3], cots[4], cots[1]))
    send_parts(cots, (5,), passed)
    sp, sp_sums = call(
        bypass_kernel,
        [shape((mine, 8, wide_in), BF16), shape((2, wide_in))],
        [table, x, lat, short_w, lshort_w],
        smem=1,
        name="bypass",
    )
    h2, fc, fc_sums = call(
        functools.partial(expand_kernel, True, mid),
        [shape((mine, 8, 128), BF16), shape((mine, 8, wide_f), BF16), shape((2, wide_f))],
        [table, inv_n, fb, sums3, fin_g[1], w_fex],
        smem=2,
        name="fast_third",
    )
    hb, sc, sums4 = call(
        functools.partial(expand_kernel, False, 0),
        [shape((mine, 8, mid), BF16), shape((mine, 8, wide_in), BF16), shape((2, 2 * wide_in + wide_f))],
        [table, inv_n, sb, sums3, in_g[1], exp_w, sp_sums, fc_sums],
        smem=2,
        name="slow_third",
    )
    sums4, _ = everywhere(sums4, sizes, cots[5])
    fast_out, dfs, fc_slopes = call(
        functools.partial(fast_out_kernel, 2 * wide_in),
        [shape((ways, mine, 8, 128), BF16), shape((mine, 8, wide_f), BF16), shape((2, wide_f))],
        [table, inv_n, fc, sums4, fout_g, fx, *cots],
        [pltpu.VMEM((8, wide_f), F32)],
        smem=2,
        name="fast_out",
    )
    *outs, dss, sums5 = call(
        slow_out_kernel,
        [*[shape(c.shape, BF16) for c in cots], shape((mine, 8, wide_in), BF16), shape((2, 2 * wide_in + wide_f))],
        [table, inv_n, sc, sp, sums4, out_g, *cots, fast_out, fc_slopes],
        [pltpu.VMEM((8, wide_in), F32)],
        smem=2,
        name="slow_out",
    )

    sums5, passed = everywhere(sums5, sizes)
    send_parts(outs, (2,), passed)
    dfc, dzfb, fb_slopes, first, last = call(
        functools.partial(expand_back_kernel, True, (2 * wide_in, 2 * wide_in, mid)),
        [shape((mine, 8, wide_f), BF16), narrow, shape((2, 128)), *edges],
        [table, inv_n, dfs, fc, sums4, fout_g, sums5, fb, sums3, fin_g[1], w_fex, sb],
        smem=2,
        name="fast_third_back",
    )
    low6, high6 = halos(first, last, ways)
    dsc, dzsb, sums6, first, last = call(
        functools.partial(expand_back_kernel, False, (0, 0, 0)),
        [shape((mine, 8, wide_in), BF16), middle, shape((2, mid + 128)), *[shape((halo, 8, mid))] * 2],
        [table, inv_n, dss, sc, sums4, out_g[0:2], sums5, sb, sums3, in_g[1], exp_w, fb_slopes],
        smem=2,
        name="slow_third_back",
    )
    low_sb, high_sb = halos(first, last, ways)
    sums6, passed = everywhere(sums6, sizes, (outs[2], low6, high6, low_sb, high_sb))
    send_parts(outs, (3, 4, 1), passed)
    dfb, dzfa, fa_slopes = call(
        functools.partial(conv_back_kernel, halo, across, per_clip, True, (mid, mid, 0, 384, 0)),
        [shape((mine, 8, 128), BF16), narrow, shape((2, 128))],
        [table, inv_n, sums3, fin_g[1], sums6, low6, fb, high6, low6, dzfb, high6, w_fsp, fa, sums1, fin_g[0]],
        fast_pad,
        smem=2,
        name="fast_second_back",
    )
    dsb, dzsa, sums7 = call(
        functools.partial(conv_back_kernel, halo, across, per_clip, False, (0, 0, 0, 128, 0)),
        [shape((mine, 8, mid), BF16), middle, shape((2, mid + 128))],
        [table, inv_n, sums3, in_g[1], sums6, low6, sb, high6, low_sb, dzsb, high_sb, spat_w, sa, sums2, in_g[0], fa_slopes],
        slow_pad,
        smem=2,
        name="slow_second_back",
    )
    dss_late, = after((dss,), sums7)
    dsp, dx, dl = call(
        bypass_back_kernel,
        [shape((mine, 8, wide_in), BF16), shape((mine, 8, wide_in), BF16), middle],
        [table, inv_n, dss_late, sp, sums4, out_g[2:4], sums5, short_w, lshort_w],
        smem=2,
        name="bypass_back",
    )

    sums7, passed = everywhere(sums7, sizes, (outs[3], outs[4], outs[1], dx, dl))
    send_parts(outs, (5,), passed)
    dsa, dslow, dzlp, sums8 = call(
        slow_back_kernel,
        [shape((mine, 8, 3 * mid), BF16), shape((ways, mine, 8, mid), BF16), middle, shape((2, mid))],
        [table, inv_n, dzsa, sa, sums2, in_g[0], sums7, red_w, lred_w, dx, dl, lp, sums1, lat_g],
        smem=2,
        name="slow_first_back",
    )
    dsc_late, dsp = after((dsc, dsp), sums8)
    (slab1,) = call(
        first_slab_kernel,
        [shape((2, 4, ways, 6, 8, wide_in), BF16)],
        [hb, dsc_late, x, lat, dsp],
        [pltpu.VMEM((6, mid, wide_in), F32)],
        name="first_slab",
    )
    sums8, passed = everywhere(sums8, sizes, (outs[5], slab1))
    dslow = all_to_all(after(dslow, passed))
    slab1 = scatter_cores(slab1, sizes, group)
    dsa, dsb_late = after((dsa, dsb), (sums8, slab1))
    (slab2,) = call(
        functools.partial(second_slab_kernel, halo, across, per_clip),
        [shape((2, 4, ways, 6, 8, wide_in), BF16)],
        [table, ha, dsb_late, dsa, x, lat],
        [*slow_pad, pltpu.VMEM((3, mid, 3 * mid), F32), pltpu.VMEM((3, mid, wide_in), F32), pltpu.VMEM((3, mid, mid), F32)],
        smem=1,
        name="second_slab",
    )
    slab1 = scatter_chips(slab1, sizes, group)
    slab2 = scatter_cores(slab2, sizes, group)
    dzlp = after(dzlp, slab2)
    slab2 = scatter_chips(slab2, sizes, group)
    dfirst, dfast = call(
        functools.partial(fast_back_kernel, mid),
        [shape((mine, 8, 896), BF16), shape((ways, mine, 8, 128), BF16)],
        [table, inv_n, sums1, fin_g[0], lat_g, sums7, sums8, dzfa, fa, dzlp, lp, dfs, w_first],
        smem=2,
        name="fast_first_back",
    )

    g_lat, g_fast = call(
        functools.partial(fast_grads_kernel, halo, across, per_clip),
        [shape((ways, 40, 8, 128), BF16), shape((28, 8, 128), BF16)],
        [table, h1, dfb, dfirst, fx, h2, dfc],
        [*fast_pad, pltpu.VMEM((3, 384, 128), F32), pltpu.VMEM((896, wide_f), F32), pltpu.VMEM((128, wide_f), F32)],
        smem=1,
        name="fast_grads",
    )
    (slow_input_grad,) = call(
        copy_kernel, [shape((places, slow_t, slow_part), BF16)], [dslow.reshape(places, slow_t, slow_part)], name="slow_grad"
    )
    slow_output, fast_output = unpacked(after(outs, slow_input_grad))
    slab1 = scatter_chan(slab1, sizes, chan, dfirst)
    slab2 = scatter_chan(after(slab2, slab1), sizes, chan, slab1)
    slabs = jnp.concatenate([slab1, slab2])
    small = [jnp.concatenate([pick(g_lat, chan ^ k, 0), g_fast]) for k in range(ways)]
    small = add(*at_once(small))
    dfast = all_to_all(after(dfast, (dslow, slabs, small)))
    for bits in stages(sizes["dp"], True):
        small = butterfly(small, "dp", sizes["dp"], bits)
    g_lat, g_fast = small[0:40].astype(F32), small[40:68].astype(F32)
    own_slabs, other_slabs = gather_cores(after(gather_chips(slabs, sizes), (slow_output, fast_output)), sizes)
    g_exp, g_short, g_lshort, g_red, g_lred, g_spat = call(
        grads_kernel,
        [shape((8, 8, wide_in)), shape((8, 4, 8, wide_in)), shape((8, 8, wide_in)), shape((3, 8, 8, wide_in)), shape((3, 8, 8, mid)),
         shape((9, 8, 8, mid))],
        [ids, own_slabs, other_slabs],
        smem=1,
        name="grads",
    )
    slow_input_grad = joined(slow_input_grad)
    fast_input_grad = pl.pallas_call(
        unpack_fast_kernel,
        grid=(places // chunk,),
        out_shape=shape((places, fast_t, fast_part), BF16),
        in_specs=[pl.BlockSpec((chunk, slow_t, 128), lambda i: (i, 0, 0))],
        out_specs=pl.BlockSpec((chunk, fast_t, fast_part), lambda i: (i, 0, 0)),
        scratch_shapes=[pltpu.VMEM((chunk * fast_t, fast_part), F32)],
        compiler_params=pltpu.CompilerParams(vmem_limit_bytes=16 * 1024 * 1024),
        name="fast_unpack",
    )(dfast.reshape(places, slow_t, 128))
    fast_input_grad = fast_input_grad.reshape(clips, height, across, fast_t, fast_part).transpose(0, 3, 1, 2, 4)
    g_fred = g_fast[0:12].reshape(3, 32, 128).transpose(0, 2, 1)
    g_fex = g_fast[12:16].reshape(32, 128)
    g_fsp = g_fast[16:28].reshape(3, 32, 128)[:, :, 0:96].reshape(3, 32, 3, 32).transpose(0, 2, 1, 3)

    def pair(slopes):
        return slopes[::-1]

    def own(v, width):
        return lax.dynamic_slice_in_dim(v, chan * width, width, v.ndim - 1)

    def fold_in(slopes):
        return jnp.sum(slopes.reshape(2, ratio, 128 // ratio), axis=1)

    lw, sw, ow = lateral_norm.shape[1], slow_inner_norm.shape[2], slow_outer_norm.shape[2]
    fast_inner_grad = jnp.stack([pair(fold_in(sums7[:, mid:])), pair(fold_in(sums6[:, mid:]))])
    fc_slopes = sums5[:, 2 * wide_in :].reshape(2, ways, ratio, fast_part)
    fast_outer_grad = pair(jnp.sum(fc_slopes, axis=2).reshape(2, -1))
    lateral_grad = pair(own(sums8, lw))
    slow_inner_grad = own(jnp.stack([pair(sums7[:, 0:mid]), pair(sums6[:, 0:mid])]), sw)
    slow_outer_grad = own(jnp.stack([pair(sums5[:, 0:wide_in]), pair(sums5[:, wide_in : 2 * wide_in])]), ow)
    return (
        slow_output,
        fast_output,
        slow_input_grad,
        fast_input_grad,
        g_fred,
        g_fsp,
        g_fex,
        g_lat.reshape(5, -1, 128).transpose(0, 2, 1),
        g_red.reshape(3, -1, wide_in).transpose(0, 2, 1),
        g_lred.reshape(3, -1, mid).transpose(0, 2, 1),
        g_spat.reshape(9, -1, mid).transpose(0, 2, 1).reshape(slow_spatial.shape),
        g_exp.reshape(-1, wide_in),
        g_short.reshape(-1, wide_in),
        g_lshort.reshape(-1, wide_in),
        fast_inner_grad,
        fast_outer_grad,
        lateral_grad,
        slow_inner_grad,
        slow_outer_grad,
    )


def solution(mesh):
    sizes = {"dp": mesh.shape["dp"], "chan": mesh.shape["chan"]}
    big = P("dp", None, None, None, "chan")
    last2, last3, last4 = P(None, "chan"), P(None, None, "chan"), P(None, None, None, "chan")
    first = P("chan", None)
    return jax.shard_map(
        functools.partial(local, sizes),
        mesh=mesh,
        in_specs=(
            big, big, P(), P(), P(), P(), P(), last3, last3, last3, last4, first, first, first,
            P(), P(), last2, last3, last3, big, big,
        ),
        out_specs=(
            big, big, big, big, P(), P(), P(), last3, last3, last3, last4, first, first, first,
            P(), P(), last2, last3, last3,
        ),
        check_vma=False,
    )
```

```python
import functools

import jax
import jax.numpy as jnp
from jax import lax
from jax.experimental import pallas as pl
from jax.experimental.pallas import tpu as pltpu
from jax.sharding import PartitionSpec as P

F32 = jnp.float32
BF16 = jnp.bfloat16
EPSILON = 1e-05
ROOT = 0.7978845608028654
CUBIC = 0.044715
BIG = 49
PARTS = ((0, 0), (1, 0), (2, 0), (2, 98), (3, 0), (3, 49))
SMALL = 7


def gelu(v):
    return 0.5 * v * (1.0 + jnp.tanh(ROOT * (v * (1.0 + CUBIC * (v * v)))))


def gelu_slope(v):
    square = v * v
    th = jnp.tanh(ROOT * (v * (1.0 + CUBIC * square)))
    half = 0.5 * (1.0 + th)
    return half + (0.5 * ROOT) * v * (1.0 - th * th) * (1.0 + 3.0 * CUBIC * square)


def gelu_pair(v):
    square = v * v
    th = jnp.tanh(ROOT * (v * (1.0 + CUBIC * square)))
    half = 0.5 * (1.0 + th)
    slope = half + (0.5 * ROOT) * v * (1.0 - th * th) * (1.0 + 3.0 * CUBIC * square)
    return v * half, slope


def rows(v):
    return v.reshape(v.shape[0] * v.shape[1], v.shape[2])


def cells(v):
    return v.reshape(v.shape[0] // 8, 8, v.shape[1])


def rows_bf(v):
    return rows(v.astype(F32)).astype(BF16)


def wide(mask, width):
    repeats = width // 128
    return mask if repeats == 1 else jnp.concatenate([mask] * repeats, axis=-1)


def nn(a, b):
    return jnp.dot(a, b, preferred_element_type=F32)


def nt(a, b):
    return lax.dot_general(a, b, (((1,), (1,)), ((), ())), preferred_element_type=F32)


def later(v):
    rolled = pltpu.roll(v, 1, 1)
    return jnp.where(lax.broadcasted_iota(jnp.int32, v.shape, 1) == 0, 0.0, rolled)


def sooner(v):
    rolled = pltpu.roll(v, 7, 1)
    return jnp.where(lax.broadcasted_iota(jnp.int32, v.shape, 1) == 7, 0.0, rolled)


def folded(v):
    out = []
    for block in range(v.shape[-1] // 128):
        part = v[:, 128 * block : 128 * block + 128]
        part = part + pltpu.roll(part, 64, 1)
        out.append(part + pltpu.roll(part, 32, 1))
    return out[0] if len(out) == 1 else jnp.concatenate(out, axis=-1)


def scale_of(sums, gains, inv_n):
    center = sums[0:1] * inv_n
    spread = sums[1:2] * inv_n - center * center
    inv_std = lax.rsqrt(spread + EPSILON)
    factor = gains[0:1] * inv_std
    return factor, gains[1:2] - center * factor, center, inv_std


def slope_of(slopes, factor, center, inv_std, inv_n):
    k1 = factor * slopes[1:2] * inv_n * inv_std
    k0 = factor * slopes[0:1] * inv_n - k1 * center
    return k0, k1


def down(v):
    return jnp.sum(v, axis=0)


def flat(v):
    return jnp.sum(v, axis=0, keepdims=True)


def steps(count, step, body, carry):
    return lax.fori_loop(0, count // step, lambda i, c: body(i * step, c), carry)


def call(kernel, outs, args, scratch=(), smem=0, flops=0, name=None):
    specs = [pl.BlockSpec(memory_space=pltpu.SMEM if i < smem else pltpu.VMEM) for i in range(len(args))]
    total = sum(a.size * a.dtype.itemsize for a in args)
    total += sum(o.size * o.dtype.itemsize for o in outs)
    def padded(v):
        dims = list(v.shape)
        if len(dims) < 2:
            return 4096
        dims[-1] = -(-dims[-1] // 128) * 128
        dims[-2] = -(-dims[-2] // 8) * 8
        amount = v.dtype.itemsize
        for d in dims:
            amount *= d
        return amount

    room = sum(padded(v) for v in (*args, *outs, *scratch)) + 6 * 1024 * 1024
    return pl.pallas_call(
        kernel,
        out_shape=tuple(outs),
        in_specs=specs,
        out_specs=tuple(pl.BlockSpec(memory_space=pltpu.VMEM) for _ in outs),
        scratch_shapes=list(scratch),
        compiler_params=pltpu.CompilerParams(vmem_limit_bytes=room),
        cost_estimate=pl.CostEstimate(flops=flops, bytes_accessed=1, transcendentals=0),
        name=name,
    )(*args)


def shape(dims, dtype=F32):
    return jax.ShapeDtypeStruct(dims, dtype)


def tile_mask(frames, width):
    tile = (lax.broadcasted_iota(jnp.int32, (8, 128), 0) < frames).astype(F32)
    return wide(tile, width)[None]


def sweep(table_ref, size, step, body, carry=0, begin=0):
    def run(i, kept):
        p = i * step
        return body(p, table_ref[1 + (begin + p) // BIG], kept)

    return lax.fori_loop(0, size // step, run, carry)


def lane_group(v, group):
    return jnp.where(lax.broadcasted_iota(jnp.int32, v.shape, v.ndim - 1) // 32 == group, v, 0.0)


def moved(v, shift):
    shift = shift % 128
    return v if shift == 0 else pltpu.roll(v, shift, v.ndim - 1)


def pack_kernel(per_clip, clips, ids_ref, counts_ref, frames_ref, x_ref, *refs):
    out_ref, tmp_ref = refs[-2:]
    clip, dp = pl.program_id(0) // per_clip, ids_ref[0]
    chunk = x_ref.shape[0]
    frames = jnp.where(clip < counts_ref[dp], frames_ref[dp * clips + clip], 0)
    tmp_ref[...] = x_ref[...].astype(F32).reshape(chunk * 32, 32)
    parts = [tmp_ref[pl.ds(r, chunk * 8, stride=4), :] for r in range(4)]
    out_ref[:, :, 0:128] = (cells(jnp.concatenate(parts, axis=1)) * tile_mask(frames, 128)).astype(BF16)
    if len(refs) == 3:
        out_ref[:, :, 128:384] = refs[0][...]


def unpack_kernel(ids_ref, *refs):
    slow_ref, fast_ref, tmp_ref = refs[-3:]
    size = refs[0].shape[0]
    for (k, first), ref in zip(PARTS, refs):
        begin = (ids_ref[1] ^ k) * size + first

        def body(p, carry, ref=ref, begin=begin):
            joined = rows(ref[pl.ds(p, BIG), :, 0:128].astype(F32))
            for r in range(4):
                tmp_ref[pl.ds(r, BIG * 8, stride=4), :] = joined[:, 32 * r : 32 * r + 32]
            fast_ref[pl.ds(begin + p, BIG)] = tmp_ref[...].reshape(BIG, 32, 32).astype(BF16)
            slow_ref[pl.ds(begin + p, BIG)] = ref[pl.ds(p, BIG), :, 128:384]
            return carry

        steps(ref.shape[0], BIG, body, 0)


def unpack_fast_kernel(x_ref, out_ref, tmp_ref):
    chunk = x_ref.shape[0]
    joined = rows(x_ref[...].astype(F32))
    for r in range(4):
        tmp_ref[pl.ds(r, chunk * 8, stride=4), :] = joined[:, 32 * r : 32 * r + 32]
    out_ref[...] = tmp_ref[...].reshape(chunk, 32, 32).astype(BF16)


def copy_kernel(x_ref, out_ref):
    def body(p, carry):
        out_ref[pl.ds(p, SMALL)] = x_ref[pl.ds(p, SMALL)]
        return carry

    steps(x_ref.shape[0], SMALL, body, 0)


def lanes_at(block, width):
    return pl.ds(pl.multiple_of(block * width, width), width)


LREDUCE = [(3, 256 * k) for k in range(3)]
LATERAL = [(4, 128 * k) for k in range(5)]
GAINS = [(3, 768), (3, 896), (4, 640), (4, 768)]
SPATIAL = [(11 + k // 4, 256 * (k % 4)) for k in range(9)]


def weight_slab_kernel(ids_ref, red_ref, lred_ref, lat_ref, exp_ref, short_ref, lshort_ref, sp_ref, ln_ref, sn_ref, on_ref, out_ref,
                       red_s, lred_s, lat_s, exp_s, short_s, lshort_s, sp_s, sem):
    group = ids_ref[2]
    eight, more = pl.ds(pl.multiple_of(group * 8, 8), 8), pl.ds(pl.multiple_of(group * 32, 32), 32)
    copies = []
    for i, (src, dst) in enumerate((
        (red_ref.at[:, eight], red_s), (lred_ref.at[:, eight], lred_s), (lat_ref.at[:, eight], lat_s), (exp_ref.at[eight], exp_s),
        (short_ref.at[more], short_s), (lshort_ref.at[eight], lshort_s), (sp_ref.at[:, eight], sp_s),
    )):
        copies.append(pltpu.make_async_copy(src, dst, sem.at[i]))
    for copy in copies:
        copy.start()
    out_ref[4, :, 896:1024] = jnp.zeros((8, 128), BF16)
    out_ref[13, :, 256:1024] = jnp.zeros((8, 768), BF16)
    blank = jnp.zeros((2, 128), F32)
    half = jnp.zeros((2, 64), F32)
    inner = jnp.concatenate([jnp.concatenate([v, half], axis=1) for v in (ln_ref[...], sn_ref[0], sn_ref[1])] + [blank], axis=0)
    outer = jnp.concatenate([on_ref[k, :, 128 * h : 128 * h + 128] for h in range(2) for k in range(2)], axis=0)
    for i, v in enumerate((inner, outer)):
        high = v.astype(BF16)
        for k, part in ((i, high), (2 + i, (v - high.astype(F32)).astype(BF16))):
            at, lane = GAINS[k]
            out_ref[at, :, lane : lane + 128] = part
    for copy in copies:
        copy.wait()
    for j in range(3):
        out_ref[j] = red_s[j].astype(BF16)
        at, lane = LREDUCE[j]
        out_ref[at, :, lane : lane + 256] = lred_s[j].astype(BF16)
    out_ref[5], out_ref[10] = exp_s[...].astype(BF16), lshort_s[...].astype(BF16)
    for a in range(4):
        out_ref[6 + a] = short_s[8 * a : 8 * a + 8].astype(BF16)
    for k in range(9):
        at, lane = SPATIAL[k]
        out_ref[at, :, lane : lane + 256] = sp_s[k].astype(BF16)
    for k in range(5):
        at, lane = LATERAL[k]
        out_ref[at, :, lane : lane + 128] = lat_s[k].astype(BF16)


def more_weights_kernel(ids_ref, own_ref, other_ref, exp_ref, short_ref, lshort_ref, sp_ref):
    me, group = ids_ref[1], ids_ref[2]

    def place(i, carry):
        chip, kz = i // 4, i % 4
        z = me ^ kz
        for core, ref in ((0, own_ref), (1, other_ref)):
            d = group ^ (2 * chip + core)
            exp_ref[z, d], lshort_ref[z, d] = ref[chip, kz, 0], ref[chip, kz, 5]
            for a in range(4):
                short_ref[z, d, a] = ref[chip, kz, 1 + a]
            for k in range(9):
                at, lane = SPATIAL[k]
                sp_ref[k, z, d] = ref[chip, kz, at - 5, :, lane : lane + 256]
        return carry

    lax.fori_loop(0, 16, place, 0)


def weights_kernel(ids_ref, own_ref, other_ref, fr_ref, fsp_ref, fex_ref, fin_ref, fout_ref, red_ref, lred_ref, first_ref, wsp_ref, wex_ref,
                   gin_ref, gout_ref, gmid_ref, gwide_ref, lat_ref):
    me, group = ids_ref[1], ids_ref[2]

    def place(i, carry):
        chip, kz = i // 4, i % 4
        z = me ^ kz
        for core, ref in ((0, own_ref), (1, other_ref)):
            d = group ^ (2 * chip + core)
            for j in range(3):
                red_ref[j, z, d] = ref[chip, kz, j]
                at, lane = LREDUCE[j]
                lred_ref[j, z, d] = ref[chip, kz, at, :, lane : lane + 256]
            for k in range(5):
                at, lane = LATERAL[k]
                lat_ref[k, z, d] = ref[chip, kz, at, :, lane : lane + 128].astype(F32)
        return carry

    lax.fori_loop(0, 16, place, 0)

    mids = [jnp.zeros((8, 128), F32) for _ in range(2)]
    for kz in range(4):
        z = me ^ kz
        parts = [own_ref[0, kz, at, :, lane : lane + 128].astype(F32) for at, lane in GAINS]
        inner, outer = parts[0] + parts[2], parts[1] + parts[3]
        for half in range(2):
            for block in range(2):
                here = (z == 2 * block + half).astype(F32)
                mids[block] = mids[block] + moved(inner, 64 * half) * here
        gwide_ref[z, :, 0:128], gwide_ref[z, :, 128:256] = outer[0:4], outer[4:8]
    gmid_ref[:, 0:128], gmid_ref[:, 128:256] = mids[0], mids[1]

    first_ref[...] = jnp.zeros_like(first_ref)
    wsp_ref[...] = jnp.zeros_like(wsp_ref)
    for z in range(4):
        lanes = slice(128 * z, 128 * z + 128)

        def put(v, r, z=z):
            return lane_group(moved(v, 32 * r - 32 * z), r)

        for q in range(4):
            total = sum(put(fr_ref[r - q + 1], r) for r in range(4) if abs(r - q) <= 1)
            first_ref[32 * q : 32 * q + 32, lanes] = total.astype(BF16)
        first_ref[128:160, lanes] = put(fr_ref[0], 3).astype(BF16)
        first_ref[352:384, lanes] = put(fr_ref[2], 0).astype(BF16)
        taps = [lat_ref[j].reshape(256, 128) for j in range(5)]
        first_ref[384:640, lanes] = sum(put(taps[2 + r], r) for r in range(3)).astype(BF16)
        first_ref[640:896, lanes] = (put(taps[0], 2) + put(taps[1], 3)).astype(BF16)
        for r in range(4):
            wex_ref[32 * r : 32 * r + 32, lanes] = put(fex_ref[...], r).astype(BF16)
        gout_ref[:, lanes] = sum(put(fout_ref[...], r) for r in range(4))
    blank = jnp.zeros((32, 96), F32)
    for k in range(9):
        tap = jnp.concatenate([fsp_ref[k], blank], axis=1)
        for r in range(4):
            wsp_ref[k, 32 * r : 32 * r + 32, :] = moved(tap, 32 * r).astype(BF16)
    gin_ref[...] = jnp.concatenate([fin_ref[...]] * 4, axis=1)


def grads_kernel(ids_ref, own_ref, other_ref, exp_ref, short_ref, lshort_ref, red_ref, lred_ref, sp_ref):
    def place(chip, carry):
        for core, ref in ((0, own_ref), (1, other_ref)):
            d = ids_ref[2] ^ (2 * chip + core)
            exp_ref[d], lshort_ref[d] = ref[chip, 0].astype(F32), ref[chip, 5].astype(F32)
            for a in range(4):
                short_ref[d, a] = ref[chip, 1 + a].astype(F32)
            for j in range(3):
                red_ref[j, d] = ref[chip, 6 + j].astype(F32)
                lred_ref[j, d] = ref[chip, 9, :, 256 * j : 256 * j + 256].astype(F32)
            for k in range(8):
                sp_ref[k, d] = ref[chip, 10 + k // 4, :, 256 * (k % 4) : 256 * (k % 4) + 256].astype(F32)
            sp_ref[8, d] = ref[chip, 9, :, 768:1024].astype(F32)
        return carry

    lax.fori_loop(0, 4, place, 0)


def fast_first_kernel(table_ref, f0_ref, f1_ref, f2_ref, f3_ref, w_ref, fx_ref, fa_ref, lp_ref, sums_ref, first_ref, last_ref):
    size = fa_ref.shape[0]

    def fill(p, carry):
        for k, ref in enumerate((f0_ref, f1_ref, f2_ref, f3_ref)):
            fx_ref[pl.ds(p, SMALL), :, lanes_at(table_ref[5] ^ k, 128)] = ref[pl.ds(p, SMALL)]
        return carry

    steps(size, SMALL, fill, 0)

    def body(p, frames, carry):
        acc = cells(nt(rows_bf(fx_ref[pl.ds(p, BIG)]), w_ref[...]))
        fa = acc[:, :, 0:128] + later(acc[:, :, 128:256]) + sooner(acc[:, :, 256:384])
        lp = acc[:, :, 384:640] + later(acc[:, :, 640:896])
        fa_ref[pl.ds(p, BIG)] = fa
        lp_ref[pl.ds(p, BIG)] = lp
        fm, lm = fa * tile_mask(frames, 128), lp * tile_mask(frames, 256)
        return tuple(c + down(v) for c, v in zip(carry, (fm, fm * fa, lm, lm * lp)))

    zero = (jnp.zeros((8, 128), F32),) * 2 + (jnp.zeros((8, 256), F32),) * 2
    a, b, c, d = sweep(table_ref, size, BIG, body, zero)
    sums_ref[0:1, 0:128], sums_ref[1:2, 0:128] = flat(a), flat(b)
    sums_ref[0:1, 128:384], sums_ref[1:2, 128:384] = flat(c), flat(d)
    halo = first_ref.shape[0]
    first_ref[...], last_ref[...] = fa_ref[0:halo], fa_ref[size - halo : size]


def fill_padded(table_ref, refs, offset, out_ref, value, halo, size):
    low, middle, high = refs
    phase = table_ref[5] * (size // SMALL)

    def put(v, at, part, count, step=SMALL):
        even = ((phase + part + 2 * count) % 2 == 0).astype(F32)
        out_ref[1, pl.ds(at, step)] = v
        if step == 1:
            out_ref[0, pl.ds(at, 1)] = v * even
            out_ref[2, pl.ds(at, 1)] = v * (1.0 - even)
            return
        out_ref[0, pl.ds(at, step)] = v
        out_ref[2, pl.ds(at, step)] = v
        out_ref[0, pl.ds(at + step - 1, 1)] = v[step - 1 : step] * even
        out_ref[2, pl.ds(at, 1)] = v[0:1] * (1.0 - even)

    width = out_ref.shape[-1]
    lo_mask, hi_mask = tile_mask(table_ref[0], width), tile_mask(table_ref[4], width)
    put(value(low, 0, 1) * lo_mask, 0, -3, 4, 1)
    put(value(low, 1, SMALL) * lo_mask, 1, -2, 4)
    put(value(low, 1 + SMALL, SMALL) * lo_mask, 1 + SMALL, -1, 4)
    parts = size // SMALL
    put(value(high, 0, SMALL) * hi_mask, halo + size, parts, 0)
    put(value(high, SMALL, SMALL) * hi_mask, halo + size + SMALL, parts + 1, 0)
    put(value(high, 2 * SMALL, 1) * hi_mask, halo + size + 2 * SMALL, parts + 2, 0, 1)

    def body(p, frames, carry):
        put(value(middle, p, SMALL) * tile_mask(frames, width), halo + p, p // SMALL, 0)
        return carry

    sweep(table_ref, size, SMALL, body)


def edge_scales(table_ref, p, per_clip):
    part = table_ref[5] * table_ref[6] + p // BIG
    return (part % per_clip != 0).astype(F32), ((part + 1) % per_clip != 0).astype(F32)


def conv_rows(table_ref, per_clip, pad_ref, weight, p, halo, row_len, dot):
    top, bottom = edge_scales(table_ref, p, per_clip)
    total = None
    for i in (1, 0, 2):
        begin = p + halo + row_len * (i - 1)
        acc = None
        for j in range(3):
            tap = rows(pad_ref[j, pl.ds(begin + j - 1, BIG)]).astype(BF16)
            part = dot(tap, weight(i, j))
            acc = part if acc is None else acc + part
        acc = cells(acc)
        if i == 0:
            acc = jnp.concatenate([acc[0:row_len] * top, acc[row_len:]], axis=0)
        if i == 2:
            acc = jnp.concatenate([acc[: BIG - row_len], acc[BIG - row_len :] * bottom], axis=0)
        total = acc if total is None else total + acc
    return total


def conv_kernel(halo, row_len, per_clip, fold, offsets, table_ref, n_ref, sums_ref, gains_ref, lo_ref, y_ref, hi_ref, w_ref, *refs):
    if fold:
        act_ref, out_ref, osums_ref, pad_ref = refs
    else:
        more_ref, act_ref, out_ref, osums_ref, pad_ref = refs
    size, width = y_ref.shape[0], y_ref.shape[2]
    sums = sums_ref[:, offsets[0] : offsets[0] + width]
    sums = folded(sums) if fold else sums
    factor, shift, _, _ = scale_of(sums, gains_ref[...], n_ref[1 if fold else 0])
    lanes = slice(offsets[1], offsets[1] + width)

    def value(ref, p, step):
        y = ref[pl.ds(p, step)] if ref is y_ref else ref[pl.ds(p, step), :, lanes]
        return gelu(y * factor[None] + shift[None]).astype(BF16).astype(F32)

    fill_padded(table_ref, (lo_ref, y_ref, hi_ref), 0, pad_ref, value, halo, size)

    def copy(p, carry):
        act_ref[pl.ds(p, 3)] = pad_ref[1, pl.ds(p, 3)].astype(BF16)
        return carry

    steps(size + 2 * halo, 3, copy, 0)

    def body(p, frames, carry):
        total = conv_rows(table_ref, per_clip, pad_ref, lambda i, j: w_ref[3 * i + j], p, halo, row_len, nn if fold else nt)
        out_ref[pl.ds(p, BIG)] = total
        masked = total * tile_mask(frames, width)
        return carry[0] + down(masked), carry[1] + down(masked * total)

    a, b = sweep(table_ref, size, BIG, body, (jnp.zeros((8, width), F32),) * 2)
    osums_ref[0:1, 0:width], osums_ref[1:2, 0:width] = flat(a), flat(b)
    if not fold:
        osums_ref[:, width:] = more_ref[...]


def slow_first_kernel(table_ref, n_ref, xs_ref, lp_ref, lsums_ref, gains_ref, w_ref, wl_ref,
                      x_ref, lat_ref, sa_ref, sums_ref, first_ref, last_ref):
    size = lp_ref.shape[0]
    factor, shift, _, _ = scale_of(lsums_ref[:, 128:384], gains_ref[...], n_ref[0])

    def fill(p, frames, carry):
        mask = tile_mask(frames, 256)
        lat_ref[pl.ds(p, SMALL)] = (gelu(lp_ref[pl.ds(p, SMALL)] * factor[None] + shift[None]) * mask).astype(BF16)
        for z in range(4):
            v = xs_ref[z, pl.ds(p, SMALL)].astype(F32) * mask
            x_ref[pl.ds(p, SMALL), :, 256 * z : 256 * z + 256] = v.astype(BF16)
        return carry

    sweep(table_ref, size, SMALL, fill)

    def body(p, frames, carry):
        acc = nt(rows_bf(x_ref[pl.ds(p, BIG)]), w_ref[...]) + nt(rows_bf(lat_ref[pl.ds(p, BIG)]), wl_ref[...])
        acc = cells(acc)
        sa = later(acc[:, :, 0:256]) + acc[:, :, 256:512] + sooner(acc[:, :, 512:768])
        sa_ref[pl.ds(p, BIG)] = sa
        masked = sa * tile_mask(frames, 256)
        return carry[0] + down(masked), carry[1] + down(masked * sa)

    a, b = sweep(table_ref, size, BIG, body, (jnp.zeros((8, 256), F32),) * 2)
    sums_ref[0:1], sums_ref[1:2] = flat(a), flat(b)
    halo = first_ref.shape[0]
    first_ref[...], last_ref[...] = sa_ref[0:halo], sa_ref[size - halo : size]


def bypass_kernel(table_ref, x_ref, lat_ref, w_ref, wl_ref, sp_ref, sums_ref):
    def body(p, frames, carry):
        sp = cells(nn(rows_bf(x_ref[pl.ds(p, BIG)]), w_ref[...]) + nn(rows_bf(lat_ref[pl.ds(p, BIG)]), wl_ref[...]))
        sp_ref[pl.ds(p, BIG)] = sp.astype(BF16)
        masked = sp * tile_mask(frames, sp.shape[-1])
        return carry[0] + down(masked), carry[1] + down(masked * sp)

    a, b = sweep(table_ref, sp_ref.shape[0], BIG, body, (jnp.zeros((8, sp_ref.shape[2]), F32),) * 2)
    sums_ref[0:1], sums_ref[1:2] = flat(a), flat(b)


def expand_kernel(fold, offset, table_ref, n_ref, y_ref, sums_ref, gains_ref, w_ref, *refs):
    more, (h_ref, out_ref, osums_ref) = refs[:-3], refs[-3:]
    size, width = y_ref.shape[0], y_ref.shape[2]
    sums = sums_ref[:, offset : offset + width]
    sums = folded(sums) if fold else sums
    factor, shift, _, _ = scale_of(sums, gains_ref[...], n_ref[1 if fold else 0])

    def fill(p, frames, carry):
        v = gelu(y_ref[pl.ds(p, SMALL)] * factor[None] + shift[None])
        h_ref[pl.ds(p, SMALL)] = (v * tile_mask(frames, width)).astype(BF16)
        return carry

    sweep(table_ref, size, SMALL, fill)

    def body(p, frames, carry):
        out = cells(nn(rows_bf(h_ref[pl.ds(p, BIG)]), w_ref[...]))
        out_ref[pl.ds(p, BIG)] = out.astype(BF16)
        masked = out * tile_mask(frames, out.shape[-1])
        return carry[0] + down(masked), carry[1] + down(masked * out)

    wide_out = out_ref.shape[2]
    a, b = sweep(table_ref, size, BIG, body, (jnp.zeros((8, wide_out), F32),) * 2)
    osums_ref[0:1, 0:wide_out], osums_ref[1:2, 0:wide_out] = flat(a), flat(b)
    for ref in more:
        osums_ref[:, wide_out : wide_out + ref.shape[1]] = ref[...]
        wide_out += ref.shape[1]


def fast_out_kernel(offset, table_ref, n_ref, fc_ref, sums_ref, gains_ref, fx_ref, *refs):
    cots, (out_ref, up_ref, slopes_ref, vec_ref) = refs[: len(PARTS)], refs[len(PARTS) :]
    width = fc_ref.shape[2]
    vecs = scale_of(folded(sums_ref[:, offset : offset + width]), gains_ref[...], n_ref[1])
    for i, v in enumerate(vecs):
        vec_ref[i : i + 1] = v
    kept = (jnp.zeros((8, 128), F32),) * 2
    for part, ((k, begin), cot_ref) in enumerate(zip(PARTS, cots)):
        lanes = lanes_at(table_ref[5] ^ k, 128)
        fz, sz, cz, rz = (vec_ref[i : i + 1, lanes][None] for i in range(4))

        def body(p, frames, carry, k=k, lanes=lanes, fz=fz, sz=sz, cz=cz, rz=rz, cot_ref=cot_ref, begin=begin):
            here = pl.ds(begin + p, SMALL)
            y = fc_ref[here, :, lanes].astype(F32)
            mask = tile_mask(frames, 128)
            total = y * fz + sz + fx_ref[here, :, lanes].astype(F32)
            value, slope = gelu_pair(total)
            out_ref[k, here] = (value * mask).astype(BF16)
            up = slope * (cot_ref[pl.ds(p, SMALL), :, 0:128].astype(F32) * mask)
            up_ref[here, :, lanes] = up.astype(BF16)
            return carry[0] + down(up), carry[1] + down(up * y)

        zero = (jnp.zeros((8, 128), F32),) * 2
        kept = sweep(table_ref, cot_ref.shape[0], SMALL, body, kept if begin else zero, begin)
        total = flat(kept[0])
        slopes_ref[0:1, lanes], slopes_ref[1:2, lanes] = total, (flat(kept[1]) - cz[0] * total) * rz[0]


def slow_out_kernel(table_ref, n_ref, sc_ref, sp_ref, sums_ref, gains_ref, *refs):
    count = len(PARTS)
    cots, (fast_ref, more_ref), outs = refs[:count], refs[count : count + 2], refs[count + 2 : 2 * count + 2]
    up_ref, slopes_ref, vec_ref = refs[2 * count + 2 :]
    width = sc_ref.shape[2]
    cf, cs, cc, cr = scale_of(sums_ref[:, 0:width], gains_ref[0:2], n_ref[0])
    pf, ps, pc, pr = scale_of(sums_ref[:, width : 2 * width], gains_ref[2:4], n_ref[0])
    for i, v in enumerate((cf, cs + ps, cc, cr, pf, pc, pr)):
        vec_ref[i : i + 1] = v
    kept = ()
    for (k, begin), cot_ref, out_ref in zip(PARTS, cots, outs):
        block = table_ref[5] ^ k
        lanes = lanes_at(block, 256)
        vecs = [vec_ref[i : i + 1, lanes][None] for i in range(7)]

        def body(p, frames, carry, k=k, lanes=lanes, vecs=vecs, cot_ref=cot_ref, out_ref=out_ref, begin=begin):
            cf, shift, _, _, pf, _, _ = vecs
            here = pl.ds(begin + p, SMALL)
            yc, yp = (ref[here, :, lanes].astype(F32) for ref in (sc_ref, sp_ref))
            mask = tile_mask(frames, 256)
            value, slope = gelu_pair(yc * cf + yp * pf + shift)
            out_ref[pl.ds(p, SMALL), :, 128:384] = (value * mask).astype(BF16)
            out_ref[pl.ds(p, SMALL), :, 0:128] = fast_ref[k, here]
            up = slope * (cot_ref[pl.ds(p, SMALL), :, 128:384].astype(F32) * mask)
            up_ref[here, :, lanes] = up.astype(BF16)
            return carry[0] + down(up), carry[1] + down(up * yc), carry[2] + down(up * yp)

        zero = (jnp.zeros((8, 256), F32),) * 3
        kept = sweep(table_ref, cot_ref.shape[0], SMALL, body, kept if begin else zero, begin)
        _, _, cc, cr, _, pc, pr = (v[0] for v in vecs)
        a, b, c = (flat(v) for v in kept)
        own, other = lanes, lanes_at(4 + block, 256)
        slopes_ref[0:1, own], slopes_ref[1:2, own] = a, (b - cc * a) * cr
        slopes_ref[0:1, other], slopes_ref[1:2, other] = a, (c - pc * a) * pr
    slopes_ref[:, 2 * width :] = more_ref[...]


def norm_back_fill(table_ref, up_ref, y_ref, dy_ref, factor, k0, k1):
    def fill(p, frames, carry):
        mask = tile_mask(frames, 128)
        for q in range(y_ref.shape[2] // 128):
            lanes = slice(128 * q, 128 * q + 128)
            y = y_ref[pl.ds(p, SMALL), :, lanes].astype(F32)
            dy = up_ref[pl.ds(p, SMALL), :, lanes].astype(F32) * factor[:, lanes][None]
            dy = dy - mask * (k0[:, lanes][None] + k1[:, lanes][None] * y)
            dy_ref[pl.ds(p, SMALL), :, lanes] = dy.astype(BF16)
        return carry

    sweep(table_ref, y_ref.shape[0], SMALL, fill)


def expand_back_kernel(fold, offsets, table_ref, n_ref, up_ref, y_ref, sums_ref, gains_ref, slopes_ref, z_ref, zsums_ref, zgains_ref,
                       w_ref, other_ref, dy_ref, dz_ref, oslopes_ref, first_ref, last_ref):
    size, width, inner = y_ref.shape[0], y_ref.shape[2], z_ref.shape[2]
    fix = folded if fold else (lambda v: v)
    inv_n = n_ref[1 if fold else 0]
    at_y, at_s, at_z = offsets
    factor, shift, center, inv_std = scale_of(fix(sums_ref[:, at_y : at_y + width]), gains_ref[...], inv_n)
    k0, k1 = slope_of(fix(slopes_ref[:, at_s : at_s + width]), factor, center, inv_std, inv_n)
    norm_back_fill(table_ref, up_ref, y_ref, dy_ref, factor, k0, k1)
    zf, zs, zc, zr = scale_of(fix(zsums_ref[:, at_z : at_z + inner]), zgains_ref[...], inv_n)

    def body(p, frames, carry):
        dh = cells(nt(rows_bf(dy_ref[pl.ds(p, BIG)]), w_ref[...]))
        z = z_ref[pl.ds(p, BIG)]
        dz = gelu_slope(z * zf[None] + zs[None]) * dh * tile_mask(frames, inner)
        dz_ref[pl.ds(p, BIG)] = dz
        return carry[0] + down(dz), carry[1] + down(dz * ((z - zc[None]) * zr[None]))

    a, b = sweep(table_ref, size, BIG, body, (jnp.zeros((8, inner), F32),) * 2)
    oslopes_ref[0:1, 0:inner], oslopes_ref[1:2, 0:inner] = flat(a), flat(b)
    halo = first_ref.shape[0]
    first_ref[:, :, 0:inner], last_ref[:, :, 0:inner] = dz_ref[0:halo], dz_ref[size - halo : size]
    if fold:
        wide_edge = inner + other_ref.shape[2]
        first_ref[:, :, inner:wide_edge], last_ref[:, :, inner:wide_edge] = other_ref[0:halo], other_ref[size - halo : size]
        first_ref[:, :, wide_edge:], last_ref[:, :, wide_edge:] = z_ref[0:halo], z_ref[size - halo : size]
    else:
        oslopes_ref[:, inner:] = other_ref[...]


def bypass_back_kernel(table_ref, n_ref, up_ref, y_ref, sums_ref, gains_ref, slopes_ref, w_ref, wl_ref, dy_ref, dx_ref, dl_ref):
    size, width = y_ref.shape[0], y_ref.shape[2]
    factor, shift, center, inv_std = scale_of(sums_ref[:, width : 2 * width], gains_ref[...], n_ref[0])
    k0, k1 = slope_of(slopes_ref[:, width : 2 * width], factor, center, inv_std, n_ref[0])
    norm_back_fill(table_ref, up_ref, y_ref, dy_ref, factor, k0, k1)

    def body(p, carry):
        dy = rows_bf(dy_ref[pl.ds(p, BIG)])
        dx_ref[pl.ds(p, BIG)] = cells(nt(dy, w_ref[...])).astype(BF16)
        dl_ref[pl.ds(p, BIG)] = cells(nt(dy, wl_ref[...]))
        return carry

    steps(size, BIG, body, 0)


def conv_back_kernel(halo, row_len, per_clip, fold, offsets, table_ref, n_ref, ysums_ref, ygains_ref, slopes_ref, ylo_ref, y_ref, yhi_ref,
                     dlo_ref, d_ref, dhi_ref, w_ref, z_ref, zsums_ref, zgains_ref, *refs):
    dy_ref, dz_ref, oslopes_ref, pad_ref = refs[-4:]
    size, width = y_ref.shape[0], y_ref.shape[2]
    fix = folded if fold else (lambda v: v)
    inv_n = n_ref[1 if fold else 0]
    at_y, at_s, at_z, at_yhalo, at_dhalo = offsets
    factor, shift, center, inv_std = scale_of(fix(ysums_ref[:, at_y : at_y + width]), ygains_ref[...], inv_n)
    k0, k1 = slope_of(fix(slopes_ref[:, at_s : at_s + width]), factor, center, inv_std, inv_n)

    def value(refs, p, step):
        y_of, d_of = refs
        if y_of is y_ref:
            y, d = y_of[pl.ds(p, step)], d_of[pl.ds(p, step)]
        else:
            y, d = y_of[pl.ds(p, step), :, at_yhalo : at_yhalo + width], d_of[pl.ds(p, step), :, at_dhalo : at_dhalo + width]
        return (d * factor[None] - (k0[None] + k1[None] * y)).astype(BF16).astype(F32)

    fill_padded(table_ref, ((ylo_ref, dlo_ref), (y_ref, d_ref), (yhi_ref, dhi_ref)), 0, pad_ref, value, halo, size)

    def copy(p, carry):
        dy_ref[pl.ds(p, SMALL)] = pad_ref[1, pl.ds(halo + p, SMALL)].astype(BF16)
        return carry

    steps(size, SMALL, copy, 0)
    zf, zs, zc, zr = scale_of(fix(zsums_ref[:, at_z : at_z + width]), zgains_ref[...], inv_n)

    def body(p, frames, carry):
        dh = conv_rows(table_ref, per_clip, pad_ref, lambda i, j: w_ref[8 - 3 * i - j], p, halo, row_len, nt if fold else nn)
        z = z_ref[pl.ds(p, BIG)]
        dz = gelu_slope(z * zf[None] + zs[None]) * dh * tile_mask(frames, width)
        dz_ref[pl.ds(p, BIG)] = dz
        return carry[0] + down(dz), carry[1] + down(dz * ((z - zc[None]) * zr[None]))

    a, b = sweep(table_ref, size, BIG, body, (jnp.zeros((8, width), F32),) * 2)
    oslopes_ref[0:1, 0:width], oslopes_ref[1:2, 0:width] = flat(a), flat(b)
    if not fold:
        oslopes_ref[:, width:] = refs[0][...]


def slow_back_kernel(table_ref, n_ref, dz_ref, y_ref, sums_ref, gains_ref, slopes_ref, w_ref, wl_ref, dx_ref, dl_ref,
                     lp_ref, lsums_ref, lgains_ref, taps_ref, out_ref, dzl_ref, oslopes_ref):
    size = y_ref.shape[0]
    factor, shift, center, inv_std = scale_of(sums_ref[:, 0:256], gains_ref[...], n_ref[0])
    k0, k1 = slope_of(slopes_ref[:, 0:256], factor, center, inv_std, n_ref[0])

    def fill(p, frames, carry):
        dy = dz_ref[pl.ds(p, SMALL)] * factor[None]
        dy = dy - tile_mask(frames, 256) * (k0[None] + k1[None] * y_ref[pl.ds(p, SMALL)])
        taps_ref[pl.ds(p, SMALL), :, 0:256] = sooner(dy).astype(BF16)
        taps_ref[pl.ds(p, SMALL), :, 256:512] = dy.astype(BF16)
        taps_ref[pl.ds(p, SMALL), :, 512:768] = later(dy).astype(BF16)
        return carry

    sweep(table_ref, size, SMALL, fill)
    lf, ls, lc, lr = scale_of(lsums_ref[:, 128:384], lgains_ref[...], n_ref[0])

    def body(p, frames, carry):
        taps = rows_bf(taps_ref[pl.ds(p, BIG)])
        mask = tile_mask(frames, 256)
        for z in range(4):
            lanes = slice(256 * z, 256 * z + 256)
            dx = cells(nn(taps, w_ref[:, lanes])) + dx_ref[pl.ds(p, BIG), :, lanes].astype(F32)
            out_ref[z, pl.ds(p, BIG)] = (dx * mask).astype(BF16)
        dl = cells(nn(taps, wl_ref[...])) + dl_ref[pl.ds(p, BIG)]
        y = lp_ref[pl.ds(p, BIG)]
        dz = gelu_slope(y * lf[None] + ls[None]) * dl * mask
        dzl_ref[pl.ds(p, BIG)] = dz
        return carry[0] + down(dz), carry[1] + down(dz * ((y - lc[None]) * lr[None]))

    a, b = sweep(table_ref, size, BIG, body, (jnp.zeros((8, 256), F32),) * 2)
    oslopes_ref[0:1], oslopes_ref[1:2] = flat(a), flat(b)


def fast_back_kernel(at_s, table_ref, n_ref, sums_ref, fgains_ref, lgains_ref, fslopes_ref, lslopes_ref, dzf_ref, fa_ref, dzl_ref, lp_ref,
                     up_ref, w_ref, taps_ref, out_ref):
    size = fa_ref.shape[0]
    ff, fs, fc, fr = scale_of(folded(sums_ref[:, 0:128]), fgains_ref[...], n_ref[1])
    f0, f1 = slope_of(folded(fslopes_ref[:, at_s : at_s + 128]), ff, fc, fr, n_ref[1])
    lf, ls, lc, lr = scale_of(sums_ref[:, 128:384], lgains_ref[...], n_ref[0])
    l0, l1 = slope_of(lslopes_ref[...], lf, lc, lr, n_ref[0])

    def fill(p, frames, carry):
        dy = dzf_ref[pl.ds(p, SMALL)] * ff[None]
        dy = dy - tile_mask(frames, 128) * (f0[None] + f1[None] * fa_ref[pl.ds(p, SMALL)])
        taps_ref[pl.ds(p, SMALL), :, 0:128] = dy.astype(BF16)
        taps_ref[pl.ds(p, SMALL), :, 128:256] = sooner(dy).astype(BF16)
        taps_ref[pl.ds(p, SMALL), :, 256:384] = later(dy).astype(BF16)
        dy = dzl_ref[pl.ds(p, SMALL)] * lf[None]
        dy = dy - tile_mask(frames, 256) * (l0[None] + l1[None] * lp_ref[pl.ds(p, SMALL)])
        taps_ref[pl.ds(p, SMALL), :, 384:640] = dy.astype(BF16)
        taps_ref[pl.ds(p, SMALL), :, 640:896] = sooner(dy).astype(BF16)
        return carry

    sweep(table_ref, size, SMALL, fill)

    def body(p, frames, carry):
        dx = cells(nn(rows_bf(taps_ref[pl.ds(p, BIG)]), w_ref[...]))
        mask = tile_mask(frames, 128)
        for z in range(4):
            lanes = slice(128 * z, 128 * z + 128)
            out_ref[z, pl.ds(p, BIG)] = ((dx[:, :, lanes] + up_ref[pl.ds(p, BIG), :, lanes].astype(F32)) * mask).astype(BF16)
        return carry

    sweep(table_ref, size, BIG, body)


def tn(a, b):
    return lax.dot_general(a, b, (((0,), (0,)), ((), ())), preferred_element_type=F32)


def chunks(size):
    return range(0, size, BIG)


def added(acc_ref, at, part, first):
    acc_ref[at] = part if first else acc_ref[at] + part


def conv_weight(halo, row_len, per_clip, fold, table_ref, act_ref, dy_ref, pad_ref, acc_ref):
    size = dy_ref.shape[0]
    phase = table_ref[5] * (size // SMALL)

    def copy(p, carry):
        v = act_ref[pl.ds(p, 3)].astype(F32)
        for k in range(3):
            pad_ref[k, pl.ds(p, 3)] = v
        return carry

    steps(size + 2 * halo, 3, copy, 0)
    parts = size // SMALL

    def clear(i, carry):
        even = ((phase + i) % 2 == 0).astype(F32)
        at = halo + (i - 2) * SMALL
        pad_ref[0, pl.ds(at + SMALL - 1, 1)] = pad_ref[0, pl.ds(at + SMALL - 1, 1)] * even
        pad_ref[2, pl.ds(at, 1)] = pad_ref[2, pl.ds(at, 1)] * (1.0 - even)
        return carry

    lax.fori_loop(0, parts + 4, clear, 0)
    low_even = ((phase + 1) % 2 == 0).astype(F32)
    pad_ref[0, 0:1] = pad_ref[0, 0:1] * low_even
    high_even = ((phase + parts) % 2 == 0).astype(F32)
    end = size + 2 * halo
    pad_ref[2, end - 1 : end] = pad_ref[2, end - 1 : end] * (1.0 - high_even)

    for p in chunks(size):
        top, bottom = edge_scales(table_ref, p, per_clip)
        dy = rows_bf(dy_ref[p : p + BIG])
        for i in range(3):
            begin = p + halo + row_len * (i - 1)
            taps = []
            for j in range(3):
                v = pad_ref[j, begin + j - 1 : begin + j - 1 + BIG]
                if i == 0:
                    v = jnp.concatenate([v[0:row_len] * top, v[row_len:]], axis=0)
                if i == 2:
                    v = jnp.concatenate([v[: BIG - row_len], v[BIG - row_len :] * bottom], axis=0)
                taps.append(rows(v).astype(BF16))
            taps = jnp.concatenate(taps, axis=1)
            added(acc_ref, i, tn(taps, dy) if fold else tn(dy, taps), p == 0)


def by_share(v):
    return v.reshape(4, 4, 2, 8, v.shape[1]).transpose(2, 1, 0, 3, 4).astype(BF16)


def first_slab_kernel(hb_ref, dsc_ref, x_ref, lat_ref, dsp_ref, out_ref, acc_ref):
    for p in chunks(hb_ref.shape[0]):
        at = slice(p, p + BIG)
        dsc, dsp = rows_bf(dsc_ref[at]), rows_bf(dsp_ref[at])
        added(acc_ref, 4, tn(rows_bf(hb_ref[at]), dsc), p == 0)
        added(acc_ref, 5, tn(rows_bf(lat_ref[at]), dsp), p == 0)
        for z in range(4):
            added(acc_ref, z, tn(rows_bf(x_ref[at, :, 256 * z : 256 * z + 256]), dsp), p == 0)
    out_ref[:, :, :, 0], out_ref[:, :, :, 5] = by_share(acc_ref[4]), by_share(acc_ref[5])
    for z in range(4):
        part = acc_ref[z].reshape(4, 2, 4, 8, 1024).astype(BF16)
        for core in range(2):
            out_ref[core, :, z, 1:5] = part[:, core]


def second_slab_kernel(halo, row_len, per_clip, table_ref, act_ref, dy_ref, taps_ref, x_ref, lat_ref, out_ref, pad_ref, acc_ref, red_ref,
                       lred_ref):
    conv_weight(halo, row_len, per_clip, False, table_ref, act_ref, dy_ref, pad_ref, acc_ref)
    for k in range(9):
        at, lane = (3, 768) if k == 8 else (4 + k // 4, 256 * (k % 4))
        out_ref[:, :, :, at, :, lane : lane + 256] = by_share(acc_ref[k // 3, :, 256 * (k % 3) : 256 * (k % 3) + 256])
    for p in chunks(dy_ref.shape[0]):
        at = slice(p, p + BIG)
        x, lat = rows_bf(x_ref[at]), rows_bf(lat_ref[at])
        for j in range(3):
            taps = rows_bf(taps_ref[at, :, 256 * j : 256 * j + 256])
            added(red_ref, j, tn(taps, x), p == 0)
            added(lred_ref, j, tn(taps, lat), p == 0)
    for j in range(3):
        out_ref[:, :, :, j] = by_share(red_ref[j])
        out_ref[:, :, :, 3, :, 256 * j : 256 * j + 256] = by_share(lred_ref[j])


def fast_grads_kernel(halo, row_len, per_clip, table_ref, act_ref, dy_ref, taps_ref, fx_ref, h_ref, dfc_ref, lat_ref, out_ref,
                      pad_ref, sp_ref, first_ref, ex_ref):
    conv_weight(halo, row_len, per_clip, True, table_ref, act_ref, dy_ref, pad_ref, sp_ref)
    for p in chunks(dy_ref.shape[0]):
        at = slice(p, p + BIG)
        added(first_ref, slice(0, 896), tn(rows_bf(taps_ref[at]), rows_bf(fx_ref[at])), p == 0)
        added(ex_ref, slice(0, 128), tn(rows_bf(h_ref[at]), rows_bf(dfc_ref[at])), p == 0)

    def gather(at, count, r, ref=first_ref):
        return sum(lane_group(moved(ref[at : at + count, 128 * z : 128 * z + 128], 32 * z - 32 * r), z) for z in range(4))

    taps = [gather(640, 256, 2), gather(640, 256, 3), gather(384, 256, 0), gather(384, 256, 1), gather(384, 256, 2)]
    for j in range(5):
        lat_ref[:, 8 * j : 8 * j + 8] = taps[j].reshape(4, 8, 8, 128).astype(BF16)

    def tiles(first, v):
        for i in range(v.shape[0] // 8):
            out_ref[first + i] = v[8 * i : 8 * i + 8].astype(BF16)

    for j in range(3):
        total = sum(gather(32 * q, 32, q + j - 1) for q in range(4) if 0 <= q + j - 1 < 4)
        if j == 0:
            total = total + gather(128, 32, 3)
        if j == 2:
            total = total + gather(352, 32, 0)
        tiles(4 * j, total)
    tiles(12, sum(gather(32 * r, 32, r, ex_ref) for r in range(4)))
    for i in range(3):
        total = None
        for j in range(3):
            tap = sum(
                lane_group(moved(sp_ref[i, 128 * j + 32 * r : 128 * j + 32 * r + 32, :], 32 * j - 32 * r), j) for r in range(4)
            )
            total = tap if total is None else total + tap
        tiles(16 + 4 * i, total)


def swap(tree, axis, size, distance):
    pairs = [(i, i ^ distance) for i in range(size)]
    return jax.tree.map(lambda v: lax.ppermute(v, axis, pairs), tree)


def add(*trees):
    def total(*vs):
        wide_vs = [v.astype(F32) for v in vs]
        out = wide_vs[0] + wide_vs[1]
        if len(vs) == 4:
            out = out + (wide_vs[2] + wide_vs[3])
        return out.astype(vs[0].dtype)

    return jax.tree.map(total, *trees)


def stages(size, first_alone):
    bits = [1 << i for i in range(size.bit_length() - 1)]
    out = []
    if first_alone and bits:
        out.append(bits[:1])
        bits = bits[1:]
    while bits:
        out.append(bits[:2])
        bits = bits[2:]
    return out


def butterfly(tree, axis, size, bits):
    if len(bits) == 1:
        return add(tree, swap(tree, axis, size, bits[0]))
    near, far, both = (swap(tree, axis, size, k) for k in (bits[0], bits[1], bits[0] + bits[1]))
    return add(tree, near, far, both)


def everywhere(tree, sizes, bulk=None, chan_last=False):
    dp, chan = sizes["dp"], sizes["chan"]
    first, *others = stages(dp, True)
    before, behind = (others, []) if chan_last else ([], others)
    for bits in [first, *before]:
        tree = butterfly(tree, "dp", dp, bits)
    if bulk is not None:
        tree = after(tree, bulk)
    for bits in stages(chan, False):
        tree = butterfly(tree, "chan", chan, bits)
    passed = tree
    for bits in behind:
        tree = butterfly(tree, "dp", dp, bits)
    return tree, passed


def halos(first, last, count):
    low = lax.ppermute(last, "chan", [(i, i + 1) for i in range(count - 1)])
    high = lax.ppermute(first, "chan", [(i + 1, i) for i in range(count - 1)])
    return low, high


def gather_chips(v, sizes):
    return [v] + [swap(v, "dp", sizes["dp"], 2 * k) for k in (1, 2, 3)]


def gather_cores(own, sizes):
    return jnp.stack(own), jnp.stack([swap(v, "dp", sizes["dp"], 1) for v in own])


def pick(v, index, axis):
    return lax.dynamic_index_in_dim(v, index, axis, keepdims=False)


def scatter_cores(v, sizes, group):
    sent, kept = pick(v, 1 - group % 2, 0), pick(v, group % 2, 0)
    got = jnp.concatenate([swap(sent[:2], "dp", sizes["dp"], 1), swap(sent[2:], "dp", sizes["dp"], 1)])
    return add(kept, got)


def scatter_chips(v, sizes, group):
    chip = group // 2
    got = [swap(pick(v, chip ^ k, 0), "dp", sizes["dp"], 2 * k) for k in (1, 2, 3)]
    return add(pick(v, chip, 0), *got)


def scatter_chan(tree, sizes, chan, gate):
    size, dp = sizes["chan"], sizes["dp"]
    got = [swap(jax.tree.map(lambda v: pick(v, chan ^ k, 0), tree), "chan", size, k) for k in (1, 2, 3)]
    tree = add(jax.tree.map(lambda v: pick(v, chan, 0), tree), *after(got, gate))
    bits = [1 << i for i in range(3, dp.bit_length() - 1)]
    while bits:
        tree = butterfly(tree, "dp", dp, bits[:2])
        bits = bits[2:]
    return tree


def after(tree, gate):
    return lax.optimization_barrier((tree, gate))[0]


def local(
    sizes,
    slow_input,
    fast_input,
    clip_counts,
    frame_counts,
    fast_reduce,
    fast_spatial,
    fast_expand,
    lateral_kernel,
    slow_reduce,
    lateral_reduce,
    slow_spatial,
    slow_expand,
    shortcut,
    lateral_shortcut,
    fast_inner_norm,
    fast_outer_norm,
    lateral_norm,
    slow_inner_norm,
    slow_outer_norm,
    slow_cotangent,
    fast_cotangent,
):
    ways = sizes["chan"]
    clips, slow_t, height, across, slow_part = slow_input.shape
    fast_t, fast_part = fast_input.shape[1], fast_input.shape[4]
    ratio = fast_t // slow_t
    area = height * across
    places = clips * area
    mine = places // ways
    halo = across + 1
    chan, dp = lax.axis_index("chan"), lax.axis_index("dp")
    group = dp % 8
    ids = jnp.stack([dp, chan, group]).astype(jnp.int32)
    wide_in = ways * slow_part
    wide_f = ways * 128
    mid = 256
    ext = mine + 2 * halo
    per_clip = area // BIG
    chunk = 98

    def packed(v, slow=None):
        v = v.transpose(0, 2, 3, 1, 4).reshape(places, fast_t, fast_part)
        more = [] if slow is None else [slow.reshape(places, slow_t, slow_part)]
        width = 128 if slow is None else 128 + slow_part
        return pl.pallas_call(
            functools.partial(pack_kernel, area // chunk, clips),
            grid=(places // chunk,),
            out_shape=shape((places, slow_t, width), BF16),
            in_specs=[pl.BlockSpec(memory_space=pltpu.SMEM)] * 3
            + [pl.BlockSpec((chunk, *u.shape[1:]), lambda i: (i, 0, 0)) for u in (v, *more)],
            out_specs=pl.BlockSpec((chunk, slow_t, width), lambda i: (i, 0, 0)),
            scratch_shapes=[pltpu.VMEM((chunk * fast_t, fast_part), F32)],
            compiler_params=pltpu.CompilerParams(vmem_limit_bytes=16 * 1024 * 1024),
            name="fast_pack",
        )(ids, clip_counts, frame_counts, v, *more).reshape(ways, mine, slow_t, width)

    def unpacked(parts):
        slow, fast = call(
            unpack_kernel,
            [shape((places, slow_t, slow_part), BF16), shape((places, fast_t, fast_part), BF16)],
            [ids, *parts],
            [pltpu.VMEM((BIG * fast_t, fast_part), F32)],
            smem=1,
            name="outputs",
        )
        return joined(slow), fast.reshape(clips, height, across, fast_t, fast_part).transpose(0, 3, 1, 2, 4)

    def split(v):
        return v.transpose(0, 2, 3, 1, 4).reshape(ways, mine, slow_t, slow_part)

    def joined(v):
        return v.reshape(clips, height, across, slow_t, slow_part).transpose(0, 3, 1, 2, 4)

    def at_once(v):
        return [v[0]] + [swap(v[k], "chan", ways, k) for k in range(1, ways)]

    def blocks_of(v):
        return [pick(v, chan ^ k, 0) for k in range(ways)]

    def all_to_all(v):
        return lax.all_to_all(v, "chan", 0, 0, tiled=True)

    def parted(blocks):
        bounds = PARTS + ((len(blocks), 0),)
        ends = [b[1] if a[0] == b[0] else mine for a, b in zip(bounds, bounds[1:])]
        return [blocks[k][begin:end] for (k, begin), end in zip(PARTS, ends)]

    def send_parts(parts, which, gate):
        for i in which:
            parts[i] = swap(after(parts[i], gate), "chan", ways, PARTS[i][0])


    all_clips = frame_counts.shape[0]
    live = (jnp.arange(all_clips, dtype=jnp.int32) % clips) < jnp.repeat(clip_counts, clips)
    valid = jnp.where(live, frame_counts, 0)
    count = jnp.sum(valid).astype(F32) * area
    inv_n = jnp.stack([1.0 / count, 1.0 / (count * ratio)])
    parts = mine // BIG
    clip = (chan * parts + jnp.arange(-1, parts + 1)) // per_clip
    clip = jnp.clip(clip, 0, clips - 1) + dp * clips
    around = jnp.sum(jnp.where(clip[:, None] == jnp.arange(all_clips)[None, :], valid[None, :], 0), axis=1)
    table = jnp.concatenate([around, jnp.stack([chan, jnp.full_like(chan, parts)])]).astype(jnp.int32)

    lat_t, red_t, lred_t = (v.transpose(0, 2, 1) for v in (lateral_kernel, slow_reduce, lateral_reduce))
    spatial_t = slow_spatial.reshape(9, slow_spatial.shape[2], -1).transpose(0, 2, 1)
    params = [red_t, lred_t, lat_t, slow_expand, shortcut, lateral_shortcut, spatial_t]
    scratch = [(3, 8, wide_in), (3, 8, mid), (5, 8, 128), (8, wide_in), (32, wide_in), (8, wide_in), (9, 8, mid)]
    small = [lateral_norm, slow_inner_norm, slow_outer_norm]
    any_spec, vmem_spec = pl.BlockSpec(memory_space=pl.ANY), pl.BlockSpec(memory_space=pltpu.VMEM)
    slab = pl.pallas_call(
        weight_slab_kernel,
        out_shape=shape((14, 8, wide_in), BF16),
        in_specs=[pl.BlockSpec(memory_space=pltpu.SMEM)] + [any_spec] * 7 + [vmem_spec] * 3,
        out_specs=vmem_spec,
        scratch_shapes=[pltpu.VMEM(dims, F32) for dims in scratch] + [pltpu.SemaphoreType.DMA((7,))],
        compiler_params=pltpu.CompilerParams(vmem_limit_bytes=58 * 1024 * 1024),
        name="weight_slab",
    )(ids, *params, *small)
    slabs = at_once([slab] * ways)
    fx_pieces = at_once(after(blocks_of(packed(after(fast_input, slab))), slabs))
    early, late = jnp.stack([v[0:5] for v in slabs]), jnp.stack([v[5:14] for v in slabs])
    early = gather_chips(early, sizes)
    xs = all_to_all(after(split(slow_input), (fx_pieces, early)))
    own_slabs, other_slabs = gather_cores(early, sizes)
    fr_t = fast_reduce.transpose(0, 2, 1)
    red_w, lred_w, w_first, w_fsp, w_fex, fin_g, fout_g, mid_g, out_g = call(
        weights_kernel,
        [
            shape((3, ways, 8, 8, wide_in), BF16),
            shape((3, ways, 8, 8, mid), BF16),
            shape((896, wide_f), BF16),
            shape((9, 128, 128), BF16),
            shape((128, wide_f), BF16),
            shape((4, 128)),
            shape((2, wide_f)),
            shape((8, mid)),
            shape((ways, 4, mid)),
        ],
        [ids, own_slabs, other_slabs, fr_t, fast_spatial.reshape(9, *fast_spatial.shape[2:]), fast_expand,
         fast_inner_norm.reshape(4, -1), fast_outer_norm],
        [pltpu.VMEM((5, ways, 8, 8, 128), F32)],
        smem=1,
        name="weights",
    )
    red_w, lred_w = red_w.reshape(-1, wide_in), lred_w.reshape(-1, mid)
    fin_g = (fin_g[0:2], fin_g[2:4])
    lat_g, in_g = mid_g[0:2], (mid_g[2:4], mid_g[4:6])
    out_g = out_g.transpose(1, 0, 2).reshape(4, wide_in)

    edge = [shape((halo, 8, 128))] * 2
    edges = [shape((halo, 8, 512))] * 2
    narrow, middle = shape((mine, 8, 128)), shape((mine, 8, mid))
    fx, fa, lp, sums1, first, last = call(
        fast_first_kernel,
        [shape((mine, 8, wide_f), BF16), narrow, middle, shape((2, 384)), *edge],
        [table, *fx_pieces, w_first],
        smem=1,
        name="fast_first",
    )
    fa_lo, fa_hi = halos(first, last, ways)
    cots = parted(blocks_of(packed(fast_cotangent, split(slow_cotangent))))
    late = gather_chips(after(late, other_slabs), sizes)
    own_late, other_late = gather_cores(late, sizes)
    exp_w, short_w, lshort_w, spat_w = call(
        more_weights_kernel,
        [
            shape((ways, 8, 8, wide_in), BF16),
            shape((ways, 8, 4, 8, wide_in), BF16),
            shape((ways, 8, 8, wide_in), BF16),
            shape((9, ways, 8, 8, mid), BF16),
        ],
        [ids, own_late, other_late],
        smem=1,
        name="more_weights",
    )
    exp_w, short_w, lshort_w = (v.reshape(-1, wide_in) for v in (exp_w, short_w, lshort_w))
    spat_w = spat_w.reshape(9, mid, mid)
    sums1, passed = everywhere(sums1, sizes, (xs, fa_lo, fa_hi, cots, late), True)
    send_parts(cots, (2,), passed)
    fast_pad = [pltpu.VMEM((3, ext, 8, 128), F32)]
    slow_pad = [pltpu.VMEM((3, ext, 8, mid), F32)]
    x, lat, sa, sums2, first, last = call(
        slow_first_kernel,
        [shape((mine, 8, wide_in), BF16), shape((mine, 8, mid), BF16), middle, shape((2, mid)), *[shape((halo, 8, mid))] * 2],
        [table, inv_n, xs, lp, sums1, lat_g, red_w, lred_w],
        smem=2,
        name="slow_first",
    )
    sa_lo, sa_hi = halos(first, last, ways)
    fa_late = after(fa, sums2)
    h1, fb, fb_sums = call(
        functools.partial(conv_kernel, halo, across, per_clip, True, (0, 0)),
        [shape((ext, 8, 128), BF16), narrow, shape((2, 128))],
        [table, inv_n, sums1, fin_g[0], fa_lo, fa_late, fa_hi, w_fsp],
        fast_pad,
        smem=2,
        name="fast_second",
    )
    sums2, passed = everywhere(sums2, sizes, (cots[2], sa_lo, sa_hi))
    send_parts(cots, (3, 4, 1), passed)
    ha, sb, sums3 = call(
        functools.partial(conv_kernel, halo, across, per_clip, False, (0, 0)),
        [shape((ext, 8, mid), BF16), middle, shape((2, mid + 128))],
        [table, inv_n, sums2, in_g[0], sa_lo, sa, sa_hi, spat_w, fb_sums],
        slow_pad,
        smem=2,
        name="slow_second",
    )
    sums3, passed = everywhere(sums3, sizes, (cots[3], cots[4], cots[1]))
    send_parts(cots, (5,), passed)
    sp, sp_sums = call(
        bypass_kernel,
        [shape((mine, 8, wide_in), BF16), shape((2, wide_in))],
        [table, x, lat, short_w, lshort_w],
        smem=1,
        name="bypass",
    )
    h2, fc, fc_sums = call(
        functools.partial(expand_kernel, True, mid),
        [shape((mine, 8, 128), BF16), shape((mine, 8, wide_f), BF16), shape((2, wide_f))],
        [table, inv_n, fb, sums3, fin_g[1], w_fex],
        smem=2,
        name="fast_third",
    )
    hb, sc, sums4 = call(
        functools.partial(expand_kernel, False, 0),
        [shape((mine, 8, mid), BF16), shape((mine, 8, wide_in), BF16), shape((2, 2 * wide_in + wide_f))],
        [table, inv_n, sb, sums3, in_g[1], exp_w, sp_sums, fc_sums],
        smem=2,
        name="slow_third",
    )
    sums4, _ = everywhere(sums4, sizes, cots[5])
    fast_out, dfs, fc_slopes = call(
        functools.partial(fast_out_kernel, 2 * wide_in),
        [shape((ways, mine, 8, 128), BF16), shape((mine, 8, wide_f), BF16), shape((2, wide_f))],
        [table, inv_n, fc, sums4, fout_g, fx, *cots],
        [pltpu.VMEM((8, wide_f), F32)],
        smem=2,
        name="fast_out",
    )
    *outs, dss, sums5 = call(
        slow_out_kernel,
        [*[shape(c.shape, BF16) for c in cots], shape((mine, 8, wide_in), BF16), shape((2, 2 * wide_in + wide_f))],
        [table, inv_n, sc, sp, sums4, out_g, *cots, fast_out, fc_slopes],
        [pltpu.VMEM((8, wide_in), F32)],
        smem=2,
        name="slow_out",
    )

    sums5, passed = everywhere(sums5, sizes)
    send_parts(outs, (2,), passed)
    dfc, dzfb, fb_slopes, first, last = call(
        functools.partial(expand_back_kernel, True, (2 * wide_in, 2 * wide_in, mid)),
        [shape((mine, 8, wide_f), BF16), narrow, shape((2, 128)), *edges],
        [table, inv_n, dfs, fc, sums4, fout_g, sums5, fb, sums3, fin_g[1], w_fex, sb],
        smem=2,
        name="fast_third_back",
    )
    low6, high6 = halos(first, last, ways)
    dsc, dzsb, sums6, first, last = call(
        functools.partial(expand_back_kernel, False, (0, 0, 0)),
        [shape((mine, 8, wide_in), BF16), middle, shape((2, mid + 128)), *[shape((halo, 8, mid))] * 2],
        [table, inv_n, dss, sc, sums4, out_g[0:2], sums5, sb, sums3, in_g[1], exp_w, fb_slopes],
        smem=2,
        name="slow_third_back",
    )
    low_sb, high_sb = halos(first, last, ways)
    sums6, passed = everywhere(sums6, sizes, (outs[2], low6, high6, low_sb, high_sb))
    send_parts(outs, (3, 4, 1), passed)
    dfb, dzfa, fa_slopes = call(
        functools.partial(conv_back_kernel, halo, across, per_clip, True, (mid, mid, 0, 384, 0)),
        [shape((mine, 8, 128), BF16), narrow, shape((2, 128))],
        [table, inv_n, sums3, fin_g[1], sums6, low6, fb, high6, low6, dzfb, high6, w_fsp, fa, sums1, fin_g[0]],
        fast_pad,
        smem=2,
        name="fast_second_back",
    )
    dsb, dzsa, sums7 = call(
        functools.partial(conv_back_kernel, halo, across, per_clip, False, (0, 0, 0, 128, 0)),
        [shape((mine, 8, mid), BF16), middle, shape((2, mid + 128))],
        [table, inv_n, sums3, in_g[1], sums6, low6, sb, high6, low_sb, dzsb, high_sb, spat_w, sa, sums2, in_g[0], fa_slopes],
        slow_pad,
        smem=2,
        name="slow_second_back",
    )
    dss_late, = after((dss,), sums7)
    dsp, dx, dl = call(
        bypass_back_kernel,
        [shape((mine, 8, wide_in), BF16), shape((mine, 8, wide_in), BF16), middle],
        [table, inv_n, dss_late, sp, sums4, out_g[2:4], sums5, short_w, lshort_w],
        smem=2,
        name="bypass_back",
    )

    sums7, passed = everywhere(sums7, sizes, (outs[3], outs[4], outs[1], dx, dl))
    send_parts(outs, (5,), passed)
    dsa, dslow, dzlp, sums8 = call(
        slow_back_kernel,
        [shape((mine, 8, 3 * mid), BF16), shape((ways, mine, 8, mid), BF16), middle, shape((2, mid))],
        [table, inv_n, dzsa, sa, sums2, in_g[0], sums7, red_w, lred_w, dx, dl, lp, sums1, lat_g],
        smem=2,
        name="slow_first_back",
    )
    dsc_late, dsp = after((dsc, dsp), sums8)
    (slab1,) = call(
        first_slab_kernel,
        [shape((2, 4, ways, 6, 8, wide_in), BF16)],
        [hb, dsc_late, x, lat, dsp],
        [pltpu.VMEM((6, mid, wide_in), F32)],
        name="first_slab",
    )
    sums8, passed = everywhere(sums8, sizes, (outs[5], slab1))
    dslow = all_to_all(after(dslow, passed))
    slab1 = scatter_cores(slab1, sizes, group)
    dsa, dsb_late = after((dsa, dsb), (sums8, slab1))
    (slab2,) = call(
        functools.partial(second_slab_kernel, halo, across, per_clip),
        [shape((2, 4, ways, 6, 8, wide_in), BF16)],
        [table, ha, dsb_late, dsa, x, lat],
        [*slow_pad, pltpu.VMEM((3, mid, 3 * mid), F32), pltpu.VMEM((3, mid, wide_in), F32), pltpu.VMEM((3, mid, mid), F32)],
        smem=1,
        name="second_slab",
    )
    slab1 = scatter_chips(slab1, sizes, group)
    slab2 = scatter_cores(slab2, sizes, group)
    dzlp = after(dzlp, slab2)
    slab2 = scatter_chips(slab2, sizes, group)
    dfirst, dfast = call(
        functools.partial(fast_back_kernel, mid),
        [shape((mine, 8, 896), BF16), shape((ways, mine, 8, 128), BF16)],
        [table, inv_n, sums1, fin_g[0], lat_g, sums7, sums8, dzfa, fa, dzlp, lp, dfs, w_first],
        smem=2,
        name="fast_first_back",
    )

    g_lat, g_fast = call(
        functools.partial(fast_grads_kernel, halo, across, per_clip),
        [shape((ways, 40, 8, 128), BF16), shape((28, 8, 128), BF16)],
        [table, h1, dfb, dfirst, fx, h2, dfc],
        [*fast_pad, pltpu.VMEM((3, 384, 128), F32), pltpu.VMEM((896, wide_f), F32), pltpu.VMEM((128, wide_f), F32)],
        smem=1,
        name="fast_grads",
    )
    (slow_input_grad,) = call(
        copy_kernel, [shape((places, slow_t, slow_part), BF16)], [dslow.reshape(places, slow_t, slow_part)], name="slow_grad"
    )
    slow_output, fast_output = unpacked(after(outs, slow_input_grad))
    slab1 = scatter_chan(slab1, sizes, chan, dfirst)
    slab2 = scatter_chan(after(slab2, slab1), sizes, chan, slab1)
    slabs = jnp.concatenate([slab1, slab2])
    small = [jnp.concatenate([pick(g_lat, chan ^ k, 0), g_fast]) for k in range(ways)]
    small = add(*at_once(small))
    dfast = all_to_all(after(dfast, (dslow, slabs, small)))
    for bits in stages(sizes["dp"], True):
        small = butterfly(small, "dp", sizes["dp"], bits)
    g_lat, g_fast = small[0:40].astype(F32), small[40:68].astype(F32)
    own_slabs, other_slabs = gather_cores(after(gather_chips(slabs, sizes), (slow_output, fast_output)), sizes)
    g_exp, g_short, g_lshort, g_red, g_lred, g_spat = call(
        grads_kernel,
        [shape((8, 8, wide_in)), shape((8, 4, 8, wide_in)), shape((8, 8, wide_in)), shape((3, 8, 8, wide_in)), shape((3, 8, 8, mid)),
         shape((9, 8, 8, mid))],
        [ids, own_slabs, other_slabs],
        smem=1,
        name="grads",
    )
    slow_input_grad = joined(slow_input_grad)
    fast_input_grad = pl.pallas_call(
        unpack_fast_kernel,
        grid=(places // chunk,),
        out_shape=shape((places, fast_t, fast_part), BF16),
        in_specs=[pl.BlockSpec((chunk, slow_t, 128), lambda i: (i, 0, 0))],
        out_specs=pl.BlockSpec((chunk, fast_t, fast_part), lambda i: (i, 0, 0)),
        scratch_shapes=[pltpu.VMEM((chunk * fast_t, fast_part), F32)],
        compiler_params=pltpu.CompilerParams(vmem_limit_bytes=16 * 1024 * 1024),
        name="fast_unpack",
    )(dfast.reshape(places, slow_t, 128))
    fast_input_grad = fast_input_grad.reshape(clips, height, across, fast_t, fast_part).transpose(0, 3, 1, 2, 4)
    g_fred = g_fast[0:12].reshape(3, 32, 128).transpose(0, 2, 1)
    g_fex = g_fast[12:16].reshape(32, 128)
    g_fsp = g_fast[16:28].reshape(3, 32, 128)[:, :, 0:96].reshape(3, 32, 3, 32).transpose(0, 2, 1, 3)

    def pair(slopes):
        return slopes[::-1]

    def own(v, width):
        return lax.dynamic_slice_in_dim(v, chan * width, width, v.ndim - 1)

    def fold_in(slopes):
        return jnp.sum(slopes.reshape(2, ratio, 128 // ratio), axis=1)

    lw, sw, ow = lateral_norm.shape[1], slow_inner_norm.shape[2], slow_outer_norm.shape[2]
    fast_inner_grad = jnp.stack([pair(fold_in(sums7[:, mid:])), pair(fold_in(sums6[:, mid:]))])
    fc_slopes = sums5[:, 2 * wide_in :].reshape(2, ways, ratio, fast_part)
    fast_outer_grad = pair(jnp.sum(fc_slopes, axis=2).reshape(2, -1))
    lateral_grad = pair(own(sums8, lw))
    slow_inner_grad = own(jnp.stack([pair(sums7[:, 0:mid]), pair(sums6[:, 0:mid])]), sw)
    slow_outer_grad = own(jnp.stack([pair(sums5[:, 0:wide_in]), pair(sums5[:, wide_in : 2 * wide_in])]), ow)
    return (
        slow_output,
        fast_output,
        slow_input_grad,
        fast_input_grad,
        g_fred,
        g_fsp,
        g_fex,
        g_lat.reshape(5, -1, 128).transpose(0, 2, 1),
        g_red.reshape(3, -1, wide_in).transpose(0, 2, 1),
        g_lred.reshape(3, -1, mid).transpose(0, 2, 1),
        g_spat.reshape(9, -1, mid).transpose(0, 2, 1).reshape(slow_spatial.shape),
        g_exp.reshape(-1, wide_in),
        g_short.reshape(-1, wide_in),
        g_lshort.reshape(-1, wide_in),
        fast_inner_grad,
        fast_outer_grad,
        lateral_grad,
        slow_inner_grad,
        slow_outer_grad,
    )


def solution(mesh):
    sizes = {"dp": mesh.shape["dp"], "chan": mesh.shape["chan"]}
    big = P("dp", None, None, None, "chan")
    last2, last3, last4 = P(None, "chan"), P(None, None, "chan"), P(None, None, None, "chan")
    first = P("chan", None)
    return jax.shard_map(
        functools.partial(local, sizes),
        mesh=mesh,
        in_specs=(
            big, big, P(), P(), P(), P(), P(), last3, last3, last3, last4, first, first, first,
            P(), P(), last2, last3, last3, big, big,
        ),
        out_specs=(
            big, big, big, big, P(), P(), P(), last3, last3, last3, last4, first, first, first,
            P(), P(), last2, last3, last3,
        ),
        check_vma=False,
    )
```
